32 devices in a mesh: gx: 4 (over z), gy: 2 (over x), gz: 4 (over y, core).
Axes of the slice: x: 2, y: 2, z: 4, core: 2. Of those that a mesh axis runs over, the one named last changes fastest.
Arguments:
- vel_x: float32 [64, 32, 256], P('gx', 'gz', 'gy'), may hold values from -6 to 6
- vel_y: float32 [64, 32, 256], P('gx', 'gz', 'gy'), may hold values from -6 to 6
- vel_z: float32 [64, 32, 256], P('gx', 'gz', 'gy'), may hold values from -6 to 6
- pressure: float32 [64, 32, 256], P('gx', 'gz', 'gy'), may hold values from -6 to 6
- phase: int32 [64, 32, 256], P('gx', 'gz', 'gy'), may hold values from 0 to 3
- visc_scale: float32 [4], replicated, may hold values from 0.5 to 2
- power_n: float32 [4], replicated, may hold values from 1 to 4
- density: float32 [4], replicated, may hold values from 0.5 to 1.5
Outputs:
- out_vx: float32 [64, 32, 256], P('gx', 'gz', 'gy')
- out_vy: float32 [64, 32, 256], P('gx', 'gz', 'gy')
- out_vz: float32 [64, 32, 256], P('gx', 'gz', 'gy')
- out_p: float32 [64, 32, 256], P('gx', 'gz', 'gy')
- out_eta: float32 [64, 32, 256], P('gx', 'gz', 'gy')
The draws below stay inside these ranges and needn't reach their ends.
All inputs are finite; a program needn't handle non-finite values.
Results may differ from the reference program's by a relative error of at most 0.00013.
Values sent between devices are 32-bit elements; how exact they have to be, the bound alone decides.
No kernel may reach another device: no remote copies, remote signals or barrier semaphores. Data moves between devices by JAX's collectives and lax.ppermute only.
A program may use at most 64 MiB of HBM per device.

```python
import math
import jax
import jax.numpy as jnp
from jax import lax

ITERS = 4
PHASES = 4
NX = 64
NZ = 32
NY = 256


def plant(drawn, key, smallest, largest):
    longest = drawn.shape.index(max(drawn.shape))
    spots = []
    for shift in (0, 1):
        where = [jax.random.randint(jax.random.fold_in(key, axis), (), 0, length) for axis, length in enumerate(drawn.shape)]
        where[longest] = (where[longest] + shift) % drawn.shape[longest]
        spots.append(tuple(where))
    return drawn.at[spots[0]].set(smallest).at[spots[1]].set(largest)


def block_levels(stream_key, shape, cuts, low, high):
    loudness, own = 1.0, jax.random.fold_in(stream_key, 6)
    for position, blocks in cuts:
        steps = jnp.exp(jax.random.uniform(jax.random.fold_in(own, position), (blocks,), jnp.float32, low / len(cuts), high / len(cuts)))
        loudness = loudness * jnp.repeat(steps, shape[position] // blocks).reshape([-1 if axis == position else 1 for axis in range(len(shape))])
    return loudness


def normal_values(rng, dims, width, reach, split=(), dtype=jnp.bfloat16):
    drawn = jax.random.normal(rng, dims, jnp.float32) * width
    if len(split) > 0:
        drawn = block_levels(rng, dims, split, -0.22, 0.18) * drawn
    return jnp.clip(drawn, min=-reach, max=reach).astype(dtype)


def setup_inputs(seed: int = 0) -> dict:
    key_of = jax.random.split(jax.random.key(seed), 9)
    vel_x = normal_values(key_of[0], (NX, NZ, NY), 1.0, 6.0, ((0, 4), (1, 4), (2, 2)), jnp.float32)
    vel_y = normal_values(key_of[1], (NX, NZ, NY), 1.0, 6.0, ((0, 4), (1, 4), (2, 2)), jnp.float32)
    vel_z = normal_values(key_of[2], (NX, NZ, NY), 1.0, 6.0, ((0, 4), (1, 4), (2, 2)), jnp.float32)
    pressure = normal_values(key_of[3], (NX, NZ, NY), 1.0, 6.0, ((0, 4), (1, 4), (2, 2)), jnp.float32)
    phase = plant(jax.random.randint(key_of[4], (NX, NZ, NY), 0, PHASES), jax.random.fold_in(key_of[4], 1), 0, PHASES - 1).astype(jnp.int32)
    visc_scale = jnp.clip(jnp.exp(jax.random.uniform(key_of[5], (PHASES,), jnp.float32, math.log(0.5), math.log(2.0))), 0.5, 2.0)
    power_n = jnp.clip(jax.random.uniform(key_of[6], (PHASES,), jnp.float32, 1.0, 4.0), 1.0, 4.0)
    density = jnp.clip(jax.random.uniform(key_of[7], (PHASES,), jnp.float32, 0.5, 1.5), 0.5, 1.5)
    return {"vel_x": vel_x, "vel_y": vel_y, "vel_z": vel_z, "pressure": pressure, "phase": phase, "visc_scale": visc_scale, "power_n": power_n, "density": density}


strain_floor = 1.0
pressure_step = 0.5
velocity_step = 0.1


def lookup(phase, table):
    out = jnp.zeros(phase.shape, jnp.float32)
    for index in range(PHASES):
        out = out + jnp.where(phase == index, table[index], jnp.float32(0.0))
    return out


def strain_rate_list(padded):
    strain_rate_first = padded[0, 2:, 1:-1, 1:-1] - padded[0, 1:-1, 1:-1, 1:-1]
    strain_rate_second = padded[1, 1:-1, 2:, 1:-1] - padded[1, 1:-1, 1:-1, 1:-1]
    strain_rate_third = padded[2, 1:-1, 1:-1, 2:] - padded[2, 1:-1, 1:-1, 1:-1]
    return strain_rate_first, strain_rate_second, strain_rate_third


def viscosity(strain_rate_first, strain_rate_second, strain_rate_third, prefactor, exponent):
    div = strain_rate_first + strain_rate_second + strain_rate_third
    third = div / 3.0
    inv = 0.5 * ((strain_rate_first - third) ** 2 + (strain_rate_second - third) ** 2 + (strain_rate_third - third) ** 2) + strain_floor
    eta = prefactor * jnp.exp(0.5 * (1.0 / exponent - 1.0) * jnp.log(inv))
    return eta, div


def slice_along(field, offset, grid_extent):
    return field[1 + offset[0]:1 + offset[0] + grid_extent[0], 1 + offset[1]:1 + offset[1] + grid_extent[1], 1 + offset[2]:1 + offset[2] + grid_extent[2]]


def unit(sweep_heading, sign):
    offset = [0, 0, 0]
    offset[sweep_heading] = sign
    return tuple(offset)


def joined(first, second):
    return tuple(first[n] + second[n] for n in range(3))


def residual_field(sweep_heading, padded_velocity, padded_pressure, padded_viscosity, grid_extent):
    zero_scalar = (0, 0, 0)
    backward_neighbor = unit(sweep_heading, -1)
    middle_slice = slice_along(padded_velocity, zero_scalar, grid_extent)
    viscosity_current = slice_along(padded_viscosity, zero_scalar, grid_extent)
    viscosity_backward = slice_along(padded_viscosity, backward_neighbor, grid_extent)
    momentum_residual = -(slice_along(padded_pressure, zero_scalar, grid_extent) - slice_along(padded_pressure, backward_neighbor, grid_extent))
    for other in range(3):
        upper_neighbor = unit(other, 1)
        lower_neighbor = unit(other, -1)
        if other == sweep_heading:
            momentum_residual = momentum_residual + viscosity_current * (slice_along(padded_velocity, upper_neighbor, grid_extent) - middle_slice) - viscosity_backward * (middle_slice - slice_along(padded_velocity, backward_neighbor, grid_extent))
        else:
            viscosity_above = 0.25 * (viscosity_current + viscosity_backward + slice_along(padded_viscosity, upper_neighbor, grid_extent) + slice_along(padded_viscosity, joined(backward_neighbor, upper_neighbor), grid_extent))
            viscosity_below = 0.25 * (viscosity_current + viscosity_backward + slice_along(padded_viscosity, lower_neighbor, grid_extent) + slice_along(padded_viscosity, joined(backward_neighbor, lower_neighbor), grid_extent))
            momentum_residual = momentum_residual + viscosity_above * (slice_along(padded_velocity, upper_neighbor, grid_extent) - middle_slice) - viscosity_below * (middle_slice - slice_along(padded_velocity, lower_neighbor, grid_extent))
    return momentum_residual, 0.5 * (viscosity_current + viscosity_backward)


def reference(vel_x, vel_y, vel_z, pressure, phase, visc_scale, power_n, density):
    grid_extent = pressure.shape
    coords = [lax.broadcasted_iota(jnp.int32, grid_extent, axis_number) for axis_number in range(3)]
    velocity = [jnp.where(coords[axis_number] == 0, jnp.float32(0.0), v) for axis_number, v in enumerate((vel_x, vel_z, vel_y))]
    prefactor = lookup(phase, visc_scale)
    exponent = lookup(phase, power_n)
    rho = lookup(phase, density)
    total_cells = float(grid_extent[0] * grid_extent[1] * grid_extent[2])
    eta = prefactor
    for step in range(ITERS):
        stacked_rates = jnp.pad(jnp.stack(velocity), ((0, 0), (1, 1), (1, 1), (1, 1)))
        strain_rate_first, strain_rate_second, strain_rate_third = strain_rate_list(stacked_rates)
        eta, div = viscosity(strain_rate_first, strain_rate_second, strain_rate_third, prefactor, exponent)
        pressure = pressure - pressure_step * eta * div
        pressure = pressure - jnp.sum(pressure) / total_cells
        padded_pressure = jnp.pad(pressure, 1)
        padded_viscosity = jnp.pad(eta, 1)
        updated = []
        for axis_number in range(3):
            momentum_residual, face_slice = residual_field(axis_number, stacked_rates[axis_number], padded_pressure, padded_viscosity, grid_extent)
            if axis_number == 1:
                momentum_residual = momentum_residual - rho
            fresh = velocity[axis_number] + velocity_step * momentum_residual / face_slice
            updated.append(jnp.where(coords[axis_number] == 0, jnp.float32(0.0), fresh))
        velocity = updated
    return velocity[0], velocity[2], velocity[1], pressure, eta
```

```python
import math

import jax
import jax.numpy as jnp
from jax import lax
from jax.experimental import pallas as pl
from jax.experimental.pallas import tpu as pltpu
from jax.sharding import PartitionSpec as P

ITERS = 4
PHASES = 4
LOW = ITERS
HIGH = 2 * ITERS
FIELDS = 5
LANE_STEP = 16

VMEM = pl.BlockSpec(memory_space=pltpu.VMEM)
SMEM = pl.BlockSpec(memory_space=pltpu.SMEM)


def z_up(a):
    return pltpu.roll(a, a.shape[0] - 1, 0)


def z_down(a):
    return pltpu.roll(a, 1, 0)


def y_up(a):
    return pltpu.roll(a, a.shape[1] - 1, 1)


def y_down(a):
    return pltpu.roll(a, 1, 1)


def reciprocal(a):
    r = pl.reciprocal(a, approx=True)
    return r * (2.0 - a * r)


def pack_kernel(vx_ref, vz_ref, vy_ref, p_ref, phase_ref, stack_ref, edge_ref):
    bx, bz, by = p_ref.shape
    ix, iz, iy = lax.axis_index("gx"), lax.axis_index("gz"), lax.axis_index("gy")
    lane = lax.broadcasted_iota(jnp.int32, (bz, by), 1)
    row = lax.broadcasted_iota(jnp.int32, (bz, by), 0)
    keep_z = (row > 0) | (iz > 0)
    keep_y = (lane > 0) | (iy > 0)

    def plane(i, carry):
        vx = vx_ref[i] * jnp.where((i > 0) | (ix > 0), 1.0, 0.0)
        vz = jnp.where(keep_z, vz_ref[i], 0.0)
        vy = jnp.where(keep_y, vy_ref[i], 0.0)
        fields = (vx, vz, vy, p_ref[i], phase_ref[i].astype(jnp.float32))
        edge = jnp.zeros((bz, by), jnp.float32)
        for f, a in enumerate(fields):
            stack_ref[i, f] = a
            at = LANE_STEP * f
            first = pltpu.roll(a, at, 1) if at else a
            edge = jnp.where((lane >= at) & (lane < at + HIGH), first, edge)
            last = pltpu.roll(a, at + LANE_STEP, 1)
            edge = jnp.where((lane >= at + LANE_STEP - LOW) & (lane < at + LANE_STEP), last, edge)
        edge_ref[i] = edge
        return carry

    lax.fori_loop(0, bx, plane, 0)


def main_kernel(
    own_ref, above_ref, below_ref, scale_ref, power_ref, rho_table_ref,
    out_vx_ref, out_vz_ref, out_vy_ref, out_p_ref, out_eta_ref, sum_ref,
    va_ref, vb_ref, p_ref, pre_ref, power_field_ref, rho_ref, weight_ref,
):
    bz, by = own_ref.shape[2:]
    bx = own_ref.shape[0] - LOW - HIGH
    rows, lanes = 3 * bz, 2 * by
    nx, nz, ny = lax.axis_size("gx"), lax.axis_size("gz"), lax.axis_size("gy")
    ix, iz, iy = lax.axis_index("gx"), lax.axis_index("gz"), lax.axis_index("gy")

    lane = lax.broadcasted_iota(jnp.int32, (bz, by), 1)
    right = (lane < HIGH) & (iy < ny - 1)
    left = (lane >= by - LOW) & (iy > 0)

    def unpack(i, carry):
        x_in = (i + ix * bx >= LOW) & (i + ix * bx < LOW + nx * bx)
        for t, (ref, z_in) in enumerate(((own_ref, None), (above_ref, iz < nz - 1), (below_ref, iz > 0))):
            at = pl.ds(t * bz, bz)
            ok = x_in if z_in is None else x_in & z_in
            ok = jnp.where(ok, 1.0, 0.0)
            edge = ref[i, FIELDS]
            for f in range(FIELDS):
                middle = ref[i, f]
                shift = LANE_STEP * f
                a = pltpu.roll(edge, (by - shift) % by, 1) if shift else edge
                b = pltpu.roll(edge, (by - LANE_STEP - shift) % by, 1)
                side = jnp.where(right, a, jnp.where(left, b, 0.0))
                if f < 3:
                    va_ref[f, i, at, 0:by] = middle
                    va_ref[f, i, at, by:lanes] = side
                elif f == 3:
                    p_ref[i, at, 0:by] = middle
                    p_ref[i, at, by:lanes] = side
                else:
                    for part, (ph, keep) in enumerate(((middle, None), (side, right | left))):
                        to = pl.ds(part * by, by)
                        values = []
                        for table in (scale_ref, power_ref, rho_table_ref):
                            value = table[0]
                            for index in range(1, PHASES):
                                value = jnp.where(ph == float(index), table[index], value)
                            values.append(jnp.broadcast_to(value, (bz, by)))
                        pre = values[0] * ok
                        if keep is not None:
                            pre = jnp.where(keep, pre, 0.0)
                        pre_ref[i, at, to] = pre
                        power_field_ref[i, at, to] = values[1]
                        rho_ref[i, at, to] = values[2]
        return carry

    lax.fori_loop(0, bx + LOW + HIGH, unpack, 0)

    r = lax.broadcasted_iota(jnp.int32, (rows, lanes), 0)
    c = lax.broadcasted_iota(jnp.int32, (rows, lanes), 1)
    zg = iz * bz + jnp.where(r < 2 * bz, r, r - rows)
    yg = iy * by + jnp.where(c < by + HIGH, c, c - lanes)
    filled = (c < by + HIGH) | (c >= lanes - LOW)
    inside = filled & (zg >= 0) & (zg < nz * bz) & (yg >= 0) & (yg < ny * by)
    weight_ref[0] = jnp.where(inside, 0.05, 0.0)
    weight_ref[1] = jnp.where(inside & (zg > 0), 0.05, 0.0)
    weight_ref[2] = jnp.where(inside & (yg > 0), 0.05, 0.0)
    weight_ref[3] = jnp.where(inside, 0.0, 1.0)

    for k in range(1, ITERS + 1):
        old, new = (va_ref, vb_ref) if k % 2 else (vb_ref, va_ref)
        last = k == ITERS

        def cell(j):
            vx, vz, vy = old[0, j], old[1, j], old[2, j]
            rx = old[0, j + 1] - vx
            rz = z_up(vz) - vz
            ry = y_up(vy) - vy
            a = rx - ry
            b = ry - rz
            inv = (a * (a + b) + b * b) * (1.0 / 3.0) + 1.0
            eta = pre_ref[j] * jnp.exp2(power_field_ref[j] * jnp.log(inv))
            quarter = 0.25 * eta
            div = rx + ry + rz
            p = p_ref[j] - quarter * (div + div)
            p_ref[j] = p
            tx, tz, ty = eta * rx - p, eta * rz - p, eta * ry - p
            sz = quarter + z_down(quarter)
            sy = quarter + y_down(quarter)
            return eta, p, quarter, tx, tz, ty, sz, sy

        def step(j, carry):
            quarter0, tx0, sz0, sy0, part_z0, part_y0, scale_z0, scale_y0 = carry
            eta, p, quarter, tx, tz, ty, sz, sy = cell(j)
            vx, vz, vy = old[0, j], old[1, j], old[2, j]
            vz0, vy0 = old[1, j - 1], old[2, j - 1]
            bias = weight_ref[3]
            sx = quarter + quarter0
            exz = sz + sz0
            exy = sy + sy0
            ezy = sz + y_down(sz)
            fxz = exz * (vx - z_down(vx))
            fxy = exy * (vx - y_down(vx))
            gzx = exz * (vz - vz0)
            hyx = exy * (vy - vy0)
            gzy = ezy * (vz - y_down(vz))
            hyz = ezy * (vy - z_down(vy))
            res_x = (tx - tx0) + ((z_up(fxz) - fxz) + (y_up(fxy) - fxy))
            new_vx = vx + weight_ref[0] * reciprocal(sx + bias) * res_x
            new_vz = vz0 + scale_z0 * (part_z0 + gzx)
            new_vy = vy0 + scale_y0 * (part_y0 + hyx)
            part_z = (tz - z_down(tz)) - rho_ref[j] + ((y_up(gzy) - gzy) - gzx)
            part_y = (ty - y_down(ty)) + ((z_up(hyz) - hyz) - hyx)
            scale_z = weight_ref[1] * reciprocal(sz + bias)
            scale_y = weight_ref[2] * reciprocal(sy + bias)
            if last:
                out_vx_ref[j - LOW] = new_vx[0:bz, 0:by]
                out_p_ref[j - LOW] = p[0:bz, 0:by]
                out_eta_ref[j - LOW] = eta[0:bz, 0:by]
                sum_ref[...] += p[0:bz, 0:by]
            else:
                new[0, j] = new_vx

            def finish():
                if last:
                    out_vz_ref[j - 1 - LOW] = new_vz[0:bz, 0:by]
                    out_vy_ref[j - 1 - LOW] = new_vy[0:bz, 0:by]
                else:
                    new[1, j - 1] = new_vz
                    new[2, j - 1] = new_vy

            return (quarter, tx, sz, sy, part_z, part_y, scale_z, scale_y), finish

        first, count = k, bx + LOW + HIGH - 3 * k
        if last:
            sum_ref[...] = jnp.zeros((bz, by), jnp.float32)
        eta, p, quarter, tx, tz, ty, sz, sy = cell(first - 1)
        zero = jnp.zeros((rows, lanes), jnp.float32)
        carry, _ = step(first, (quarter, tx, sz, sy, zero, zero, zero, zero))

        def loop(j, carry):
            carry, finish = step(j, carry)
            finish()
            return carry

        carry = lax.fori_loop(first + 1, first + count, loop, carry)
        j = first + count
        quarter0, tx0, sz0, sy0, part_z0, part_y0, scale_z0, scale_y0 = carry
        eta, p, quarter, tx, tz, ty, sz, sy = cell(j)
        gzx = (sz + sz0) * (old[1, j] - old[1, j - 1])
        hyx = (sy + sy0) * (old[2, j] - old[2, j - 1])
        new_vz = old[1, j - 1] + scale_z0 * (part_z0 + gzx)
        new_vy = old[2, j - 1] + scale_y0 * (part_y0 + hyx)
        if last:
            out_vz_ref[j - 1 - LOW] = new_vz[0:bz, 0:by]
            out_vy_ref[j - 1 - LOW] = new_vy[0:bz, 0:by]
        else:
            new[1, j - 1] = new_vz
            new[2, j - 1] = new_vy

        if last:
            @pl.when(ix == 0)
            def _():
                out_vx_ref[0] = jnp.zeros((bz, by), jnp.float32)
        else:
            plane = jnp.zeros((rows, lanes), jnp.float32)

            @pl.when(ix == 0)
            def _():
                for i in range(k, LOW):
                    for d in range(3):
                        new[d, i] = plane
                new[0, LOW] = plane

            @pl.when(ix == nx - 1)
            def _():
                for i in range(LOW + bx, first + count):
                    for d in range(3):
                        new[d, i] = plane


def final_kernel(p_ref, sum_ref, out_ref, *, cells):
    mean = jnp.sum(sum_ref[...]) * (1.0 / cells)
    out_ref[...] = p_ref[...] - mean


def shift(a, axis, step):
    count = lax.axis_size(axis)
    return lax.ppermute(a, axis, [(i, i + step) for i in range(count) if 0 <= i + step < count])


def swap_sum(a, axis):
    count = lax.axis_size(axis)
    if count & (count - 1):
        return lax.psum(a, axis)
    bit = 1
    while bit < count:
        a = a + lax.ppermute(a, axis, [(i, i ^ bit) for i in range(count)])
        bit *= 2
    return a


def local(vel_x, vel_y, vel_z, pressure, phase, visc_scale, power_n, density):
    bx, bz, by = pressure.shape
    f32 = jnp.float32
    counts = [lax.axis_size(a) for a in ("gx", "gz", "gy")]
    cells = bx * bz * by * math.prod(counts)
    deep = bx + LOW + HIGH
    block = jax.ShapeDtypeStruct((bx, bz, by), f32)

    stack, edge = pl.pallas_call(
        pack_kernel,
        out_shape=(jax.ShapeDtypeStruct((bx, FIELDS, bz, by), f32), block),
        in_specs=[VMEM] * 5,
        out_specs=(VMEM, VMEM),
    )(vel_x, vel_z, vel_y, pressure, phase)

    lane = lax.broadcasted_iota(jnp.int32, (bx, bz, by), 2)
    if counts[2] == 2:
        side = lax.ppermute(edge, "gy", [(0, 1), (1, 0)])
    else:
        side = jnp.where(lane % LANE_STEP < HIGH, shift(edge, "gy", -1), shift(edge, "gy", 1))
    stack = jnp.concatenate([stack, side[:, None]], axis=1)
    low = shift(stack[bx - LOW :], "gx", 1)
    high = shift(stack[:HIGH], "gx", -1)
    stack = jnp.concatenate([low, stack, high], axis=0)
    above = shift(stack, "gz", -1)
    below = shift(stack, "gz", 1)

    power = (0.5 / math.log(2.0)) * (1.0 / power_n - 1.0)
    scratch = lambda *shape: pltpu.VMEM(shape, f32)
    rows, lanes = 3 * bz, 2 * by
    vx, vz, vy, p, eta, total = pl.pallas_call(
        main_kernel,
        out_shape=(block,) * 5 + (jax.ShapeDtypeStruct((bz, by), f32),),
        in_specs=[VMEM] * 3 + [SMEM] * 3,
        out_specs=(VMEM,) * 6,
        scratch_shapes=[
            scratch(3, deep, rows, lanes),
            scratch(3, deep, rows, lanes),
            scratch(deep, rows, lanes),
            scratch(deep, rows, lanes),
            scratch(deep, rows, lanes),
            scratch(deep, rows, lanes),
            scratch(4, rows, lanes),
        ],
        compiler_params=pltpu.CompilerParams(vmem_limit_bytes=32 * 1024 * 1024),
    )(stack, above, below, visc_scale, power, density)

    for axis in ("gz", "gy", "gx"):
        total = swap_sum(total, axis)
    p = pl.pallas_call(
        lambda *refs: final_kernel(*refs, cells=float(cells)),
        out_shape=block,
        in_specs=[VMEM] * 2,
        out_specs=VMEM,
    )(p, total)
    return (vx, vy, vz, p, eta)


def solution(mesh):
    spec = P("gx", "gz", "gy")
    return jax.shard_map(
        local,
        mesh=mesh,
        in_specs=(spec,) * 5 + (P(),) * 3,
        out_specs=(spec,) * 5,
        check_vma=False,
    )
```

```python
import math

import jax
import jax.numpy as jnp
from jax import lax
from jax.experimental import pallas as pl
from jax.experimental.pallas import tpu as pltpu
from jax.sharding import PartitionSpec as P

ITERS = 4
PHASES = 4
LOW = ITERS
HIGH = 2 * ITERS
FIELDS = 5
LANE_STEP = 16
UNROLL = 3

VMEM = pl.BlockSpec(memory_space=pltpu.VMEM)
SMEM = pl.BlockSpec(memory_space=pltpu.SMEM)


def z_up(a):
    return pltpu.roll(a, a.shape[-2] - 1, a.ndim - 2)


def z_down(a):
    return pltpu.roll(a, 1, a.ndim - 2)


def y_up(a):
    return pltpu.roll(a, a.shape[-1] - 1, a.ndim - 1)


def y_down(a):
    return pltpu.roll(a, 1, a.ndim - 1)


def reciprocal(a):
    r = pl.reciprocal(a, approx=True)
    return r * (2.0 - a * r)


def merged(k, bz):
    return 3 * (ITERS - k + 1) <= bz


def pack_kernel(vx_ref, vz_ref, vy_ref, p_ref, phase_ref, stack_ref, edge_ref):
    bx, bz, by = p_ref.shape
    ix, iz, iy = lax.axis_index("gx"), lax.axis_index("gz"), lax.axis_index("gy")
    lane = lax.broadcasted_iota(jnp.int32, (bz, by), 1)
    row = lax.broadcasted_iota(jnp.int32, (bz, by), 0)
    keep_z = (row > 0) | (iz > 0)
    keep_y = (lane > 0) | (iy > 0)

    def plane(i, carry):
        vx = vx_ref[i] * jnp.where((i > 0) | (ix > 0), 1.0, 0.0)
        vz = jnp.where(keep_z, vz_ref[i], 0.0)
        vy = jnp.where(keep_y, vy_ref[i], 0.0)
        fields = (vx, vz, vy, p_ref[i], phase_ref[i].astype(jnp.float32))
        edge = jnp.zeros((bz, by), jnp.float32)
        for f, a in enumerate(fields):
            stack_ref[i, f] = a
            at = LANE_STEP * f
            first = pltpu.roll(a, at, 1) if at else a
            edge = jnp.where((lane >= at) & (lane < at + HIGH), first, edge)
            last = pltpu.roll(a, at + LANE_STEP, 1)
            edge = jnp.where((lane >= at + LANE_STEP - LOW) & (lane < at + LANE_STEP), last, edge)
        edge_ref[i] = edge
        return carry

    lax.fori_loop(0, bx, plane, 0)


def main_kernel(
    own_ref, above_ref, below_ref, scale_ref, power_ref, rho_table_ref,
    out_vx_ref, out_vz_ref, out_vy_ref, out_p_ref, out_eta_ref, sum_ref,
    va_ref, vb_ref, p_ref, pre_ref, power_field_ref, rho_ref, pre2_ref, power2_field_ref, rho2_ref,
    weight_ref, weight2_ref,
):
    bz, by = own_ref.shape[2:]
    bx = own_ref.shape[0] - LOW - HIGH
    lanes = 2 * by
    nx, nz, ny = lax.axis_size("gx"), lax.axis_size("gz"), lax.axis_size("gy")
    ix, iz, iy = lax.axis_index("gx"), lax.axis_index("gz"), lax.axis_index("gy")

    lane = lax.broadcasted_iota(jnp.int32, (bz, by), 1)
    right = (lane < HIGH) & (iy < ny - 1)
    left = (lane >= by - LOW) & (iy > 0)

    def unpack(i, carry):
        x_in = (i + ix * bx >= LOW) & (i + ix * bx < LOW + nx * bx)
        for t, (ref, z_in) in enumerate(((own_ref, None), (above_ref, iz < nz - 1), (below_ref, iz > 0))):
            at = pl.ds(t * bz, bz)
            ok = x_in if z_in is None else x_in & z_in
            ok = jnp.where(ok, 1.0, 0.0)
            edge = ref[i, FIELDS]
            for f in range(FIELDS):
                middle = ref[i, f]
                shift = LANE_STEP * f
                a = pltpu.roll(edge, (by - shift) % by, 1) if shift else edge
                b = pltpu.roll(edge, (by - LANE_STEP - shift) % by, 1)
                side = jnp.where(right, a, jnp.where(left, b, 0.0))
                if f < 3:
                    va_ref[f, i, at, 0:by] = middle
                    va_ref[f, i, at, by:lanes] = side
                elif f == 3:
                    p_ref[i, at, 0:by] = middle
                    p_ref[i, at, by:lanes] = side
                else:
                    for part, (ph, keep) in enumerate(((middle, None), (side, right | left))):
                        to = pl.ds(part * by, by)
                        values = []
                        for table in (scale_ref, power_ref, rho_table_ref):
                            value = table[0]
                            for index in range(1, PHASES):
                                value = jnp.where(ph == float(index), table[index], value)
                            values.append(jnp.broadcast_to(value, (bz, by)))
                        pre = values[0] * ok
                        if keep is not None:
                            pre = jnp.where(keep, pre, 0.0)
                        pre_ref[i, at, to] = pre
                        power_field_ref[i, at, to] = values[1]
                        rho_ref[i, at, to] = values[2]
        row = lax.broadcasted_iota(jnp.int32, (bz, lanes), 0)
        for full, half in ((pre_ref, pre2_ref), (power_field_ref, power2_field_ref), (rho_ref, rho2_ref)):
            half[i, 0:bz] = full[i, 0:bz]
            half[i, bz : 2 * bz] = jnp.where(row < bz // 2, full[i, bz : 2 * bz], full[i, 2 * bz :])
        return carry

    lax.fori_loop(0, bx + LOW + HIGH, unpack, 0)

    for ref, high in ((weight_ref, 2 * bz), (weight2_ref, bz + bz // 2)):
        shape = ref.shape[1:]
        r = lax.broadcasted_iota(jnp.int32, shape, 0)
        c = lax.broadcasted_iota(jnp.int32, shape, 1)
        zg = iz * bz + jnp.where(r < high, r, r - shape[0])
        yg = iy * by + jnp.where(c < by + HIGH, c, c - lanes)
        filled = (c < by + HIGH) | (c >= lanes - LOW)
        inside = filled & (zg >= 0) & (zg < nz * bz) & (yg >= 0) & (yg < ny * by)
        ref[0] = jnp.where(inside, 0.05, 0.0)
        ref[1] = jnp.where(inside & (zg > 0), 0.05, 0.0)
        ref[2] = jnp.where(inside & (yg > 0), 0.05, 0.0)
        ref[3] = jnp.where(inside, 0.0, 1.0)

    for k in range(1, ITERS + 1):
        old, new = (va_ref, vb_ref) if k % 2 else (vb_ref, va_ref)
        last = k == ITERS
        rows = 2 * bz if merged(k, bz) else 3 * bz
        constants = (pre2_ref, power2_field_ref, rho2_ref) if merged(k, bz) else (pre_ref, power_field_ref, rho_ref)
        weight = weight2_ref if merged(k, bz) else weight_ref
        narrow = merged(k + 1, bz) and not merged(k, bz)
        all_rows = pl.ds(0, rows)

        def keep(value):
            if narrow:
                row = lax.broadcasted_iota(jnp.int32, (bz, lanes), 0)
                halo = jnp.where(row < bz // 2, value[..., bz : 2 * bz, :], value[..., 2 * bz :, :])
                return [(pl.ds(0, bz), value[..., 0:bz, :]), (pl.ds(bz, bz), halo)]
            return [(all_rows, value)]

        def store(d, j, count, value):
            for at, part in keep(value):
                new[d, pl.ds(j, count), at, :] = part

        def cells(j, count):
            planes = pl.ds(j, count)
            vx1 = old[0, pl.ds(j, count + 1), all_rows, :]
            vx = vx1[:count]
            vz, vy = old[1, planes, all_rows, :], old[2, planes, all_rows, :]
            p = p_ref[planes, all_rows, :]
            rx = vx1[1:] - vx
            rz = z_up(vz) - vz
            ry = y_up(vy) - vy
            a = rx - ry
            b = ry - rz
            inv = (a * (a + b) + b * b) * (1.0 / 3.0) + 1.0
            eta = constants[0][planes] * jnp.exp2(constants[1][planes] * jnp.log(inv))
            quarter = 0.25 * eta
            div = rx + ry + rz
            p = p - quarter * (div + div)
            tx, tz, ty = eta * rx - p, eta * rz - p, eta * ry - p
            sz = quarter + z_down(quarter)
            sy = quarter + y_down(quarter)
            return vx, vz, vy, eta, p, quarter, tx, tz, ty, sz, sy

        def chunk(j, count, carry, start=False):
            planes = pl.ds(j, count)
            vx, vz, vy, eta, p, quarter, tx, tz, ty, sz, sy = cells(j, count)
            vz0, vy0 = old[1, pl.ds(j - 1, 1), all_rows, :], old[2, pl.ds(j - 1, 1), all_rows, :]
            quarter0, tx0, sz0, sy0, part_z0, part_y0, scale_z0, scale_y0 = carry
            join = lambda first, rest: jnp.concatenate([first, rest[:-1]], axis=0) if count > 1 else first
            bias = weight[3:4]
            sx = quarter + join(quarter0, quarter)
            exz = sz + join(sz0, sz)
            exy = sy + join(sy0, sy)
            ezy = sz + y_down(sz)
            fxz = exz * (vx - z_down(vx))
            fxy = exy * (vx - y_down(vx))
            low_vz, low_vy = join(vz0, vz), join(vy0, vy)
            gzx = exz * (vz - low_vz)
            hyx = exy * (vy - low_vy)
            gzy = ezy * (vz - y_down(vz))
            hyz = ezy * (vy - z_down(vy))
            res_x = (tx - join(tx0, tx)) + ((z_up(fxz) - fxz) + (y_up(fxy) - fxy))
            new_vx = vx + weight[0:1] * reciprocal(sx + bias) * res_x
            part_z = (tz - z_down(tz)) - constants[2][planes] + ((y_up(gzy) - gzy) - gzx)
            part_y = (ty - y_down(ty)) + ((z_up(hyz) - hyz) - hyx)
            scale_z = weight[1:2] * reciprocal(sz + bias)
            scale_y = weight[2:3] * reciprocal(sy + bias)
            new_vz = low_vz + join(scale_z0, scale_z) * (join(part_z0, part_z) + gzx)
            new_vy = low_vy + join(scale_y0, scale_y) * (join(part_y0, part_y) + hyx)
            if last:
                at = pl.ds(j - LOW, count)
                out_vx_ref[at] = new_vx[:, 0:bz, 0:by]
                out_p_ref[at] = p[:, 0:bz, 0:by]
                out_eta_ref[at] = eta[:, 0:bz, 0:by]
                sum_ref[...] += jnp.sum(p[:, 0:bz, 0:by], axis=0)
                if not start:
                    at = pl.ds(j - 1 - LOW, count)
                    out_vz_ref[at] = new_vz[:, 0:bz, 0:by]
                    out_vy_ref[at] = new_vy[:, 0:bz, 0:by]
            else:
                for at, part in keep(p):
                    p_ref[planes, at, :] = part
                store(0, j, count, new_vx)
                if not start:
                    store(1, j - 1, count, new_vz)
                    store(2, j - 1, count, new_vy)
            return tuple(a[-1:] for a in (quarter, tx, sz, sy, part_z, part_y, scale_z, scale_y))

        first, count = k, bx + LOW + HIGH - 3 * k
        if last:
            sum_ref[...] = jnp.zeros((bz, by), jnp.float32)
        _, _, _, _, p, quarter, tx, _, _, sz, sy = cells(first - 1, 1)
        if not last:
            for at, part in keep(p):
                p_ref[pl.ds(first - 1, 1), at, :] = part
        zero = jnp.zeros((1, rows, lanes), jnp.float32)
        carry = chunk(first, 1, (quarter, tx, sz, sy, zero, zero, zero, zero), start=True)
        steps, rest = divmod(count - 1, UNROLL)
        carry = lax.fori_loop(
            0, steps, lambda s, carry: chunk(first + 1 + s * UNROLL, UNROLL, carry), carry
        )
        if rest:
            carry = chunk(first + 1 + steps * UNROLL, rest, carry)
        j = first + count
        quarter0, tx0, sz0, sy0, part_z0, part_y0, scale_z0, scale_y0 = carry
        _, vz, vy, _, p, quarter, tx, _, _, sz, sy = cells(j, 1)
        vz0, vy0 = old[1, pl.ds(j - 1, 1), all_rows, :], old[2, pl.ds(j - 1, 1), all_rows, :]
        new_vz = vz0 + scale_z0 * (part_z0 + (sz + sz0) * (vz - vz0))
        new_vy = vy0 + scale_y0 * (part_y0 + (sy + sy0) * (vy - vy0))
        if last:
            out_vz_ref[pl.ds(j - 1 - LOW, 1)] = new_vz[:, 0:bz, 0:by]
            out_vy_ref[pl.ds(j - 1 - LOW, 1)] = new_vy[:, 0:bz, 0:by]
        else:
            for at, part in keep(p):
                p_ref[pl.ds(j, 1), at, :] = part
            store(1, j - 1, 1, new_vz)
            store(2, j - 1, 1, new_vy)

        if last:
            @pl.when(ix == 0)
            def _():
                out_vx_ref[0] = jnp.zeros((bz, by), jnp.float32)
        else:
            plane = jnp.zeros((3 * bz, lanes), jnp.float32)

            @pl.when(ix == 0)
            def _():
                for i in range(k, LOW):
                    for d in range(3):
                        new[d, i] = plane
                new[0, LOW] = plane

            @pl.when(ix == nx - 1)
            def _():
                for i in range(LOW + bx, first + count):
                    for d in range(3):
                        new[d, i] = plane


def final_kernel(p_ref, sum_ref, out_ref, *, cells):
    mean = jnp.sum(sum_ref[...]) * (1.0 / cells)
    out_ref[...] = p_ref[...] - mean


def shift(a, axis, step):
    count = lax.axis_size(axis)
    return lax.ppermute(a, axis, [(i, i + step) for i in range(count) if 0 <= i + step < count])


def swap_sum(a, axis):
    count = lax.axis_size(axis)
    if count & (count - 1):
        return lax.psum(a, axis)
    bit = 1
    while bit < count:
        a = a + lax.ppermute(a, axis, [(i, i ^ bit) for i in range(count)])
        bit *= 2
    return a


def local(vel_x, vel_y, vel_z, pressure, phase, visc_scale, power_n, density):
    bx, bz, by = pressure.shape
    f32 = jnp.float32
    counts = [lax.axis_size(a) for a in ("gx", "gz", "gy")]
    cells = bx * bz * by * math.prod(counts)
    deep = bx + LOW + HIGH
    block = jax.ShapeDtypeStruct((bx, bz, by), f32)

    stack, edge = pl.pallas_call(
        pack_kernel,
        out_shape=(jax.ShapeDtypeStruct((bx, FIELDS, bz, by), f32), block),
        in_specs=[VMEM] * 5,
        out_specs=(VMEM, VMEM),
        compiler_params=pltpu.CompilerParams(vmem_limit_bytes=4 * 1024 * 1024),
    )(vel_x, vel_z, vel_y, pressure, phase)

    lane = lax.broadcasted_iota(jnp.int32, (bx, bz, by), 2)
    if counts[2] == 2:
        side = lax.ppermute(edge, "gy", [(0, 1), (1, 0)])
    else:
        side = jnp.where(lane % LANE_STEP < HIGH, shift(edge, "gy", -1), shift(edge, "gy", 1))
    stack = jnp.concatenate([stack, side[:, None]], axis=1)
    low = shift(stack[bx - LOW :], "gx", 1)
    high = shift(stack[:HIGH], "gx", -1)
    stack = jnp.concatenate([low, stack, high], axis=0)
    above = shift(stack, "gz", -1)
    below = shift(stack, "gz", 1)

    power = (0.5 / math.log(2.0)) * (1.0 / power_n - 1.0)
    scratch = lambda *shape: pltpu.VMEM(shape, f32)
    rows, lanes = 3 * bz, 2 * by
    vx, vz, vy, p, eta, total = pl.pallas_call(
        main_kernel,
        out_shape=(block,) * 5 + (jax.ShapeDtypeStruct((bz, by), f32),),
        in_specs=[VMEM] * 3 + [SMEM] * 3,
        out_specs=(VMEM,) * 6,
        scratch_shapes=[
            scratch(3, deep, rows, lanes),
            scratch(3, deep, rows, lanes),
            scratch(deep, rows, lanes),
            scratch(deep, rows, lanes),
            scratch(deep, rows, lanes),
            scratch(deep, rows, lanes),
            scratch(deep, 2 * bz, lanes),
            scratch(deep, 2 * bz, lanes),
            scratch(deep, 2 * bz, lanes),
            scratch(4, rows, lanes),
            scratch(4, 2 * bz, lanes),
        ],
        compiler_params=pltpu.CompilerParams(vmem_limit_bytes=32 * 1024 * 1024),
    )(stack, above, below, visc_scale, power, density)

    for axis in ("gz", "gy", "gx"):
        total = swap_sum(total, axis)
    p = pl.pallas_call(
        lambda *refs: final_kernel(*refs, cells=float(cells)),
        out_shape=block,
        in_specs=[VMEM] * 2,
        out_specs=VMEM,
        compiler_params=pltpu.CompilerParams(vmem_limit_bytes=4 * 1024 * 1024),
    )(p, total)
    return (vx, vy, vz, p, eta)


def solution(mesh):
    spec = P("gx", "gz", "gy")
    return jax.shard_map(
        local,
        mesh=mesh,
        in_specs=(spec,) * 5 + (P(),) * 3,
        out_specs=(spec,) * 5,
        check_vma=False,
    )
```

```python
import math

import jax
import jax.numpy as jnp
from jax import lax
from jax.experimental import pallas as pl
from jax.experimental.pallas import tpu as pltpu
from jax.sharding import PartitionSpec as P

ITERS = 4
PHASES = 4
LOW = ITERS
HIGH = 2 * ITERS
FIELDS = 5
LANE_STEP = 16
UNROLL = 3

VMEM = pl.BlockSpec(memory_space=pltpu.VMEM)
SMEM = pl.BlockSpec(memory_space=pltpu.SMEM)


def z_up(a):
    return pltpu.roll(a, a.shape[-2] - 1, a.ndim - 2)


def z_down(a):
    return pltpu.roll(a, 1, a.ndim - 2)


def y_up(a):
    return pltpu.roll(a, a.shape[-1] - 1, a.ndim - 1)


def y_down(a):
    return pltpu.roll(a, 1, a.ndim - 1)


def reciprocal(a):
    r = pl.reciprocal(a, approx=True)
    return r * (2.0 - a * r)


def merged(k, bz):
    return 3 * (ITERS - k + 1) <= bz


def pack_kernel(vx_ref, vz_ref, vy_ref, p_ref, phase_ref, stack_ref, edge_ref):
    bx, bz, by = p_ref.shape
    ix, iz, iy = lax.axis_index("gx"), lax.axis_index("gz"), lax.axis_index("gy")
    lane = lax.broadcasted_iota(jnp.int32, (bz, by), 1)
    row = lax.broadcasted_iota(jnp.int32, (bz, by), 0)
    keep_z = (row > 0) | (iz > 0)
    keep_y = (lane > 0) | (iy > 0)

    def plane(i, carry):
        vx = vx_ref[i] * jnp.where((i > 0) | (ix > 0), 1.0, 0.0)
        vz = jnp.where(keep_z, vz_ref[i], 0.0)
        vy = jnp.where(keep_y, vy_ref[i], 0.0)
        fields = (vx, vz, vy, p_ref[i], phase_ref[i].astype(jnp.float32))
        edge = jnp.zeros((bz, by), jnp.float32)
        for f, a in enumerate(fields):
            stack_ref[i, f] = a
            at = LANE_STEP * f
            first = pltpu.roll(a, at, 1) if at else a
            edge = jnp.where((lane >= at) & (lane < at + HIGH), first, edge)
            last = pltpu.roll(a, at + LANE_STEP, 1)
            edge = jnp.where((lane >= at + LANE_STEP - LOW) & (lane < at + LANE_STEP), last, edge)
        edge_ref[i] = edge
        return carry

    lax.fori_loop(0, bx, plane, 0)


def main_kernel(
    own_ref, above_ref, below_ref, scale_ref, power_ref, rho_table_ref,
    out_vx_ref, out_vz_ref, out_vy_ref, out_p_ref, out_eta_ref, sum_ref,
    va_ref, vb_ref, p_ref, pre_ref, power_field_ref, rho_ref, pre2_ref, power2_field_ref, rho2_ref,
    weight_ref, weight2_ref,
):
    bz, by = own_ref.shape[2:]
    bx = own_ref.shape[0] - LOW - HIGH
    lanes = 2 * by
    nx, nz, ny = lax.axis_size("gx"), lax.axis_size("gz"), lax.axis_size("gy")
    ix, iz, iy = lax.axis_index("gx"), lax.axis_index("gz"), lax.axis_index("gy")

    lane = lax.broadcasted_iota(jnp.int32, (bz, by), 1)
    right = (lane < HIGH) & (iy < ny - 1)
    left = (lane >= by - LOW) & (iy > 0)

    def unpack(i, carry):
        x_in = (i + ix * bx >= LOW) & (i + ix * bx < LOW + nx * bx)
        for t, (ref, z_in) in enumerate(((own_ref, None), (above_ref, iz < nz - 1), (below_ref, iz > 0))):
            at = pl.ds(t * bz, bz)
            ok = x_in if z_in is None else x_in & z_in
            ok = jnp.where(ok, 1.0, 0.0)
            edge = ref[i, FIELDS]
            for f in range(FIELDS):
                middle = ref[i, f]
                shift = LANE_STEP * f
                a = pltpu.roll(edge, (by - shift) % by, 1) if shift else edge
                b = pltpu.roll(edge, (by - LANE_STEP - shift) % by, 1)
                side = jnp.where(right, a, jnp.where(left, b, 0.0))
                if f < 3:
                    va_ref[f, i, at, 0:by] = middle
                    va_ref[f, i, at, by:lanes] = side
                elif f == 3:
                    p_ref[i, at, 0:by] = middle
                    p_ref[i, at, by:lanes] = side
                else:
                    for part, (ph, keep) in enumerate(((middle, None), (side, right | left))):
                        to = pl.ds(part * by, by)
                        values = []
                        for table in (scale_ref, power_ref, rho_table_ref):
                            value = table[0]
                            for index in range(1, PHASES):
                                value = jnp.where(ph == float(index), table[index], value)
                            values.append(jnp.broadcast_to(value, (bz, by)))
                        pre = values[0] * ok
                        if keep is not None:
                            pre = jnp.where(keep, pre, 0.0)
                        pre_ref[i, at, to] = pre
                        power_field_ref[i, at, to] = values[1]
                        rho_ref[i, at, to] = values[2]
        row = lax.broadcasted_iota(jnp.int32, (bz, lanes), 0)
        for full, half in ((pre_ref, pre2_ref), (power_field_ref, power2_field_ref), (rho_ref, rho2_ref)):
            half[i, 0:bz] = full[i, 0:bz]
            half[i, bz : 2 * bz] = jnp.where(row < bz // 2, full[i, bz : 2 * bz], full[i, 2 * bz :])
        return carry

    lax.fori_loop(0, bx + LOW + HIGH, unpack, 0)

    for ref, high in ((weight_ref, 2 * bz), (weight2_ref, bz + bz // 2)):
        shape = ref.shape[1:]
        r = lax.broadcasted_iota(jnp.int32, shape, 0)
        c = lax.broadcasted_iota(jnp.int32, shape, 1)
        zg = iz * bz + jnp.where(r < high, r, r - shape[0])
        yg = iy * by + jnp.where(c < by + HIGH, c, c - lanes)
        filled = (c < by + HIGH) | (c >= lanes - LOW)
        inside = filled & (zg >= 0) & (zg < nz * bz) & (yg >= 0) & (yg < ny * by)
        ref[0] = jnp.where(inside, 0.05, 0.0)
        ref[1] = jnp.where(inside & (zg > 0), 0.05, 0.0)
        ref[2] = jnp.where(inside & (yg > 0), 0.05, 0.0)
        ref[3] = jnp.where(inside, 0.0, 1.0)

    for k in range(1, ITERS + 1):
        old, new = (va_ref, vb_ref) if k % 2 else (vb_ref, va_ref)
        last = k == ITERS
        rows = 2 * bz if merged(k, bz) else 3 * bz
        constants = (pre2_ref, power2_field_ref, rho2_ref) if merged(k, bz) else (pre_ref, power_field_ref, rho_ref)
        weight = weight2_ref if merged(k, bz) else weight_ref
        narrow = merged(k + 1, bz) and not merged(k, bz)
        all_rows = pl.ds(0, rows)

        def keep(value):
            if narrow:
                row = lax.broadcasted_iota(jnp.int32, (bz, lanes), 0)
                halo = jnp.where(row < bz // 2, value[..., bz : 2 * bz, :], value[..., 2 * bz :, :])
                return [(pl.ds(0, bz), value[..., 0:bz, :]), (pl.ds(bz, bz), halo)]
            return [(all_rows, value)]

        def store(d, j, count, value):
            for at, part in keep(value):
                new[d, pl.ds(j, count), at, :] = part

        def cells(j, count):
            planes = pl.ds(j, count)
            vx1 = old[0, pl.ds(j, count + 1), all_rows, :]
            vx = vx1[:count]
            vz, vy = old[1, planes, all_rows, :], old[2, planes, all_rows, :]
            p = p_ref[planes, all_rows, :]
            rx = vx1[1:] - vx
            rz = z_up(vz) - vz
            ry = y_up(vy) - vy
            a = rx - ry
            b = ry - rz
            inv = (a * (a + b) + b * b) * (1.0 / 3.0) + 1.0
            eta = constants[0][planes] * jnp.exp2(constants[1][planes] * jnp.log(inv))
            quarter = 0.25 * eta
            div = rx + ry + rz
            p = p - quarter * (div + div)
            tx, tz, ty = eta * rx - p, eta * rz - p, eta * ry - p
            sz = quarter + z_down(quarter)
            sy = quarter + y_down(quarter)
            return vx, vz, vy, eta, p, quarter, tx, tz, ty, sz, sy

        def chunk(j, count, carry, start=False):
            planes = pl.ds(j, count)
            vx, vz, vy, eta, p, quarter, tx, tz, ty, sz, sy = cells(j, count)
            vz0, vy0 = old[1, pl.ds(j - 1, 1), all_rows, :], old[2, pl.ds(j - 1, 1), all_rows, :]
            quarter0, tx0, sz0, sy0, part_z0, part_y0, scale_z0, scale_y0 = carry
            join = lambda first, rest: jnp.concatenate([first, rest[:-1]], axis=0) if count > 1 else first
            bias = weight[3:4]
            sx = quarter + join(quarter0, quarter)
            exz = sz + join(sz0, sz)
            exy = sy + join(sy0, sy)
            ezy = sz + y_down(sz)
            fxz = exz * (vx - z_down(vx))
            fxy = exy * (vx - y_down(vx))
            low_vz, low_vy = join(vz0, vz), join(vy0, vy)
            gzx = exz * (vz - low_vz)
            hyx = exy * (vy - low_vy)
            gzy = ezy * (vz - y_down(vz))
            hyz = ezy * (vy - z_down(vy))
            res_x = (tx - join(tx0, tx)) + ((z_up(fxz) - fxz) + (y_up(fxy) - fxy))
            new_vx = vx + weight[0:1] * reciprocal(sx + bias) * res_x
            part_z = (tz - z_down(tz)) - constants[2][planes] + ((y_up(gzy) - gzy) - gzx)
            part_y = (ty - y_down(ty)) + ((z_up(hyz) - hyz) - hyx)
            scale_z = weight[1:2] * reciprocal(sz + bias)
            scale_y = weight[2:3] * reciprocal(sy + bias)
            new_vz = low_vz + join(scale_z0, scale_z) * (join(part_z0, part_z) + gzx)
            new_vy = low_vy + join(scale_y0, scale_y) * (join(part_y0, part_y) + hyx)
            if last:
                at = pl.ds(j - LOW, count)
                out_vx_ref[at] = new_vx[:, 0:bz, 0:by]
                out_p_ref[at] = p[:, 0:bz, 0:by]
                out_eta_ref[at] = eta[:, 0:bz, 0:by]
                sum_ref[...] += jnp.sum(p[:, 0:bz, 0:by], axis=0)
                if not start:
                    at = pl.ds(j - 1 - LOW, count)
                    out_vz_ref[at] = new_vz[:, 0:bz, 0:by]
                    out_vy_ref[at] = new_vy[:, 0:bz, 0:by]
            else:
                for at, part in keep(p):
                    p_ref[planes, at, :] = part
                store(0, j, count, new_vx)
                if not start:
                    store(1, j - 1, count, new_vz)
                    store(2, j - 1, count, new_vy)
            return tuple(a[-1:] for a in (quarter, tx, sz, sy, part_z, part_y, scale_z, scale_y))

        first, count = k, bx + LOW + HIGH - 3 * k
        if last:
            sum_ref[...] = jnp.zeros((bz, by), jnp.float32)
        _, _, _, _, p, quarter, tx, _, _, sz, sy = cells(first - 1, 1)
        if not last:
            for at, part in keep(p):
                p_ref[pl.ds(first - 1, 1), at, :] = part
        zero = jnp.zeros((1, rows, lanes), jnp.float32)
        carry = chunk(first, 1, (quarter, tx, sz, sy, zero, zero, zero, zero), start=True)
        steps, rest = divmod(count - 1, UNROLL)
        carry = lax.fori_loop(
            0, steps, lambda s, carry: chunk(first + 1 + s * UNROLL, UNROLL, carry), carry
        )
        if rest:
            carry = chunk(first + 1 + steps * UNROLL, rest, carry)
        j = first + count
        quarter0, tx0, sz0, sy0, part_z0, part_y0, scale_z0, scale_y0 = carry
        _, vz, vy, _, p, quarter, tx, _, _, sz, sy = cells(j, 1)
        vz0, vy0 = old[1, pl.ds(j - 1, 1), all_rows, :], old[2, pl.ds(j - 1, 1), all_rows, :]
        new_vz = vz0 + scale_z0 * (part_z0 + (sz + sz0) * (vz - vz0))
        new_vy = vy0 + scale_y0 * (part_y0 + (sy + sy0) * (vy - vy0))
        if last:
            out_vz_ref[pl.ds(j - 1 - LOW, 1)] = new_vz[:, 0:bz, 0:by]
            out_vy_ref[pl.ds(j - 1 - LOW, 1)] = new_vy[:, 0:bz, 0:by]
        else:
            for at, part in keep(p):
                p_ref[pl.ds(j, 1), at, :] = part
            store(1, j - 1, 1, new_vz)
            store(2, j - 1, 1, new_vy)

        if last:
            @pl.when(ix == 0)
            def _():
                out_vx_ref[0] = jnp.zeros((bz, by), jnp.float32)
        else:
            plane = jnp.zeros((3 * bz, lanes), jnp.float32)

            @pl.when(ix == 0)
            def _():
                for i in range(k, LOW):
                    for d in range(3):
                        new[d, i] = plane
                new[0, LOW] = plane

            @pl.when(ix == nx - 1)
            def _():
                for i in range(LOW + bx, first + count):
                    for d in range(3):
                        new[d, i] = plane


def final_kernel(p_ref, sum_ref, out_ref, *, cells):
    mean = jnp.sum(sum_ref[...]) * (1.0 / cells)
    out_ref[...] = p_ref[...] - mean


def shift(a, axis, step):
    count = lax.axis_size(axis)
    return lax.ppermute(a, axis, [(i, i + step) for i in range(count) if 0 <= i + step < count])


def local(vel_x, vel_y, vel_z, pressure, phase, visc_scale, power_n, density):
    bx, bz, by = pressure.shape
    f32 = jnp.float32
    counts = [lax.axis_size(a) for a in ("gx", "gz", "gy")]
    cells = bx * bz * by * math.prod(counts)
    deep = bx + LOW + HIGH
    block = jax.ShapeDtypeStruct((bx, bz, by), f32)

    stack, edge = pl.pallas_call(
        pack_kernel,
        out_shape=(jax.ShapeDtypeStruct((bx, FIELDS, bz, by), f32), block),
        in_specs=[VMEM] * 5,
        out_specs=(VMEM, VMEM),
        compiler_params=pltpu.CompilerParams(vmem_limit_bytes=4 * 1024 * 1024),
    )(vel_x, vel_z, vel_y, pressure, phase)

    lane = lax.broadcasted_iota(jnp.int32, (bx, bz, by), 2)
    if counts[2] == 2:
        side = lax.ppermute(edge, "gy", [(0, 1), (1, 0)])
    else:
        side = jnp.where(lane % LANE_STEP < HIGH, shift(edge, "gy", -1), shift(edge, "gy", 1))
    stack = jnp.concatenate([stack, side[:, None]], axis=1)
    low = shift(stack[bx - LOW :], "gx", 1)
    high = shift(stack[:HIGH], "gx", -1)
    stack = jnp.concatenate([low, stack, high], axis=0)
    above = shift(stack, "gz", -1)
    below = shift(stack, "gz", 1)

    power = (0.5 / math.log(2.0)) * (1.0 / power_n - 1.0)
    scratch = lambda *shape: pltpu.VMEM(shape, f32)
    rows, lanes = 3 * bz, 2 * by
    vx, vz, vy, p, eta, total = pl.pallas_call(
        main_kernel,
        out_shape=(block,) * 5 + (jax.ShapeDtypeStruct((bz, by), f32),),
        in_specs=[VMEM] * 3 + [SMEM] * 3,
        out_specs=(VMEM,) * 6,
        scratch_shapes=[
            scratch(3, deep, rows, lanes),
            scratch(3, deep, rows, lanes),
            scratch(deep, rows, lanes),
            scratch(deep, rows, lanes),
            scratch(deep, rows, lanes),
            scratch(deep, rows, lanes),
            scratch(deep, 2 * bz, lanes),
            scratch(deep, 2 * bz, lanes),
            scratch(deep, 2 * bz, lanes),
            scratch(4, rows, lanes),
            scratch(4, 2 * bz, lanes),
        ],
        compiler_params=pltpu.CompilerParams(vmem_limit_bytes=32 * 1024 * 1024),
    )(stack, above, below, visc_scale, power, density)

    devices = math.prod(counts)
    total = jnp.broadcast_to(jnp.sum(total, axis=0, keepdims=True), (devices, by))
    total = lax.all_to_all(total, ("gx", "gy", "gz"), 0, 0, tiled=True)
    p = pl.pallas_call(
        lambda *refs: final_kernel(*refs, cells=float(cells)),
        out_shape=block,
        in_specs=[VMEM] * 2,
        out_specs=VMEM,
        compiler_params=pltpu.CompilerParams(vmem_limit_bytes=4 * 1024 * 1024),
    )(p, total)
    return (vx, vy, vz, p, eta)


def solution(mesh):
    spec = P("gx", "gz", "gy")
    return jax.shard_map(
        local,
        mesh=mesh,
        in_specs=(spec,) * 5 + (P(),) * 3,
        out_specs=(spec,) * 5,
        check_vma=False,
    )
```

```python
import math

import jax
import jax.numpy as jnp
from jax import lax
from jax.experimental import pallas as pl
from jax.experimental.pallas import tpu as pltpu
from jax.sharding import PartitionSpec as P

ITERS = 4
PHASES = 4
LOW = ITERS
HIGH = 2 * ITERS
FIELDS = 5
LANE_STEP = 16
UNROLL = 3

VMEM = pl.BlockSpec(memory_space=pltpu.VMEM)
SMEM = pl.BlockSpec(memory_space=pltpu.SMEM)


def z_up(a):
    return pltpu.roll(a, a.shape[-2] - 1, a.ndim - 2)


def z_down(a):
    return pltpu.roll(a, 1, a.ndim - 2)


def y_up(a):
    return pltpu.roll(a, a.shape[-1] - 1, a.ndim - 1)


def y_down(a):
    return pltpu.roll(a, 1, a.ndim - 1)


def reciprocal(a):
    r = pl.reciprocal(a, approx=True)
    return r * (2.0 - a * r)


def merged(k, bz):
    return 3 * (ITERS - k + 1) <= bz


def own_place(i, bx):
    return lax.rem(i + (1 - lax.rem(lax.axis_index("gx"), 2)) * HIGH, bx)


def pack_kernel(vx_hbm, vz_hbm, vy_hbm, p_hbm, phase_hbm, stack_ref, edge_ref, field_ref, phase_ref, sems):
    bx, bz, by = phase_ref.shape
    sources = (vx_hbm, vz_hbm, vy_hbm, p_hbm, phase_hbm)
    targets = [field_ref.at[f] for f in range(FIELDS - 1)] + [phase_ref]
    copies = [pltpu.make_async_copy(a, b, sems.at[f]) for f, (a, b) in enumerate(zip(sources, targets))]
    for copy in copies:
        copy.start()
    ix, iz, iy = lax.axis_index("gx"), lax.axis_index("gz"), lax.axis_index("gy")
    lane = lax.broadcasted_iota(jnp.int32, (1, bz, by), 2)
    row = lax.broadcasted_iota(jnp.int32, (1, bz, by), 1)
    keep_z = (row > 0) | (iz > 0)
    keep_y = (lane > 0) | (iy > 0)
    for copy in copies:
        copy.wait()

    @pl.when(ix == 0)
    def _():
        field_ref[0, 0] = jnp.zeros((bz, by), jnp.float32)

    count = 4

    def planes(step, carry):
        at = pl.ds(step * count, count)
        to = pl.ds(own_place(step * count, bx), count)
        vx, vz, vy, p = (field_ref[f, at] for f in range(FIELDS - 1))
        vz = jnp.where(keep_z, vz, 0.0)
        vy = jnp.where(keep_y, vy, 0.0)
        edge = jnp.zeros((count, bz, by), jnp.float32)
        for f, a in enumerate((vx, vz, vy, p, phase_ref[at].astype(jnp.float32))):
            stack_ref[to, f] = a
            base = LANE_STEP * f
            first = pltpu.roll(a, base, 2) if base else a
            edge = jnp.where((lane >= base) & (lane < base + HIGH), first, edge)
            last = pltpu.roll(a, base + LANE_STEP, 2)
            edge = jnp.where((lane >= base + LANE_STEP - LOW) & (lane < base + LANE_STEP), last, edge)
        edge_ref[to] = edge
        return carry

    lax.fori_loop(0, bx // count, planes, 0)


def main_kernel(
    own_ref, side_ref, face_0_ref, face_1_ref, corner_0_ref, corner_1_ref, scale_ref, power_ref, rho_table_ref,
    out_vx_ref, out_vz_ref, out_vy_ref, out_p_ref, out_eta_ref, sum_ref,
    va_ref, vb_ref, p_ref, pre_ref, power_field_ref, rho_ref, pre2_ref, power2_field_ref, rho2_ref,
    weight_ref, weight2_ref,
):
    bx, _, bz, by = own_ref.shape
    lanes = 2 * by
    nx, nz, ny = lax.axis_size("gx"), lax.axis_size("gz"), lax.axis_size("gy")
    ix, iz, iy = lax.axis_index("gx"), lax.axis_index("gz"), lax.axis_index("gy")

    lane = lax.broadcasted_iota(jnp.int32, (bz, by), 1)
    right = (lane < HIGH) & (iy < ny - 1)
    left = (lane >= by - LOW) & (iy > 0)

    def unpack(ref, source, i, t, ok):
        at = pl.ds(t * bz, bz)
        ok = jnp.where(ok, 1.0, 0.0)
        edge = ref[source, FIELDS]
        for f in range(FIELDS):
            middle = ref[source, f]
            shift = LANE_STEP * f
            a = pltpu.roll(edge, (by - shift) % by, 1) if shift else edge
            b = pltpu.roll(edge, (by - LANE_STEP - shift) % by, 1)
            side = jnp.where(right, a, jnp.where(left, b, 0.0))
            if f < 3:
                va_ref[f, i, at, 0:by] = middle
                va_ref[f, i, at, by:lanes] = side
            elif f == 3:
                p_ref[i, at, 0:by] = middle
                p_ref[i, at, by:lanes] = side
            else:
                for part, (ph, keep) in enumerate(((middle, None), (side, right | left))):
                    to = pl.ds(part * by, by)
                    values = []
                    for table in (scale_ref, power_ref, rho_table_ref):
                        value = table[0]
                        for index in range(1, PHASES):
                            value = jnp.where(ph == float(index), table[index], value)
                        values.append(jnp.broadcast_to(value, (bz, by)))
                    pre = values[0] * ok
                    if keep is not None:
                        pre = jnp.where(keep, pre, 0.0)
                    pre_ref[i, at, to] = pre
                    power_field_ref[i, at, to] = values[1]
                    rho_ref[i, at, to] = values[2]

    def unpack_planes(own, side, t, ok):
        def own_plane(i, carry):
            unpack(own, own_place(i, bx), LOW + i, t, ok)
            return carry

        def side_plane(i, carry):
            unpack(side, i, lax.rem(LOW + bx + i, LOW + bx + HIGH), t, ok & jnp.where(i < HIGH, ix < nx - 1, ix > 0))
            return carry

        lax.fori_loop(0, bx, own_plane, 0)
        lax.fori_loop(0, LOW + HIGH, side_plane, 0)

    unpack_planes(own_ref, side_ref, 0, iz >= 0)
    for parity in range(2):
        @pl.when(lax.rem(iz, 2) == parity)
        def _():
            faces, corners = (face_0_ref, face_1_ref), (corner_0_ref, corner_1_ref)
            unpack_planes(faces[parity], corners[parity], 1, iz < nz - 1)
            unpack_planes(faces[1 - parity], corners[1 - parity], 2, iz > 0)

    def merge(i, carry):
        row = lax.broadcasted_iota(jnp.int32, (bz, lanes), 0)
        for full, half in ((pre_ref, pre2_ref), (power_field_ref, power2_field_ref), (rho_ref, rho2_ref)):
            half[i, 0:bz] = full[i, 0:bz]
            half[i, bz : 2 * bz] = jnp.where(row < bz // 2, full[i, bz : 2 * bz], full[i, 2 * bz :])
        return carry

    lax.fori_loop(2, bx + LOW + HIGH - 4, merge, 0)

    for ref, high in ((weight_ref, 2 * bz), (weight2_ref, bz + bz // 2)):
        shape = ref.shape[1:]
        r = lax.broadcasted_iota(jnp.int32, shape, 0)
        c = lax.broadcasted_iota(jnp.int32, shape, 1)
        zg = iz * bz + jnp.where(r < high, r, r - shape[0])
        yg = iy * by + jnp.where(c < by + HIGH, c, c - lanes)
        filled = (c < by + HIGH) | (c >= lanes - LOW)
        inside = filled & (zg >= 0) & (zg < nz * bz) & (yg >= 0) & (yg < ny * by)
        ref[0] = jnp.where(inside, 0.05, 0.0)
        ref[1] = jnp.where(inside & (zg > 0), 0.05, 0.0)
        ref[2] = jnp.where(inside & (yg > 0), 0.05, 0.0)
        ref[3] = jnp.where(inside, 0.0, 1.0)

    for k in range(1, ITERS + 1):
        old, new = (va_ref, vb_ref) if k % 2 else (vb_ref, va_ref)
        last = k == ITERS
        rows = 2 * bz if merged(k, bz) else 3 * bz
        constants = (pre2_ref, power2_field_ref, rho2_ref) if merged(k, bz) else (pre_ref, power_field_ref, rho_ref)
        weight = weight2_ref if merged(k, bz) else weight_ref
        narrow = merged(k + 1, bz) and not merged(k, bz)
        all_rows = pl.ds(0, rows)

        def keep(value):
            if narrow:
                row = lax.broadcasted_iota(jnp.int32, (bz, lanes), 0)
                halo = jnp.where(row < bz // 2, value[..., bz : 2 * bz, :], value[..., 2 * bz :, :])
                return [(pl.ds(0, bz), value[..., 0:bz, :]), (pl.ds(bz, bz), halo)]
            return [(all_rows, value)]

        def store(d, j, count, value):
            for at, part in keep(value):
                new[d, pl.ds(j, count), at, :] = part

        def cells(j, count):
            planes = pl.ds(j, count)
            vx1 = old[0, pl.ds(j, count + 1), all_rows, :]
            vx = vx1[:count]
            vz, vy = old[1, planes, all_rows, :], old[2, planes, all_rows, :]
            p = p_ref[planes, all_rows, :]
            rx = vx1[1:] - vx
            rz = z_up(vz) - vz
            ry = y_up(vy) - vy
            a = rx - ry
            b = ry - rz
            inv = (a * (a + b) + b * b) * (1.0 / 3.0) + 1.0
            eta = constants[0][planes] * jnp.exp2(constants[1][planes] * jnp.log(inv))
            quarter = 0.25 * eta
            div = rx + ry + rz
            p = p - quarter * (div + div)
            tx, tz, ty = eta * rx - p, eta * rz - p, eta * ry - p
            sz = quarter + z_down(quarter)
            sy = quarter + y_down(quarter)
            return vx, vz, vy, eta, p, quarter, tx, tz, ty, sz, sy

        def chunk(j, count, carry, start=False):
            planes = pl.ds(j, count)
            vx, vz, vy, eta, p, quarter, tx, tz, ty, sz, sy = cells(j, count)
            vz0, vy0 = old[1, pl.ds(j - 1, 1), all_rows, :], old[2, pl.ds(j - 1, 1), all_rows, :]
            quarter0, tx0, sz0, sy0, part_z0, part_y0, scale_z0, scale_y0 = carry
            join = lambda first, rest: jnp.concatenate([first, rest[:-1]], axis=0) if count > 1 else first
            bias = weight[3:4]
            sx = quarter + join(quarter0, quarter)
            exz = sz + join(sz0, sz)
            exy = sy + join(sy0, sy)
            ezy = sz + y_down(sz)
            fxz = exz * (vx - z_down(vx))
            fxy = exy * (vx - y_down(vx))
            low_vz, low_vy = join(vz0, vz), join(vy0, vy)
            gzx = exz * (vz - low_vz)
            hyx = exy * (vy - low_vy)
            gzy = ezy * (vz - y_down(vz))
            hyz = ezy * (vy - z_down(vy))
            res_x = (tx - join(tx0, tx)) + ((z_up(fxz) - fxz) + (y_up(fxy) - fxy))
            new_vx = vx + weight[0:1] * reciprocal(sx + bias) * res_x
            part_z = (tz - z_down(tz)) - constants[2][planes] + ((y_up(gzy) - gzy) - gzx)
            part_y = (ty - y_down(ty)) + ((z_up(hyz) - hyz) - hyx)
            scale_z = weight[1:2] * reciprocal(sz + bias)
            scale_y = weight[2:3] * reciprocal(sy + bias)
            new_vz = low_vz + join(scale_z0, scale_z) * (join(part_z0, part_z) + gzx)
            new_vy = low_vy + join(scale_y0, scale_y) * (join(part_y0, part_y) + hyx)
            if last:
                at = pl.ds(j - LOW, count)
                out_vx_ref[at] = new_vx[:, 0:bz, 0:by]
                out_p_ref[at] = p[:, 0:bz, 0:by]
                out_eta_ref[at] = eta[:, 0:bz, 0:by]
                sum_ref[...] += jnp.sum(p[:, 0:bz, 0:by], axis=0)
                if not start:
                    at = pl.ds(j - 1 - LOW, count)
                    out_vz_ref[at] = new_vz[:, 0:bz, 0:by]
                    out_vy_ref[at] = new_vy[:, 0:bz, 0:by]
            else:
                for at, part in keep(p):
                    p_ref[planes, at, :] = part
                store(0, j, count, new_vx)
                if not start:
                    store(1, j - 1, count, new_vz)
                    store(2, j - 1, count, new_vy)
            return tuple(a[-1:] for a in (quarter, tx, sz, sy, part_z, part_y, scale_z, scale_y))

        first, count = k, bx + LOW + HIGH - 3 * k
        if last:
            sum_ref[...] = jnp.zeros((bz, by), jnp.float32)
        _, _, _, _, p, quarter, tx, _, _, sz, sy = cells(first - 1, 1)
        if not last:
            for at, part in keep(p):
                p_ref[pl.ds(first - 1, 1), at, :] = part
        zero = jnp.zeros((1, rows, lanes), jnp.float32)
        carry = chunk(first, 1, (quarter, tx, sz, sy, zero, zero, zero, zero), start=True)
        steps, rest = divmod(count - 1, UNROLL)
        carry = lax.fori_loop(
            0, steps, lambda s, carry: chunk(first + 1 + s * UNROLL, UNROLL, carry), carry
        )
        if rest:
            carry = chunk(first + 1 + steps * UNROLL, rest, carry)
        j = first + count
        quarter0, tx0, sz0, sy0, part_z0, part_y0, scale_z0, scale_y0 = carry
        _, vz, vy, _, p, quarter, tx, _, _, sz, sy = cells(j, 1)
        vz0, vy0 = old[1, pl.ds(j - 1, 1), all_rows, :], old[2, pl.ds(j - 1, 1), all_rows, :]
        new_vz = vz0 + scale_z0 * (part_z0 + (sz + sz0) * (vz - vz0))
        new_vy = vy0 + scale_y0 * (part_y0 + (sy + sy0) * (vy - vy0))
        if last:
            out_vz_ref[pl.ds(j - 1 - LOW, 1)] = new_vz[:, 0:bz, 0:by]
            out_vy_ref[pl.ds(j - 1 - LOW, 1)] = new_vy[:, 0:bz, 0:by]
        else:
            for at, part in keep(p):
                p_ref[pl.ds(j, 1), at, :] = part
            store(1, j - 1, 1, new_vz)
            store(2, j - 1, 1, new_vy)

        if last:
            @pl.when(ix == 0)
            def _():
                out_vx_ref[0] = jnp.zeros((bz, by), jnp.float32)
        else:
            plane = jnp.zeros((3 * bz, lanes), jnp.float32)

            @pl.when(ix == 0)
            def _():
                for i in range(k, LOW):
                    for d in range(3):
                        new[d, i] = plane
                new[0, LOW] = plane

            @pl.when(ix == nx - 1)
            def _():
                for i in range(LOW + bx, first + count):
                    for d in range(3):
                        new[d, i] = plane


def final_kernel(p_ref, sum_ref, out_ref, *, cells):
    mean = jnp.sum(sum_ref[...]) * (1.0 / cells)
    out_ref[...] = p_ref[...] - mean


def swap(a, axis, start):
    count = lax.axis_size(axis)
    return lax.ppermute(a, axis, [(i, j) for k in range(start, count - 1, 2) for i, j in ((k, k + 1), (k + 1, k))])


def exchange_sum(total, axes):
    count = math.prod(lax.axis_size(a) for a in axes)
    total = jnp.broadcast_to(jnp.sum(total, axis=0, keepdims=True), (count, total.shape[1]))
    return lax.all_to_all(total, axes, 0, 0, tiled=True)


def local(vel_x, vel_y, vel_z, pressure, phase, visc_scale, power_n, density):
    bx, bz, by = pressure.shape
    assert bx == 2 * HIGH and bz == HIGH
    f32 = jnp.float32
    ny = lax.axis_size("gy")
    cells = bx * bz * by * math.prod(lax.axis_size(a) for a in ("gx", "gz", "gy"))
    deep = bx + LOW + HIGH
    block = jax.ShapeDtypeStruct((bx, bz, by), f32)
    scratch = lambda *shape: pltpu.VMEM(shape, f32)
    small = pltpu.CompilerParams(vmem_limit_bytes=4 * 1024 * 1024)

    stack, edge = pl.pallas_call(
        pack_kernel,
        out_shape=(jax.ShapeDtypeStruct((bx, FIELDS, bz, by), f32), block),
        in_specs=[pl.BlockSpec(memory_space=pltpu.HBM)] * 5,
        out_specs=(VMEM, VMEM),
        scratch_shapes=[
            scratch(FIELDS - 1, bx, bz, by),
            pltpu.VMEM((bx, bz, by), jnp.int32),
            pltpu.SemaphoreType.DMA((FIELDS,)),
        ],
        compiler_params=small,
    )(vel_x, vel_z, vel_y, pressure, phase)

    side = swap(edge, "gy", 0)
    if ny > 2:
        even = lax.rem(lax.axis_index("gy"), 2) == 0
        other = swap(edge, "gy", 1)
        lane = lax.broadcasted_iota(jnp.int32, (bx, bz, by), 2)
        side = jnp.where((lane % LANE_STEP < HIGH) == even, side, other)
    stack = jnp.concatenate([stack, side[:, None]], axis=1)

    face_1 = swap(stack, "gz", 1)
    x_0, x_1 = swap(stack[:HIGH], "gx", 0), swap(stack[HIGH:], "gx", 1)
    face_0 = swap(stack, "gz", 0)
    even = lax.rem(lax.axis_index("gx"), 2) == 0
    low = jnp.where(even, x_1[HIGH - LOW :], x_0[HIGH - LOW :])
    sides = jnp.concatenate([jnp.where(even, x_0, x_1), low], axis=0)
    corner_1 = swap(sides, "gz", 1)
    corner_0 = swap(sides, "gz", 0)

    power = (0.5 / math.log(2.0)) * (1.0 / power_n - 1.0)
    rows, lanes = 3 * bz, 2 * by
    vx, vz, vy, p, eta, total = pl.pallas_call(
        main_kernel,
        out_shape=(block,) * 5 + (jax.ShapeDtypeStruct((bz, by), f32),),
        in_specs=[VMEM] * 6 + [SMEM] * 3,
        out_specs=(VMEM,) * 6,
        scratch_shapes=[
            scratch(3, deep, rows, lanes),
            scratch(3, deep, rows, lanes),
            scratch(deep, rows, lanes),
            scratch(deep, rows, lanes),
            scratch(deep, rows, lanes),
            scratch(deep, rows, lanes),
            scratch(deep, 2 * bz, lanes),
            scratch(deep, 2 * bz, lanes),
            scratch(deep, 2 * bz, lanes),
            scratch(4, rows, lanes),
            scratch(4, 2 * bz, lanes),
        ],
        compiler_params=pltpu.CompilerParams(vmem_limit_bytes=32 * 1024 * 1024),
    )(stack, sides, face_0, face_1, corner_0, corner_1, visc_scale, power, density)

    total = exchange_sum(total, ("gy", "gz"))
    total = exchange_sum(total, ("gx",))
    p = pl.pallas_call(
        lambda *refs: final_kernel(*refs, cells=float(cells)),
        out_shape=block,
        in_specs=[VMEM] * 2,
        out_specs=VMEM,
        compiler_params=small,
    )(p, total)
    return (vx, vy, vz, p, eta)


def solution(mesh):
    spec = P("gx", "gz", "gy")
    return jax.shard_map(
        local,
        mesh=mesh,
        in_specs=(spec,) * 5 + (P(),) * 3,
        out_specs=(spec,) * 5,
        check_vma=False,
    )
```

```python
import math

import jax
import jax.numpy as jnp
from jax import lax
from jax.experimental import pallas as pl
from jax.experimental.pallas import tpu as pltpu
from jax.sharding import PartitionSpec as P

ITERS = 4
PHASES = 4
LOW = ITERS
HIGH = 2 * ITERS
FIELDS = 5
LANE_STEP = 16
UNROLL = 3
GROUP = 4

VMEM = pl.BlockSpec(memory_space=pltpu.VMEM)
SMEM = pl.BlockSpec(memory_space=pltpu.SMEM)


def z_up(a):
    return pltpu.roll(a, a.shape[-2] - 1, a.ndim - 2)


def z_down(a):
    return pltpu.roll(a, 1, a.ndim - 2)


def y_up(a):
    return pltpu.roll(a, a.shape[-1] - 1, a.ndim - 1)


def y_down(a):
    return pltpu.roll(a, 1, a.ndim - 1)


def reciprocal(a):
    r = pl.reciprocal(a, approx=True)
    return r * (2.0 - a * r)


def merged(k, bz):
    return 3 * (ITERS - k + 1) <= bz


def edge_kernel(vx_hbm, vz_hbm, vy_hbm, p_hbm, phase_hbm, edge_hbm, field_ref, phase_ref, edge_ref, sems, out_sems):
    bx, bz, by = phase_ref.shape
    sources = (vx_hbm, vz_hbm, vy_hbm, p_hbm, phase_hbm)
    targets = [field_ref.at[f] for f in range(FIELDS - 1)] + [phase_ref]
    groups = bx // GROUP
    copies = []
    for g in range(groups):
        at = pl.ds(g * GROUP, GROUP)
        copies.append(
            [pltpu.make_async_copy(a.at[at], b.at[at], sems.at[g, f]) for f, (a, b) in enumerate(zip(sources, targets))]
        )
        for copy in copies[-1]:
            copy.start()
    ix, iz, iy = lax.axis_index("gx"), lax.axis_index("gz"), lax.axis_index("gy")
    lane = lax.broadcasted_iota(jnp.int32, (1, bz, by), 2)
    row = lax.broadcasted_iota(jnp.int32, (1, bz, by), 1)
    plane = lax.broadcasted_iota(jnp.int32, (GROUP, bz, by), 0)
    outs = []
    for g in range(groups):
        for copy in copies[g]:
            copy.wait()
        at = pl.ds(g * GROUP, GROUP)
        vx, vz, vy, p = (field_ref[f, at] for f in range(FIELDS - 1))
        if g == 0:
            vx = jnp.where((plane > 0) | (ix > 0), vx, 0.0)
        vz = jnp.where((row > 0) | (iz > 0), vz, 0.0)
        vy = jnp.where((lane > 0) | (iy > 0), vy, 0.0)
        edge = jnp.zeros((GROUP, bz, by), jnp.float32)
        for f, a in enumerate((vx, vz, vy, p, phase_ref[at].astype(jnp.float32))):
            base = LANE_STEP * f
            first = pltpu.roll(a, base, 2) if base else a
            edge = jnp.where((lane >= base) & (lane < base + HIGH), first, edge)
            last = pltpu.roll(a, base + LANE_STEP, 2)
            edge = jnp.where((lane >= base + LANE_STEP - LOW) & (lane < base + LANE_STEP), last, edge)
        edge_ref[at] = edge
        outs.append(pltpu.make_async_copy(edge_ref.at[at], edge_hbm.at[at], out_sems.at[g]))
        outs[-1].start()
    for copy in outs:
        copy.wait()


def unpack(block, ok, tables):
    count, _, bz, by = block.shape
    iy = lax.axis_index("gy")
    lane = lax.broadcasted_iota(jnp.int32, (1, bz, by), 2)
    right = (lane < HIGH) & (iy < lax.axis_size("gy") - 1)
    left = (lane >= by - LOW) & (iy > 0)
    ok = jnp.where(ok, 1.0, 0.0)
    edge = block[:, FIELDS]
    out = []
    for f in range(FIELDS):
        shift = LANE_STEP * f
        a = pltpu.roll(edge, (by - shift) % by, 2) if shift else edge
        b = pltpu.roll(edge, (by - LANE_STEP - shift) % by, 2)
        out.append([block[:, f], jnp.where(right, a, jnp.where(left, b, 0.0))])
    pair = out.pop()
    for number, table in enumerate(tables):
        values = []
        for part, ph in enumerate(pair):
            value = jnp.broadcast_to(table[0], ph.shape)
            for index in range(1, PHASES):
                value = jnp.where(ph == float(index), table[index], value)
            if number == 0:
                value = value * ok
                if part:
                    value = jnp.where(right | left, value, 0.0)
            values.append(value)
        out.append(values)
    return out


def unpack_planes(own_ref, side_ref, ok, tables, store):
    bx = own_ref.shape[0]
    ix, nx = lax.axis_index("gx"), lax.axis_size("gx")

    def group(g, carry):
        store(pl.ds(LOW + g * GROUP, GROUP), unpack(own_ref[pl.ds(g * GROUP, GROUP)], ok, tables))
        return carry

    lax.fori_loop(0, bx // GROUP, group, 0)
    for g in range((LOW + HIGH) // GROUP):
        at = g * GROUP
        high = at < HIGH
        values = unpack(side_ref[pl.ds(at, GROUP)], ok & (ix < nx - 1 if high else ix > 0), tables)
        store(pl.ds(LOW + bx + at if high else at - HIGH, GROUP), values)


def own_kernel(own_ref, side_ref, scale_ref, power_ref, rho_table_ref, v_ref, p_ref, pre_ref, power_field_ref, rho_ref):
    by = own_ref.shape[-1]
    refs = [v_ref.at[d] for d in range(3)] + [p_ref, pre_ref, power_field_ref, rho_ref]

    def store(planes, values):
        for ref, (own, beside) in zip(refs, values):
            ref[planes, :, 0:by] = own
            ref[planes, :, by : 2 * by] = beside

    unpack_planes(own_ref, side_ref, lax.axis_index("gz") >= 0, (scale_ref, power_ref, rho_table_ref), store)


def main_kernel(
    v_ref, p0_ref, pre_ref, power_field_ref, rho_ref,
    face_0_ref, face_1_ref, corner_0_ref, corner_1_ref, scale_ref, power_ref, rho_table_ref,
    out_vx_ref, out_vz_ref, out_vy_ref, out_p_ref, out_eta_ref, sum_ref,
    va_ref, vb_ref, p_ref, halo_ref, shared_ref, weight_ref, weight2_ref,
):
    bx, _, bz, by = face_0_ref.shape
    lanes = 2 * by
    nx, nz, ny = lax.axis_size("gx"), lax.axis_size("gz"), lax.axis_size("gy")
    ix, iz, iy = lax.axis_index("gx"), lax.axis_index("gz"), lax.axis_index("gy")
    tables = (scale_ref, power_ref, rho_table_ref)

    def store(t):
        def store_rows(planes, values):
            for n, pair in enumerate(values):
                for part, value in enumerate(pair):
                    halo_ref[n, planes, t * bz : (t + 1) * bz, part * by : (part + 1) * by] = value
                    if n >= 4:
                        half = bz // 2
                        rows = slice(t * half, (t + 1) * half)
                        shared_ref[n - 4, planes, rows, part * by : (part + 1) * by] = value[:, rows]

        return store_rows

    for parity in range(2):
        @pl.when(lax.rem(iz, 2) == parity)
        def _():
            faces, corners = (face_0_ref, face_1_ref), (corner_0_ref, corner_1_ref)
            unpack_planes(faces[parity], corners[parity], iz < nz - 1, tables, store(0))
            unpack_planes(faces[1 - parity], corners[1 - parity], iz > 0, tables, store(1))

    for ref, high in ((weight_ref, 2 * bz), (weight2_ref, bz + bz // 2)):
        shape = ref.shape[1:]
        r = lax.broadcasted_iota(jnp.int32, shape, 0)
        c = lax.broadcasted_iota(jnp.int32, shape, 1)
        zg = iz * bz + jnp.where(r < high, r, r - shape[0])
        yg = iy * by + jnp.where(c < by + HIGH, c, c - lanes)
        filled = (c < by + HIGH) | (c >= lanes - LOW)
        inside = filled & (zg >= 0) & (zg < nz * bz) & (yg >= 0) & (yg < ny * by)
        ref[0] = jnp.where(inside, 0.05, 0.0)
        ref[1] = jnp.where(inside & (zg > 0), 0.05, 0.0)
        ref[2] = jnp.where(inside & (yg > 0), 0.05, 0.0)
        ref[3] = jnp.where(inside, 0.0, 1.0)

    for k in range(1, ITERS + 1):
        old, new = (va_ref, vb_ref) if k % 2 else (vb_ref, va_ref)
        last = k == ITERS
        rows = 2 * bz if merged(k, bz) else 3 * bz
        own_constants = (pre_ref, power_field_ref, rho_ref)
        weight = weight2_ref if merged(k, bz) else weight_ref
        narrow = merged(k + 1, bz) and not merged(k, bz)
        all_rows = pl.ds(0, rows)

        def keep(value):
            if narrow:
                row = lax.broadcasted_iota(jnp.int32, (bz, lanes), 0)
                halo = jnp.where(row < bz // 2, value[..., bz : 2 * bz, :], value[..., 2 * bz :, :])
                return [(pl.ds(0, bz), value[..., 0:bz, :]), (pl.ds(bz, bz), halo)]
            return [(all_rows, value)]

        def store(d, j, count, value):
            for at, part in keep(value):
                new[d, pl.ds(j, count), at, :] = part

        def constant(n, planes):
            halo = shared_ref[n, planes] if merged(k, bz) else halo_ref[4 + n, planes]
            return jnp.concatenate([own_constants[n][planes], halo], axis=1)

        def load(d, j, count):
            planes = pl.ds(j, count)
            if k == 1:
                return jnp.concatenate([v_ref[d, planes], halo_ref[d, planes]], axis=1)
            return old[d, planes, all_rows, :]

        def cells(j, count):
            planes = pl.ds(j, count)
            vx1 = load(0, j, count + 1)
            vx = vx1[:count]
            vz, vy = load(1, j, count), load(2, j, count)
            if k == 1:
                p = jnp.concatenate([p0_ref[planes], halo_ref[3, planes]], axis=1)
            else:
                p = p_ref[planes, all_rows, :]
            rx = vx1[1:] - vx
            rz = z_up(vz) - vz
            ry = y_up(vy) - vy
            a = rx - ry
            b = ry - rz
            inv = (a * (a + b) + b * b) * (1.0 / 3.0) + 1.0
            eta = constant(0, planes) * jnp.exp2(constant(1, planes) * jnp.log(inv))
            quarter = 0.25 * eta
            div = rx + ry + rz
            p = p - quarter * (div + div)
            tx, tz, ty = eta * rx - p, eta * rz - p, eta * ry - p
            sz = quarter + z_down(quarter)
            sy = quarter + y_down(quarter)
            return vx, vz, vy, eta, p, quarter, tx, tz, ty, sz, sy

        def chunk(j, count, carry, start=False):
            planes = pl.ds(j, count)
            vx, vz, vy, eta, p, quarter, tx, tz, ty, sz, sy = cells(j, count)
            vz0, vy0 = load(1, j - 1, 1), load(2, j - 1, 1)
            quarter0, tx0, sz0, sy0, part_z0, part_y0, scale_z0, scale_y0 = carry
            join = lambda first, rest: jnp.concatenate([first, rest[:-1]], axis=0) if count > 1 else first
            bias = weight[3:4]
            sx = quarter + join(quarter0, quarter)
            exz = sz + join(sz0, sz)
            exy = sy + join(sy0, sy)
            ezy = sz + y_down(sz)
            fxz = exz * (vx - z_down(vx))
            fxy = exy * (vx - y_down(vx))
            low_vz, low_vy = join(vz0, vz), join(vy0, vy)
            gzx = exz * (vz - low_vz)
            hyx = exy * (vy - low_vy)
            gzy = ezy * (vz - y_down(vz))
            hyz = ezy * (vy - z_down(vy))
            res_x = (tx - join(tx0, tx)) + ((z_up(fxz) - fxz) + (y_up(fxy) - fxy))
            new_vx = vx + weight[0:1] * reciprocal(sx + bias) * res_x
            part_z = (tz - z_down(tz)) - constant(2, planes) + ((y_up(gzy) - gzy) - gzx)
            part_y = (ty - y_down(ty)) + ((z_up(hyz) - hyz) - hyx)
            scale_z = weight[1:2] * reciprocal(sz + bias)
            scale_y = weight[2:3] * reciprocal(sy + bias)
            new_vz = low_vz + join(scale_z0, scale_z) * (join(part_z0, part_z) + gzx)
            new_vy = low_vy + join(scale_y0, scale_y) * (join(part_y0, part_y) + hyx)
            if last:
                at = pl.ds(j - LOW, count)
                out_vx_ref[at] = new_vx[:, 0:bz, 0:by]
                out_p_ref[at] = p[:, 0:bz, 0:by]
                out_eta_ref[at] = eta[:, 0:bz, 0:by]
                sum_ref[...] += jnp.sum(p[:, 0:bz, 0:by], axis=0)
                if not start:
                    at = pl.ds(j - 1 - LOW, count)
                    out_vz_ref[at] = new_vz[:, 0:bz, 0:by]
                    out_vy_ref[at] = new_vy[:, 0:bz, 0:by]
            else:
                for at, part in keep(p):
                    p_ref[planes, at, :] = part
                store(0, j, count, new_vx)
                if not start:
                    store(1, j - 1, count, new_vz)
                    store(2, j - 1, count, new_vy)
            return tuple(a[-1:] for a in (quarter, tx, sz, sy, part_z, part_y, scale_z, scale_y))

        first, count = k, bx + LOW + HIGH - 3 * k
        if last:
            sum_ref[...] = jnp.zeros((bz, by), jnp.float32)
        _, _, _, _, p, quarter, tx, _, _, sz, sy = cells(first - 1, 1)
        if not last:
            for at, part in keep(p):
                p_ref[pl.ds(first - 1, 1), at, :] = part
        zero = jnp.zeros((1, rows, lanes), jnp.float32)
        carry = chunk(first, 1, (quarter, tx, sz, sy, zero, zero, zero, zero), start=True)
        steps, rest = divmod(count - 1, UNROLL)
        carry = lax.fori_loop(
            0, steps, lambda s, carry: chunk(first + 1 + s * UNROLL, UNROLL, carry), carry
        )
        if rest:
            carry = chunk(first + 1 + steps * UNROLL, rest, carry)
        j = first + count
        quarter0, tx0, sz0, sy0, part_z0, part_y0, scale_z0, scale_y0 = carry
        _, vz, vy, _, p, quarter, tx, _, _, sz, sy = cells(j, 1)
        vz0, vy0 = load(1, j - 1, 1), load(2, j - 1, 1)
        new_vz = vz0 + scale_z0 * (part_z0 + (sz + sz0) * (vz - vz0))
        new_vy = vy0 + scale_y0 * (part_y0 + (sy + sy0) * (vy - vy0))
        if last:
            out_vz_ref[pl.ds(j - 1 - LOW, 1)] = new_vz[:, 0:bz, 0:by]
            out_vy_ref[pl.ds(j - 1 - LOW, 1)] = new_vy[:, 0:bz, 0:by]
        else:
            for at, part in keep(p):
                p_ref[pl.ds(j, 1), at, :] = part
            store(1, j - 1, 1, new_vz)
            store(2, j - 1, 1, new_vy)

        if last:
            @pl.when(ix == 0)
            def _():
                out_vx_ref[0] = jnp.zeros((bz, by), jnp.float32)
        else:
            plane = jnp.zeros((3 * bz, lanes), jnp.float32)

            @pl.when(ix == 0)
            def _():
                for i in range(k, LOW):
                    for d in range(3):
                        new[d, i] = plane
                new[0, LOW] = plane

            @pl.when(ix == nx - 1)
            def _():
                for i in range(LOW + bx, first + count):
                    for d in range(3):
                        new[d, i] = plane


def final_kernel(p_ref, sum_ref, out_ref, *, cells):
    mean = jnp.sum(sum_ref[...]) * (1.0 / cells)
    out_ref[...] = p_ref[...] - mean


def swap(a, axis, start):
    count = lax.axis_size(axis)
    return lax.ppermute(a, axis, [(i, j) for k in range(start, count - 1, 2) for i, j in ((k, k + 1), (k + 1, k))])


def sum_everywhere(total):
    axes = ("gx", "gy", "gz")
    devices = math.prod(lax.axis_size(a) for a in axes)
    if devices & (devices - 1):
        return lax.psum(total, axes)
    bits = [1 << n for n in range(devices.bit_length() - 1)]
    stages = [bits[:1]] + [bits[n : n + 2] for n in range(1, len(bits), 2)]
    for stage in stages:
        masks = [stage[0]] if len(stage) == 1 else [stage[0], stage[1], stage[0] + stage[1]]
        parts = [lax.ppermute(total, axes, [(i, i ^ m) for i in range(devices)]) for m in masks]
        total = sum(parts, total)
    return total


def local(vel_x, vel_y, vel_z, pressure, phase, visc_scale, power_n, density):
    bx, bz, by = pressure.shape
    assert bx == 2 * HIGH and bz == HIGH
    f32 = jnp.float32
    ix, iz, iy = lax.axis_index("gx"), lax.axis_index("gz"), lax.axis_index("gy")
    ny = lax.axis_size("gy")
    cells = bx * bz * by * math.prod(lax.axis_size(a) for a in ("gx", "gz", "gy"))
    deep = bx + LOW + HIGH
    rows, lanes = 3 * bz, 2 * by
    shape = lambda *dims: jax.ShapeDtypeStruct(dims, f32)
    block = shape(bx, bz, by)
    scratch = lambda *dims: pltpu.VMEM(dims, f32)
    mebibyte = 1024 * 1024

    edge = pl.pallas_call(
        edge_kernel,
        out_shape=block,
        in_specs=[pl.BlockSpec(memory_space=pltpu.HBM)] * 5,
        out_specs=pl.BlockSpec(memory_space=pltpu.HBM),
        scratch_shapes=[
            scratch(FIELDS - 1, bx, bz, by),
            pltpu.VMEM((bx, bz, by), jnp.int32),
            scratch(bx, bz, by),
            pltpu.SemaphoreType.DMA((bx // GROUP, FIELDS)),
            pltpu.SemaphoreType.DMA((bx // GROUP,)),
        ],
        compiler_params=pltpu.CompilerParams(vmem_limit_bytes=58 * mebibyte),
    )(vel_x, vel_z, vel_y, pressure, phase)

    side = swap(edge, "gy", 0)
    if ny > 2:
        even = lax.rem(iy, 2) == 0
        other = swap(edge, "gy", 1)
        lane = lax.broadcasted_iota(jnp.int32, (bx, bz, by), 2)
        side = jnp.where((lane % LANE_STEP < HIGH) == even, side, other)
    clear = lambda v, axis, at: jnp.where((lax.broadcasted_iota(jnp.int32, v.shape, axis) == 0) & (at == 0), 0.0, v)
    fields = (clear(vel_x, 0, ix), clear(vel_z, 1, iz), clear(vel_y, 2, iy), pressure, phase.astype(f32))
    stack = jnp.concatenate([jnp.stack(fields, axis=1), side[:, None]], axis=1)

    even = lax.rem(ix, 2) == 0
    face_1 = swap(stack, "gz", 1)
    x_0 = swap(jnp.where(even, stack[HIGH:], stack[:HIGH]), "gx", 0)
    x_1 = swap(jnp.where(even, stack[:HIGH], stack[HIGH:]), "gx", 1)
    face_0 = swap(stack, "gz", 0)
    low = jnp.where(even, x_1[HIGH - LOW :], x_0[HIGH - LOW :])
    sides = jnp.concatenate([jnp.where(even, x_0, x_1), low], axis=0)
    corner_1 = swap(sides, "gz", 1)
    corner_0 = swap(sides, "gz", 0)

    tables = (visc_scale, (0.5 / math.log(2.0)) * (1.0 / power_n - 1.0), density)
    field = shape(deep, bz, lanes)
    own = pl.pallas_call(
        own_kernel,
        out_shape=(shape(3, deep, bz, lanes),) + (field,) * 4,
        in_specs=[VMEM] * 2 + [SMEM] * 3,
        out_specs=(VMEM,) * 5,
        compiler_params=pltpu.CompilerParams(vmem_limit_bytes=8 * mebibyte),
        cost_estimate=pl.CostEstimate(flops=deep * 30 * bz * lanes, bytes_accessed=12 * deep * bz * lanes * 4, transcendentals=0),
    )(stack, sides, *tables)
    vx, vz, vy, p, eta, total = pl.pallas_call(
        main_kernel,
        out_shape=(block,) * 5 + (shape(bz, by),),
        in_specs=[VMEM] * 9 + [SMEM] * 3,
        out_specs=(VMEM,) * 6,
        scratch_shapes=[
            scratch(3, deep, rows, lanes),
            scratch(3, deep, rows, lanes),
            scratch(deep, rows, lanes),
            scratch(7, deep, 2 * bz, lanes),
            scratch(3, deep, bz, lanes),
            scratch(4, rows, lanes),
            scratch(4, 2 * bz, lanes),
        ],
        compiler_params=pltpu.CompilerParams(vmem_limit_bytes=32 * mebibyte),
    )(*own, face_0, face_1, corner_0, corner_1, *tables)

    total = sum_everywhere(total)
    p = pl.pallas_call(
        lambda *refs: final_kernel(*refs, cells=float(cells)),
        out_shape=block,
        in_specs=[VMEM] * 2,
        out_specs=VMEM,
        compiler_params=pltpu.CompilerParams(vmem_limit_bytes=4 * mebibyte),
    )(p, total)
    return (vx, vy, vz, p, eta)


def solution(mesh):
    spec = P("gx", "gz", "gy")
    return jax.shard_map(
        local,
        mesh=mesh,
        in_specs=(spec,) * 5 + (P(),) * 3,
        out_specs=(spec,) * 5,
        check_vma=False,
    )
```

```python
import math

import jax
import jax.numpy as jnp
from jax import lax
from jax.experimental import pallas as pl
from jax.experimental.pallas import tpu as pltpu
from jax.sharding import PartitionSpec as P

ITERS = 4
PHASES = 4
LOW = ITERS
HIGH = 2 * ITERS
FIELDS = 5
LANE_STEP = LOW + HIGH
UNROLL = 3
GROUP = 4

VMEM = pl.BlockSpec(memory_space=pltpu.VMEM)
SMEM = pl.BlockSpec(memory_space=pltpu.SMEM)


def z_up(a):
    return pltpu.roll(a, a.shape[-2] - 1, a.ndim - 2)


def z_down(a):
    return pltpu.roll(a, 1, a.ndim - 2)


def y_up(a):
    return pltpu.roll(a, a.shape[-1] - 1, a.ndim - 1)


def y_down(a):
    return pltpu.roll(a, 1, a.ndim - 1)


def reciprocal(a):
    r = pl.reciprocal(a, approx=True)
    return r * (2.0 - a * r)


def merged(k, bz):
    return 3 * (ITERS - k + 1) <= bz


def start_copies(sources, targets, sems):
    copies = []
    for g in range(sources[0].shape[0] // GROUP):
        at = pl.ds(g * GROUP, GROUP)
        copies.append(
            [pltpu.make_async_copy(a.at[at], b.at[at], sems.at[g, f]) for f, (a, b) in enumerate(zip(sources, targets))]
        )
        for copy in copies[-1]:
            copy.start()
    return copies


def clean_group(g, field_ref, phase_ref):
    bx, bz, by = phase_ref.shape
    ix, iz, iy = lax.axis_index("gx"), lax.axis_index("gz"), lax.axis_index("gy")
    plane, row, lane = (lax.broadcasted_iota(jnp.int32, (GROUP, bz, by), d) for d in range(3))
    at = pl.ds(g * GROUP, GROUP)
    vx, vz, vy, p = (field_ref[f, at] for f in range(FIELDS - 1))
    if g == 0:
        vx = jnp.where((plane > 0) | (ix > 0), vx, 0.0)
    vz = jnp.where((row > 0) | (iz > 0), vz, 0.0)
    vy = jnp.where((lane > 0) | (iy > 0), vy, 0.0)
    return vx, vz, vy, p, phase_ref[at].astype(jnp.float32)


def edge_kernel(vx_hbm, vz_hbm, vy_hbm, p_hbm, phase_hbm, edge_hbm, field_ref, phase_ref, edge_ref, sems, out_sems):
    bx, bz, by = phase_ref.shape
    targets = [field_ref.at[f] for f in range(FIELDS - 1)] + [phase_ref]
    copies = start_copies((vx_hbm, vz_hbm, vy_hbm, p_hbm, phase_hbm), targets, sems)
    lane = lax.broadcasted_iota(jnp.int32, (1, bz, by), 2)
    half = bx // GROUP // 2
    outs = []
    for g in range(half):
        edge = jnp.zeros((GROUP, bz, by), jnp.float32)
        for upper in range(2):
            for copy in copies[g + upper * half]:
                copy.wait()
            for f, a in enumerate(clean_group(g + upper * half, field_ref, phase_ref)):
                base = by // 2 * upper + LANE_STEP * f
                first = pltpu.roll(a, base, 2) if base else a
                edge = jnp.where((lane >= base) & (lane < base + HIGH), first, edge)
                last = pltpu.roll(a, (base + LANE_STEP) % by, 2)
                edge = jnp.where((lane >= base + HIGH) & (lane < base + LANE_STEP), last, edge)
        at = pl.ds(g * GROUP, GROUP)
        edge_ref[at] = edge
        outs.append(pltpu.make_async_copy(edge_ref.at[at], edge_hbm.at[at], out_sems.at[g]))
        outs[-1].start()
    for copy in outs:
        copy.wait()


def stack_kernel(vx_hbm, vz_hbm, vy_hbm, p_hbm, phase_hbm, stack_hbm, field_ref, phase_ref, stack_ref, sems, out_sems):
    targets = [field_ref.at[f] for f in range(FIELDS - 1)] + [phase_ref]
    copies = start_copies((vx_hbm, vz_hbm, vy_hbm, p_hbm, phase_hbm), targets, sems)
    outs = []
    for g in range(len(copies)):
        for copy in copies[g]:
            copy.wait()
        at = pl.ds(g * GROUP, GROUP)
        for f, a in enumerate(clean_group(g, field_ref, phase_ref)):
            stack_ref[at, f] = a
        outs.append(pltpu.make_async_copy(stack_ref.at[at], stack_hbm.at[at], out_sems.at[g]))
        outs[-1].start()
    for copy in outs:
        copy.wait()


def unpack(block, upper, ok, tables):
    count, _, bz, by = block.shape
    iy = lax.axis_index("gy")
    lane = lax.broadcasted_iota(jnp.int32, (1, bz, by), 2)
    right = (lane < HIGH) & (iy < lax.axis_size("gy") - 1)
    left = (lane >= by - LOW) & (iy > 0)
    ok = jnp.where(ok, 1.0, 0.0)
    edge = block[:, FIELDS]
    out = []
    for f in range(FIELDS):
        shift = by // 2 * upper + LANE_STEP * f
        a = pltpu.roll(edge, (by - shift) % by, 2) if shift else edge
        b = pltpu.roll(edge, (by - LANE_STEP - shift) % by, 2)
        out.append([block[:, f], jnp.where(right, a, jnp.where(left, b, 0.0))])
    pair = out.pop()
    for number, table in enumerate(tables):
        values = []
        for part, ph in enumerate(pair):
            value = jnp.broadcast_to(table[0], ph.shape)
            for index in range(1, PHASES):
                value = jnp.where(ph == float(index), table[index], value)
            if number == 0:
                value = value * ok
                if part:
                    value = jnp.where(right | left, value, 0.0)
            values.append(value)
        out.append(values)
    return out


def unpack_own(ref, ok, tables, store):
    groups = ref.shape[0] // GROUP // 2
    for upper in range(2):

        def group(g, carry):
            at = g * GROUP + upper * HIGH
            store(pl.ds(LOW + at, GROUP), unpack(ref[pl.ds(at, GROUP)], upper, ok, tables))
            return carry

        lax.fori_loop(0, groups, group, 0)


def unpack_sides(ref, bx, ok, tables, store):
    ix, nx = lax.axis_index("gx"), lax.axis_size("gx")
    for at in range(0, HIGH + LOW, GROUP):
        low = at >= HIGH
        values = unpack(ref[pl.ds(at, GROUP)], int(low), ok & (ix > 0 if low else ix < nx - 1), tables)
        store(pl.ds(at - HIGH if low else LOW + bx + at, GROUP), values)


def own_kernel(own_ref, side_ref, scale_ref, power_ref, rho_table_ref, v_ref, p_ref, pre_ref, power_field_ref, rho_ref):
    by = own_ref.shape[-1]
    refs = [v_ref.at[d] for d in range(3)] + [p_ref, pre_ref, power_field_ref, rho_ref]

    def store(planes, values):
        for ref, (own, beside) in zip(refs, values):
            ref[planes, :, 0:by] = own
            ref[planes, :, by : 2 * by] = beside

    tables = (scale_ref, power_ref, rho_table_ref)
    unpack_own(own_ref, True, tables, store)
    unpack_sides(side_ref, own_ref.shape[0], True, tables, store)


def halo_store(halo_ref, shared_ref, t):
    bz = shared_ref.shape[-2]
    by = shared_ref.shape[-1] // 2
    rows = slice(t * bz // 2, (t + 1) * bz // 2)

    def store(planes, values):
        for n, pair in enumerate(values):
            for part, value in enumerate(pair):
                at = slice(part * by, (part + 1) * by)
                halo_ref[n, planes, t * bz : (t + 1) * bz, at] = value
                if n >= 4:
                    shared_ref[n - 4, planes, rows, at] = value[:, rows]

    return store


def face_kernel(face_0_ref, face_1_ref, scale_ref, power_ref, rho_table_ref, halo_ref, shared_ref):
    iz, nz = lax.axis_index("gz"), lax.axis_size("gz")
    tables = (scale_ref, power_ref, rho_table_ref)
    for parity in range(2):
        @pl.when(lax.rem(iz, 2) == parity)
        def _():
            faces = (face_0_ref, face_1_ref)
            unpack_own(faces[parity], iz < nz - 1, tables, halo_store(halo_ref, shared_ref, 0))
            unpack_own(faces[1 - parity], iz > 0, tables, halo_store(halo_ref, shared_ref, 1))


def main_kernel(
    v_ref, p0_ref, pre_ref, power_field_ref, rho_ref, _halo, _shared,
    corner_0_ref, corner_1_ref, scale_ref, power_ref, rho_table_ref,
    out_vx_ref, out_vz_ref, out_vy_ref, out_p_ref, out_eta_ref, sum_ref, halo_ref, shared_ref,
    va_ref, vb_ref, p_ref, weight_ref, weight2_ref,
):
    bx, bz, by = out_p_ref.shape
    lanes = 2 * by
    nx, nz, ny = lax.axis_size("gx"), lax.axis_size("gz"), lax.axis_size("gy")
    ix, iz, iy = lax.axis_index("gx"), lax.axis_index("gz"), lax.axis_index("gy")
    tables = (scale_ref, power_ref, rho_table_ref)
    for parity in range(2):
        @pl.when(lax.rem(iz, 2) == parity)
        def _():
            corners = (corner_0_ref, corner_1_ref)
            unpack_sides(corners[parity], bx, iz < nz - 1, tables, halo_store(halo_ref, shared_ref, 0))
            unpack_sides(corners[1 - parity], bx, iz > 0, tables, halo_store(halo_ref, shared_ref, 1))

    for ref, high in ((weight_ref, 2 * bz), (weight2_ref, bz + bz // 2)):
        shape = ref.shape[1:]
        r = lax.broadcasted_iota(jnp.int32, shape, 0)
        c = lax.broadcasted_iota(jnp.int32, shape, 1)
        zg = iz * bz + jnp.where(r < high, r, r - shape[0])
        yg = iy * by + jnp.where(c < by + HIGH, c, c - lanes)
        filled = (c < by + HIGH) | (c >= lanes - LOW)
        inside = filled & (zg >= 0) & (zg < nz * bz) & (yg >= 0) & (yg < ny * by)
        ref[0] = jnp.where(inside, 0.05, 0.0)
        ref[1] = jnp.where(inside & (zg > 0), 0.05, 0.0)
        ref[2] = jnp.where(inside & (yg > 0), 0.05, 0.0)
        ref[3] = jnp.where(inside, 0.0, 1.0)

    for k in range(1, ITERS + 1):
        old, new = (va_ref, vb_ref) if k % 2 else (vb_ref, va_ref)
        last = k == ITERS
        rows = 2 * bz if merged(k, bz) else 3 * bz
        own_constants = (pre_ref, power_field_ref, rho_ref)
        weight = weight2_ref if merged(k, bz) else weight_ref
        narrow = merged(k + 1, bz) and not merged(k, bz)
        all_rows = pl.ds(0, rows)

        def keep(value):
            if narrow:
                row = lax.broadcasted_iota(jnp.int32, (bz, lanes), 0)
                halo = jnp.where(row < bz // 2, value[..., bz : 2 * bz, :], value[..., 2 * bz :, :])
                return [(pl.ds(0, bz), value[..., 0:bz, :]), (pl.ds(bz, bz), halo)]
            return [(all_rows, value)]

        def store(d, j, count, value):
            for at, part in keep(value):
                new[d, pl.ds(j, count), at, :] = part

        def constant(n, planes):
            halo = shared_ref[n, planes] if merged(k, bz) else halo_ref[4 + n, planes]
            return jnp.concatenate([own_constants[n][planes], halo], axis=1)

        def load(d, j, count):
            planes = pl.ds(j, count)
            if k == 1:
                return jnp.concatenate([v_ref[d, planes], halo_ref[d, planes]], axis=1)
            return old[d, planes, all_rows, :]

        def cells(j, count):
            planes = pl.ds(j, count)
            vx1 = load(0, j, count + 1)
            vx = vx1[:count]
            vz, vy = load(1, j, count), load(2, j, count)
            if k == 1:
                p = jnp.concatenate([p0_ref[planes], halo_ref[3, planes]], axis=1)
            else:
                p = p_ref[planes, all_rows, :]
            rx = vx1[1:] - vx
            rz = z_up(vz) - vz
            ry = y_up(vy) - vy
            a = rx - ry
            b = ry - rz
            inv = (a * (a + b) + b * b) * (1.0 / 3.0) + 1.0
            eta = constant(0, planes) * jnp.exp2(constant(1, planes) * jnp.log(inv))
            quarter = 0.25 * eta
            div = rx + ry + rz
            p = p - quarter * (div + div)
            tx, tz, ty = eta * rx - p, eta * rz - p, eta * ry - p
            sz = quarter + z_down(quarter)
            sy = quarter + y_down(quarter)
            return vx, vz, vy, eta, p, quarter, tx, tz, ty, sz, sy

        def chunk(j, count, carry, start=False):
            planes = pl.ds(j, count)
            vx, vz, vy, eta, p, quarter, tx, tz, ty, sz, sy = cells(j, count)
            vz0, vy0 = load(1, j - 1, 1), load(2, j - 1, 1)
            quarter0, tx0, sz0, sy0, part_z0, part_y0, scale_z0, scale_y0 = carry
            join = lambda first, rest: jnp.concatenate([first, rest[:-1]], axis=0) if count > 1 else first
            bias = weight[3:4]
            sx = quarter + join(quarter0, quarter)
            exz = sz + join(sz0, sz)
            exy = sy + join(sy0, sy)
            ezy = sz + y_down(sz)
            fxz = exz * (vx - z_down(vx))
            fxy = exy * (vx - y_down(vx))
            low_vz, low_vy = join(vz0, vz), join(vy0, vy)
            gzx = exz * (vz - low_vz)
            hyx = exy * (vy - low_vy)
            gzy = ezy * (vz - y_down(vz))
            hyz = ezy * (vy - z_down(vy))
            res_x = (tx - join(tx0, tx)) + ((z_up(fxz) - fxz) + (y_up(fxy) - fxy))
            new_vx = vx + weight[0:1] * reciprocal(sx + bias) * res_x
            part_z = (tz - z_down(tz)) - constant(2, planes) + ((y_up(gzy) - gzy) - gzx)
            part_y = (ty - y_down(ty)) + ((z_up(hyz) - hyz) - hyx)
            scale_z = weight[1:2] * reciprocal(sz + bias)
            scale_y = weight[2:3] * reciprocal(sy + bias)
            new_vz = low_vz + join(scale_z0, scale_z) * (join(part_z0, part_z) + gzx)
            new_vy = low_vy + join(scale_y0, scale_y) * (join(part_y0, part_y) + hyx)
            if last:
                at = pl.ds(j - LOW, count)
                out_vx_ref[at] = new_vx[:, 0:bz, 0:by]
                out_p_ref[at] = p[:, 0:bz, 0:by]
                out_eta_ref[at] = eta[:, 0:bz, 0:by]
                sum_ref[...] += jnp.sum(p[:, 0:bz, 0:by], axis=0)
                if not start:
                    at = pl.ds(j - 1 - LOW, count)
                    out_vz_ref[at] = new_vz[:, 0:bz, 0:by]
                    out_vy_ref[at] = new_vy[:, 0:bz, 0:by]
            else:
                for at, part in keep(p):
                    p_ref[planes, at, :] = part
                store(0, j, count, new_vx)
                if not start:
                    store(1, j - 1, count, new_vz)
                    store(2, j - 1, count, new_vy)
            return tuple(a[-1:] for a in (quarter, tx, sz, sy, part_z, part_y, scale_z, scale_y))

        first, count = k, bx + LOW + HIGH - 3 * k
        if last:
            sum_ref[...] = jnp.zeros((bz, by), jnp.float32)
        _, _, _, _, p, quarter, tx, _, _, sz, sy = cells(first - 1, 1)
        if not last:
            for at, part in keep(p):
                p_ref[pl.ds(first - 1, 1), at, :] = part
        zero = jnp.zeros((1, rows, lanes), jnp.float32)
        carry = chunk(first, 1, (quarter, tx, sz, sy, zero, zero, zero, zero), start=True)
        steps, rest = divmod(count - 1, UNROLL)
        carry = lax.fori_loop(
            0, steps, lambda s, carry: chunk(first + 1 + s * UNROLL, UNROLL, carry), carry
        )
        if rest:
            carry = chunk(first + 1 + steps * UNROLL, rest, carry)
        j = first + count
        quarter0, tx0, sz0, sy0, part_z0, part_y0, scale_z0, scale_y0 = carry
        _, vz, vy, _, p, quarter, tx, _, _, sz, sy = cells(j, 1)
        vz0, vy0 = load(1, j - 1, 1), load(2, j - 1, 1)
        new_vz = vz0 + scale_z0 * (part_z0 + (sz + sz0) * (vz - vz0))
        new_vy = vy0 + scale_y0 * (part_y0 + (sy + sy0) * (vy - vy0))
        if last:
            out_vz_ref[pl.ds(j - 1 - LOW, 1)] = new_vz[:, 0:bz, 0:by]
            out_vy_ref[pl.ds(j - 1 - LOW, 1)] = new_vy[:, 0:bz, 0:by]
        else:
            for at, part in keep(p):
                p_ref[pl.ds(j, 1), at, :] = part
            store(1, j - 1, 1, new_vz)
            store(2, j - 1, 1, new_vy)

        if last:
            @pl.when(ix == 0)
            def _():
                out_vx_ref[0] = jnp.zeros((bz, by), jnp.float32)
        else:
            plane = jnp.zeros((3 * bz, lanes), jnp.float32)

            @pl.when(ix == 0)
            def _():
                for i in range(k, LOW):
                    for d in range(3):
                        new[d, i] = plane
                new[0, LOW] = plane

            @pl.when(ix == nx - 1)
            def _():
                for i in range(LOW + bx, first + count):
                    for d in range(3):
                        new[d, i] = plane


def final_kernel(p_ref, sum_ref, out_ref, *, cells):
    mean = jnp.sum(sum_ref[...]) * (1.0 / cells)
    out_ref[...] = p_ref[...] - mean


def swap(a, axis, start):
    count = lax.axis_size(axis)
    return lax.ppermute(a, axis, [(i, j) for k in range(start, count - 1, 2) for i, j in ((k, k + 1), (k + 1, k))])


def sum_everywhere(total):
    axes = ("gx", "gy", "gz")
    devices = math.prod(lax.axis_size(a) for a in axes)
    if devices & (devices - 1):
        return lax.psum(total, axes)
    odd = range(1, devices, 2)
    first = lax.rem(lax.axis_index("gz"), 2) == 0
    total = jnp.where(first, 0.0, total + lax.ppermute(total, axes, [(i ^ 1, i) for i in odd]))
    bits = [1 << n for n in range(1, devices.bit_length() - 1)]
    for stage in [bits[n : n + 2] for n in range(0, len(bits), 2)]:
        masks = stage if len(stage) == 1 else [stage[0], stage[1], stage[0] + stage[1]]
        total = sum([lax.ppermute(total, axes, [(i, i ^ m) for i in odd]) for m in masks], total)
    return total + lax.ppermute(total, axes, [(i, i ^ 1) for i in odd])


def local(vel_x, vel_y, vel_z, pressure, phase, visc_scale, power_n, density):
    bx, bz, by = pressure.shape
    assert bx == 2 * HIGH and bz == HIGH
    f32 = jnp.float32
    ix, iz, iy = lax.axis_index("gx"), lax.axis_index("gz"), lax.axis_index("gy")
    ny = lax.axis_size("gy")
    cells = bx * bz * by * math.prod(lax.axis_size(a) for a in ("gx", "gz", "gy"))
    deep = bx + LOW + HIGH
    rows, lanes = 3 * bz, 2 * by
    shape = lambda *dims: jax.ShapeDtypeStruct(dims, f32)
    block = shape(bx, bz, by)
    scratch = lambda *dims: pltpu.VMEM(dims, f32)
    mebibyte = 1024 * 1024

    hbm = pl.BlockSpec(memory_space=pltpu.HBM)

    def packing(kernel, *dims):
        groups = bx // GROUP
        return pl.pallas_call(
            kernel,
            out_shape=shape(*dims),
            in_specs=[hbm] * 5,
            out_specs=hbm,
            scratch_shapes=[
                scratch(FIELDS - 1, bx, bz, by),
                pltpu.VMEM((bx, bz, by), jnp.int32),
                scratch(*dims),
                pltpu.SemaphoreType.DMA((groups, FIELDS)),
                pltpu.SemaphoreType.DMA((groups,)),
            ],
            compiler_params=pltpu.CompilerParams(vmem_limit_bytes=58 * mebibyte),
            cost_estimate=pl.CostEstimate(flops=0, bytes_accessed=10 * bx * bz * by * 4, transcendentals=0),
        )(vel_x, vel_z, vel_y, pressure, phase)

    edge = packing(edge_kernel, bx // 2, bz, by)
    side = swap(edge, "gy", 0)
    if ny > 2:
        even = lax.rem(iy, 2) == 0
        other = swap(edge, "gy", 1)
        lane = lax.broadcasted_iota(jnp.int32, side.shape, 2) % (by // 2) % LANE_STEP
        side = jnp.where((lane < HIGH) == even, side, other)
    fields = packing(stack_kernel, bx, FIELDS, bz, by)
    stack = jnp.concatenate([fields, jnp.concatenate([side, side])[:, None]], axis=1)

    even = lax.rem(ix, 2) == 0
    face_1 = swap(stack, "gz", 1)
    x_0 = swap(jnp.where(even, stack[HIGH:], stack[:HIGH]), "gx", 0)
    x_1 = swap(jnp.where(even, stack[:HIGH], stack[HIGH:]), "gx", 1)
    face_0 = swap(stack, "gz", 0)
    low = jnp.where(even, x_1[HIGH - LOW :], x_0[HIGH - LOW :])
    sides = jnp.concatenate([jnp.where(even, x_0, x_1), low], axis=0)
    corner_1 = swap(sides, "gz", 1)
    corner_0 = swap(sides, "gz", 0)

    tables = (visc_scale, (0.5 / math.log(2.0)) * (1.0 / power_n - 1.0), density)
    field = shape(deep, bz, lanes)
    own = pl.pallas_call(
        own_kernel,
        out_shape=(shape(3, deep, bz, lanes),) + (field,) * 4,
        in_specs=[VMEM] * 2 + [SMEM] * 3,
        out_specs=(VMEM,) * 5,
        compiler_params=pltpu.CompilerParams(vmem_limit_bytes=8 * mebibyte),
        cost_estimate=pl.CostEstimate(flops=deep * 30 * bz * lanes, bytes_accessed=12 * deep * bz * lanes * 4, transcendentals=0),
    )(stack, sides, *tables)
    halo = pl.pallas_call(
        face_kernel,
        out_shape=(shape(7, deep, 2 * bz, lanes), shape(3, deep, bz, lanes)),
        in_specs=[VMEM] * 2 + [SMEM] * 3,
        out_specs=(VMEM,) * 2,
        compiler_params=pltpu.CompilerParams(vmem_limit_bytes=8 * mebibyte),
        cost_estimate=pl.CostEstimate(flops=deep * 30 * bz * lanes, bytes_accessed=24 * bx * bz * lanes * 4, transcendentals=0),
    )(face_0, face_1, *tables)
    vx, vz, vy, p, eta, total, _, _ = pl.pallas_call(
        main_kernel,
        out_shape=(block,) * 5 + (shape(bz, by),) + tuple(shape(*a.shape) for a in halo),
        in_specs=[VMEM] * 9 + [SMEM] * 3,
        out_specs=(VMEM,) * 8,
        input_output_aliases={5: 6, 6: 7},
        scratch_shapes=[
            scratch(3, deep, rows, lanes),
            scratch(3, deep, rows, lanes),
            scratch(deep, rows, lanes),
            scratch(4, rows, lanes),
            scratch(4, 2 * bz, lanes),
        ],
        compiler_params=pltpu.CompilerParams(vmem_limit_bytes=32 * mebibyte),
    )(*own, *halo, corner_0, corner_1, *tables)

    total = sum_everywhere(total)
    p = pl.pallas_call(
        lambda *refs: final_kernel(*refs, cells=float(cells)),
        out_shape=block,
        in_specs=[VMEM] * 2,
        out_specs=VMEM,
        compiler_params=pltpu.CompilerParams(vmem_limit_bytes=4 * mebibyte),
    )(p, total)
    return (vx, vy, vz, p, eta)


def solution(mesh):
    spec = P("gx", "gz", "gy")
    return jax.shard_map(
        local,
        mesh=mesh,
        in_specs=(spec,) * 5 + (P(),) * 3,
        out_specs=(spec,) * 5,
        check_vma=False,
    )
```

```python
import math

import jax
import jax.numpy as jnp
from jax import lax
from jax.experimental import pallas as pl
from jax.experimental.pallas import tpu as pltpu
from jax.sharding import PartitionSpec as P

ITERS = 4
PHASES = 4
LOW = ITERS
HIGH = 2 * ITERS
FIELDS = 5
LANE_STEP = LOW + HIGH
UNROLL = 3
GROUP = 4

VMEM = pl.BlockSpec(memory_space=pltpu.VMEM)
SMEM = pl.BlockSpec(memory_space=pltpu.SMEM)


def z_up(a):
    return pltpu.roll(a, a.shape[-2] - 1, a.ndim - 2)


def z_down(a):
    return pltpu.roll(a, 1, a.ndim - 2)


def y_up(a):
    return pltpu.roll(a, a.shape[-1] - 1, a.ndim - 1)


def y_down(a):
    return pltpu.roll(a, 1, a.ndim - 1)


def reciprocal(a):
    r = pl.reciprocal(a, approx=True)
    return r * (2.0 - a * r)


def merged(k, bz):
    return 3 * (ITERS - k + 1) <= bz


def start_copies(sources, targets, sems):
    copies = []
    for g in range(sources[0].shape[0] // GROUP):
        at = pl.ds(g * GROUP, GROUP)
        copies.append(
            [pltpu.make_async_copy(a.at[at], b.at[at], sems.at[g, f]) for f, (a, b) in enumerate(zip(sources, targets))]
        )
        for copy in copies[-1]:
            copy.start()
    return copies


def clean_group(g, field_ref, phase_ref):
    bx, bz, by = phase_ref.shape
    ix, iz, iy = lax.axis_index("gx"), lax.axis_index("gz"), lax.axis_index("gy")
    plane, row, lane = (lax.broadcasted_iota(jnp.int32, (GROUP, bz, by), d) for d in range(3))
    at = pl.ds(g * GROUP, GROUP)
    vx, vz, vy, p = (field_ref[f, at] for f in range(FIELDS - 1))
    if g == 0:
        vx = jnp.where((plane > 0) | (ix > 0), vx, 0.0)
    vz = jnp.where((row > 0) | (iz > 0), vz, 0.0)
    vy = jnp.where((lane > 0) | (iy > 0), vy, 0.0)
    return vx, vz, vy, p, phase_ref[at].astype(jnp.float32)


def pack_kernel(
    vx_hbm, vz_hbm, vy_hbm, p_hbm, phase_hbm, edge_hbm, x_0_hbm, x_1_hbm, stack_hbm,
    field_ref, phase_ref, edge_ref, stack_ref, sems, out_sems,
):
    bx, bz, by = phase_ref.shape
    targets = [field_ref.at[f] for f in range(FIELDS - 1)] + [phase_ref]
    copies = start_copies((vx_hbm, vz_hbm, vy_hbm, p_hbm, phase_hbm), targets, sems)
    lane = lax.broadcasted_iota(jnp.int32, (1, bz, by), 2)
    half = bx // GROUP // 2
    outs = []

    def out(source, target):
        outs.append(pltpu.make_async_copy(source, target, out_sems.at[len(outs)]))
        outs[-1].start()

    for g in range(half):
        edge = jnp.zeros((GROUP, bz, by), jnp.float32)
        for upper in range(2):
            at = pl.ds((g + upper * half) * GROUP, GROUP)
            for copy in copies[g + upper * half]:
                copy.wait()
            for f, a in enumerate(clean_group(g + upper * half, field_ref, phase_ref)):
                stack_ref[at, f] = a
                base = by // 2 * upper + LANE_STEP * f
                first = pltpu.roll(a, base, 2) if base else a
                edge = jnp.where((lane >= base) & (lane < base + HIGH), first, edge)
                last = pltpu.roll(a, (base + LANE_STEP) % by, 2)
                edge = jnp.where((lane >= base + HIGH) & (lane < base + LANE_STEP), last, edge)
            out(stack_ref.at[at], stack_hbm.at[at])
        at = pl.ds(g * GROUP, GROUP)
        edge_ref[at] = edge
        out(edge_ref.at[at], edge_hbm.at[at])
    sem = out_sems.at[len(outs)], out_sems.at[len(outs) + 1]
    lower, upper = stack_ref.at[pl.ds(0, HIGH)], stack_ref.at[pl.ds(HIGH, HIGH)]
    for parity, (first, second) in enumerate(((upper, lower), (lower, upper))):
        @pl.when(lax.rem(lax.axis_index("gx"), 2) == parity)
        def _():
            pair = pltpu.make_async_copy(first, x_0_hbm, sem[0]), pltpu.make_async_copy(second, x_1_hbm, sem[1])
            for copy in pair:
                copy.start()
            for copy in pair:
                copy.wait()

    for copy in outs:
        copy.wait()


def unpack(ref, at, side, upper, ok, tables):
    bz, by = ref.shape[-2:]
    block = ref[pl.ds(at * FIELDS, GROUP * FIELDS)].reshape(GROUP, FIELDS, bz, by)
    edge = ref[pl.ds(side, GROUP)]
    iy = lax.axis_index("gy")
    lane = lax.broadcasted_iota(jnp.int32, (1, bz, by), 2)
    right = (lane < HIGH) & (iy < lax.axis_size("gy") - 1)
    left = (lane >= by - LOW) & (iy > 0)
    ok = jnp.where(ok, 1.0, 0.0)
    out = []
    for f in range(FIELDS):
        shift = by // 2 * upper + LANE_STEP * f
        a = pltpu.roll(edge, (by - shift) % by, 2) if shift else edge
        b = pltpu.roll(edge, (by - LANE_STEP - shift) % by, 2)
        out.append([block[:, f], jnp.where(right, a, jnp.where(left, b, 0.0))])
    pair = out.pop()
    for number, table in enumerate(tables):
        values = []
        for part, ph in enumerate(pair):
            value = jnp.broadcast_to(table[0], ph.shape)
            for index in range(1, PHASES):
                value = jnp.where(ph == float(index), table[index], value)
            if number == 0:
                value = value * ok
                if part:
                    value = jnp.where(right | left, value, 0.0)
            values.append(value)
        out.append(values)
    return out


def unpack_own(ref, ok, tables, store):
    bx = 2 * HIGH
    for upper in range(2):

        def group(g, carry):
            at = g * GROUP + upper * HIGH
            store(pl.ds(LOW + at, GROUP), unpack(ref, at, bx * FIELDS + g * GROUP, upper, ok, tables))
            return carry

        lax.fori_loop(0, HIGH // GROUP, group, 0)


def unpack_sides(ref, bx, ok, tables, store):
    ix, nx = lax.axis_index("gx"), lax.axis_size("gx")
    for at in range(0, HIGH + LOW, GROUP):
        low = at >= HIGH
        side = (HIGH + LOW) * FIELDS + at
        values = unpack(ref, at, side, int(low), ok & (ix > 0 if low else ix < nx - 1), tables)
        store(pl.ds(at - HIGH if low else LOW + bx + at, GROUP), values)


def own_kernel(own_ref, side_ref, scale_ref, power_ref, rho_table_ref, v_ref, p_ref, pre_ref, power_field_ref, rho_ref):
    by = own_ref.shape[-1]
    refs = [v_ref.at[d] for d in range(3)] + [p_ref, pre_ref, power_field_ref, rho_ref]

    def store(planes, values):
        for ref, (own, beside) in zip(refs, values):
            ref[planes, :, 0:by] = own
            ref[planes, :, by : 2 * by] = beside

    tables = (scale_ref, power_ref, rho_table_ref)
    unpack_own(own_ref, True, tables, store)
    unpack_sides(side_ref, 2 * HIGH, True, tables, store)


def halo_store(halo_ref, shared_ref, t):
    bz = shared_ref.shape[-2]
    by = shared_ref.shape[-1] // 2
    rows = slice(t * bz // 2, (t + 1) * bz // 2)

    def store(planes, values):
        for n, pair in enumerate(values):
            for part, value in enumerate(pair):
                at = slice(part * by, (part + 1) * by)
                halo_ref[n, planes, t * bz : (t + 1) * bz, at] = value
                if n >= 4:
                    shared_ref[n - 4, planes, rows, at] = value[:, rows]

    return store


def face_kernel(face_0_ref, face_1_ref, scale_ref, power_ref, rho_table_ref, halo_ref, shared_ref):
    iz, nz = lax.axis_index("gz"), lax.axis_size("gz")
    tables = (scale_ref, power_ref, rho_table_ref)
    for parity in range(2):
        @pl.when(lax.rem(iz, 2) == parity)
        def _():
            faces = (face_0_ref, face_1_ref)
            unpack_own(faces[parity], iz < nz - 1, tables, halo_store(halo_ref, shared_ref, 0))
            unpack_own(faces[1 - parity], iz > 0, tables, halo_store(halo_ref, shared_ref, 1))


def main_kernel(
    v_ref, p0_ref, pre_ref, power_field_ref, rho_ref, _halo, _shared,
    corner_0_ref, corner_1_ref, scale_ref, power_ref, rho_table_ref,
    out_vx_ref, out_vz_ref, out_vy_ref, out_p_ref, out_eta_ref, sum_ref, halo_ref, shared_ref,
    va_ref, vb_ref, p_ref, weight_ref, weight2_ref,
):
    bx, bz, by = out_p_ref.shape
    lanes = 2 * by
    nx, nz, ny = lax.axis_size("gx"), lax.axis_size("gz"), lax.axis_size("gy")
    ix, iz, iy = lax.axis_index("gx"), lax.axis_index("gz"), lax.axis_index("gy")
    tables = (scale_ref, power_ref, rho_table_ref)
    for parity in range(2):
        @pl.when(lax.rem(iz, 2) == parity)
        def _():
            corners = (corner_0_ref, corner_1_ref)
            unpack_sides(corners[parity], bx, iz < nz - 1, tables, halo_store(halo_ref, shared_ref, 0))
            unpack_sides(corners[1 - parity], bx, iz > 0, tables, halo_store(halo_ref, shared_ref, 1))

    for ref, high in ((weight_ref, 2 * bz), (weight2_ref, bz + bz // 2)):
        shape = ref.shape[1:]
        r = lax.broadcasted_iota(jnp.int32, shape, 0)
        c = lax.broadcasted_iota(jnp.int32, shape, 1)
        zg = iz * bz + jnp.where(r < high, r, r - shape[0])
        yg = iy * by + jnp.where(c < by + HIGH, c, c - lanes)
        filled = (c < by + HIGH) | (c >= lanes - LOW)
        inside = filled & (zg >= 0) & (zg < nz * bz) & (yg >= 0) & (yg < ny * by)
        ref[0] = jnp.where(inside, 0.05, 0.0)
        ref[1] = jnp.where(inside & (zg > 0), 0.05, 0.0)
        ref[2] = jnp.where(inside & (yg > 0), 0.05, 0.0)
        ref[3] = jnp.where(inside, 0.0, 1.0)

    for k in range(1, ITERS + 1):
        old, new = (va_ref, vb_ref) if k % 2 else (vb_ref, va_ref)
        last = k == ITERS
        rows = 2 * bz if merged(k, bz) else 3 * bz
        own_constants = (pre_ref, power_field_ref, rho_ref)
        weight = weight2_ref if merged(k, bz) else weight_ref
        narrow = merged(k + 1, bz) and not merged(k, bz)
        all_rows = pl.ds(0, rows)

        def keep(value):
            if narrow:
                row = lax.broadcasted_iota(jnp.int32, (bz, lanes), 0)
                halo = jnp.where(row < bz // 2, value[..., bz : 2 * bz, :], value[..., 2 * bz :, :])
                return [(pl.ds(0, bz), value[..., 0:bz, :]), (pl.ds(bz, bz), halo)]
            return [(all_rows, value)]

        def store(d, j, count, value):
            for at, part in keep(value):
                new[d, pl.ds(j, count), at, :] = part

        def constant(n, planes):
            halo = shared_ref[n, planes] if merged(k, bz) else halo_ref[4 + n, planes]
            return jnp.concatenate([own_constants[n][planes], halo], axis=1)

        def load(d, j, count):
            planes = pl.ds(j, count)
            if k == 1:
                return jnp.concatenate([v_ref[d, planes], halo_ref[d, planes]], axis=1)
            return old[d, planes, all_rows, :]

        def cells(j, count):
            planes = pl.ds(j, count)
            vx1 = load(0, j, count + 1)
            vx = vx1[:count]
            vz, vy = load(1, j, count), load(2, j, count)
            if k == 1:
                p = jnp.concatenate([p0_ref[planes], halo_ref[3, planes]], axis=1)
            else:
                p = p_ref[planes, all_rows, :]
            rx = vx1[1:] - vx
            rz = z_up(vz) - vz
            ry = y_up(vy) - vy
            a = rx - ry
            b = ry - rz
            inv = (a * (a + b) + b * b) * (1.0 / 3.0) + 1.0
            eta = constant(0, planes) * jnp.exp2(constant(1, planes) * jnp.log(inv))
            quarter = 0.25 * eta
            div = rx + ry + rz
            p = p - quarter * (div + div)
            tx, tz, ty = eta * rx - p, eta * rz - p, eta * ry - p
            sz = quarter + z_down(quarter)
            sy = quarter + y_down(quarter)
            return vx, vz, vy, eta, p, quarter, tx, tz, ty, sz, sy

        def chunk(j, count, carry, start=False):
            planes = pl.ds(j, count)
            vx, vz, vy, eta, p, quarter, tx, tz, ty, sz, sy = cells(j, count)
            vz0, vy0 = load(1, j - 1, 1), load(2, j - 1, 1)
            quarter0, tx0, sz0, sy0, part_z0, part_y0, scale_z0, scale_y0 = carry
            join = lambda first, rest: jnp.concatenate([first, rest[:-1]], axis=0) if count > 1 else first
            bias = weight[3:4]
            sx = quarter + join(quarter0, quarter)
            exz = sz + join(sz0, sz)
            exy = sy + join(sy0, sy)
            ezy = sz + y_down(sz)
            fxz = exz * (vx - z_down(vx))
            fxy = exy * (vx - y_down(vx))
            low_vz, low_vy = join(vz0, vz), join(vy0, vy)
            gzx = exz * (vz - low_vz)
            hyx = exy * (vy - low_vy)
            gzy = ezy * (vz - y_down(vz))
            hyz = ezy * (vy - z_down(vy))
            res_x = (tx - join(tx0, tx)) + ((z_up(fxz) - fxz) + (y_up(fxy) - fxy))
            new_vx = vx + weight[0:1] * reciprocal(sx + bias) * res_x
            part_z = (tz - z_down(tz)) - constant(2, planes) + ((y_up(gzy) - gzy) - gzx)
            part_y = (ty - y_down(ty)) + ((z_up(hyz) - hyz) - hyx)
            scale_z = weight[1:2] * reciprocal(sz + bias)
            scale_y = weight[2:3] * reciprocal(sy + bias)
            new_vz = low_vz + join(scale_z0, scale_z) * (join(part_z0, part_z) + gzx)
            new_vy = low_vy + join(scale_y0, scale_y) * (join(part_y0, part_y) + hyx)
            if last:
                at = pl.ds(j - LOW, count)
                out_vx_ref[at] = new_vx[:, 0:bz, 0:by]
                out_p_ref[at] = p[:, 0:bz, 0:by]
                out_eta_ref[at] = eta[:, 0:bz, 0:by]
                sum_ref[...] += jnp.sum(p[:, 0:bz, 0:by], axis=0)
                if not start:
                    at = pl.ds(j - 1 - LOW, count)
                    out_vz_ref[at] = new_vz[:, 0:bz, 0:by]
                    out_vy_ref[at] = new_vy[:, 0:bz, 0:by]
            else:
                for at, part in keep(p):
                    p_ref[planes, at, :] = part
                store(0, j, count, new_vx)
                if not start:
                    store(1, j - 1, count, new_vz)
                    store(2, j - 1, count, new_vy)
            return tuple(a[-1:] for a in (quarter, tx, sz, sy, part_z, part_y, scale_z, scale_y))

        first, count = k, bx + LOW + HIGH - 3 * k
        if last:
            sum_ref[...] = jnp.zeros((bz, by), jnp.float32)
        _, _, _, _, p, quarter, tx, _, _, sz, sy = cells(first - 1, 1)
        if not last:
            for at, part in keep(p):
                p_ref[pl.ds(first - 1, 1), at, :] = part
        zero = jnp.zeros((1, rows, lanes), jnp.float32)
        carry = chunk(first, 1, (quarter, tx, sz, sy, zero, zero, zero, zero), start=True)
        steps, rest = divmod(count - 1, UNROLL)
        carry = lax.fori_loop(
            0, steps, lambda s, carry: chunk(first + 1 + s * UNROLL, UNROLL, carry), carry
        )
        if rest:
            carry = chunk(first + 1 + steps * UNROLL, rest, carry)
        j = first + count
        quarter0, tx0, sz0, sy0, part_z0, part_y0, scale_z0, scale_y0 = carry
        _, vz, vy, _, p, quarter, tx, _, _, sz, sy = cells(j, 1)
        vz0, vy0 = load(1, j - 1, 1), load(2, j - 1, 1)
        new_vz = vz0 + scale_z0 * (part_z0 + (sz + sz0) * (vz - vz0))
        new_vy = vy0 + scale_y0 * (part_y0 + (sy + sy0) * (vy - vy0))
        if last:
            out_vz_ref[pl.ds(j - 1 - LOW, 1)] = new_vz[:, 0:bz, 0:by]
            out_vy_ref[pl.ds(j - 1 - LOW, 1)] = new_vy[:, 0:bz, 0:by]
        else:
            for at, part in keep(p):
                p_ref[pl.ds(j, 1), at, :] = part
            store(1, j - 1, 1, new_vz)
            store(2, j - 1, 1, new_vy)

        if last:
            @pl.when(ix == 0)
            def _():
                out_vx_ref[0] = jnp.zeros((bz, by), jnp.float32)
        else:
            plane = jnp.zeros((3 * bz, lanes), jnp.float32)

            @pl.when(ix == 0)
            def _():
                for i in range(k, LOW):
                    for d in range(3):
                        new[d, i] = plane
                new[0, LOW] = plane

            @pl.when(ix == nx - 1)
            def _():
                for i in range(LOW + bx, first + count):
                    for d in range(3):
                        new[d, i] = plane


def final_kernel(p_ref, sum_ref, out_ref, *, cells):
    mean = jnp.sum(sum_ref[...]) * (1.0 / cells)
    out_ref[...] = p_ref[...] - mean


def swap(a, axis, start):
    count = lax.axis_size(axis)
    return lax.ppermute(a, axis, [(i, j) for k in range(start, count - 1, 2) for i, j in ((k, k + 1), (k + 1, k))])


def sum_everywhere(total):
    axes = ("gx", "gy", "gz")
    devices = math.prod(lax.axis_size(a) for a in axes)
    if devices & (devices - 1):
        return lax.psum(total, axes)
    bits = [1 << n for n in range(devices.bit_length() - 1)]
    for stage in [bits[:1]] + [bits[n : n + 2] for n in range(1, len(bits), 2)]:
        masks = stage if len(stage) == 1 else [stage[0], stage[1], stage[0] + stage[1]]
        total = sum([lax.ppermute(total, axes, [(i, i ^ m) for i in range(devices)]) for m in masks], total)
    return total


def local(vel_x, vel_y, vel_z, pressure, phase, visc_scale, power_n, density):
    bx, bz, by = pressure.shape
    assert bx == 2 * HIGH and bz == HIGH
    f32 = jnp.float32
    ix, iz, iy = lax.axis_index("gx"), lax.axis_index("gz"), lax.axis_index("gy")
    ny = lax.axis_size("gy")
    cells = bx * bz * by * math.prod(lax.axis_size(a) for a in ("gx", "gz", "gy"))
    deep = bx + LOW + HIGH
    rows, lanes = 3 * bz, 2 * by
    shape = lambda *dims: jax.ShapeDtypeStruct(dims, f32)
    block = shape(bx, bz, by)
    scratch = lambda *dims: pltpu.VMEM(dims, f32)
    mebibyte = 1024 * 1024

    hbm = pl.BlockSpec(memory_space=pltpu.HBM)

    groups = bx // GROUP
    edge, half_0, half_1, stack = pl.pallas_call(
        pack_kernel,
        out_shape=(
            shape(HIGH, bz, by),
            shape(HIGH, FIELDS, bz, by),
            shape(HIGH, FIELDS, bz, by),
            shape(bx, FIELDS, bz, by),
        ),
        in_specs=[hbm] * 5,
        out_specs=(hbm,) * 4,
        scratch_shapes=[
            scratch(FIELDS - 1, bx, bz, by),
            pltpu.VMEM((bx, bz, by), jnp.int32),
            scratch(HIGH, bz, by),
            scratch(bx, FIELDS, bz, by),
            pltpu.SemaphoreType.DMA((groups, FIELDS)),
            pltpu.SemaphoreType.DMA((groups + groups // 2 + 2,)),
        ],
        compiler_params=pltpu.CompilerParams(vmem_limit_bytes=58 * mebibyte),
        cost_estimate=pl.CostEstimate(flops=0, bytes_accessed=16 * bx * bz * by * 4, transcendentals=0),
    )(vel_x, vel_z, vel_y, pressure, phase)

    side = swap(edge, "gy", 0)
    x_0, x_1 = swap(half_0, "gx", 0), swap(half_1, "gx", 1)
    if ny > 2:
        even = lax.rem(iy, 2) == 0
        other = swap(edge, "gy", 1)
        lane = lax.broadcasted_iota(jnp.int32, side.shape, 2) % (by // 2) % LANE_STEP
        side = jnp.where((lane < HIGH) == even, side, other)
    side_0, side_1 = swap(side, "gx", 0), swap(side, "gx", 1)

    face = jnp.concatenate([stack.reshape(bx * FIELDS, bz, by), side])
    face_1 = swap(face, "gz", 1)
    face_0 = swap(face, "gz", 0)
    even = lax.rem(ix, 2) == 0
    choose = lambda a, b: (jnp.where(even, a, b), jnp.where(even, b, a)[HIGH - LOW :])
    tiles = [a.reshape(-1, bz, by) for a in choose(x_0, x_1) + choose(side_0, side_1)]
    sides = jnp.concatenate(tiles)
    corner_1 = swap(sides, "gz", 1)
    corner_0 = swap(sides, "gz", 0)

    tables = (visc_scale, (0.5 / math.log(2.0)) * (1.0 / power_n - 1.0), density)
    field = shape(deep, bz, lanes)
    own = pl.pallas_call(
        own_kernel,
        out_shape=(shape(3, deep, bz, lanes),) + (field,) * 4,
        in_specs=[VMEM] * 2 + [SMEM] * 3,
        out_specs=(VMEM,) * 5,
        compiler_params=pltpu.CompilerParams(vmem_limit_bytes=8 * mebibyte),
        cost_estimate=pl.CostEstimate(flops=deep * 30 * bz * lanes, bytes_accessed=12 * deep * bz * lanes * 4, transcendentals=0),
    )(face, sides, *tables)
    halo = pl.pallas_call(
        face_kernel,
        out_shape=(shape(7, deep, 2 * bz, lanes), shape(3, deep, bz, lanes)),
        in_specs=[VMEM] * 2 + [SMEM] * 3,
        out_specs=(VMEM,) * 2,
        compiler_params=pltpu.CompilerParams(vmem_limit_bytes=8 * mebibyte),
        cost_estimate=pl.CostEstimate(flops=deep * 30 * bz * lanes, bytes_accessed=24 * bx * bz * lanes * 4, transcendentals=0),
    )(face_0, face_1, *tables)
    vx, vz, vy, p, eta, total, _, _ = pl.pallas_call(
        main_kernel,
        out_shape=(block,) * 5 + (shape(bz, by),) + tuple(shape(*a.shape) for a in halo),
        in_specs=[VMEM] * 9 + [SMEM] * 3,
        out_specs=(VMEM,) * 8,
        input_output_aliases={5: 6, 6: 7},
        scratch_shapes=[
            scratch(3, deep, rows, lanes),
            scratch(3, deep, rows, lanes),
            scratch(deep, rows, lanes),
            scratch(4, rows, lanes),
            scratch(4, 2 * bz, lanes),
        ],
        compiler_params=pltpu.CompilerParams(vmem_limit_bytes=32 * mebibyte),
    )(*own, *halo, corner_0, corner_1, *tables)

    total = sum_everywhere(total)
    p = pl.pallas_call(
        lambda *refs: final_kernel(*refs, cells=float(cells)),
        out_shape=block,
        in_specs=[VMEM] * 2,
        out_specs=VMEM,
        compiler_params=pltpu.CompilerParams(vmem_limit_bytes=4 * mebibyte),
    )(p, total)
    return (vx, vy, vz, p, eta)


def solution(mesh):
    spec = P("gx", "gz", "gy")
    return jax.shard_map(
        local,
        mesh=mesh,
        in_specs=(spec,) * 5 + (P(),) * 3,
        out_specs=(spec,) * 5,
        check_vma=False,
    )
```

```python
import math

import jax
import jax.numpy as jnp
from jax import lax
from jax.experimental import pallas as pl
from jax.experimental.pallas import tpu as pltpu
from jax.sharding import PartitionSpec as P

ITERS = 4
PHASES = 4
LOW = ITERS
HIGH = 2 * ITERS
FIELDS = 5
LANE_STEP = LOW + HIGH
UNROLL = 3
GROUP = 4

VMEM = pl.BlockSpec(memory_space=pltpu.VMEM)
SMEM = pl.BlockSpec(memory_space=pltpu.SMEM)


def z_up(a):
    return pltpu.roll(a, a.shape[-2] - 1, a.ndim - 2)


def z_down(a):
    return pltpu.roll(a, 1, a.ndim - 2)


def y_up(a):
    return pltpu.roll(a, a.shape[-1] - 1, a.ndim - 1)


def y_down(a):
    return pltpu.roll(a, 1, a.ndim - 1)


def reciprocal(a):
    r = pl.reciprocal(a, approx=True)
    return r * (2.0 - a * r)


def merged(k, bz):
    return 3 * (ITERS - k + 1) <= bz


def start_copies(sources, targets, sems):
    copies = []
    for g in range(sources[0].shape[0] // GROUP):
        at = pl.ds(g * GROUP, GROUP)
        copies.append(
            [pltpu.make_async_copy(a.at[at], b.at[at], sems.at[g, f]) for f, (a, b) in enumerate(zip(sources, targets))]
        )
        for copy in copies[-1]:
            copy.start()
    return copies


def clean_group(g, field_ref, phase_ref):
    bx, bz, by = phase_ref.shape
    ix, iz, iy = lax.axis_index("gx"), lax.axis_index("gz"), lax.axis_index("gy")
    plane, row, lane = (lax.broadcasted_iota(jnp.int32, (GROUP, bz, by), d) for d in range(3))
    at = pl.ds(g * GROUP, GROUP)
    vx, vz, vy, p = (field_ref[f, at] for f in range(FIELDS - 1))
    if g == 0:
        vx = jnp.where((plane > 0) | (ix > 0), vx, 0.0)
    vz = jnp.where((row > 0) | (iz > 0), vz, 0.0)
    vy = jnp.where((lane > 0) | (iy > 0), vy, 0.0)
    return vx, vz, vy, p, phase_ref[at].astype(jnp.float32)


def add_edges(edge, fields, upper):
    by = edge.shape[-1]
    lane = lax.broadcasted_iota(jnp.int32, (1,) + edge.shape[1:], 2)
    for f, a in enumerate(fields):
        base = by // 2 * upper + LANE_STEP * f
        first = pltpu.roll(a, base, 2) if base else a
        edge = jnp.where((lane >= base) & (lane < base + HIGH), first, edge)
        last = pltpu.roll(a, (base + LANE_STEP) % by, 2)
        edge = jnp.where((lane >= base + HIGH) & (lane < base + LANE_STEP), last, edge)
    return edge


def sides_kernel(x_0_ref, x_1_ref, sides_ref, edge_ref):
    bz, by = edge_ref.shape[1:]
    for parity in range(2):
        @pl.when(lax.rem(lax.axis_index("gx"), 2) == parity)
        def _():
            high, low = (x_0_ref, x_1_ref) if parity == 0 else (x_1_ref, x_0_ref)
            for g in range(HIGH // GROUP):
                edge = jnp.zeros((GROUP, bz, by), jnp.float32)
                for upper, ref in enumerate((high, low)):
                    at = g * GROUP
                    if upper and at < HIGH - LOW:
                        continue
                    block = ref[pl.ds(at, GROUP)]
                    to = HIGH + at - (HIGH - LOW) if upper else at
                    sides_ref[pl.ds(to * FIELDS, GROUP * FIELDS)] = block.reshape(GROUP * FIELDS, bz, by)
                    edge = add_edges(edge, [block[:, f] for f in range(FIELDS)], upper)
                edge_ref[pl.ds(g * GROUP, GROUP)] = edge


def pack_kernel(
    vx_hbm, vz_hbm, vy_hbm, p_hbm, phase_hbm, edge_hbm, x_0_hbm, x_1_hbm, stack_hbm,
    field_ref, phase_ref, edge_ref, stack_ref, sems, out_sems,
):
    bx, bz, by = phase_ref.shape
    targets = [field_ref.at[f] for f in range(FIELDS - 1)] + [phase_ref]
    copies = start_copies((vx_hbm, vz_hbm, vy_hbm, p_hbm, phase_hbm), targets, sems)
    half = bx // GROUP // 2
    outs = []

    def out(source, target):
        outs.append(pltpu.make_async_copy(source, target, out_sems.at[len(outs)]))
        outs[-1].start()

    for g in range(half):
        edge = jnp.zeros((GROUP, bz, by), jnp.float32)
        for upper in range(2):
            at = pl.ds((g + upper * half) * GROUP, GROUP)
            for copy in copies[g + upper * half]:
                copy.wait()
            fields = clean_group(g + upper * half, field_ref, phase_ref)
            for f, a in enumerate(fields):
                stack_ref[at, f] = a
            edge = add_edges(edge, fields, upper)
            out(stack_ref.at[at], stack_hbm.at[at])
        at = pl.ds(g * GROUP, GROUP)
        edge_ref[at] = edge
        out(edge_ref.at[at], edge_hbm.at[at])
    sem = out_sems.at[len(outs)], out_sems.at[len(outs) + 1]
    lower, upper = stack_ref.at[pl.ds(0, HIGH)], stack_ref.at[pl.ds(HIGH, HIGH)]
    for parity, (first, second) in enumerate(((upper, lower), (lower, upper))):
        @pl.when(lax.rem(lax.axis_index("gx"), 2) == parity)
        def _():
            pair = pltpu.make_async_copy(first, x_0_hbm, sem[0]), pltpu.make_async_copy(second, x_1_hbm, sem[1])
            for copy in pair:
                copy.start()
            for copy in pair:
                copy.wait()

    for copy in outs:
        copy.wait()


def read_tables(ref):
    return [[ref[n, index] for index in range(PHASES)] for n in range(3)]


def unpack(ref, at, side, upper, ok, tables):
    bz, by = ref.shape[-2:]
    block = ref[pl.ds(at * FIELDS, GROUP * FIELDS)].reshape(GROUP, FIELDS, bz, by)
    edge = ref[pl.ds(side, GROUP)]
    iy = lax.axis_index("gy")
    lane = lax.broadcasted_iota(jnp.int32, (1, bz, by), 2)
    right = (lane < HIGH) & (iy < lax.axis_size("gy") - 1)
    left = (lane >= by - LOW) & (iy > 0)
    ok = jnp.where(ok, 1.0, 0.0)
    out = []
    for f in range(FIELDS):
        shift = by // 2 * upper + LANE_STEP * f
        a = pltpu.roll(edge, (by - shift) % by, 2) if shift else edge
        b = pltpu.roll(edge, (by - LANE_STEP - shift) % by, 2)
        out.append([block[:, f], jnp.where(right, a, jnp.where(left, b, 0.0))])
    pair = out.pop()
    for number, table in enumerate(tables):
        values = []
        for part, ph in enumerate(pair):
            value = jnp.broadcast_to(table[0], ph.shape)
            for index in range(1, PHASES):
                value = jnp.where(ph == float(index), table[index], value)
            if number == 0:
                value = value * ok
                if part:
                    value = jnp.where(right | left, value, 0.0)
            values.append(value)
        out.append(values)
    return out


def unpack_own(ref, ok, tables, store):
    bx = 2 * HIGH
    for upper in range(2):

        def group(g, carry):
            at = g * GROUP + upper * HIGH
            store(pl.ds(LOW + at, GROUP), unpack(ref, at, bx * FIELDS + g * GROUP, upper, ok, tables))
            return carry

        lax.fori_loop(0, HIGH // GROUP, group, 0)


def unpack_sides(ref, bx, ok, tables, store):
    ix, nx = lax.axis_index("gx"), lax.axis_size("gx")
    for at in range(0, HIGH + LOW, GROUP):
        low = at >= HIGH
        side = (HIGH + LOW) * FIELDS + (at - LOW if low else at)
        values = unpack(ref, at, side, int(low), ok & (ix > 0 if low else ix < nx - 1), tables)
        store(pl.ds(at - HIGH if low else LOW + bx + at, GROUP), values)


def own_kernel(own_ref, side_ref, tables_ref, v_ref, p_ref, pre_ref, power_field_ref, rho_ref):
    by = own_ref.shape[-1]
    refs = [v_ref.at[d] for d in range(3)] + [p_ref, pre_ref, power_field_ref, rho_ref]

    def store(planes, values):
        for ref, (own, beside) in zip(refs, values):
            ref[planes, :, 0:by] = own
            ref[planes, :, by : 2 * by] = beside

    tables = read_tables(tables_ref)
    unpack_own(own_ref, True, tables, store)
    unpack_sides(side_ref, 2 * HIGH, True, tables, store)


def halo_store(halo_ref, shared_ref, t):
    bz = shared_ref.shape[-2]
    by = shared_ref.shape[-1] // 2
    rows = slice(t * bz // 2, (t + 1) * bz // 2)

    def store(planes, values):
        for n, pair in enumerate(values):
            for part, value in enumerate(pair):
                at = slice(part * by, (part + 1) * by)
                halo_ref[n, planes, t * bz : (t + 1) * bz, at] = value
                if n >= 4:
                    shared_ref[n - 4, planes, rows, at] = value[:, rows]

    return store


def face_kernel(face_0_ref, face_1_ref, tables_ref, halo_ref, shared_ref):
    iz, nz = lax.axis_index("gz"), lax.axis_size("gz")
    tables = read_tables(tables_ref)
    for parity in range(2):
        @pl.when(lax.rem(iz, 2) == parity)
        def _():
            faces = (face_0_ref, face_1_ref)
            unpack_own(faces[parity], iz < nz - 1, tables, halo_store(halo_ref, shared_ref, 0))
            unpack_own(faces[1 - parity], iz > 0, tables, halo_store(halo_ref, shared_ref, 1))


def main_kernel(
    v_ref, p0_ref, pre_ref, power_field_ref, rho_ref, _halo, _shared,
    corner_0_ref, corner_1_ref, tables_ref,
    out_vx_ref, out_vz_ref, out_vy_ref, out_p_ref, out_eta_ref, sum_ref, halo_ref, shared_ref,
    va_ref, vb_ref, p_ref, weight_ref, weight2_ref,
):
    bx, bz, by = out_p_ref.shape
    lanes = 2 * by
    nx, nz, ny = lax.axis_size("gx"), lax.axis_size("gz"), lax.axis_size("gy")
    ix, iz, iy = lax.axis_index("gx"), lax.axis_index("gz"), lax.axis_index("gy")
    tables = read_tables(tables_ref)
    for parity in range(2):
        @pl.when(lax.rem(iz, 2) == parity)
        def _():
            corners = (corner_0_ref, corner_1_ref)
            unpack_sides(corners[parity], bx, iz < nz - 1, tables, halo_store(halo_ref, shared_ref, 0))
            unpack_sides(corners[1 - parity], bx, iz > 0, tables, halo_store(halo_ref, shared_ref, 1))

    for ref, high in ((weight_ref, 2 * bz), (weight2_ref, bz + bz // 2)):
        shape = ref.shape[1:]
        r = lax.broadcasted_iota(jnp.int32, shape, 0)
        c = lax.broadcasted_iota(jnp.int32, shape, 1)
        zg = iz * bz + jnp.where(r < high, r, r - shape[0])
        yg = iy * by + jnp.where(c < by + HIGH, c, c - lanes)
        filled = (c < by + HIGH) | (c >= lanes - LOW)
        inside = filled & (zg >= 0) & (zg < nz * bz) & (yg >= 0) & (yg < ny * by)
        ref[0] = jnp.where(inside, 0.05, 0.0)
        ref[1] = jnp.where(inside & (zg > 0), 0.05, 0.0)
        ref[2] = jnp.where(inside & (yg > 0), 0.05, 0.0)
        ref[3] = jnp.where(inside, 0.0, 1.0)

    for k in range(1, ITERS + 1):
        old, new = (va_ref, vb_ref) if k % 2 else (vb_ref, va_ref)
        last = k == ITERS
        rows = 2 * bz if merged(k, bz) else 3 * bz
        own_constants = (pre_ref, power_field_ref, rho_ref)
        weight = weight2_ref if merged(k, bz) else weight_ref
        narrow = merged(k + 1, bz) and not merged(k, bz)
        all_rows = pl.ds(0, rows)

        def keep(value):
            if narrow:
                row = lax.broadcasted_iota(jnp.int32, (bz, lanes), 0)
                halo = jnp.where(row < bz // 2, value[..., bz : 2 * bz, :], value[..., 2 * bz :, :])
                return [(pl.ds(0, bz), value[..., 0:bz, :]), (pl.ds(bz, bz), halo)]
            return [(all_rows, value)]

        def store(d, j, count, value):
            for at, part in keep(value):
                new[d, pl.ds(j, count), at, :] = part

        def constant(n, planes):
            halo = shared_ref[n, planes] if merged(k, bz) else halo_ref[4 + n, planes]
            return jnp.concatenate([own_constants[n][planes], halo], axis=1)

        def load(d, j, count):
            planes = pl.ds(j, count)
            if k == 1:
                return jnp.concatenate([v_ref[d, planes], halo_ref[d, planes]], axis=1)
            return old[d, planes, all_rows, :]

        def cells(j, count):
            planes = pl.ds(j, count)
            vx1 = load(0, j, count + 1)
            vx = vx1[:count]
            vz, vy = load(1, j, count), load(2, j, count)
            if k == 1:
                p = jnp.concatenate([p0_ref[planes], halo_ref[3, planes]], axis=1)
            else:
                p = p_ref[planes, all_rows, :]
            rx = vx1[1:] - vx
            rz = z_up(vz) - vz
            ry = y_up(vy) - vy
            a = rx - ry
            b = ry - rz
            inv = (a * (a + b) + b * b) * (1.0 / 3.0) + 1.0
            eta = constant(0, planes) * jnp.exp2(constant(1, planes) * jnp.log(inv))
            quarter = 0.25 * eta
            div = rx + ry + rz
            p = p - quarter * (div + div)
            tx, tz, ty = eta * rx - p, eta * rz - p, eta * ry - p
            sz = quarter + z_down(quarter)
            sy = quarter + y_down(quarter)
            return vx, vz, vy, eta, p, quarter, tx, tz, ty, sz, sy

        def chunk(j, count, carry, start=False):
            planes = pl.ds(j, count)
            vx, vz, vy, eta, p, quarter, tx, tz, ty, sz, sy = cells(j, count)
            vz0, vy0 = load(1, j - 1, 1), load(2, j - 1, 1)
            quarter0, tx0, sz0, sy0, part_z0, part_y0, scale_z0, scale_y0 = carry
            join = lambda first, rest: jnp.concatenate([first, rest[:-1]], axis=0) if count > 1 else first
            bias = weight[3:4]
            sx = quarter + join(quarter0, quarter)
            exz = sz + join(sz0, sz)
            exy = sy + join(sy0, sy)
            ezy = sz + y_down(sz)
            fxz = exz * (vx - z_down(vx))
            fxy = exy * (vx - y_down(vx))
            low_vz, low_vy = join(vz0, vz), join(vy0, vy)
            gzx = exz * (vz - low_vz)
            hyx = exy * (vy - low_vy)
            gzy = ezy * (vz - y_down(vz))
            hyz = ezy * (vy - z_down(vy))
            res_x = (tx - join(tx0, tx)) + ((z_up(fxz) - fxz) + (y_up(fxy) - fxy))
            new_vx = vx + weight[0:1] * reciprocal(sx + bias) * res_x
            part_z = (tz - z_down(tz)) - constant(2, planes) + ((y_up(gzy) - gzy) - gzx)
            part_y = (ty - y_down(ty)) + ((z_up(hyz) - hyz) - hyx)
            scale_z = weight[1:2] * reciprocal(sz + bias)
            scale_y = weight[2:3] * reciprocal(sy + bias)
            new_vz = low_vz + join(scale_z0, scale_z) * (join(part_z0, part_z) + gzx)
            new_vy = low_vy + join(scale_y0, scale_y) * (join(part_y0, part_y) + hyx)
            if last:
                at = pl.ds(j - LOW, count)
                out_vx_ref[at] = new_vx[:, 0:bz, 0:by]
                out_p_ref[at] = p[:, 0:bz, 0:by]
                out_eta_ref[at] = eta[:, 0:bz, 0:by]
                sum_ref[...] += jnp.sum(p[:, 0:bz, 0:by], axis=0)
                if not start:
                    at = pl.ds(j - 1 - LOW, count)
                    out_vz_ref[at] = new_vz[:, 0:bz, 0:by]
                    out_vy_ref[at] = new_vy[:, 0:bz, 0:by]
            else:
                for at, part in keep(p):
                    p_ref[planes, at, :] = part
                store(0, j, count, new_vx)
                if not start:
                    store(1, j - 1, count, new_vz)
                    store(2, j - 1, count, new_vy)
            return tuple(a[-1:] for a in (quarter, tx, sz, sy, part_z, part_y, scale_z, scale_y))

        first, count = k, bx + LOW + HIGH - 3 * k
        if last:
            sum_ref[...] = jnp.zeros((bz, by), jnp.float32)
        _, _, _, _, p, quarter, tx, _, _, sz, sy = cells(first - 1, 1)
        if not last:
            for at, part in keep(p):
                p_ref[pl.ds(first - 1, 1), at, :] = part
        zero = jnp.zeros((1, rows, lanes), jnp.float32)
        carry = chunk(first, 1, (quarter, tx, sz, sy, zero, zero, zero, zero), start=True)
        steps, rest = divmod(count - 1, UNROLL)
        carry = lax.fori_loop(
            0, steps, lambda s, carry: chunk(first + 1 + s * UNROLL, UNROLL, carry), carry
        )
        if rest:
            carry = chunk(first + 1 + steps * UNROLL, rest, carry)
        j = first + count
        quarter0, tx0, sz0, sy0, part_z0, part_y0, scale_z0, scale_y0 = carry
        _, vz, vy, _, p, quarter, tx, _, _, sz, sy = cells(j, 1)
        vz0, vy0 = load(1, j - 1, 1), load(2, j - 1, 1)
        new_vz = vz0 + scale_z0 * (part_z0 + (sz + sz0) * (vz - vz0))
        new_vy = vy0 + scale_y0 * (part_y0 + (sy + sy0) * (vy - vy0))
        if last:
            out_vz_ref[pl.ds(j - 1 - LOW, 1)] = new_vz[:, 0:bz, 0:by]
            out_vy_ref[pl.ds(j - 1 - LOW, 1)] = new_vy[:, 0:bz, 0:by]
        else:
            for at, part in keep(p):
                p_ref[pl.ds(j, 1), at, :] = part
            store(1, j - 1, 1, new_vz)
            store(2, j - 1, 1, new_vy)

        if last:
            @pl.when(ix == 0)
            def _():
                out_vx_ref[0] = jnp.zeros((bz, by), jnp.float32)
        else:
            plane = jnp.zeros((3 * bz, lanes), jnp.float32)

            @pl.when(ix == 0)
            def _():
                for i in range(k, LOW):
                    for d in range(3):
                        new[d, i] = plane
                new[0, LOW] = plane

            @pl.when(ix == nx - 1)
            def _():
                for i in range(LOW + bx, first + count):
                    for d in range(3):
                        new[d, i] = plane


def final_kernel(p_ref, sum_ref, out_ref, *, cells):
    mean = jnp.sum(sum_ref[...]) * (1.0 / cells)
    out_ref[...] = p_ref[...] - mean


def swap(a, axis, start):
    count = lax.axis_size(axis)
    return lax.ppermute(a, axis, [(i, j) for k in range(start, count - 1, 2) for i, j in ((k, k + 1), (k + 1, k))])


def sum_everywhere(total):
    axes = ("gx", "gy", "gz")
    devices = math.prod(lax.axis_size(a) for a in axes)
    if devices & (devices - 1):
        return lax.psum(total, axes)
    bits = [1 << n for n in range(devices.bit_length() - 1)]
    for stage in [bits[:1]] + [bits[n : n + 2] for n in range(1, len(bits), 2)]:
        masks = stage if len(stage) == 1 else [stage[0], stage[1], stage[0] + stage[1]]
        total = sum([lax.ppermute(total, axes, [(i, i ^ m) for i in range(devices)]) for m in masks], total)
    return total


def local(vel_x, vel_y, vel_z, pressure, phase, visc_scale, power_n, density):
    bx, bz, by = pressure.shape
    assert bx == 2 * HIGH and bz == HIGH
    f32 = jnp.float32
    ix, iz, iy = lax.axis_index("gx"), lax.axis_index("gz"), lax.axis_index("gy")
    ny = lax.axis_size("gy")
    cells = bx * bz * by * math.prod(lax.axis_size(a) for a in ("gx", "gz", "gy"))
    deep = bx + LOW + HIGH
    rows, lanes = 3 * bz, 2 * by
    shape = lambda *dims: jax.ShapeDtypeStruct(dims, f32)
    block = shape(bx, bz, by)
    scratch = lambda *dims: pltpu.VMEM(dims, f32)
    mebibyte = 1024 * 1024

    hbm = pl.BlockSpec(memory_space=pltpu.HBM)

    tables = jnp.stack([visc_scale, (0.5 / math.log(2.0)) * (1.0 / power_n - 1.0), density])
    groups = bx // GROUP
    edge, half_0, half_1, stack = pl.pallas_call(
        pack_kernel,
        out_shape=(
            shape(HIGH, bz, by),
            shape(HIGH, FIELDS, bz, by),
            shape(HIGH, FIELDS, bz, by),
            shape(bx, FIELDS, bz, by),
        ),
        in_specs=[hbm] * 5,
        out_specs=(hbm,) * 4,
        scratch_shapes=[
            scratch(FIELDS - 1, bx, bz, by),
            pltpu.VMEM((bx, bz, by), jnp.int32),
            scratch(HIGH, bz, by),
            scratch(bx, FIELDS, bz, by),
            pltpu.SemaphoreType.DMA((groups, FIELDS)),
            pltpu.SemaphoreType.DMA((groups + groups // 2 + 2,)),
        ],
        compiler_params=pltpu.CompilerParams(vmem_limit_bytes=58 * mebibyte),
        cost_estimate=pl.CostEstimate(flops=0, bytes_accessed=16 * bx * bz * by * 4, transcendentals=0),
    )(vel_x, vel_z, vel_y, pressure, phase)

    def edges_beside(edge):
        side = swap(edge, "gy", 0)
        if ny == 2:
            return side
        lane = lax.broadcasted_iota(jnp.int32, side.shape, 2) % (by // 2) % LANE_STEP
        return jnp.where((lane < HIGH) == (lax.rem(iy, 2) == 0), side, swap(edge, "gy", 1))

    side = edges_beside(edge)
    x_0, x_1 = swap(half_0, "gx", 0), swap(half_1, "gx", 1)
    face = jnp.concatenate([stack.reshape(bx * FIELDS, bz, by), side])
    face_1 = swap(face, "gz", 1)
    face_0 = swap(face, "gz", 0)
    sides, edge = pl.pallas_call(
        sides_kernel,
        out_shape=(shape((HIGH + LOW) * FIELDS, bz, by), shape(HIGH, bz, by)),
        in_specs=[VMEM] * 2,
        out_specs=(VMEM,) * 2,
        compiler_params=pltpu.CompilerParams(vmem_limit_bytes=4 * mebibyte),
    )(x_0, x_1)
    sides = jnp.concatenate([sides, edges_beside(edge)])
    corner_1 = swap(sides, "gz", 1)
    corner_0 = swap(sides, "gz", 0)

    field = shape(deep, bz, lanes)
    own = pl.pallas_call(
        own_kernel,
        out_shape=(shape(3, deep, bz, lanes),) + (field,) * 4,
        in_specs=[VMEM] * 2 + [SMEM],
        out_specs=(VMEM,) * 5,
        compiler_params=pltpu.CompilerParams(vmem_limit_bytes=8 * mebibyte),
        cost_estimate=pl.CostEstimate(flops=deep * 30 * bz * lanes, bytes_accessed=12 * deep * bz * lanes * 4, transcendentals=0),
    )(face, sides, tables)
    halo = pl.pallas_call(
        face_kernel,
        out_shape=(shape(7, deep, 2 * bz, lanes), shape(3, deep, bz, lanes)),
        in_specs=[VMEM] * 2 + [SMEM],
        out_specs=(VMEM,) * 2,
        compiler_params=pltpu.CompilerParams(vmem_limit_bytes=8 * mebibyte),
        cost_estimate=pl.CostEstimate(flops=deep * 30 * bz * lanes, bytes_accessed=24 * bx * bz * lanes * 4, transcendentals=0),
    )(face_0, face_1, tables)
    vx, vz, vy, p, eta, total, _, _ = pl.pallas_call(
        main_kernel,
        out_shape=(block,) * 5 + (shape(bz, by),) + tuple(shape(*a.shape) for a in halo),
        in_specs=[VMEM] * 9 + [SMEM],
        out_specs=(VMEM,) * 8,
        input_output_aliases={5: 6, 6: 7},
        scratch_shapes=[
            scratch(3, deep, rows, lanes),
            scratch(3, deep, rows, lanes),
            scratch(deep, rows, lanes),
            scratch(4, rows, lanes),
            scratch(4, 2 * bz, lanes),
        ],
        compiler_params=pltpu.CompilerParams(vmem_limit_bytes=32 * mebibyte),
    )(*own, *halo, corner_0, corner_1, tables)

    total = sum_everywhere(total)
    p = pl.pallas_call(
        lambda *refs: final_kernel(*refs, cells=float(cells)),
        out_shape=block,
        in_specs=[VMEM] * 2,
        out_specs=VMEM,
        compiler_params=pltpu.CompilerParams(vmem_limit_bytes=4 * mebibyte),
    )(p, total)
    return (vx, vy, vz, p, eta)


def solution(mesh):
    spec = P("gx", "gz", "gy")
    return jax.shard_map(
        local,
        mesh=mesh,
        in_specs=(spec,) * 5 + (P(),) * 3,
        out_specs=(spec,) * 5,
        check_vma=False,
    )
```

```python
import math

import jax
import jax.numpy as jnp
from jax import lax
from jax.experimental import pallas as pl
from jax.experimental.pallas import tpu as pltpu
from jax.sharding import PartitionSpec as P

ITERS = 4
PHASES = 4
LOW = ITERS
HIGH = 2 * ITERS
FIELDS = 5
LANE_STEP = LOW + HIGH
UNROLL = 3
GROUP = 4

VMEM = pl.BlockSpec(memory_space=pltpu.VMEM)
SMEM = pl.BlockSpec(memory_space=pltpu.SMEM)


def z_up(a):
    return pltpu.roll(a, a.shape[-2] - 1, a.ndim - 2)


def z_down(a):
    return pltpu.roll(a, 1, a.ndim - 2)


def y_up(a):
    return pltpu.roll(a, a.shape[-1] - 1, a.ndim - 1)


def y_down(a):
    return pltpu.roll(a, 1, a.ndim - 1)


def reciprocal(a):
    r = pl.reciprocal(a, approx=True)
    return r * (2.0 - a * r)


def merged(k, bz):
    return 3 * (ITERS - k + 1) <= bz


def start_copies(sources, targets, sems):
    copies = []
    for g in range(sources[0].shape[0] // GROUP):
        at = pl.ds(g * GROUP, GROUP)
        copies.append(
            [pltpu.make_async_copy(a.at[at], b.at[at], sems.at[g, f]) for f, (a, b) in enumerate(zip(sources, targets))]
        )
        for copy in copies[-1]:
            copy.start()
    return copies


def clean_group(g, field_ref, phase_ref):
    bx, bz, by = phase_ref.shape
    ix, iz, iy = lax.axis_index("gx"), lax.axis_index("gz"), lax.axis_index("gy")
    plane, row, lane = (lax.broadcasted_iota(jnp.int32, (GROUP, bz, by), d) for d in range(3))
    at = pl.ds(g * GROUP, GROUP)
    vx, vz, vy, p = (field_ref[f, at] for f in range(FIELDS - 1))
    if g == 0:
        vx = jnp.where((plane > 0) | (ix > 0), vx, 0.0)
    vz = jnp.where((row > 0) | (iz > 0), vz, 0.0)
    vy = jnp.where((lane > 0) | (iy > 0), vy, 0.0)
    return vx, vz, vy, p, phase_ref[at].astype(jnp.float32)


def add_edges(edge, fields, upper):
    by = edge.shape[-1]
    lane = lax.broadcasted_iota(jnp.int32, (1,) + edge.shape[1:], 2)
    for f, a in enumerate(fields):
        base = by // 2 * upper + LANE_STEP * f
        first = pltpu.roll(a, base, 2) if base else a
        edge = jnp.where((lane >= base) & (lane < base + HIGH), first, edge)
        last = pltpu.roll(a, (base + LANE_STEP) % by, 2)
        edge = jnp.where((lane >= base + HIGH) & (lane < base + LANE_STEP), last, edge)
    return edge


def high_and_low(x_0_ref, x_1_ref, body):
    for parity, pair in enumerate(((x_0_ref, x_1_ref), (x_1_ref, x_0_ref))):
        pl.when(lax.rem(lax.axis_index("gx"), 2) == parity)(lambda: body(*pair))


def side_edge_kernel(x_0_ref, x_1_ref, own_edge_ref, edge_ref):
    bz, by = edge_ref.shape[1:]
    edge_ref[0:HIGH] = own_edge_ref[...]

    def body(high, low):
        for at in range(0, HIGH, GROUP):
            edge = jnp.zeros((GROUP, bz, by), jnp.float32)
            for upper, ref in enumerate((high, low)):
                if not upper or at >= HIGH - LOW:
                    block = ref[pl.ds(at, GROUP)]
                    edge = add_edges(edge, [block[:, f] for f in range(FIELDS)], upper)
            edge_ref[pl.ds(HIGH + at, GROUP)] = edge

    high_and_low(x_0_ref, x_1_ref, body)


def sides_kernel(x_0_ref, x_1_ref, _edge_ref, sides_ref):
    bz, by = sides_ref.shape[1:]

    def body(high, low):
        for at in range(0, HIGH, GROUP):
            sides_ref[pl.ds(at * FIELDS, GROUP * FIELDS)] = high[pl.ds(at, GROUP)].reshape(-1, bz, by)
        for at in range(HIGH - LOW, HIGH, GROUP):
            sides_ref[pl.ds((at + LOW) * FIELDS, GROUP * FIELDS)] = low[pl.ds(at, GROUP)].reshape(-1, bz, by)

    high_and_low(x_0_ref, x_1_ref, body)


def pack_kernel(
    vx_hbm, vz_hbm, vy_hbm, p_hbm, phase_hbm, edge_hbm, x_0_hbm, x_1_hbm, stack_hbm,
    field_ref, phase_ref, edge_ref, stack_ref, sems, out_sems,
):
    bx, bz, by = phase_ref.shape
    targets = [field_ref.at[f] for f in range(FIELDS - 1)] + [phase_ref]
    copies = start_copies((vx_hbm, vz_hbm, vy_hbm, p_hbm, phase_hbm), targets, sems)
    half = bx // GROUP // 2
    outs = []

    def out(source, target):
        outs.append(pltpu.make_async_copy(source, target, out_sems.at[len(outs)]))
        outs[-1].start()

    for g in range(half):
        edge = jnp.zeros((GROUP, bz, by), jnp.float32)
        for upper in range(2):
            at = pl.ds((g + upper * half) * GROUP, GROUP)
            for copy in copies[g + upper * half]:
                copy.wait()
            fields = clean_group(g + upper * half, field_ref, phase_ref)
            for f, a in enumerate(fields):
                stack_ref[at, f] = a
            edge = add_edges(edge, fields, upper)
            out(stack_ref.at[at], stack_hbm.at[at])
        at = pl.ds(g * GROUP, GROUP)
        edge_ref[at] = edge
        out(edge_ref.at[at], edge_hbm.at[at])
    sem = out_sems.at[len(outs)], out_sems.at[len(outs) + 1]
    lower, upper = stack_ref.at[pl.ds(0, HIGH)], stack_ref.at[pl.ds(HIGH, HIGH)]
    for parity, (first, second) in enumerate(((upper, lower), (lower, upper))):
        @pl.when(lax.rem(lax.axis_index("gx"), 2) == parity)
        def _():
            pair = pltpu.make_async_copy(first, x_0_hbm, sem[0]), pltpu.make_async_copy(second, x_1_hbm, sem[1])
            for copy in pair:
                copy.start()
            for copy in pair:
                copy.wait()

    for copy in outs:
        copy.wait()


def read_tables(ref):
    return [[ref[n * PHASES + index] for index in range(PHASES)] for n in range(3)]


def lookups(fields, ok, keep, tables):
    *rest, phase = fields
    for number, table in enumerate(tables):
        value = jnp.broadcast_to(table[0], phase.shape)
        for index in range(1, PHASES):
            value = jnp.where(phase == float(index), table[index], value)
        if number == 0:
            value = value * jnp.where(ok, 1.0, 0.0)
            if keep is not None:
                value = jnp.where(keep, value, 0.0)
        elif number == 1:
            value = (0.5 / math.log(2.0)) * (reciprocal(value) - 1.0)
        rest.append(value)
    return rest


def own_lanes(ref, at, ok, tables):
    block = ref[pl.ds(at * FIELDS, GROUP * FIELDS)].reshape(GROUP, FIELDS, *ref.shape[-2:])
    return lookups([block[:, f] for f in range(FIELDS)], ok, None, tables)


def edge_lanes(ref, at, upper, ok, tables):
    bz, by = ref.shape[-2:]
    edge = ref[pl.ds(at, GROUP)]
    iy = lax.axis_index("gy")
    lane = lax.broadcasted_iota(jnp.int32, (1, bz, by), 2)
    right = (lane < HIGH) & (iy < lax.axis_size("gy") - 1)
    left = (lane >= by - LOW) & (iy > 0)
    fields = []
    for f in range(FIELDS):
        shift = by // 2 * upper + LANE_STEP * f
        a = pltpu.roll(edge, (by - shift) % by, 2) if shift else edge
        b = pltpu.roll(edge, (by - LANE_STEP - shift) % by, 2)
        fields.append(jnp.where(right, a, jnp.where(left, b, 0.0)))
    return lookups(fields, ok, right | left, tables)


def unpack_block(ref, part, ok, tables, store):
    for upper in range(2):

        def group(g, carry):
            at = g * GROUP + upper * HIGH
            values = edge_lanes(ref, g * GROUP, upper, ok, tables) if part else own_lanes(ref, at, ok, tables)
            store(pl.ds(LOW + at, GROUP), part, values)
            return carry

        lax.fori_loop(0, HIGH // GROUP, group, 0)


def unpack_sides(ref, part, ok, tables, store):
    ix, nx = lax.axis_index("gx"), lax.axis_size("gx")
    for at in range(0, HIGH + LOW, GROUP):
        low = at >= HIGH
        here = ok & (ix > 0 if low else ix < nx - 1)
        if part:
            values = edge_lanes(ref, HIGH + (at - LOW if low else at), int(low), here, tables)
        else:
            values = own_lanes(ref, at, here, tables)
        store(pl.ds(at - HIGH if low else LOW + 2 * HIGH + at, GROUP), part, values)


def own_store(v_ref, *rest):
    refs = [v_ref.at[d] for d in range(3)] + list(rest)

    def store(planes, part, values):
        by = values[0].shape[-1]
        for ref, value in zip(refs, values):
            ref[planes, :, part * by : (part + 1) * by] = value

    return store


def halo_store(halo_ref, shared_ref, t):
    bz = shared_ref.shape[-2]
    rows = slice(t * bz // 2, (t + 1) * bz // 2)

    def store(planes, part, values):
        by = values[0].shape[-1]
        at = slice(part * by, (part + 1) * by)
        for n, value in enumerate(values):
            halo_ref[n, planes, t * bz : (t + 1) * bz, at] = value
            if n >= 4:
                shared_ref[n - 4, planes, rows, at] = value[:, rows]

    return store


def own_kernel(stack_in_ref, edge_in_ref, tables_ref, stack_ref, edge_ref, *refs):
    edge_ref[...] = edge_in_ref[...]
    stack_ref[...] = stack_in_ref[...]
    unpack_block(stack_in_ref, 0, True, read_tables(tables_ref), own_store(*refs))


def own_sides_kernel(sides_ref, edge_ref, tables_ref, *refs):
    tables = read_tables(tables_ref)
    refs = refs[len(refs) // 2 :]
    unpack_sides(sides_ref, 0, True, tables, own_store(*refs))
    unpack_block(edge_ref, 1, True, tables, own_store(*refs))
    unpack_sides(edge_ref, 1, True, tables, own_store(*refs))


def by_parity(body):
    for parity in range(2):
        pl.when(lax.rem(lax.axis_index("gz"), 2) == parity)(lambda: body(parity, 1 - parity))


def halo_kernel(face_0_ref, face_1_ref, corner_0_ref, corner_1_ref, tables_ref, halo_ref, shared_ref):
    iz, nz = lax.axis_index("gz"), lax.axis_size("gz")
    tables = read_tables(tables_ref)
    faces, corners = (face_0_ref, face_1_ref), (corner_0_ref, corner_1_ref)

    @by_parity
    def _(above, below):
        for t, (n, ok) in enumerate(((above, iz < nz - 1), (below, iz > 0))):
            unpack_block(faces[n], 0, ok, tables, halo_store(halo_ref, shared_ref, t))
            unpack_sides(corners[n], 0, ok, tables, halo_store(halo_ref, shared_ref, t))


def main_kernel(
    v_ref, p0_ref, pre_ref, power_field_ref, rho_ref, _halo, _shared,
    edge_0_ref, edge_1_ref, tables_ref,
    out_vx_ref, out_vz_ref, out_vy_ref, out_p_ref, out_eta_ref, sum_ref, halo_ref, shared_ref,
    va_ref, vb_ref, p_ref, weight_ref, weight2_ref,
):
    bx, bz, by = out_p_ref.shape
    lanes = 2 * by
    nx, nz, ny = lax.axis_size("gx"), lax.axis_size("gz"), lax.axis_size("gy")
    ix, iz, iy = lax.axis_index("gx"), lax.axis_index("gz"), lax.axis_index("gy")
    tables = read_tables(tables_ref)
    tables = read_tables(tables_ref)
    edges = (edge_0_ref, edge_1_ref)

    @by_parity
    def _(above, below):
        for t, (n, ok) in enumerate(((above, iz < nz - 1), (below, iz > 0))):
            unpack_block(edges[n], 1, ok, tables, halo_store(halo_ref, shared_ref, t))
            unpack_sides(edges[n], 1, ok, tables, halo_store(halo_ref, shared_ref, t))

    for ref, high in ((weight_ref, 2 * bz), (weight2_ref, bz + bz // 2)):
        shape = ref.shape[1:]
        r = lax.broadcasted_iota(jnp.int32, shape, 0)
        c = lax.broadcasted_iota(jnp.int32, shape, 1)
        zg = iz * bz + jnp.where(r < high, r, r - shape[0])
        yg = iy * by + jnp.where(c < by + HIGH, c, c - lanes)
        filled = (c < by + HIGH) | (c >= lanes - LOW)
        inside = filled & (zg >= 0) & (zg < nz * bz) & (yg >= 0) & (yg < ny * by)
        ref[0] = jnp.where(inside, 0.05, 0.0)
        ref[1] = jnp.where(inside & (zg > 0), 0.05, 0.0)
        ref[2] = jnp.where(inside & (yg > 0), 0.05, 0.0)
        ref[3] = jnp.where(inside, 0.0, 1.0)

    for k in range(1, ITERS + 1):
        old, new = (va_ref, vb_ref) if k % 2 else (vb_ref, va_ref)
        last = k == ITERS
        rows = 2 * bz if merged(k, bz) else 3 * bz
        own_constants = (pre_ref, power_field_ref, rho_ref)
        weight = weight2_ref if merged(k, bz) else weight_ref
        narrow = merged(k + 1, bz) and not merged(k, bz)
        all_rows = pl.ds(0, rows)

        def keep(value):
            if narrow:
                row = lax.broadcasted_iota(jnp.int32, (bz, lanes), 0)
                halo = jnp.where(row < bz // 2, value[..., bz : 2 * bz, :], value[..., 2 * bz :, :])
                return [(pl.ds(0, bz), value[..., 0:bz, :]), (pl.ds(bz, bz), halo)]
            return [(all_rows, value)]

        def store(d, j, count, value):
            for at, part in keep(value):
                new[d, pl.ds(j, count), at, :] = part

        def constant(n, planes):
            halo = shared_ref[n, planes] if merged(k, bz) else halo_ref[4 + n, planes]
            return jnp.concatenate([own_constants[n][planes], halo], axis=1)

        def load(d, j, count):
            planes = pl.ds(j, count)
            if k == 1:
                return jnp.concatenate([v_ref[d, planes], halo_ref[d, planes]], axis=1)
            return old[d, planes, all_rows, :]

        def cells(j, count):
            planes = pl.ds(j, count)
            vx1 = load(0, j, count + 1)
            vx = vx1[:count]
            vz, vy = load(1, j, count), load(2, j, count)
            if k == 1:
                p = jnp.concatenate([p0_ref[planes], halo_ref[3, planes]], axis=1)
            else:
                p = p_ref[planes, all_rows, :]
            rx = vx1[1:] - vx
            rz = z_up(vz) - vz
            ry = y_up(vy) - vy
            a = rx - ry
            b = ry - rz
            inv = (a * (a + b) + b * b) * (1.0 / 3.0) + 1.0
            eta = constant(0, planes) * jnp.exp2(constant(1, planes) * jnp.log(inv))
            quarter = 0.25 * eta
            div = rx + ry + rz
            p = p - quarter * (div + div)
            tx, tz, ty = eta * rx - p, eta * rz - p, eta * ry - p
            sz = quarter + z_down(quarter)
            sy = quarter + y_down(quarter)
            return vx, vz, vy, eta, p, quarter, tx, tz, ty, sz, sy

        def chunk(j, count, carry, start=False):
            planes = pl.ds(j, count)
            vx, vz, vy, eta, p, quarter, tx, tz, ty, sz, sy = cells(j, count)
            vz0, vy0 = load(1, j - 1, 1), load(2, j - 1, 1)
            quarter0, tx0, sz0, sy0, part_z0, part_y0, scale_z0, scale_y0 = carry
            join = lambda first, rest: jnp.concatenate([first, rest[:-1]], axis=0) if count > 1 else first
            bias = weight[3:4]
            sx = quarter + join(quarter0, quarter)
            exz = sz + join(sz0, sz)
            exy = sy + join(sy0, sy)
            ezy = sz + y_down(sz)
            fxz = exz * (vx - z_down(vx))
            fxy = exy * (vx - y_down(vx))
            low_vz, low_vy = join(vz0, vz), join(vy0, vy)
            gzx = exz * (vz - low_vz)
            hyx = exy * (vy - low_vy)
            gzy = ezy * (vz - y_down(vz))
            hyz = ezy * (vy - z_down(vy))
            res_x = (tx - join(tx0, tx)) + ((z_up(fxz) - fxz) + (y_up(fxy) - fxy))
            new_vx = vx + weight[0:1] * reciprocal(sx + bias) * res_x
            part_z = (tz - z_down(tz)) - constant(2, planes) + ((y_up(gzy) - gzy) - gzx)
            part_y = (ty - y_down(ty)) + ((z_up(hyz) - hyz) - hyx)
            scale_z = weight[1:2] * reciprocal(sz + bias)
            scale_y = weight[2:3] * reciprocal(sy + bias)
            new_vz = low_vz + join(scale_z0, scale_z) * (join(part_z0, part_z) + gzx)
            new_vy = low_vy + join(scale_y0, scale_y) * (join(part_y0, part_y) + hyx)
            if last:
                at = pl.ds(j - LOW, count)
                out_vx_ref[at] = new_vx[:, 0:bz, 0:by]
                out_p_ref[at] = p[:, 0:bz, 0:by]
                out_eta_ref[at] = eta[:, 0:bz, 0:by]
                sum_ref[...] += jnp.sum(p[:, 0:bz, 0:by], axis=0)
                if not start:
                    at = pl.ds(j - 1 - LOW, count)
                    out_vz_ref[at] = new_vz[:, 0:bz, 0:by]
                    out_vy_ref[at] = new_vy[:, 0:bz, 0:by]
            else:
                for at, part in keep(p):
                    p_ref[planes, at, :] = part
                store(0, j, count, new_vx)
                if not start:
                    store(1, j - 1, count, new_vz)
                    store(2, j - 1, count, new_vy)
            return tuple(a[-1:] for a in (quarter, tx, sz, sy, part_z, part_y, scale_z, scale_y))

        first, count = k, bx + LOW + HIGH - 3 * k
        if last:
            sum_ref[...] = jnp.zeros((bz, by), jnp.float32)
        _, _, _, _, p, quarter, tx, _, _, sz, sy = cells(first - 1, 1)
        if not last:
            for at, part in keep(p):
                p_ref[pl.ds(first - 1, 1), at, :] = part
        zero = jnp.zeros((1, rows, lanes), jnp.float32)
        carry = chunk(first, 1, (quarter, tx, sz, sy, zero, zero, zero, zero), start=True)
        steps, rest = divmod(count - 1, UNROLL)
        carry = lax.fori_loop(
            0, steps, lambda s, carry: chunk(first + 1 + s * UNROLL, UNROLL, carry), carry
        )
        if rest:
            carry = chunk(first + 1 + steps * UNROLL, rest, carry)
        j = first + count
        quarter0, tx0, sz0, sy0, part_z0, part_y0, scale_z0, scale_y0 = carry
        _, vz, vy, _, p, quarter, tx, _, _, sz, sy = cells(j, 1)
        vz0, vy0 = load(1, j - 1, 1), load(2, j - 1, 1)
        new_vz = vz0 + scale_z0 * (part_z0 + (sz + sz0) * (vz - vz0))
        new_vy = vy0 + scale_y0 * (part_y0 + (sy + sy0) * (vy - vy0))
        if last:
            out_vz_ref[pl.ds(j - 1 - LOW, 1)] = new_vz[:, 0:bz, 0:by]
            out_vy_ref[pl.ds(j - 1 - LOW, 1)] = new_vy[:, 0:bz, 0:by]
        else:
            for at, part in keep(p):
                p_ref[pl.ds(j, 1), at, :] = part
            store(1, j - 1, 1, new_vz)
            store(2, j - 1, 1, new_vy)

        if last:
            @pl.when(ix == 0)
            def _():
                out_vx_ref[0] = jnp.zeros((bz, by), jnp.float32)
        else:
            plane = jnp.zeros((3 * bz, lanes), jnp.float32)

            @pl.when(ix == 0)
            def _():
                for i in range(k, LOW):
                    for d in range(3):
                        new[d, i] = plane
                new[0, LOW] = plane

            @pl.when(ix == nx - 1)
            def _():
                for i in range(LOW + bx, first + count):
                    for d in range(3):
                        new[d, i] = plane


def final_kernel(p_ref, sum_ref, out_ref, *, cells):
    mean = jnp.sum(sum_ref[...]) * (1.0 / cells)
    out_ref[...] = p_ref[...] - mean


def swap(a, axis, start):
    count = lax.axis_size(axis)
    return lax.ppermute(a, axis, [(i, j) for k in range(start, count - 1, 2) for i, j in ((k, k + 1), (k + 1, k))])


def sum_everywhere(total):
    axes = ("gx", "gy", "gz")
    devices = math.prod(lax.axis_size(a) for a in axes)
    if devices & (devices - 1):
        return lax.psum(total, axes)
    bits = [1 << n for n in range(devices.bit_length() - 1)]
    for stage in [bits[:1]] + [bits[n : n + 2] for n in range(1, len(bits), 2)]:
        masks = stage if len(stage) == 1 else [stage[0], stage[1], stage[0] + stage[1]]
        total = sum([lax.ppermute(total, axes, [(i, i ^ m) for i in range(devices)]) for m in masks], total)
    return total


def local(vel_x, vel_y, vel_z, pressure, phase, visc_scale, power_n, density):
    bx, bz, by = pressure.shape
    assert bx == 2 * HIGH and bz == HIGH
    f32 = jnp.float32
    ix, iz, iy = lax.axis_index("gx"), lax.axis_index("gz"), lax.axis_index("gy")
    ny = lax.axis_size("gy")
    cells = bx * bz * by * math.prod(lax.axis_size(a) for a in ("gx", "gz", "gy"))
    deep = bx + LOW + HIGH
    rows, lanes = 3 * bz, 2 * by
    shape = lambda *dims: jax.ShapeDtypeStruct(dims, f32)
    block = shape(bx, bz, by)
    scratch = lambda *dims: pltpu.VMEM(dims, f32)
    mebibyte = 1024 * 1024

    hbm = pl.BlockSpec(memory_space=pltpu.HBM)

    tables = jnp.concatenate([visc_scale, power_n, density])
    groups = bx // GROUP
    edge, half_0, half_1, stack = pl.pallas_call(
        pack_kernel,
        out_shape=(
            shape(HIGH, bz, by),
            shape(HIGH, FIELDS, bz, by),
            shape(HIGH, FIELDS, bz, by),
            shape(bx, FIELDS, bz, by),
        ),
        in_specs=[hbm] * 5,
        out_specs=(hbm,) * 4,
        scratch_shapes=[
            scratch(FIELDS - 1, bx, bz, by),
            pltpu.VMEM((bx, bz, by), jnp.int32),
            scratch(HIGH, bz, by),
            scratch(bx, FIELDS, bz, by),
            pltpu.SemaphoreType.DMA((groups, FIELDS)),
            pltpu.SemaphoreType.DMA((groups + groups // 2 + 2,)),
        ],
        compiler_params=pltpu.CompilerParams(vmem_limit_bytes=58 * mebibyte),
        cost_estimate=pl.CostEstimate(flops=0, bytes_accessed=16 * bx * bz * by * 4, transcendentals=0),
    )(vel_x, vel_z, vel_y, pressure, phase)

    def edges_beside(edge):
        side = swap(edge, "gy", 0)
        if ny == 2:
            return side
        lane = lax.broadcasted_iota(jnp.int32, side.shape, 2) % (by // 2) % LANE_STEP
        return jnp.where((lane < HIGH) == (lax.rem(iy, 2) == 0), side, swap(edge, "gy", 1))

    x_0, x_1 = swap(half_0, "gx", 0), swap(half_1, "gx", 1)
    stack = stack.reshape(bx * FIELDS, bz, by)
    def unpacking(kernel, tiles, out_shape, *args, aliases={}):
        return pl.pallas_call(
            kernel,
            out_shape=out_shape,
            in_specs=[VMEM if a is not tables else SMEM for a in args],
            out_specs=(VMEM,) * len(out_shape),
            input_output_aliases=aliases,
            compiler_params=pltpu.CompilerParams(vmem_limit_bytes=16 * mebibyte),
            cost_estimate=pl.CostEstimate(
                flops=tiles * 56000 * bz * by, bytes_accessed=tiles * 1400 * bz * by * 4, transcendentals=0
            ),
        )(*args)

    small = pltpu.CompilerParams(vmem_limit_bytes=4 * mebibyte)
    field = shape(deep, bz, lanes)
    own_shape = (shape(3, deep, bz, lanes),) + (field,) * 4
    stack, edge, *own = unpacking(
        own_kernel, bx, (shape(*stack.shape), shape(*edge.shape)) + own_shape, stack, edge, tables
    )
    face_1 = swap(stack, "gz", 1)
    face_0 = swap(stack, "gz", 0)
    edge = pl.pallas_call(
        side_edge_kernel,
        out_shape=shape(2 * HIGH, bz, by),
        in_specs=[VMEM] * 3,
        out_specs=VMEM,
        compiler_params=small,
    )(x_0, x_1, edge)
    sides = pl.pallas_call(
        sides_kernel,
        out_shape=shape((HIGH + LOW) * FIELDS, bz, by),
        in_specs=[VMEM] * 3,
        out_specs=VMEM,
        compiler_params=small,
    )(x_0, x_1, edge)
    edge = edges_beside(edge)
    corner_1 = swap(sides, "gz", 1)
    corner_0 = swap(sides, "gz", 0)
    edge_1 = swap(edge, "gz", 1)
    edge_0 = swap(edge, "gz", 0)

    own = unpacking(
        own_sides_kernel, 12 + deep, own_shape, sides, edge, tables, *own, aliases={n + 3: n for n in range(5)}
    )
    halo_shape = (shape(7, deep, 2 * bz, lanes), shape(3, deep, bz, lanes))
    halo = unpacking(halo_kernel, 2 * deep, halo_shape, face_0, face_1, corner_0, corner_1, tables)
    vx, vz, vy, p, eta, total, _, _ = pl.pallas_call(
        main_kernel,
        out_shape=(block,) * 5 + (shape(bz, by),) + tuple(shape(*a.shape) for a in halo),
        in_specs=[VMEM] * 9 + [SMEM],
        out_specs=(VMEM,) * 8,
        input_output_aliases={5: 6, 6: 7},
        scratch_shapes=[
            scratch(3, deep, rows, lanes),
            scratch(3, deep, rows, lanes),
            scratch(deep, rows, lanes),
            scratch(4, rows, lanes),
            scratch(4, 2 * bz, lanes),
        ],
        compiler_params=pltpu.CompilerParams(vmem_limit_bytes=32 * mebibyte),
    )(*own, *halo, edge_0, edge_1, tables)

    total = sum_everywhere(total)
    p = pl.pallas_call(
        lambda *refs: final_kernel(*refs, cells=float(cells)),
        out_shape=block,
        in_specs=[VMEM] * 2,
        out_specs=VMEM,
        compiler_params=pltpu.CompilerParams(vmem_limit_bytes=4 * mebibyte),
    )(p, total)
    return (vx, vy, vz, p, eta)


def solution(mesh):
    spec = P("gx", "gz", "gy")
    return jax.shard_map(
        local,
        mesh=mesh,
        in_specs=(spec,) * 5 + (P(),) * 3,
        out_specs=(spec,) * 5,
        check_vma=False,
    )
```

```python
import math

import jax
import jax.numpy as jnp
from jax import lax
from jax.experimental import pallas as pl
from jax.experimental.pallas import tpu as pltpu
from jax.sharding import PartitionSpec as P

ITERS = 4
PHASES = 4
FIELDS = 5
DEPTH = ITERS
LANE_STEP = 2 * DEPTH + 1
UNROLL = 4
GROUP = 4

VMEM = pl.BlockSpec(memory_space=pltpu.VMEM)
SMEM = pl.BlockSpec(memory_space=pltpu.SMEM)
HBM = pl.BlockSpec(memory_space=pltpu.HBM)


def z_up(a):
    return pltpu.roll(a, a.shape[-2] - 1, a.ndim - 2)


def z_down(a):
    return pltpu.roll(a, 1, a.ndim - 2)


def y_up(a):
    return pltpu.roll(a, a.shape[-1] - 1, a.ndim - 1)


def y_down(a):
    return pltpu.roll(a, 1, a.ndim - 1)


def reciprocal(a):
    r = pl.reciprocal(a, approx=True)
    return r * (2.0 - a * r)


def iota(shape, axis):
    return lax.broadcasted_iota(jnp.int32, shape, axis)


def odd(axis):
    return lax.rem(lax.axis_index(axis), 2) == 1


def by_parity(axis, pair, body):
    pl.when(jnp.logical_not(odd(axis)))(lambda: body(pair[0], pair[1]))
    pl.when(odd(axis))(lambda: body(pair[1], pair[0]))


def start_copies(sources, targets, sems):
    copies = []
    for g in range(sources[0].shape[0] // GROUP):
        at = pl.ds(g * GROUP, GROUP)
        copies.append(
            [pltpu.make_async_copy(a.at[at], b.at[at], sems.at[g, f]) for f, (a, b) in enumerate(zip(sources, targets))]
        )
        for copy in copies[-1]:
            copy.start()
    return copies


def clean_group(g, field_ref, phase_ref):
    bx, bz, by = phase_ref.shape
    ix, iz, iy = lax.axis_index("gx"), lax.axis_index("gz"), lax.axis_index("gy")
    plane, row, lane = (iota((GROUP, bz, by), d) for d in range(3))
    at = pl.ds(g * GROUP, GROUP)
    vx, vz, vy, p = (field_ref[f, at] for f in range(FIELDS - 1))
    if g == 0:
        vx = jnp.where((plane > 0) | (ix > 0), vx, 0.0)
    vz = jnp.where((row > 0) | (iz > 0), vz, 0.0)
    vy = jnp.where((lane > 0) | (iy > 0), vy, 0.0)
    return vx, vz, vy, p, phase_ref[at].astype(jnp.float32)


def add_edge(edge, a, base):
    by = edge.shape[-1]
    lane = iota((1,) * (edge.ndim - 1) + (by,), edge.ndim - 1)
    first = pltpu.roll(a, base, a.ndim - 1) if base else a
    edge = jnp.where((lane >= base) & (lane <= base + DEPTH), first, edge)
    last = pltpu.roll(a, (base + LANE_STEP) % by, a.ndim - 1)
    return jnp.where((lane > base + DEPTH) & (lane < base + LANE_STEP), last, edge)


def add_edges(edge, fields, upper):
    for f, a in enumerate(fields):
        edge = add_edge(edge, a, edge.shape[-1] // 2 * upper + LANE_STEP * f)
    return edge


def beside(edge, f, upper):
    by = edge.shape[-1]
    iy = lax.axis_index("gy")
    lane = iota((1,) * (edge.ndim - 1) + (by,), edge.ndim - 1)
    right = (lane <= DEPTH) & (iy < lax.axis_size("gy") - 1)
    left = (lane >= by - DEPTH) & (iy > 0)
    shift = by // 2 * upper + LANE_STEP * f
    a = pltpu.roll(edge, by - shift, edge.ndim - 1) if shift else edge
    b = pltpu.roll(edge, (by - LANE_STEP - shift) % by, edge.ndim - 1)
    return jnp.where(right, a, jnp.where(left, b, 0.0))


def pack_kernel(
    vx_hbm, vz_hbm, vy_hbm, p_hbm, phase_hbm, edge_hbm, x_0_hbm, x_1_hbm, stack_hbm,
    field_ref, phase_ref, edge_ref, stack_ref, sems, out_sems,
):
    bx, bz, by = phase_ref.shape
    targets = [field_ref.at[f] for f in range(FIELDS - 1)] + [phase_ref]
    copies = start_copies((vx_hbm, vz_hbm, vy_hbm, p_hbm, phase_hbm), targets, sems)
    half = bx // GROUP // 2
    outs = []

    def out(source, target):
        outs.append(pltpu.make_async_copy(source, target, out_sems.at[len(outs)]))
        outs[-1].start()

    for g in range(half):
        edge = jnp.zeros((GROUP, bz, by), jnp.float32)
        for upper in range(2):
            at = (g + upper * half) * GROUP
            for copy in copies[g + upper * half]:
                copy.wait()
            fields = clean_group(g + upper * half, field_ref, phase_ref)
            for f, a in enumerate(fields):
                for i in range(GROUP):
                    stack_ref[(at + i) * FIELDS + f] = a[i]
            edge = add_edges(edge, fields, upper)
            at = pl.ds(at * FIELDS, GROUP * FIELDS)
            out(stack_ref.at[at], stack_hbm.at[at])
        at = pl.ds(g * GROUP, GROUP)
        edge_ref[at] = edge
        out(edge_ref.at[at], edge_hbm.at[at])
    count = x_0_hbm.shape[0]
    down, up = stack_ref.at[pl.ds(0, count)], stack_ref.at[pl.ds(bx * FIELDS - count, count)]
    sem = out_sems.at[len(outs)], out_sems.at[len(outs) + 1]

    def send(to_above, to_below):
        pair = pltpu.make_async_copy(up, to_above, sem[0]), pltpu.make_async_copy(down, to_below, sem[1])
        for copy in pair:
            copy.start()
        for copy in pair:
            copy.wait()

    by_parity("gx", (x_0_hbm, x_1_hbm), send)
    for copy in outs:
        copy.wait()


def side_edge_kernel(x_0_ref, x_1_ref, own_edge_ref, edge_ref):
    bz, by = edge_ref.shape[1:]
    own = own_edge_ref.shape[0]
    edge_ref[0:own] = own_edge_ref[...]

    def body(above, below):
        edge = jnp.zeros((DEPTH, bz, by), jnp.float32)
        for upper, (ref, at) in enumerate(((above, 0), (below, 1))):
            block = ref[pl.ds(at, DEPTH * FIELDS)].reshape(DEPTH, FIELDS, bz, by)
            edge = add_edges(edge, [block[:, f] for f in range(FIELDS)], upper)
        edge_ref[own:] = edge
        edge_ref[own] = add_edge(edge[0], above[DEPTH * FIELDS], FIELDS * LANE_STEP)

    by_parity("gx", (x_0_ref, x_1_ref), body)


def half_rows(tiles, swap):
    down = odd("gz") if swap == 0 else jnp.logical_not(odd("gz"))
    half = tiles.shape[-2] // 2
    return jnp.where(down, tiles[..., :half, :], tiles[..., half:, :])


def store_next_rows(refs, at, tiles):
    half = tiles.shape[-2] // 2
    for ref in refs:
        for i in range(tiles.shape[0]):
            ref[at + i // half, i % half : i % half + 1, :] = tiles[i, half : half + 1, :]


def sides_kernel(x_0_ref, x_1_ref, _edge_ref, sides_ref, z_0_ref, z_1_ref):
    count = DEPTH * FIELDS
    bz, by = sides_ref.shape[1:]

    def body(above, below):
        sides_ref[0:count] = above[0:count]
        sides_ref[count : 2 * count] = below[1 : count + 1]
        sides_ref[2 * count] = above[count]

    by_parity("gx", (x_0_ref, x_1_ref), body)
    tiles = sides_ref[...]
    for swap, ref in enumerate((z_0_ref, z_1_ref)):
        ref[0 : 2 * count + 1] = half_rows(tiles, swap)
    vz = tiles[0 : 2 * count].reshape(2 * DEPTH, FIELDS, bz, by)[:, 1]
    store_next_rows((z_0_ref, z_1_ref), 2 * count + 1, vz)


def edge_rows_kernel(edge_ref, z_0_ref, z_1_ref):
    tiles = edge_ref[...]
    for swap, ref in enumerate((z_0_ref, z_1_ref)):
        ref[0 : tiles.shape[0]] = half_rows(tiles, swap)
    store_next_rows((z_0_ref, z_1_ref), tiles.shape[0], tiles)


def lookups(fields, ok, keep, table_ref):
    *rest, phase = fields
    for number in range(3):
        table = [table_ref[number * PHASES + index] for index in range(PHASES)]
        value = jnp.broadcast_to(table[0], phase.shape)
        for index in range(1, PHASES):
            value = jnp.where(phase == float(index), table[index], value)
        if number == 0:
            value = value * jnp.where(ok, 1.0, 0.0)
            if keep is not None:
                value = jnp.where(keep, value, 0.0)
        elif number == 1:
            value = (0.5 / math.log(2.0)) * (reciprocal(value) - 1.0)
        rest.append(value)
    return rest


def own_lanes(block, ok, tables):
    block = block.reshape(-1, FIELDS, *block.shape[-2:])
    return lookups([block[:, f] for f in range(FIELDS)], ok, None, tables)


def edge_lanes(edge, upper, ok, tables):
    by = edge.shape[-1]
    iy = lax.axis_index("gy")
    lane = iota((1, 1, by), 2)
    keep = ((lane <= DEPTH) & (iy < lax.axis_size("gy") - 1)) | ((lane >= by - DEPTH) & (iy > 0))
    return lookups([beside(edge, f, upper) for f in range(FIELDS)], ok, keep, tables)


def store_to(refs):
    def store(planes, part, values):
        by = values[0].shape[-1]
        for ref, value in zip(refs, values):
            ref[planes, :, part * by : (part + 1) * by] = value

    return store


def unpack_own(load, bx, ok, tables, store):
    def group(g, carry):
        at = g * GROUP
        store(pl.ds(DEPTH + at, GROUP), 0, own_lanes(load(at * FIELDS, GROUP * FIELDS), ok, tables))
        return carry

    lax.fori_loop(0, bx // GROUP, group, 0)


def unpack_own_edges(load, bx, ok, tables, store):
    half = bx // 2
    for upper in range(2):

        def group(g, carry):
            at = g * GROUP
            values = edge_lanes(load(at, GROUP), upper, ok, tables)
            store(pl.ds(DEPTH + upper * half + at, GROUP), 1, values)
            return carry

        lax.fori_loop(0, half // GROUP, group, 0)


def side_places(bx):
    ix = lax.axis_index("gx")
    return (pl.ds(DEPTH + bx, DEPTH), ix < lax.axis_size("gx") - 1), (pl.ds(0, DEPTH), ix > 0)


def unpack_sides(load, bx, ok, tables, store, vx_ref):
    count = DEPTH * FIELDS
    for n, (planes, inside) in enumerate(side_places(bx)):
        store(planes, 0, own_lanes(load(n * count, count), ok & inside, tables))
    vx = load(2 * count, 1)
    vx_ref[pl.ds(bx + 2 * DEPTH, 1), :, 0 : vx.shape[-1]] = vx


def unpack_side_edges(load, bx, ok, tables, store, vx_ref):
    half = bx // 2
    edge = load(half, DEPTH)
    for upper, (planes, inside) in enumerate(side_places(bx)):
        store(planes, 1, edge_lanes(edge, upper, ok & inside, tables))
    by = edge.shape[-1]
    vx_ref[pl.ds(bx + 2 * DEPTH, 1), :, by : 2 * by] = beside(edge[0:1], FIELDS, 0)


def own_kernel(stack_ref, edge_in_ref, tables_ref, z_0_ref, z_1_ref, edge_ref, v_ref, *rest):
    edge_ref[...] = edge_in_ref[...]
    count = stack_ref.shape[0]
    bx = count // FIELDS
    size = GROUP * FIELDS

    def group(g, carry):
        at = pl.ds(g * size, size)
        tiles = stack_ref[at]
        for swap, ref in enumerate((z_0_ref, z_1_ref)):
            ref[at] = half_rows(tiles, swap)
        return carry

    lax.fori_loop(0, bx // GROUP, group, 0)
    for g in range(bx // GROUP):
        vz = stack_ref[pl.ds(g * size, size)].reshape(GROUP, FIELDS, *stack_ref.shape[1:])[:, 1]
        store_next_rows((z_0_ref, z_1_ref), count + g * GROUP // (stack_ref.shape[1] // 2), vz)
    store = store_to([v_ref.at[d] for d in range(3)] + list(rest))
    unpack_own(lambda at, n: stack_ref[pl.ds(at, n)], bx, True, tables_ref, store)


def own_sides_kernel(sides_ref, edge_ref, tables_ref, *refs):
    v_ref, *rest = refs[len(refs) // 2 :]
    bx = v_ref.shape[1] - 2 * DEPTH - 1
    store = store_to([v_ref.at[d] for d in range(3)] + list(rest))
    unpack_sides(lambda at, n: sides_ref[pl.ds(at, n)], bx, True, tables_ref, store, v_ref.at[0])
    load = lambda at, n: edge_ref[pl.ds(at, n)]
    unpack_own_edges(load, bx, True, tables_ref, store)
    unpack_side_edges(load, bx, True, tables_ref, store, v_ref.at[0])


def rows_in_grid(bz):
    iz = lax.axis_index("gz")
    row = iota((1, bz, 1), 1)
    return ((row < bz // 2) & (iz < lax.axis_size("gz") - 1)) | ((row >= bz // 2) & (iz > 0))


def load_both(above, below):
    return lambda at, n: jnp.concatenate([above[pl.ds(at, n)], below[pl.ds(at, n)]], axis=1)


def halo_kernel(face_0_ref, face_1_ref, corner_0_ref, corner_1_ref, tables_ref, halo_ref, next_ref):
    half, by = face_0_ref.shape[1:]
    bz = 2 * half
    bx = halo_ref.shape[1] - 2 * DEPTH - 1
    ok = rows_in_grid(bz)
    store = store_to([halo_ref.at[n] for n in range(7)])

    def faces(above, below):
        unpack_own(load_both(above, below), bx, ok, tables_ref, store)
        for i in range(bx):
            n = i % half
            next_ref[DEPTH + i, half - 1 : half, 0:by] = above[bx * FIELDS + i // half, n : n + 1, :]

    def corners(above, below):
        unpack_sides(load_both(above, below), bx, ok, tables_ref, store, halo_ref.at[0])
        for i in range(2 * DEPTH):
            n = i % half
            to = DEPTH + bx + i if i < DEPTH else i - DEPTH
            next_ref[to, half - 1 : half, 0:by] = above[2 * DEPTH * FIELDS + 1 + i // half, n : n + 1, :]

    by_parity("gz", (face_0_ref, face_1_ref), faces)
    by_parity("gz", (corner_0_ref, corner_1_ref), corners)


def unpack_halo_edges(edge_0_ref, edge_1_ref, tables_ref, halo_ref, next_ref):
    half, by = edge_0_ref.shape[1:]
    bx = halo_ref.shape[1] - 2 * DEPTH - 1
    ok = rows_in_grid(2 * half)
    store = store_to([halo_ref.at[n] for n in range(7)])
    tiles = bx // 2 + DEPTH

    def body(above, below):
        load = load_both(above, below)
        unpack_own_edges(load, bx, ok, tables_ref, store)
        unpack_side_edges(load, bx, ok, tables_ref, store, halo_ref.at[0])
        for n in range(tiles // half):
            rows = above[tiles + n]
            for upper in range(2):
                values = beside(rows, 1, upper)
                for i in range(half):
                    tile = n * half + i
                    if tile < bx // 2:
                        to = DEPTH + upper * (bx // 2) + tile
                    else:
                        to = tile - bx // 2 + (0 if upper else DEPTH + bx)
                    next_ref[to, half - 1 : half, by : 2 * by] = values[i : i + 1]

    by_parity("gz", (edge_0_ref, edge_1_ref), body)


def main_kernel(
    v_ref, p0_ref, pre_ref, power_field_ref, rho_ref, _halo, _next, edge_0_ref, edge_1_ref, tables_ref,
    out_vx_ref, out_vz_ref, out_vy_ref, out_p_ref, out_eta_ref, sum_ref, halo_ref, next_ref,
    va_ref, vb_ref, p_ref, weight_ref,
):
    bx, bz, by = out_p_ref.shape
    rows, lanes = 2 * bz, 2 * by
    nx, nz, ny = lax.axis_size("gx"), lax.axis_size("gz"), lax.axis_size("gy")
    ix, iz, iy = lax.axis_index("gx"), lax.axis_index("gz"), lax.axis_index("gy")
    unpack_halo_edges(edge_0_ref, edge_1_ref, tables_ref, halo_ref, next_ref)

    shape = (rows, lanes)
    r, c = iota(shape, 0), iota(shape, 1)
    zg = iz * bz + jnp.where(r < bz + bz // 2, r, r - rows)
    yg = iy * by + jnp.where(c <= by + DEPTH, c, c - lanes)
    filled = (c <= by + DEPTH) | (c >= lanes - DEPTH)
    inside = filled & (zg >= 0) & (zg < nz * bz) & (yg >= 0) & (yg < ny * by)
    weight_ref[0] = jnp.where(inside, 0.05, 0.0)
    weight_ref[1] = jnp.where(inside & (zg > 0), 0.05, 0.0)
    weight_ref[2] = jnp.where(inside & (yg > 0), 0.05, 0.0)
    weight_ref[3] = jnp.where(inside, 0.0, 1.0)

    def with_halo(own, n, planes):
        return jnp.concatenate([own[planes], halo_ref[n, planes]], axis=1)

    for k in range(1, ITERS + 1):
        old, new = (va_ref, vb_ref) if k % 2 else (vb_ref, va_ref)
        last = k == ITERS

        def load(d, j, count):
            planes = pl.ds(j, count)
            return with_halo(v_ref.at[d], d, planes) if k == 1 else old[d, planes]

        def cells(j, count):
            planes = pl.ds(j, count)
            vx1 = load(0, j, count + 1)
            vx = vx1[:count]
            vz, vy = load(1, j, count), load(2, j, count)
            p = with_halo(p0_ref, 3, planes) if k == 1 else p_ref[planes]
            up = z_up(vz)
            if k == 1:
                after = next_ref[planes]
                after = jnp.concatenate([after, after], axis=1)
                up = jnp.where(iota((1, rows, lanes), 1) == bz + bz // 2 - 1, after, up)
            rx = vx1[1:] - vx
            rz = up - vz
            ry = y_up(vy) - vy
            a = rx - ry
            b = ry - rz
            inv = (a * (a + b) + b * b) * (1.0 / 3.0) + 1.0
            eta = with_halo(pre_ref, 4, planes) * jnp.exp2(with_halo(power_field_ref, 5, planes) * jnp.log(inv))
            quarter = 0.25 * eta
            div = rx + ry + rz
            p = p - quarter * (div + div)
            tx, tz, ty = eta * rx - p, eta * rz - p, eta * ry - p
            sz = quarter + z_down(quarter)
            sy = quarter + y_down(quarter)
            return vx, vz, vy, eta, p, quarter, tx, tz, ty, sz, sy

        def chunk(j, count, carry, start=False):
            planes = pl.ds(j, count)
            vx, vz, vy, eta, p, quarter, tx, tz, ty, sz, sy = cells(j, count)
            vz0, vy0 = load(1, j - 1, 1), load(2, j - 1, 1)
            quarter0, tx0, sz0, sy0, part_z0, part_y0, scale_z0, scale_y0 = carry
            join = lambda first, rest: jnp.concatenate([first, rest[:-1]], axis=0) if count > 1 else first
            bias = weight_ref[3:4]
            sx = quarter + join(quarter0, quarter)
            exz = sz + join(sz0, sz)
            exy = sy + join(sy0, sy)
            ezy = sz + y_down(sz)
            fxz = exz * (vx - z_down(vx))
            fxy = exy * (vx - y_down(vx))
            low_vz, low_vy = join(vz0, vz), join(vy0, vy)
            gzx = exz * (vz - low_vz)
            hyx = exy * (vy - low_vy)
            gzy = ezy * (vz - y_down(vz))
            hyz = ezy * (vy - z_down(vy))
            res_x = (tx - join(tx0, tx)) + ((z_up(fxz) - fxz) + (y_up(fxy) - fxy))
            new_vx = vx + weight_ref[0:1] * reciprocal(sx + bias) * res_x
            part_z = (tz - z_down(tz)) - with_halo(rho_ref, 6, planes) + ((y_up(gzy) - gzy) - gzx)
            part_y = (ty - y_down(ty)) + ((z_up(hyz) - hyz) - hyx)
            scale_z = weight_ref[1:2] * reciprocal(sz + bias)
            scale_y = weight_ref[2:3] * reciprocal(sy + bias)
            new_vz = low_vz + join(scale_z0, scale_z) * (join(part_z0, part_z) + gzx)
            new_vy = low_vy + join(scale_y0, scale_y) * (join(part_y0, part_y) + hyx)
            if last:
                at = pl.ds(j - DEPTH, count)
                out_vx_ref[at] = new_vx[:, 0:bz, 0:by]
                out_p_ref[at] = p[:, 0:bz, 0:by]
                out_eta_ref[at] = eta[:, 0:bz, 0:by]
                sum_ref[...] += jnp.sum(p[:, 0:bz, 0:by], axis=0)
                if not start:
                    at = pl.ds(j - 1 - DEPTH, count)
                    out_vz_ref[at] = new_vz[:, 0:bz, 0:by]
                    out_vy_ref[at] = new_vy[:, 0:bz, 0:by]
            else:
                p_ref[planes] = p
                new[0, planes] = new_vx
                if not start:
                    new[1, pl.ds(j - 1, count)] = new_vz
                    new[2, pl.ds(j - 1, count)] = new_vy
            return tuple(a[-1:] for a in (quarter, tx, sz, sy, part_z, part_y, scale_z, scale_y))

        first, end = k, bx + 2 * DEPTH - k
        if last:
            sum_ref[...] = jnp.zeros((bz, by), jnp.float32)
        _, _, _, _, p, quarter, tx, _, _, sz, sy = cells(first - 1, 1)
        if not last:
            p_ref[pl.ds(first - 1, 1)] = p
        zero = jnp.zeros((1, rows, lanes), jnp.float32)
        carry = chunk(first, 1, (quarter, tx, sz, sy, zero, zero, zero, zero), start=True)
        steps, rest = divmod((end - 1 if last else end) - first, UNROLL)
        carry = lax.fori_loop(
            0, steps, lambda s, carry: chunk(first + 1 + s * UNROLL, UNROLL, carry), carry
        )
        if rest:
            carry = chunk(first + 1 + steps * UNROLL, rest, carry)
        if last:
            quarter0, tx0, sz0, sy0, part_z0, part_y0, scale_z0, scale_y0 = carry
            _, vz, vy, _, _, _, _, _, _, sz, sy = cells(end, 1)
            vz0, vy0 = load(1, end - 1, 1), load(2, end - 1, 1)
            new_vz = vz0 + scale_z0 * (part_z0 + (sz + sz0) * (vz - vz0))
            new_vy = vy0 + scale_y0 * (part_y0 + (sy + sy0) * (vy - vy0))
            out_vz_ref[pl.ds(end - 1 - DEPTH, 1)] = new_vz[:, 0:bz, 0:by]
            out_vy_ref[pl.ds(end - 1 - DEPTH, 1)] = new_vy[:, 0:bz, 0:by]

            @pl.when(ix == 0)
            def _():
                out_vx_ref[0] = jnp.zeros((bz, by), jnp.float32)
        else:
            plane = jnp.zeros((rows, lanes), jnp.float32)

            @pl.when(ix == 0)
            def _():
                for i in range(first, DEPTH):
                    for d in range(3):
                        new[d, i] = plane
                new[0, DEPTH] = plane

            @pl.when(ix == nx - 1)
            def _():
                for i in range(DEPTH + bx, end + 1):
                    for d in range(3):
                        new[d, i] = plane


def final_kernel(p_ref, sum_ref, out_ref, *, cells):
    mean = jnp.sum(sum_ref[...]) * (1.0 / cells)
    out_ref[...] = p_ref[...] - mean


def swap(a, axis, start):
    count = lax.axis_size(axis)
    return lax.ppermute(a, axis, [(i, j) for k in range(start, count - 1, 2) for i, j in ((k, k + 1), (k + 1, k))])


def sum_everywhere(total):
    axes = ("gx", "gy", "gz")
    devices = math.prod(lax.axis_size(a) for a in axes)
    if devices & (devices - 1):
        return lax.psum(total, axes)
    bits = [1 << n for n in range(devices.bit_length() - 1)]
    for stage in [bits[:1]] + [bits[n : n + 2] for n in range(1, len(bits), 2)]:
        masks = stage if len(stage) == 1 else [stage[0], stage[1], stage[0] + stage[1]]
        total = sum([lax.ppermute(total, axes, [(i, i ^ m) for i in range(devices)]) for m in masks], total)
    return total


def local(vel_x, vel_y, vel_z, pressure, phase, visc_scale, power_n, density):
    bx, bz, by = pressure.shape
    assert bx % (2 * GROUP) == 0 and bz == 2 * DEPTH and DEPTH == GROUP
    f32 = jnp.float32
    iy, ny = lax.axis_index("gy"), lax.axis_size("gy")
    cells = bx * bz * by * math.prod(lax.axis_size(a) for a in ("gx", "gz", "gy"))
    deep = bx + 2 * DEPTH + 1
    rows, lanes = 2 * bz, 2 * by
    shape = lambda *dims: jax.ShapeDtypeStruct(dims, f32)
    block = shape(bx, bz, by)
    scratch = lambda *dims: pltpu.VMEM(dims, f32)
    limit = lambda mebibytes: pltpu.CompilerParams(vmem_limit_bytes=mebibytes * 1024 * 1024)
    tables = jnp.concatenate([visc_scale, power_n, density])

    groups = bx // GROUP
    sent = shape(DEPTH * FIELDS + 1, bz, by)
    edge, x_0, x_1, stack = pl.pallas_call(
        pack_kernel,
        out_shape=(shape(bx // 2, bz, by), sent, sent, shape(bx * FIELDS, bz, by)),
        in_specs=[HBM] * 5,
        out_specs=(HBM,) * 4,
        scratch_shapes=[
            scratch(FIELDS - 1, bx, bz, by),
            pltpu.VMEM((bx, bz, by), jnp.int32),
            scratch(bx // 2, bz, by),
            scratch(bx * FIELDS, bz, by),
            pltpu.SemaphoreType.DMA((groups, FIELDS)),
            pltpu.SemaphoreType.DMA((groups + groups // 2 + 2,)),
        ],
        compiler_params=limit(58),
    )(vel_x, vel_z, vel_y, pressure, phase)

    def edges_beside(edge):
        side = swap(edge, "gy", 0)
        if ny == 2:
            return side
        lane = iota(side.shape, 2) % (by // 2) % LANE_STEP
        return jnp.where((lane <= DEPTH) == (lax.rem(iy, 2) == 0), side, swap(edge, "gy", 1))

    estimate = lambda size: pl.CostEstimate(
        flops=4 * size * bz * by, bytes_accessed=size * bz * by * 4, transcendentals=0
    )
    long = estimate(100000)

    def unpacking(kernel, tiles, out_shape, *args, aliases={}):
        return pl.pallas_call(
            kernel,
            out_shape=out_shape,
            in_specs=[VMEM if a is not tables else SMEM for a in args],
            out_specs=(VMEM,) * len(out_shape),
            input_output_aliases=aliases,
            compiler_params=limit(16),
            cost_estimate=estimate(13 * tiles),
        )(*args)

    field = shape(deep, bz, lanes)
    own_shape = (shape(3, deep, bz, lanes),) + (field,) * 4
    half = lambda tiles, planes: shape(tiles + planes // (bz // 2), bz // 2, by)
    x_0, x_1 = swap(x_0, "gx", 0), swap(x_1, "gx", 1)
    face = half(bx * FIELDS, bx)
    z_0, z_1, edge, *own = unpacking(own_kernel, bx, (face, face, shape(*edge.shape)) + own_shape, stack, edge, tables)
    face_1, face_0 = swap(z_1, "gz", 1), swap(z_0, "gz", 0)

    tiles = bx // 2 + DEPTH
    edge = pl.pallas_call(
        side_edge_kernel,
        out_shape=shape(tiles, bz, by),
        in_specs=[VMEM] * 3,
        out_specs=VMEM,
        compiler_params=limit(4),
    )(x_0, x_1, edge)
    corner = half(2 * DEPTH * FIELDS + 1, 2 * DEPTH)
    sides, z_0, z_1 = pl.pallas_call(
        sides_kernel,
        out_shape=(shape(2 * DEPTH * FIELDS + 1, bz, by), corner, corner),
        in_specs=[VMEM] * 3,
        out_specs=(VMEM,) * 3,
        compiler_params=limit(4),
    )(x_0, x_1, edge)
    edge = edges_beside(edge)
    corner_1, corner_0 = swap(z_1, "gz", 1), swap(z_0, "gz", 0)
    z_0, z_1 = pl.pallas_call(
        edge_rows_kernel,
        out_shape=(half(tiles, tiles),) * 2,
        in_specs=[VMEM],
        out_specs=(VMEM,) * 2,
        compiler_params=limit(4),
        cost_estimate=long,
    )(edge)
    edge_1, edge_0 = swap(z_1, "gz", 1), swap(z_0, "gz", 0)

    own = unpacking(
        own_sides_kernel, 2 * deep, own_shape, sides, edge, tables, *own, aliases={n + 3: n for n in range(5)}
    )
    halo = unpacking(
        halo_kernel, deep, (shape(7, deep, bz, lanes), field), face_0, face_1, corner_0, corner_1, tables
    )
    vx, vz, vy, p, eta, total, _, _ = pl.pallas_call(
        main_kernel,
        out_shape=(block,) * 5 + (shape(bz, by),) + tuple(shape(*a.shape) for a in halo),
        in_specs=[VMEM] * 9 + [SMEM],
        out_specs=(VMEM,) * 8,
        input_output_aliases={5: 6, 6: 7},
        scratch_shapes=[
            scratch(3, deep, rows, lanes),
            scratch(3, deep, rows, lanes),
            scratch(deep, rows, lanes),
            scratch(4, rows, lanes),
        ],
        compiler_params=limit(32),
    )(*own, *halo, edge_0, edge_1, tables)

    total = sum_everywhere(total)
    p = pl.pallas_call(
        lambda *refs: final_kernel(*refs, cells=float(cells)),
        out_shape=block,
        in_specs=[VMEM] * 2,
        out_specs=VMEM,
        compiler_params=limit(4),
    )(p, total)
    return (vx, vy, vz, p, eta)


def solution(mesh):
    spec = P("gx", "gz", "gy")
    return jax.shard_map(
        local,
        mesh=mesh,
        in_specs=(spec,) * 5 + (P(),) * 3,
        out_specs=(spec,) * 5,
        check_vma=False,
    )
```

```python
import math

import jax
import jax.numpy as jnp
from jax import lax
from jax.experimental import pallas as pl
from jax.experimental.pallas import tpu as pltpu
from jax.sharding import PartitionSpec as P

ITERS = 4
PHASES = 4
FIELDS = 5
DEPTH = ITERS
LANE_STEP = 2 * DEPTH + 1
UNROLL = 4
GROUP = 4

VMEM = pl.BlockSpec(memory_space=pltpu.VMEM)
SMEM = pl.BlockSpec(memory_space=pltpu.SMEM)
HBM = pl.BlockSpec(memory_space=pltpu.HBM)


def z_up(a):
    return pltpu.roll(a, a.shape[-2] - 1, a.ndim - 2)


def z_down(a):
    return pltpu.roll(a, 1, a.ndim - 2)


def y_up(a):
    return pltpu.roll(a, a.shape[-1] - 1, a.ndim - 1)


def y_down(a):
    return pltpu.roll(a, 1, a.ndim - 1)


def reciprocal(a):
    r = pl.reciprocal(a, approx=True)
    return r * (2.0 - a * r)


def iota(shape, axis):
    return lax.broadcasted_iota(jnp.int32, shape, axis)


def odd(axis):
    return lax.rem(lax.axis_index(axis), 2) == 1


def by_parity(axis, pair, body):
    pl.when(jnp.logical_not(odd(axis)))(lambda: body(pair[0], pair[1]))
    pl.when(odd(axis))(lambda: body(pair[1], pair[0]))


def start_copies(sources, targets, sems):
    copies = []
    for g in range(sources[0].shape[0] // GROUP):
        at = pl.ds(g * GROUP, GROUP)
        copies.append(
            [pltpu.make_async_copy(a.at[at], b.at[at], sems.at[g, f]) for f, (a, b) in enumerate(zip(sources, targets))]
        )
        for copy in copies[-1]:
            copy.start()
    return copies


def clean_group(g, field_ref, phase_ref):
    bx, bz, by = phase_ref.shape
    ix, iz, iy = lax.axis_index("gx"), lax.axis_index("gz"), lax.axis_index("gy")
    plane, row, lane = (iota((GROUP, bz, by), d) for d in range(3))
    at = pl.ds(g * GROUP, GROUP)
    vx, vz, vy, p = (field_ref[f, at] for f in range(FIELDS - 1))
    if g == 0:
        vx = jnp.where((plane > 0) | (ix > 0), vx, 0.0)
    vz = jnp.where((row > 0) | (iz > 0), vz, 0.0)
    vy = jnp.where((lane > 0) | (iy > 0), vy, 0.0)
    return vx, vz, vy, p, phase_ref[at].astype(jnp.float32)


def add_edge(edge, a, base):
    by = edge.shape[-1]
    lane = iota((1,) * (edge.ndim - 1) + (by,), edge.ndim - 1)
    first = pltpu.roll(a, base, a.ndim - 1) if base else a
    edge = jnp.where((lane >= base) & (lane <= base + DEPTH), first, edge)
    last = pltpu.roll(a, (base + LANE_STEP) % by, a.ndim - 1)
    return jnp.where((lane > base + DEPTH) & (lane < base + LANE_STEP), last, edge)


def add_edges(edge, fields, upper):
    for f, a in enumerate(fields):
        edge = add_edge(edge, a, edge.shape[-1] // 2 * upper + LANE_STEP * f)
    return edge


def beside(edge, f, upper):
    by = edge.shape[-1]
    iy = lax.axis_index("gy")
    lane = iota((1,) * (edge.ndim - 1) + (by,), edge.ndim - 1)
    right = (lane <= DEPTH) & (iy < lax.axis_size("gy") - 1)
    left = (lane >= by - DEPTH) & (iy > 0)
    shift = by // 2 * upper + LANE_STEP * f
    a = pltpu.roll(edge, by - shift, edge.ndim - 1) if shift else edge
    b = pltpu.roll(edge, (by - LANE_STEP - shift) % by, edge.ndim - 1)
    return jnp.where(right, a, jnp.where(left, b, 0.0))


def pack_kernel(
    vx_hbm, vz_hbm, vy_hbm, p_hbm, phase_hbm, scale_ref, power_ref, rho_ref, edge_hbm, x_0_hbm, x_1_hbm, stack_hbm,
    field_ref, phase_ref, edge_ref, stack_ref, sems, out_sems,
):
    bx, bz, by = phase_ref.shape
    targets = [field_ref.at[f] for f in range(FIELDS - 1)] + [phase_ref]
    copies = start_copies((vx_hbm, vz_hbm, vy_hbm, p_hbm, phase_hbm), targets, sems)
    half = bx // GROUP // 2
    outs = []

    def out(source, target):
        outs.append(pltpu.make_async_copy(source, target, out_sems.at[len(outs)]))
        outs[-1].start()

    for g in range(half):
        edge = jnp.zeros((GROUP, bz, by), jnp.float32)
        for upper in range(2):
            at = (g + upper * half) * GROUP
            for copy in copies[g + upper * half]:
                copy.wait()
            fields = clean_group(g + upper * half, field_ref, phase_ref)
            for f, a in enumerate(fields):
                for i in range(GROUP):
                    stack_ref[(at + i) * FIELDS + f] = a[i]
            edge = add_edges(edge, fields, upper)
            at = pl.ds(at * FIELDS, GROUP * FIELDS)
            out(stack_ref.at[at], stack_hbm.at[at])
        at = pl.ds(g * GROUP, GROUP)
        edge_ref[at] = edge
        out(edge_ref.at[at], edge_hbm.at[at])
        stack_ref[pl.ds(bx * FIELDS + g * GROUP, GROUP)] = edge
    count = bx * FIELDS + bx // 2
    row = iota((bz, by), 0)
    entries = [ref[index] for ref in (scale_ref, power_ref, rho_ref) for index in range(PHASES)]
    for n in range(2):
        tile = jnp.zeros((bz, by), jnp.float32)
        for r, entry in enumerate(entries[n * bz : (n + 1) * bz]):
            tile = jnp.where(row == r, entry, tile)
        stack_ref[count + n] = tile
    at = pl.ds(bx * FIELDS, count + 2 - bx * FIELDS)
    out(stack_ref.at[at], stack_hbm.at[at])
    count = x_0_hbm.shape[0]
    down, up = stack_ref.at[pl.ds(0, count)], stack_ref.at[pl.ds(bx * FIELDS - count, count)]
    sem = out_sems.at[len(outs)], out_sems.at[len(outs) + 1]

    def send(to_above, to_below):
        pair = pltpu.make_async_copy(up, to_above, sem[0]), pltpu.make_async_copy(down, to_below, sem[1])
        for copy in pair:
            copy.start()
        for copy in pair:
            copy.wait()

    by_parity("gx", (x_0_hbm, x_1_hbm), send)
    for copy in outs:
        copy.wait()


def side_edge_kernel(x_0_ref, x_1_ref, own_edge_ref, edge_ref):
    bz, by = edge_ref.shape[1:]
    own = own_edge_ref.shape[0]
    edge_ref[0:own] = own_edge_ref[...]

    def body(above, below):
        edge = jnp.zeros((DEPTH, bz, by), jnp.float32)
        for upper, (ref, at) in enumerate(((above, 0), (below, 1))):
            block = ref[pl.ds(at, DEPTH * FIELDS)].reshape(DEPTH, FIELDS, bz, by)
            edge = add_edges(edge, [block[:, f] for f in range(FIELDS)], upper)
        edge_ref[own:] = edge
        edge_ref[own] = add_edge(edge[0], above[DEPTH * FIELDS], FIELDS * LANE_STEP)

    by_parity("gx", (x_0_ref, x_1_ref), body)


def half_rows(tiles, swap):
    down = odd("gz") if swap == 0 else jnp.logical_not(odd("gz"))
    half = tiles.shape[-2] // 2
    return jnp.where(down, tiles[..., :half, :], tiles[..., half:, :])


def store_next_rows(refs, at, tiles):
    half = tiles.shape[-2] // 2
    for ref in refs:
        for i in range(tiles.shape[0]):
            ref[at + i // half, i % half : i % half + 1, :] = tiles[i, half : half + 1, :]


def sides_kernel(x_0_ref, x_1_ref, edge_ref, sides_ref, z_0_ref, z_1_ref):
    count = DEPTH * FIELDS
    bz, by = sides_ref.shape[1:]

    def body(above, below):
        sides_ref[0:count] = above[0:count]
        sides_ref[count : 2 * count] = below[1 : count + 1]
        sides_ref[2 * count] = above[count]

    by_parity("gx", (x_0_ref, x_1_ref), body)
    tiles = sides_ref[...]
    vz = tiles[0 : 2 * count].reshape(2 * DEPTH, FIELDS, bz, by)[:, 1]
    at = 0
    for whole, after in ((tiles, vz), (edge_ref[...], edge_ref[...])):
        for swap, ref in enumerate((z_0_ref, z_1_ref)):
            ref[at : at + whole.shape[0]] = half_rows(whole, swap)
        at += whole.shape[0]
        store_next_rows((z_0_ref, z_1_ref), at, after)
        at += after.shape[0] // (bz // 2)


def lookups(fields, ok, keep, table_ref):
    *rest, phase = fields
    for number in range(3):
        rows = [divmod(number * PHASES + index, table_ref.shape[1]) for index in range(PHASES)]
        table = [table_ref[n, r : r + 1, :] for n, r in rows]
        value = jnp.broadcast_to(table[0], phase.shape)
        for index in range(1, PHASES):
            value = jnp.where(phase == float(index), table[index], value)
        if number == 0:
            value = value * jnp.where(ok, 1.0, 0.0)
            if keep is not None:
                value = jnp.where(keep, value, 0.0)
        elif number == 1:
            value = (0.5 / math.log(2.0)) * (reciprocal(value) - 1.0)
        rest.append(value)
    return rest


def own_lanes(block, ok, tables):
    block = block.reshape(-1, FIELDS, *block.shape[-2:])
    return lookups([block[:, f] for f in range(FIELDS)], ok, None, tables)


def edge_lanes(edge, upper, ok, tables):
    by = edge.shape[-1]
    iy = lax.axis_index("gy")
    lane = iota((1, 1, by), 2)
    keep = ((lane <= DEPTH) & (iy < lax.axis_size("gy") - 1)) | ((lane >= by - DEPTH) & (iy > 0))
    return lookups([beside(edge, f, upper) for f in range(FIELDS)], ok, keep, tables)


def store_to(refs):
    def store(planes, part, values):
        by = values[0].shape[-1]
        for ref, value in zip(refs, values):
            ref[planes, :, part * by : (part + 1) * by] = value

    return store


def unpack_own(load, bx, ok, tables, store):
    def group(g, carry):
        at = g * GROUP
        store(pl.ds(DEPTH + at, GROUP), 0, own_lanes(load(at * FIELDS, GROUP * FIELDS), ok, tables))
        return carry

    lax.fori_loop(0, bx // GROUP, group, 0)


def unpack_own_edges(load, bx, ok, tables, store):
    half = bx // 2
    for upper in range(2):

        def group(g, carry):
            at = g * GROUP
            values = edge_lanes(load(at, GROUP), upper, ok, tables)
            store(pl.ds(DEPTH + upper * half + at, GROUP), 1, values)
            return carry

        lax.fori_loop(0, half // GROUP, group, 0)


def side_places(bx):
    ix = lax.axis_index("gx")
    return (pl.ds(DEPTH + bx, DEPTH), ix < lax.axis_size("gx") - 1), (pl.ds(0, DEPTH), ix > 0)


def unpack_sides(load, bx, ok, tables, store, vx_ref):
    count = DEPTH * FIELDS
    for n, (planes, inside) in enumerate(side_places(bx)):
        store(planes, 0, own_lanes(load(n * count, count), ok & inside, tables))
    vx = load(2 * count, 1)
    vx_ref[pl.ds(bx + 2 * DEPTH, 1), :, 0 : vx.shape[-1]] = vx


def unpack_side_edges(load, bx, ok, tables, store, vx_ref):
    half = bx // 2
    edge = load(half, DEPTH)
    for upper, (planes, inside) in enumerate(side_places(bx)):
        store(planes, 1, edge_lanes(edge, upper, ok & inside, tables))
    by = edge.shape[-1]
    vx_ref[pl.ds(bx + 2 * DEPTH, 1), :, by : 2 * by] = beside(edge[0:1], FIELDS, 0)


def own_kernel(stack_ref, z_0_ref, z_1_ref, edge_ref, tables_ref, v_ref, *rest):
    bx = v_ref.shape[1] - 2 * DEPTH - 1
    count = bx * FIELDS
    edge_ref[...] = stack_ref[count : count + bx // 2]
    tables_ref[...] = stack_ref[count + bx // 2 :]
    size = GROUP * FIELDS

    def group(g, carry):
        at = pl.ds(g * size, size)
        tiles = stack_ref[at]
        for swap, ref in enumerate((z_0_ref, z_1_ref)):
            ref[at] = half_rows(tiles, swap)
        return carry

    lax.fori_loop(0, bx // GROUP, group, 0)
    for g in range(bx // GROUP):
        vz = stack_ref[pl.ds(g * size, size)].reshape(GROUP, FIELDS, *stack_ref.shape[1:])[:, 1]
        store_next_rows((z_0_ref, z_1_ref), count + g * GROUP // (stack_ref.shape[1] // 2), vz)
    store = store_to([v_ref.at[d] for d in range(3)] + list(rest))
    unpack_own(lambda at, n: stack_ref[pl.ds(at, n)], bx, True, tables_ref, store)


def own_sides_kernel(sides_ref, edge_ref, tables_ref, *refs):
    v_ref, *rest = refs[len(refs) // 2 :]
    bx = v_ref.shape[1] - 2 * DEPTH - 1
    store = store_to([v_ref.at[d] for d in range(3)] + list(rest))
    unpack_sides(lambda at, n: sides_ref[pl.ds(at, n)], bx, True, tables_ref, store, v_ref.at[0])
    load = lambda at, n: edge_ref[pl.ds(at, n)]
    unpack_own_edges(load, bx, True, tables_ref, store)
    unpack_side_edges(load, bx, True, tables_ref, store, v_ref.at[0])


def rows_in_grid(bz):
    iz = lax.axis_index("gz")
    row = iota((1, bz, 1), 1)
    return ((row < bz // 2) & (iz < lax.axis_size("gz") - 1)) | ((row >= bz // 2) & (iz > 0))


def load_both(above, below):
    return lambda at, n: jnp.concatenate([above[pl.ds(at, n)], below[pl.ds(at, n)]], axis=1)


def halo_kernel(face_0_ref, face_1_ref, tables_ref, halo_ref, next_ref):
    half, by = face_0_ref.shape[1:]
    bx = halo_ref.shape[1] - 2 * DEPTH - 1
    store = store_to([halo_ref.at[n] for n in range(7)])

    def body(above, below):
        unpack_own(load_both(above, below), bx, rows_in_grid(2 * half), tables_ref, store)
        for i in range(bx):
            n = i % half
            next_ref[DEPTH + i, half - 1 : half, 0:by] = above[bx * FIELDS + i // half, n : n + 1, :]

    by_parity("gz", (face_0_ref, face_1_ref), body)


def unpack_corners(corner_0_ref, corner_1_ref, tables_ref, halo_ref, next_ref):
    half, by = corner_0_ref.shape[1:]
    bx = halo_ref.shape[1] - 2 * DEPTH - 1
    ok = rows_in_grid(2 * half)
    store = store_to([halo_ref.at[n] for n in range(7)])
    fields = 2 * DEPTH * FIELDS + 1
    edges = fields + 2 * DEPTH // half
    tiles = bx // 2 + DEPTH

    def body(above, below):
        unpack_sides(load_both(above, below), bx, ok, tables_ref, store, halo_ref.at[0])
        for i in range(2 * DEPTH):
            n = i % half
            to = DEPTH + bx + i if i < DEPTH else i - DEPTH
            next_ref[to, half - 1 : half, 0:by] = above[fields + i // half, n : n + 1, :]
        load = load_both(above.at[pl.ds(edges, tiles)], below.at[pl.ds(edges, tiles)])
        unpack_own_edges(load, bx, ok, tables_ref, store)
        unpack_side_edges(load, bx, ok, tables_ref, store, halo_ref.at[0])
        for n in range(tiles // half):
            rows = above[edges + tiles + n]
            for upper in range(2):
                values = beside(rows, 1, upper)
                for i in range(half):
                    tile = n * half + i
                    if tile < bx // 2:
                        to = DEPTH + upper * (bx // 2) + tile
                    else:
                        to = tile - bx // 2 + (0 if upper else DEPTH + bx)
                    next_ref[to, half - 1 : half, by : 2 * by] = values[i : i + 1]

    by_parity("gz", (corner_0_ref, corner_1_ref), body)


def main_kernel(
    v_ref, p0_ref, pre_ref, power_field_ref, rho_ref, _halo, _next, corner_0_ref, corner_1_ref, tables_ref,
    out_vx_ref, out_vz_ref, out_vy_ref, out_p_ref, out_eta_ref, sum_ref, halo_ref, next_ref,
    va_ref, vb_ref, p_ref, weight_ref,
):
    bx, bz, by = out_p_ref.shape
    rows, lanes = 2 * bz, 2 * by
    nx, nz, ny = lax.axis_size("gx"), lax.axis_size("gz"), lax.axis_size("gy")
    ix, iz, iy = lax.axis_index("gx"), lax.axis_index("gz"), lax.axis_index("gy")
    unpack_corners(corner_0_ref, corner_1_ref, tables_ref, halo_ref, next_ref)

    shape = (rows, lanes)
    r, c = iota(shape, 0), iota(shape, 1)
    zg = iz * bz + jnp.where(r < bz + bz // 2, r, r - rows)
    yg = iy * by + jnp.where(c <= by + DEPTH, c, c - lanes)
    filled = (c <= by + DEPTH) | (c >= lanes - DEPTH)
    inside = filled & (zg >= 0) & (zg < nz * bz) & (yg >= 0) & (yg < ny * by)
    weight_ref[0] = jnp.where(inside, 0.05, 0.0)
    weight_ref[1] = jnp.where(inside & (zg > 0), 0.05, 0.0)
    weight_ref[2] = jnp.where(inside & (yg > 0), 0.05, 0.0)
    weight_ref[3] = jnp.where(inside, 0.0, 1.0)

    def with_halo(own, n, planes):
        return jnp.concatenate([own[planes], halo_ref[n, planes]], axis=1)

    for k in range(1, ITERS + 1):
        old, new = (va_ref, vb_ref) if k % 2 else (vb_ref, va_ref)
        last = k == ITERS

        def load(d, j, count):
            planes = pl.ds(j, count)
            return with_halo(v_ref.at[d], d, planes) if k == 1 else old[d, planes]

        def cells(j, count):
            planes = pl.ds(j, count)
            vx1 = load(0, j, count + 1)
            vx = vx1[:count]
            vz, vy = load(1, j, count), load(2, j, count)
            p = with_halo(p0_ref, 3, planes) if k == 1 else p_ref[planes]
            up = z_up(vz)
            if k == 1:
                after = next_ref[planes]
                after = jnp.concatenate([after, after], axis=1)
                up = jnp.where(iota((1, rows, lanes), 1) == bz + bz // 2 - 1, after, up)
            rx = vx1[1:] - vx
            rz = up - vz
            ry = y_up(vy) - vy
            a = rx - ry
            b = ry - rz
            inv = (a * (a + b) + b * b) * (1.0 / 3.0) + 1.0
            eta = with_halo(pre_ref, 4, planes) * jnp.exp2(with_halo(power_field_ref, 5, planes) * jnp.log(inv))
            quarter = 0.25 * eta
            div = rx + ry + rz
            p = p - quarter * (div + div)
            tx, tz, ty = eta * rx - p, eta * rz - p, eta * ry - p
            sz = quarter + z_down(quarter)
            sy = quarter + y_down(quarter)
            return vx, vz, vy, eta, p, quarter, tx, tz, ty, sz, sy

        def chunk(j, count, carry, start=False):
            planes = pl.ds(j, count)
            vx, vz, vy, eta, p, quarter, tx, tz, ty, sz, sy = cells(j, count)
            vz0, vy0 = load(1, j - 1, 1), load(2, j - 1, 1)
            quarter0, tx0, sz0, sy0, part_z0, part_y0, scale_z0, scale_y0 = carry
            join = lambda first, rest: jnp.concatenate([first, rest[:-1]], axis=0) if count > 1 else first
            bias = weight_ref[3:4]
            sx = quarter + join(quarter0, quarter)
            exz = sz + join(sz0, sz)
            exy = sy + join(sy0, sy)
            ezy = sz + y_down(sz)
            fxz = exz * (vx - z_down(vx))
            fxy = exy * (vx - y_down(vx))
            low_vz, low_vy = join(vz0, vz), join(vy0, vy)
            gzx = exz * (vz - low_vz)
            hyx = exy * (vy - low_vy)
            gzy = ezy * (vz - y_down(vz))
            hyz = ezy * (vy - z_down(vy))
            res_x = (tx - join(tx0, tx)) + ((z_up(fxz) - fxz) + (y_up(fxy) - fxy))
            new_vx = vx + weight_ref[0:1] * reciprocal(sx + bias) * res_x
            part_z = (tz - z_down(tz)) - with_halo(rho_ref, 6, planes) + ((y_up(gzy) - gzy) - gzx)
            part_y = (ty - y_down(ty)) + ((z_up(hyz) - hyz) - hyx)
            scale_z = weight_ref[1:2] * reciprocal(sz + bias)
            scale_y = weight_ref[2:3] * reciprocal(sy + bias)
            new_vz = low_vz + join(scale_z0, scale_z) * (join(part_z0, part_z) + gzx)
            new_vy = low_vy + join(scale_y0, scale_y) * (join(part_y0, part_y) + hyx)
            if last:
                at = pl.ds(j - DEPTH, count)
                out_vx_ref[at] = new_vx[:, 0:bz, 0:by]
                out_p_ref[at] = p[:, 0:bz, 0:by]
                out_eta_ref[at] = eta[:, 0:bz, 0:by]
                sum_ref[...] += jnp.sum(p[:, 0:bz, 0:by], axis=0)
                if not start:
                    at = pl.ds(j - 1 - DEPTH, count)
                    out_vz_ref[at] = new_vz[:, 0:bz, 0:by]
                    out_vy_ref[at] = new_vy[:, 0:bz, 0:by]
            else:
                p_ref[planes] = p
                new[0, planes] = new_vx
                if not start:
                    new[1, pl.ds(j - 1, count)] = new_vz
                    new[2, pl.ds(j - 1, count)] = new_vy
            return tuple(a[-1:] for a in (quarter, tx, sz, sy, part_z, part_y, scale_z, scale_y))

        first, end = k, bx + 2 * DEPTH - k
        if last:
            sum_ref[...] = jnp.zeros((bz, by), jnp.float32)
        _, _, _, _, p, quarter, tx, _, _, sz, sy = cells(first - 1, 1)
        if not last:
            p_ref[pl.ds(first - 1, 1)] = p
        zero = jnp.zeros((1, rows, lanes), jnp.float32)
        carry = chunk(first, 1, (quarter, tx, sz, sy, zero, zero, zero, zero), start=True)
        steps, rest = divmod((end - 1 if last else end) - first, UNROLL)
        carry = lax.fori_loop(
            0, steps, lambda s, carry: chunk(first + 1 + s * UNROLL, UNROLL, carry), carry
        )
        if rest:
            carry = chunk(first + 1 + steps * UNROLL, rest, carry)
        if last:
            quarter0, tx0, sz0, sy0, part_z0, part_y0, scale_z0, scale_y0 = carry
            _, vz, vy, _, _, _, _, _, _, sz, sy = cells(end, 1)
            vz0, vy0 = load(1, end - 1, 1), load(2, end - 1, 1)
            new_vz = vz0 + scale_z0 * (part_z0 + (sz + sz0) * (vz - vz0))
            new_vy = vy0 + scale_y0 * (part_y0 + (sy + sy0) * (vy - vy0))
            out_vz_ref[pl.ds(end - 1 - DEPTH, 1)] = new_vz[:, 0:bz, 0:by]
            out_vy_ref[pl.ds(end - 1 - DEPTH, 1)] = new_vy[:, 0:bz, 0:by]

            @pl.when(ix == 0)
            def _():
                out_vx_ref[0] = jnp.zeros((bz, by), jnp.float32)
        else:
            plane = jnp.zeros((rows, lanes), jnp.float32)

            @pl.when(ix == 0)
            def _():
                for i in range(first, DEPTH):
                    for d in range(3):
                        new[d, i] = plane
                new[0, DEPTH] = plane

            @pl.when(ix == nx - 1)
            def _():
                for i in range(DEPTH + bx, end + 1):
                    for d in range(3):
                        new[d, i] = plane


def final_kernel(p_ref, sum_ref, out_ref, *, cells):
    mean = jnp.sum(sum_ref[...]) * (1.0 / cells)
    out_ref[...] = p_ref[...] - mean


def swap(a, axis, start):
    count = lax.axis_size(axis)
    return lax.ppermute(a, axis, [(i, j) for k in range(start, count - 1, 2) for i, j in ((k, k + 1), (k + 1, k))])


def sum_everywhere(total):
    axes = ("gx", "gy", "gz")
    devices = math.prod(lax.axis_size(a) for a in axes)
    if devices & (devices - 1):
        return lax.psum(total, axes)
    bits = [1 << n for n in range(devices.bit_length() - 1)]
    for stage in [bits[:1]] + [bits[n : n + 2] for n in range(1, len(bits), 2)]:
        masks = stage if len(stage) == 1 else [stage[0], stage[1], stage[0] + stage[1]]
        total = sum([lax.ppermute(total, axes, [(i, i ^ m) for i in range(devices)]) for m in masks], total)
    return total


def local(vel_x, vel_y, vel_z, pressure, phase, visc_scale, power_n, density):
    bx, bz, by = pressure.shape
    assert bx % (2 * GROUP) == 0 and bz == 2 * DEPTH and DEPTH == GROUP
    f32 = jnp.float32
    iy, ny = lax.axis_index("gy"), lax.axis_size("gy")
    cells = bx * bz * by * math.prod(lax.axis_size(a) for a in ("gx", "gz", "gy"))
    deep = bx + 2 * DEPTH + 1
    rows, lanes = 2 * bz, 2 * by
    shape = lambda *dims: jax.ShapeDtypeStruct(dims, f32)
    block = shape(bx, bz, by)
    scratch = lambda *dims: pltpu.VMEM(dims, f32)
    limit = lambda mebibytes: pltpu.CompilerParams(vmem_limit_bytes=mebibytes * 1024 * 1024)
    groups = bx // GROUP
    stacked = bx * FIELDS + bx // 2 + 2
    sent = shape(DEPTH * FIELDS + 1, bz, by)
    edge, x_0, x_1, stack = pl.pallas_call(
        pack_kernel,
        out_shape=(shape(bx // 2, bz, by), sent, sent, shape(stacked, bz, by)),
        in_specs=[HBM] * 5 + [SMEM] * 3,
        out_specs=(HBM,) * 4,
        scratch_shapes=[
            scratch(FIELDS - 1, bx, bz, by),
            pltpu.VMEM((bx, bz, by), jnp.int32),
            scratch(bx // 2, bz, by),
            scratch(stacked, bz, by),
            pltpu.SemaphoreType.DMA((groups, FIELDS)),
            pltpu.SemaphoreType.DMA((groups + groups // 2 + 3,)),
        ],
        compiler_params=limit(58),
    )(vel_x, vel_z, vel_y, pressure, phase, visc_scale, power_n, density)

    def edges_beside(edge):
        side = swap(edge, "gy", 0)
        if ny == 2:
            return side
        lane = iota(side.shape, 2) % (by // 2) % LANE_STEP
        return jnp.where((lane <= DEPTH) == (lax.rem(iy, 2) == 0), side, swap(edge, "gy", 1))

    estimate = lambda size: pl.CostEstimate(
        flops=4 * size * bz * by, bytes_accessed=size * bz * by * 4, transcendentals=0
    )

    def unpacking(kernel, tiles, out_shape, *args, aliases={}):
        return pl.pallas_call(
            kernel,
            out_shape=out_shape,
            in_specs=[VMEM] * len(args),
            out_specs=(VMEM,) * len(out_shape),
            input_output_aliases=aliases,
            compiler_params=limit(16),
            cost_estimate=estimate(13 * tiles),
        )(*args)

    field = shape(deep, bz, lanes)
    own_shape = (shape(3, deep, bz, lanes),) + (field,) * 4
    half = lambda tiles, planes: shape(tiles + planes // (bz // 2), bz // 2, by)
    x_0, x_1 = swap(x_0, "gx", 0), swap(x_1, "gx", 1)
    face = half(bx * FIELDS, bx)
    extra = (shape(bx // 2, bz, by), shape(2, bz, by))
    z_0, z_1, edge, tables, *own = unpacking(own_kernel, bx, (face, face) + extra + own_shape, stack)
    face_1, face_0 = swap(z_1, "gz", 1), swap(z_0, "gz", 0)

    tiles = bx // 2 + DEPTH
    edge = pl.pallas_call(
        side_edge_kernel,
        out_shape=shape(tiles, bz, by),
        in_specs=[VMEM] * 3,
        out_specs=VMEM,
        compiler_params=limit(4),
    )(x_0, x_1, edge)
    edge = edges_beside(edge)
    corner = half(2 * DEPTH * FIELDS + 1 + tiles, 2 * DEPTH + tiles)
    sides, z_0, z_1 = pl.pallas_call(
        sides_kernel,
        out_shape=(shape(2 * DEPTH * FIELDS + 1, bz, by), corner, corner),
        in_specs=[VMEM] * 3,
        out_specs=(VMEM,) * 3,
        compiler_params=limit(4),
    )(x_0, x_1, edge)
    corner_1, corner_0 = swap(z_1, "gz", 1), swap(z_0, "gz", 0)

    own = unpacking(
        own_sides_kernel, 2 * deep, own_shape, sides, edge, tables, *own, aliases={n + 3: n for n in range(5)}
    )
    halo = unpacking(halo_kernel, deep, (shape(7, deep, bz, lanes), field), face_0, face_1, tables)
    vx, vz, vy, p, eta, total, _, _ = pl.pallas_call(
        main_kernel,
        out_shape=(block,) * 5 + (shape(bz, by),) + tuple(shape(*a.shape) for a in halo),
        in_specs=[VMEM] * 10,
        out_specs=(VMEM,) * 8,
        input_output_aliases={5: 6, 6: 7},
        scratch_shapes=[
            scratch(3, deep, rows, lanes),
            scratch(3, deep, rows, lanes),
            scratch(deep, rows, lanes),
            scratch(4, rows, lanes),
        ],
        compiler_params=limit(32),
    )(*own, *halo, corner_0, corner_1, tables)

    total = sum_everywhere(total)
    p = pl.pallas_call(
        lambda *refs: final_kernel(*refs, cells=float(cells)),
        out_shape=block,
        in_specs=[VMEM] * 2,
        out_specs=VMEM,
        compiler_params=limit(4),
    )(p, total)
    return (vx, vy, vz, p, eta)


def solution(mesh):
    spec = P("gx", "gz", "gy")
    return jax.shard_map(
        local,
        mesh=mesh,
        in_specs=(spec,) * 5 + (P(),) * 3,
        out_specs=(spec,) * 5,
        check_vma=False,
    )
```

```python
import math

import jax
import jax.numpy as jnp
from jax import lax
from jax.experimental import pallas as pl
from jax.experimental.pallas import tpu as pltpu
from jax.sharding import PartitionSpec as P

ITERS = 4
PHASES = 4
FIELDS = 5
DEPTH = ITERS
LANE_STEP = 2 * DEPTH + 1
UNROLL = 4
GROUP = 4

VMEM = pl.BlockSpec(memory_space=pltpu.VMEM)
SMEM = pl.BlockSpec(memory_space=pltpu.SMEM)
HBM = pl.BlockSpec(memory_space=pltpu.HBM)


def z_up(a):
    return pltpu.roll(a, a.shape[-2] - 1, a.ndim - 2)


def z_down(a):
    return pltpu.roll(a, 1, a.ndim - 2)


def y_up(a):
    return pltpu.roll(a, a.shape[-1] - 1, a.ndim - 1)


def y_down(a):
    return pltpu.roll(a, 1, a.ndim - 1)


def reciprocal(a):
    r = pl.reciprocal(a, approx=True)
    return r * (2.0 - a * r)


def iota(shape, axis):
    return lax.broadcasted_iota(jnp.int32, shape, axis)


def odd(axis):
    return lax.rem(lax.axis_index(axis), 2) == 1


def by_parity(axis, pair, body):
    pl.when(jnp.logical_not(odd(axis)))(lambda: body(pair[0], pair[1]))
    pl.when(odd(axis))(lambda: body(pair[1], pair[0]))


def start_copies(sources, targets, sems):
    copies = []
    for g in range(sources[0].shape[0] // GROUP):
        at = pl.ds(g * GROUP, GROUP)
        copies.append(
            [pltpu.make_async_copy(a.at[at], b.at[at], sems.at[g, f]) for f, (a, b) in enumerate(zip(sources, targets))]
        )
        for copy in copies[-1]:
            copy.start()
    return copies


def clean_group(g, field_ref, phase_ref):
    bx, bz, by = phase_ref.shape
    ix, iz, iy = lax.axis_index("gx"), lax.axis_index("gz"), lax.axis_index("gy")
    plane, row, lane = (iota((GROUP, bz, by), d) for d in range(3))
    at = pl.ds(g * GROUP, GROUP)
    vx, vz, vy, p = (field_ref[f, at] for f in range(FIELDS - 1))
    if g == 0:
        vx = jnp.where((plane > 0) | (ix > 0), vx, 0.0)
    vz = jnp.where((row > 0) | (iz > 0), vz, 0.0)
    vy = jnp.where((lane > 0) | (iy > 0), vy, 0.0)
    return vx, vz, vy, p, phase_ref[at].astype(jnp.float32)


def add_edge(edge, a, base):
    by = edge.shape[-1]
    lane = iota((1,) * (edge.ndim - 1) + (by,), edge.ndim - 1)
    first = pltpu.roll(a, base, a.ndim - 1) if base else a
    edge = jnp.where((lane >= base) & (lane <= base + DEPTH), first, edge)
    last = pltpu.roll(a, (base + LANE_STEP) % by, a.ndim - 1)
    return jnp.where((lane > base + DEPTH) & (lane < base + LANE_STEP), last, edge)


def add_edges(edge, fields, upper):
    for f, a in enumerate(fields):
        edge = add_edge(edge, a, edge.shape[-1] // 2 * upper + LANE_STEP * f)
    return edge


def beside(edge, f, upper):
    by = edge.shape[-1]
    iy = lax.axis_index("gy")
    lane = iota((1,) * (edge.ndim - 1) + (by,), edge.ndim - 1)
    right = (lane <= DEPTH) & (iy < lax.axis_size("gy") - 1)
    left = (lane >= by - DEPTH) & (iy > 0)
    shift = by // 2 * upper + LANE_STEP * f
    a = pltpu.roll(edge, by - shift, edge.ndim - 1) if shift else edge
    b = pltpu.roll(edge, (by - LANE_STEP - shift) % by, edge.ndim - 1)
    return jnp.where(right, a, jnp.where(left, b, 0.0))


def pack_kernel(
    vx_hbm, vz_hbm, vy_hbm, p_hbm, phase_hbm, scale_ref, power_ref, rho_ref, edge_hbm, x_0_hbm, x_1_hbm, stack_hbm,
    field_ref, phase_ref, edge_ref, stack_ref, sems, out_sems,
):
    bx, bz, by = phase_ref.shape
    targets = [field_ref.at[f] for f in range(FIELDS - 1)] + [phase_ref]
    copies = start_copies((vx_hbm, vz_hbm, vy_hbm, p_hbm, phase_hbm), targets, sems)
    half = bx // GROUP // 2
    outs = []

    def out(source, target):
        outs.append(pltpu.make_async_copy(source, target, out_sems.at[len(outs)]))
        outs[-1].start()

    for g in range(half):
        edge = jnp.zeros((GROUP, bz, by), jnp.float32)
        for upper in range(2):
            at = (g + upper * half) * GROUP
            for copy in copies[g + upper * half]:
                copy.wait()
            fields = clean_group(g + upper * half, field_ref, phase_ref)
            for f, a in enumerate(fields):
                for i in range(GROUP):
                    stack_ref[(at + i) * FIELDS + f] = a[i]
            edge = add_edges(edge, fields, upper)
            at = pl.ds(at * FIELDS, GROUP * FIELDS)
            out(stack_ref.at[at], stack_hbm.at[at])
        at = pl.ds(g * GROUP, GROUP)
        edge_ref[at] = edge
        out(edge_ref.at[at], edge_hbm.at[at])
        stack_ref[pl.ds(bx * FIELDS + g * GROUP, GROUP)] = edge
    count = bx * FIELDS + bx // 2
    row = iota((bz, by), 0)
    entries = [ref[index] for ref in (scale_ref, power_ref, rho_ref) for index in range(PHASES)]
    for n in range(2):
        tile = jnp.zeros((bz, by), jnp.float32)
        for r, entry in enumerate(entries[n * bz : (n + 1) * bz]):
            tile = jnp.where(row == r, entry, tile)
        stack_ref[count + n] = tile
    at = pl.ds(bx * FIELDS, count + 2 - bx * FIELDS)
    out(stack_ref.at[at], stack_hbm.at[at])
    count = x_0_hbm.shape[0]
    down, up = stack_ref.at[pl.ds(0, count)], stack_ref.at[pl.ds(bx * FIELDS - count, count)]
    sem = out_sems.at[len(outs)], out_sems.at[len(outs) + 1]

    def send(to_above, to_below):
        pair = pltpu.make_async_copy(up, to_above, sem[0]), pltpu.make_async_copy(down, to_below, sem[1])
        for copy in pair:
            copy.start()
        for copy in pair:
            copy.wait()

    by_parity("gx", (x_0_hbm, x_1_hbm), send)
    for copy in outs:
        copy.wait()


def side_edge_kernel(x_0_ref, x_1_ref, own_edge_ref, edge_ref):
    bz, by = edge_ref.shape[1:]
    own = own_edge_ref.shape[0]
    edge_ref[0:own] = own_edge_ref[...]

    def body(above, below):
        edge = jnp.zeros((DEPTH, bz, by), jnp.float32)
        for upper, (ref, at) in enumerate(((above, 0), (below, 1))):
            block = ref[pl.ds(at, DEPTH * FIELDS)].reshape(DEPTH, FIELDS, bz, by)
            edge = add_edges(edge, [block[:, f] for f in range(FIELDS)], upper)
        edge_ref[own:] = edge
        edge_ref[own] = add_edge(edge[0], above[DEPTH * FIELDS], FIELDS * LANE_STEP)

    by_parity("gx", (x_0_ref, x_1_ref), body)


def half_rows(tiles, swap):
    down = odd("gz") if swap == 0 else jnp.logical_not(odd("gz"))
    half = tiles.shape[-2] // 2
    return jnp.where(down, tiles[..., :half, :], tiles[..., half:, :])


def store_next_rows(refs, at, tiles):
    half = tiles.shape[-2] // 2
    for ref in refs:
        for i in range(tiles.shape[0]):
            ref[at + i // half, i % half : i % half + 1, :] = tiles[i, half : half + 1, :]


def sides_kernel(x_0_ref, x_1_ref, edge_ref, sides_ref, z_0_ref, z_1_ref):
    count = DEPTH * FIELDS
    bz, by = sides_ref.shape[1:]

    def body(above, below):
        sides_ref[0:count] = above[0:count]
        sides_ref[count : 2 * count] = below[1 : count + 1]
        sides_ref[2 * count] = above[count]

    by_parity("gx", (x_0_ref, x_1_ref), body)
    tiles = sides_ref[...]
    vz = tiles[0 : 2 * count].reshape(2 * DEPTH, FIELDS, bz, by)[:, 1]
    at = 0
    for whole, after in ((tiles, vz), (edge_ref[...], edge_ref[...])):
        for swap, ref in enumerate((z_0_ref, z_1_ref)):
            ref[at : at + whole.shape[0]] = half_rows(whole, swap)
        at += whole.shape[0]
        store_next_rows((z_0_ref, z_1_ref), at, after)
        at += after.shape[0] // (bz // 2)


def lookups(fields, ok, keep, table_ref):
    *rest, phase = fields
    for number in range(3):
        rows = [divmod(number * PHASES + index, table_ref.shape[1]) for index in range(PHASES)]
        table = [table_ref[n, r : r + 1, :] for n, r in rows]
        value = jnp.broadcast_to(table[0], phase.shape)
        for index in range(1, PHASES):
            value = jnp.where(phase == float(index), table[index], value)
        if number == 0:
            value = value * jnp.where(ok, 1.0, 0.0)
            if keep is not None:
                value = jnp.where(keep, value, 0.0)
        elif number == 1:
            value = (0.5 / math.log(2.0)) * (reciprocal(value) - 1.0)
        rest.append(value)
    return rest


def own_lanes(block, ok, tables):
    block = block.reshape(-1, FIELDS, *block.shape[-2:])
    return lookups([block[:, f] for f in range(FIELDS)], ok, None, tables)


def edge_lanes(edge, upper, ok, tables):
    by = edge.shape[-1]
    iy = lax.axis_index("gy")
    lane = iota((1, 1, by), 2)
    keep = ((lane <= DEPTH) & (iy < lax.axis_size("gy") - 1)) | ((lane >= by - DEPTH) & (iy > 0))
    return lookups([beside(edge, f, upper) for f in range(FIELDS)], ok, keep, tables)


def store_to(refs):
    def store(planes, part, values):
        by = values[0].shape[-1]
        for ref, value in zip(refs, values):
            ref[planes, :, part * by : (part + 1) * by] = value

    return store


def unpack_own(load, bx, ok, tables, store):
    def group(g, carry):
        at = g * GROUP
        store(pl.ds(DEPTH + at, GROUP), 0, own_lanes(load(at * FIELDS, GROUP * FIELDS), ok, tables))
        return carry

    lax.fori_loop(0, bx // GROUP, group, 0)


def unpack_own_edges(load, bx, ok, tables, store):
    half = bx // 2
    for upper in range(2):

        def group(g, carry):
            at = g * GROUP
            values = edge_lanes(load(at, GROUP), upper, ok, tables)
            store(pl.ds(DEPTH + upper * half + at, GROUP), 1, values)
            return carry

        lax.fori_loop(0, half // GROUP, group, 0)


def side_places(bx):
    ix = lax.axis_index("gx")
    return (pl.ds(DEPTH + bx, DEPTH), ix < lax.axis_size("gx") - 1), (pl.ds(0, DEPTH), ix > 0)


def unpack_sides(load, bx, ok, tables, store, vx_ref):
    count = DEPTH * FIELDS
    for n, (planes, inside) in enumerate(side_places(bx)):
        store(planes, 0, own_lanes(load(n * count, count), ok & inside, tables))
    vx = load(2 * count, 1)
    vx_ref[pl.ds(bx + 2 * DEPTH, 1), :, 0 : vx.shape[-1]] = vx


def unpack_side_edges(load, bx, ok, tables, store, vx_ref):
    half = bx // 2
    edge = load(half, DEPTH)
    for upper, (planes, inside) in enumerate(side_places(bx)):
        store(planes, 1, edge_lanes(edge, upper, ok & inside, tables))
    by = edge.shape[-1]
    vx_ref[pl.ds(bx + 2 * DEPTH, 1), :, by : 2 * by] = beside(edge[0:1], FIELDS, 0)


def own_kernel(stack_ref, z_0_ref, z_1_ref, edge_ref, tables_ref, v_ref, *rest):
    bx = v_ref.shape[1] - 2 * DEPTH - 1
    count = bx * FIELDS
    edge_ref[...] = stack_ref[count : count + bx // 2]
    tables_ref[...] = stack_ref[count + bx // 2 :]
    size = GROUP * FIELDS

    def group(g, carry):
        at = pl.ds(g * size, size)
        tiles = stack_ref[at]
        for swap, ref in enumerate((z_0_ref, z_1_ref)):
            ref[at] = half_rows(tiles, swap)
        return carry

    lax.fori_loop(0, bx // GROUP, group, 0)
    for g in range(bx // GROUP):
        vz = stack_ref[pl.ds(g * size, size)].reshape(GROUP, FIELDS, *stack_ref.shape[1:])[:, 1]
        store_next_rows((z_0_ref, z_1_ref), count + g * GROUP // (stack_ref.shape[1] // 2), vz)
    store = store_to([v_ref.at[d] for d in range(3)] + list(rest))
    unpack_own(lambda at, n: stack_ref[pl.ds(at, n)], bx, True, tables_ref, store)


def own_sides_kernel(sides_ref, edge_ref, tables_ref, *refs):
    v_ref, *rest = refs[len(refs) // 2 :]
    bx = v_ref.shape[1] - 2 * DEPTH - 1
    store = store_to([v_ref.at[d] for d in range(3)] + list(rest))
    unpack_sides(lambda at, n: sides_ref[pl.ds(at, n)], bx, True, tables_ref, store, v_ref.at[0])
    load = lambda at, n: edge_ref[pl.ds(at, n)]
    unpack_own_edges(load, bx, True, tables_ref, store)
    unpack_side_edges(load, bx, True, tables_ref, store, v_ref.at[0])


def rows_in_grid(bz):
    iz = lax.axis_index("gz")
    row = iota((1, bz, 1), 1)
    return ((row < bz // 2) & (iz < lax.axis_size("gz") - 1)) | ((row >= bz // 2) & (iz > 0))


def load_both(above, below):
    return lambda at, n: jnp.concatenate([above[pl.ds(at, n)], below[pl.ds(at, n)]], axis=1)


def halo_kernel(face_0_ref, face_1_ref, tables_ref, halo_ref, next_ref):
    half, by = face_0_ref.shape[1:]
    bx = halo_ref.shape[1] - 2 * DEPTH - 1
    store = store_to([halo_ref.at[n] for n in range(7)])

    def body(above, below):
        unpack_own(load_both(above, below), bx, rows_in_grid(2 * half), tables_ref, store)
        for i in range(bx):
            n = i % half
            next_ref[DEPTH + i, half - 1 : half, 0:by] = above[bx * FIELDS + i // half, n : n + 1, :]

    by_parity("gz", (face_0_ref, face_1_ref), body)


def unpack_corners(corner_0_ref, corner_1_ref, tables_ref, halo_ref, next_ref):
    half, by = corner_0_ref.shape[1:]
    bx = halo_ref.shape[1] - 2 * DEPTH - 1
    ok = rows_in_grid(2 * half)
    store = store_to([halo_ref.at[n] for n in range(7)])
    fields = 2 * DEPTH * FIELDS + 1
    edges = fields + 2 * DEPTH // half
    tiles = bx // 2 + DEPTH

    def body(above, below):
        unpack_sides(load_both(above, below), bx, ok, tables_ref, store, halo_ref.at[0])
        for i in range(2 * DEPTH):
            n = i % half
            to = DEPTH + bx + i if i < DEPTH else i - DEPTH
            next_ref[to, half - 1 : half, 0:by] = above[fields + i // half, n : n + 1, :]
        load = load_both(above.at[pl.ds(edges, tiles)], below.at[pl.ds(edges, tiles)])
        unpack_own_edges(load, bx, ok, tables_ref, store)
        unpack_side_edges(load, bx, ok, tables_ref, store, halo_ref.at[0])
        for n in range(tiles // half):
            rows = above[edges + tiles + n]
            for upper in range(2):
                values = beside(rows, 1, upper)
                for i in range(half):
                    tile = n * half + i
                    if tile < bx // 2:
                        to = DEPTH + upper * (bx // 2) + tile
                    else:
                        to = tile - bx // 2 + (0 if upper else DEPTH + bx)
                    next_ref[to, half - 1 : half, by : 2 * by] = values[i : i + 1]

    by_parity("gz", (corner_0_ref, corner_1_ref), body)


def main_kernel(
    v_ref, p0_ref, pre_ref, power_field_ref, rho_ref, _halo, _next, corner_0_ref, corner_1_ref, tables_ref,
    out_vx_ref, out_vz_ref, out_vy_ref, out_p_ref, out_eta_ref, sum_ref, halo_ref, next_ref,
    va_ref, vb_ref, p_ref, weight_ref,
):
    bx, bz, by = out_p_ref.shape
    rows, lanes = 2 * bz, 2 * by
    nx, nz, ny = lax.axis_size("gx"), lax.axis_size("gz"), lax.axis_size("gy")
    ix, iz, iy = lax.axis_index("gx"), lax.axis_index("gz"), lax.axis_index("gy")
    unpack_corners(corner_0_ref, corner_1_ref, tables_ref, halo_ref, next_ref)

    shape = (rows, lanes)
    r, c = iota(shape, 0), iota(shape, 1)
    zg = iz * bz + jnp.where(r < bz + bz // 2, r, r - rows)
    yg = iy * by + jnp.where(c <= by + DEPTH, c, c - lanes)
    filled = (c <= by + DEPTH) | (c >= lanes - DEPTH)
    inside = filled & (zg >= 0) & (zg < nz * bz) & (yg >= 0) & (yg < ny * by)
    weight_ref[0] = jnp.where(inside, 0.05, 0.0)
    weight_ref[1] = jnp.where(inside & (zg > 0), 0.05, 0.0)
    weight_ref[2] = jnp.where(inside & (yg > 0), 0.05, 0.0)
    weight_ref[3] = jnp.where(inside, 0.0, 1.0)

    def with_halo(own, n, planes):
        return jnp.concatenate([own[planes], halo_ref[n, planes]], axis=1)

    for k in range(1, ITERS + 1):
        old, new = (va_ref, vb_ref) if k % 2 else (vb_ref, va_ref)
        last = k == ITERS

        def load(d, j, count):
            planes = pl.ds(j, count)
            return with_halo(v_ref.at[d], d, planes) if k == 1 else old[d, planes]

        def cells(j, count):
            planes = pl.ds(j, count)
            vx1 = load(0, j, count + 1)
            vx = vx1[:count]
            vz, vy = load(1, j, count), load(2, j, count)
            p = with_halo(p0_ref, 3, planes) if k == 1 else p_ref[planes]
            up = z_up(vz)
            if k == 1:
                after = next_ref[planes]
                after = jnp.concatenate([after, after], axis=1)
                up = jnp.where(iota((1, rows, lanes), 1) == bz + bz // 2 - 1, after, up)
            rx = vx1[1:] - vx
            rz = up - vz
            ry = y_up(vy) - vy
            a = rx - ry
            b = ry - rz
            inv = (a * (a + b) + b * b) * (1.0 / 3.0) + 1.0
            eta = with_halo(pre_ref, 4, planes) * jnp.exp2(with_halo(power_field_ref, 5, planes) * jnp.log(inv))
            quarter = 0.25 * eta
            div = rx + ry + rz
            p = p - quarter * (div + div)
            tx, tz, ty = eta * rx - p, eta * rz - p, eta * ry - p
            sz = quarter + z_down(quarter)
            sy = quarter + y_down(quarter)
            return vx, vz, vy, eta, p, quarter, tx, tz, ty, sz, sy

        def chunk(j, count, carry, start=False):
            planes = pl.ds(j, count)
            vx, vz, vy, eta, p, quarter, tx, tz, ty, sz, sy = cells(j, count)
            vz0, vy0 = load(1, j - 1, 1), load(2, j - 1, 1)
            quarter0, tx0, sz0, sy0, part_z0, part_y0, scale_z0, scale_y0 = carry
            join = lambda first, rest: jnp.concatenate([first, rest[:-1]], axis=0) if count > 1 else first
            bias = weight_ref[3:4]
            sx = quarter + join(quarter0, quarter)
            exz = sz + join(sz0, sz)
            exy = sy + join(sy0, sy)
            ezy = sz + y_down(sz)
            fxz = exz * (vx - z_down(vx))
            fxy = exy * (vx - y_down(vx))
            low_vz, low_vy = join(vz0, vz), join(vy0, vy)
            gzx = exz * (vz - low_vz)
            hyx = exy * (vy - low_vy)
            gzy = ezy * (vz - y_down(vz))
            hyz = ezy * (vy - z_down(vy))
            res_x = (tx - join(tx0, tx)) + ((z_up(fxz) - fxz) + (y_up(fxy) - fxy))
            new_vx = vx + weight_ref[0:1] * reciprocal(sx + bias) * res_x
            part_z = (tz - z_down(tz)) - with_halo(rho_ref, 6, planes) + ((y_up(gzy) - gzy) - gzx)
            part_y = (ty - y_down(ty)) + ((z_up(hyz) - hyz) - hyx)
            scale_z = weight_ref[1:2] * reciprocal(sz + bias)
            scale_y = weight_ref[2:3] * reciprocal(sy + bias)
            new_vz = low_vz + join(scale_z0, scale_z) * (join(part_z0, part_z) + gzx)
            new_vy = low_vy + join(scale_y0, scale_y) * (join(part_y0, part_y) + hyx)
            if last:
                at = pl.ds(j - DEPTH, count)
                out_vx_ref[at] = new_vx[:, 0:bz, 0:by]
                out_p_ref[at] = p[:, 0:bz, 0:by]
                out_eta_ref[at] = eta[:, 0:bz, 0:by]
                sum_ref[...] += jnp.sum(p[:, 0:bz, 0:by], axis=0)
                if not start:
                    at = pl.ds(j - 1 - DEPTH, count)
                    out_vz_ref[at] = new_vz[:, 0:bz, 0:by]
                    out_vy_ref[at] = new_vy[:, 0:bz, 0:by]
            else:
                p_ref[planes] = p
                new[0, planes] = new_vx
                if not start:
                    new[1, pl.ds(j - 1, count)] = new_vz
                    new[2, pl.ds(j - 1, count)] = new_vy
            return tuple(a[-1:] for a in (quarter, tx, sz, sy, part_z, part_y, scale_z, scale_y))

        first, end = k, bx + 2 * DEPTH - k
        if last:
            sum_ref[...] = jnp.zeros((bz, by), jnp.float32)
        _, _, _, _, p, quarter, tx, _, _, sz, sy = cells(first - 1, 1)
        if not last:
            p_ref[pl.ds(first - 1, 1)] = p
        zero = jnp.zeros((1, rows, lanes), jnp.float32)
        carry = chunk(first, 1, (quarter, tx, sz, sy, zero, zero, zero, zero), start=True)
        steps, rest = divmod((end - 1 if last else end) - first, UNROLL)
        carry = lax.fori_loop(
            0, steps, lambda s, carry: chunk(first + 1 + s * UNROLL, UNROLL, carry), carry
        )
        if rest:
            carry = chunk(first + 1 + steps * UNROLL, rest, carry)
        if last:
            quarter0, tx0, sz0, sy0, part_z0, part_y0, scale_z0, scale_y0 = carry
            _, vz, vy, _, _, _, _, _, _, sz, sy = cells(end, 1)
            vz0, vy0 = load(1, end - 1, 1), load(2, end - 1, 1)
            new_vz = vz0 + scale_z0 * (part_z0 + (sz + sz0) * (vz - vz0))
            new_vy = vy0 + scale_y0 * (part_y0 + (sy + sy0) * (vy - vy0))
            out_vz_ref[pl.ds(end - 1 - DEPTH, 1)] = new_vz[:, 0:bz, 0:by]
            out_vy_ref[pl.ds(end - 1 - DEPTH, 1)] = new_vy[:, 0:bz, 0:by]

            @pl.when(ix == 0)
            def _():
                out_vx_ref[0] = jnp.zeros((bz, by), jnp.float32)
        else:
            plane = jnp.zeros((rows, lanes), jnp.float32)

            @pl.when(ix == 0)
            def _():
                for i in range(first, DEPTH):
                    for d in range(3):
                        new[d, i] = plane
                new[0, DEPTH] = plane

            @pl.when(ix == nx - 1)
            def _():
                for i in range(DEPTH + bx, end + 1):
                    for d in range(3):
                        new[d, i] = plane


def final_kernel(p_ref, sum_ref, out_ref, *, cells):
    mean = jnp.sum(sum_ref[...]) * (1.0 / cells)
    out_ref[...] = p_ref[...] - mean


def swap(a, axis, start):
    count = lax.axis_size(axis)
    return lax.ppermute(a, axis, [(i, j) for k in range(start, count - 1, 2) for i, j in ((k, k + 1), (k + 1, k))])


def local(vel_x, vel_y, vel_z, pressure, phase, visc_scale, power_n, density):
    bx, bz, by = pressure.shape
    assert bx % (2 * GROUP) == 0 and bz == 2 * DEPTH and DEPTH == GROUP
    f32 = jnp.float32
    iy, ny = lax.axis_index("gy"), lax.axis_size("gy")
    cells = bx * bz * by * math.prod(lax.axis_size(a) for a in ("gx", "gz", "gy"))
    deep = bx + 2 * DEPTH + 1
    rows, lanes = 2 * bz, 2 * by
    shape = lambda *dims: jax.ShapeDtypeStruct(dims, f32)
    block = shape(bx, bz, by)
    scratch = lambda *dims: pltpu.VMEM(dims, f32)
    limit = lambda mebibytes: pltpu.CompilerParams(vmem_limit_bytes=mebibytes * 1024 * 1024)
    groups = bx // GROUP
    stacked = bx * FIELDS + bx // 2 + 2
    sent = shape(DEPTH * FIELDS + 1, bz, by)
    edge, x_0, x_1, stack = pl.pallas_call(
        pack_kernel,
        out_shape=(shape(bx // 2, bz, by), sent, sent, shape(stacked, bz, by)),
        in_specs=[HBM] * 5 + [SMEM] * 3,
        out_specs=(HBM,) * 4,
        scratch_shapes=[
            scratch(FIELDS - 1, bx, bz, by),
            pltpu.VMEM((bx, bz, by), jnp.int32),
            scratch(bx // 2, bz, by),
            scratch(stacked, bz, by),
            pltpu.SemaphoreType.DMA((groups, FIELDS)),
            pltpu.SemaphoreType.DMA((groups + groups // 2 + 3,)),
        ],
        compiler_params=limit(58),
    )(vel_x, vel_z, vel_y, pressure, phase, visc_scale, power_n, density)

    def edges_beside(edge):
        side = swap(edge, "gy", 0)
        if ny == 2:
            return side
        lane = iota(side.shape, 2) % (by // 2) % LANE_STEP
        return jnp.where((lane <= DEPTH) == (lax.rem(iy, 2) == 0), side, swap(edge, "gy", 1))

    estimate = lambda size: pl.CostEstimate(
        flops=4 * size * bz * by, bytes_accessed=size * bz * by * 4, transcendentals=0
    )

    def unpacking(kernel, tiles, out_shape, *args, aliases={}):
        return pl.pallas_call(
            kernel,
            out_shape=out_shape,
            in_specs=[VMEM] * len(args),
            out_specs=(VMEM,) * len(out_shape),
            input_output_aliases=aliases,
            compiler_params=limit(16),
            cost_estimate=estimate(13 * tiles),
        )(*args)

    field = shape(deep, bz, lanes)
    own_shape = (shape(3, deep, bz, lanes),) + (field,) * 4
    half = lambda tiles, planes: shape(tiles + planes // (bz // 2), bz // 2, by)
    x_0, x_1 = swap(x_0, "gx", 0), swap(x_1, "gx", 1)
    face = half(bx * FIELDS, bx)
    extra = (shape(bx // 2, bz, by), shape(2, bz, by))
    z_0, z_1, edge, tables, *own = unpacking(own_kernel, bx, (face, face) + extra + own_shape, stack)
    face_1, face_0 = swap(z_1, "gz", 1), swap(z_0, "gz", 0)

    tiles = bx // 2 + DEPTH
    edge = pl.pallas_call(
        side_edge_kernel,
        out_shape=shape(tiles, bz, by),
        in_specs=[VMEM] * 3,
        out_specs=VMEM,
        compiler_params=limit(4),
    )(x_0, x_1, edge)
    edge = edges_beside(edge)
    corner = half(2 * DEPTH * FIELDS + 1 + tiles, 2 * DEPTH + tiles)
    sides, z_0, z_1 = pl.pallas_call(
        sides_kernel,
        out_shape=(shape(2 * DEPTH * FIELDS + 1, bz, by), corner, corner),
        in_specs=[VMEM] * 3,
        out_specs=(VMEM,) * 3,
        compiler_params=limit(4),
    )(x_0, x_1, edge)
    corner_1, corner_0 = swap(z_1, "gz", 1), swap(z_0, "gz", 0)

    own = unpacking(
        own_sides_kernel, 2 * deep, own_shape, sides, edge, tables, *own, aliases={n + 3: n for n in range(5)}
    )
    halo = unpacking(halo_kernel, deep, (shape(7, deep, bz, lanes), field), face_0, face_1, tables)
    vx, vz, vy, p, eta, total, _, _ = pl.pallas_call(
        main_kernel,
        out_shape=(block,) * 5 + (shape(bz, by),) + tuple(shape(*a.shape) for a in halo),
        in_specs=[VMEM] * 10,
        out_specs=(VMEM,) * 8,
        input_output_aliases={5: 6, 6: 7},
        scratch_shapes=[
            scratch(3, deep, rows, lanes),
            scratch(3, deep, rows, lanes),
            scratch(deep, rows, lanes),
            scratch(4, rows, lanes),
        ],
        compiler_params=limit(32),
    )(*own, *halo, corner_0, corner_1, tables)

    total = lax.all_gather(jnp.sum(total, axis=0, keepdims=True), ("gx", "gy", "gz"), axis=0, tiled=True)
    p = pl.pallas_call(
        lambda *refs: final_kernel(*refs, cells=float(cells)),
        out_shape=block,
        in_specs=[VMEM] * 2,
        out_specs=VMEM,
        compiler_params=limit(4),
    )(p, total)
    return (vx, vy, vz, p, eta)


def solution(mesh):
    spec = P("gx", "gz", "gy")
    return jax.shard_map(
        local,
        mesh=mesh,
        in_specs=(spec,) * 5 + (P(),) * 3,
        out_specs=(spec,) * 5,
        check_vma=False,
    )
```

```python
import math

import jax
import jax.numpy as jnp
from jax import lax
from jax.experimental import pallas as pl
from jax.experimental.pallas import tpu as pltpu
from jax.sharding import PartitionSpec as P

ITERS = 4
PHASES = 4
FIELDS = 5
DEPTH = ITERS
LANE_STEP = 2 * DEPTH + 1
UNROLL = 4
GROUP = 4

VMEM = pl.BlockSpec(memory_space=pltpu.VMEM)
HBM = pl.BlockSpec(memory_space=pltpu.HBM)


def z_up(a):
    return pltpu.roll(a, a.shape[-2] - 1, a.ndim - 2)


def z_down(a):
    return pltpu.roll(a, 1, a.ndim - 2)


def y_up(a):
    return pltpu.roll(a, a.shape[-1] - 1, a.ndim - 1)


def y_down(a):
    return pltpu.roll(a, 1, a.ndim - 1)


def reciprocal(a):
    r = pl.reciprocal(a, approx=True)
    return r * (2.0 - a * r)


def iota(shape, axis):
    return lax.broadcasted_iota(jnp.int32, shape, axis)


def odd(axis):
    return lax.rem(lax.axis_index(axis), 2) == 1


def by_parity(axis, pair, body):
    pl.when(jnp.logical_not(odd(axis)))(lambda: body(pair[0], pair[1]))
    pl.when(odd(axis))(lambda: body(pair[1], pair[0]))


def start_copies(sources, targets, sems):
    copies = []
    for g in range(sources[0].shape[0] // GROUP):
        at = pl.ds(g * GROUP, GROUP)
        copies.append(
            [pltpu.make_async_copy(a.at[at], b.at[at], sems.at[g, f]) for f, (a, b) in enumerate(zip(sources, targets))]
        )
        for copy in copies[-1]:
            copy.start()
    return copies


def clean_group(g, field_ref, phase_ref):
    bx, bz, by = phase_ref.shape
    ix, iz, iy = lax.axis_index("gx"), lax.axis_index("gz"), lax.axis_index("gy")
    plane, row, lane = (iota((GROUP, bz, by), d) for d in range(3))
    at = pl.ds(g * GROUP, GROUP)
    vx, vz, vy, p = (field_ref[f, at] for f in range(FIELDS - 1))
    if g == 0:
        vx = jnp.where((plane > 0) | (ix > 0), vx, 0.0)
    vz = jnp.where((row > 0) | (iz > 0), vz, 0.0)
    vy = jnp.where((lane > 0) | (iy > 0), vy, 0.0)
    return vx, vz, vy, p, phase_ref[at].astype(jnp.float32)


def add_edge(edge, a, base):
    by = edge.shape[-1]
    lane = iota((1,) * (edge.ndim - 1) + (by,), edge.ndim - 1)
    first = pltpu.roll(a, base, a.ndim - 1) if base else a
    edge = jnp.where((lane >= base) & (lane <= base + DEPTH), first, edge)
    last = pltpu.roll(a, (base + LANE_STEP) % by, a.ndim - 1)
    return jnp.where((lane > base + DEPTH) & (lane < base + LANE_STEP), last, edge)


def add_edges(edge, fields, upper):
    for f, a in enumerate(fields):
        edge = add_edge(edge, a, edge.shape[-1] // 2 * upper + LANE_STEP * f)
    return edge


def beside(edge, f, upper):
    by = edge.shape[-1]
    iy = lax.axis_index("gy")
    lane = iota((1,) * (edge.ndim - 1) + (by,), edge.ndim - 1)
    right = (lane <= DEPTH) & (iy < lax.axis_size("gy") - 1)
    left = (lane >= by - DEPTH) & (iy > 0)
    shift = by // 2 * upper + LANE_STEP * f
    a = pltpu.roll(edge, by - shift, edge.ndim - 1) if shift else edge
    b = pltpu.roll(edge, (by - LANE_STEP - shift) % by, edge.ndim - 1)
    return jnp.where(right, a, jnp.where(left, b, 0.0))


def pack_kernel(
    vx_hbm, vz_hbm, vy_hbm, p_hbm, phase_hbm, scale_hbm, power_hbm, rho_hbm, edge_hbm, x_0_hbm, x_1_hbm, stack_hbm,
    field_ref, phase_ref, edge_ref, stack_ref, scale_ref, power_ref, rho_ref, sems, out_sems, table_sems,
):
    bx, bz, by = phase_ref.shape
    targets = [field_ref.at[f] for f in range(FIELDS - 1)] + [phase_ref]
    copies = start_copies((vx_hbm, vz_hbm, vy_hbm, p_hbm, phase_hbm), targets, sems)
    table_refs = (scale_ref, power_ref, rho_ref)
    pairs = zip((scale_hbm, power_hbm, rho_hbm), table_refs)
    table_copies = [pltpu.make_async_copy(a, b, table_sems.at[n]) for n, (a, b) in enumerate(pairs)]
    for copy in table_copies:
        copy.start()
    half = bx // GROUP // 2
    outs = []

    def out(source, target):
        outs.append(pltpu.make_async_copy(source, target, out_sems.at[len(outs)]))
        outs[-1].start()

    for g in range(half):
        edge = jnp.zeros((GROUP, bz, by), jnp.float32)
        for upper in range(2):
            at = (g + upper * half) * GROUP
            for copy in copies[g + upper * half]:
                copy.wait()
            fields = clean_group(g + upper * half, field_ref, phase_ref)
            for f, a in enumerate(fields):
                for i in range(GROUP):
                    stack_ref[(at + i) * FIELDS + f] = a[i]
            edge = add_edges(edge, fields, upper)
            at = pl.ds(at * FIELDS, GROUP * FIELDS)
            out(stack_ref.at[at], stack_hbm.at[at])
        at = pl.ds(g * GROUP, GROUP)
        edge_ref[at] = edge
        out(edge_ref.at[at], edge_hbm.at[at])
        stack_ref[pl.ds(bx * FIELDS + g * GROUP, GROUP)] = edge
    count = bx * FIELDS + bx // 2
    row = iota((bz, by), 0)
    for copy in table_copies:
        copy.wait()
    entries = [ref[index] for ref in table_refs for index in range(PHASES)]
    for n in range(2):
        tile = jnp.zeros((bz, by), jnp.float32)
        for r, entry in enumerate(entries[n * bz : (n + 1) * bz]):
            tile = jnp.where(row == r, entry, tile)
        stack_ref[count + n] = tile
    at = pl.ds(bx * FIELDS, count + 2 - bx * FIELDS)
    out(stack_ref.at[at], stack_hbm.at[at])
    count = x_0_hbm.shape[0]
    down, up = stack_ref.at[pl.ds(0, count)], stack_ref.at[pl.ds(bx * FIELDS - count, count)]
    sem = out_sems.at[len(outs)], out_sems.at[len(outs) + 1]

    def send(to_above, to_below):
        pair = pltpu.make_async_copy(up, to_above, sem[0]), pltpu.make_async_copy(down, to_below, sem[1])
        for copy in pair:
            copy.start()
        for copy in pair:
            copy.wait()

    by_parity("gx", (x_0_hbm, x_1_hbm), send)
    for copy in outs:
        copy.wait()


def side_edge_kernel(x_0_ref, x_1_ref, own_edge_ref, edge_ref):
    bz, by = edge_ref.shape[1:]
    own = own_edge_ref.shape[0]
    edge_ref[0:own] = own_edge_ref[...]

    def body(above, below):
        edge = jnp.zeros((DEPTH, bz, by), jnp.float32)
        for upper, (ref, at) in enumerate(((above, 0), (below, 1))):
            block = ref[pl.ds(at, DEPTH * FIELDS)].reshape(DEPTH, FIELDS, bz, by)
            edge = add_edges(edge, [block[:, f] for f in range(FIELDS)], upper)
        edge_ref[own:] = edge
        edge_ref[own] = add_edge(edge[0], above[DEPTH * FIELDS], FIELDS * LANE_STEP)

    by_parity("gx", (x_0_ref, x_1_ref), body)


def half_rows(tiles, swap):
    down = odd("gz") if swap == 0 else jnp.logical_not(odd("gz"))
    half = tiles.shape[-2] // 2
    return jnp.where(down, tiles[..., :half, :], tiles[..., half:, :])


def store_next_rows(refs, at, tiles):
    half = tiles.shape[-2] // 2
    for ref in refs:
        for i in range(tiles.shape[0]):
            ref[at + i // half, i % half : i % half + 1, :] = tiles[i, half : half + 1, :]


def sides_kernel(x_0_ref, x_1_ref, _edge_ref, sides_ref, z_0_ref, z_1_ref):
    count = DEPTH * FIELDS
    bz, by = sides_ref.shape[1:]

    def body(above, below):
        sides_ref[0:count] = above[0:count]
        sides_ref[count : 2 * count] = below[1 : count + 1]
        sides_ref[2 * count] = above[count]

    by_parity("gx", (x_0_ref, x_1_ref), body)
    tiles = sides_ref[...]
    for swap, ref in enumerate((z_0_ref, z_1_ref)):
        ref[0 : 2 * count + 1] = half_rows(tiles, swap)
    vz = tiles[0 : 2 * count].reshape(2 * DEPTH, FIELDS, bz, by)[:, 1]
    store_next_rows((z_0_ref, z_1_ref), 2 * count + 1, vz)


def edge_rows_kernel(edge_ref, z_0_ref, z_1_ref):
    tiles = edge_ref[...]
    for swap, ref in enumerate((z_0_ref, z_1_ref)):
        ref[0 : tiles.shape[0]] = half_rows(tiles, swap)
    store_next_rows((z_0_ref, z_1_ref), tiles.shape[0], tiles)


def lookups(fields, ok, keep, table_ref):
    *rest, phase = fields
    for number in range(3):
        rows = [divmod(number * PHASES + index, table_ref.shape[1]) for index in range(PHASES)]
        table = [table_ref[n, r : r + 1, :] for n, r in rows]
        value = jnp.broadcast_to(table[0], phase.shape)
        for index in range(1, PHASES):
            value = jnp.where(phase == float(index), table[index], value)
        if number == 0:
            value = value * jnp.where(ok, 1.0, 0.0)
            if keep is not None:
                value = jnp.where(keep, value, 0.0)
        elif number == 1:
            value = (0.5 / math.log(2.0)) * (reciprocal(value) - 1.0)
        rest.append(value)
    return rest


def own_lanes(block, ok, tables):
    block = block.reshape(-1, FIELDS, *block.shape[-2:])
    return lookups([block[:, f] for f in range(FIELDS)], ok, None, tables)


def edge_lanes(edge, upper, ok, tables):
    by = edge.shape[-1]
    iy = lax.axis_index("gy")
    lane = iota((1, 1, by), 2)
    keep = ((lane <= DEPTH) & (iy < lax.axis_size("gy") - 1)) | ((lane >= by - DEPTH) & (iy > 0))
    return lookups([beside(edge, f, upper) for f in range(FIELDS)], ok, keep, tables)


def store_to(refs):
    def store(planes, part, values):
        by = values[0].shape[-1]
        for ref, value in zip(refs, values):
            ref[planes, :, part * by : (part + 1) * by] = value

    return store


def unpack_own(load, bx, ok, tables, store):
    def group(g, carry):
        at = g * GROUP
        store(pl.ds(DEPTH + at, GROUP), 0, own_lanes(load(at * FIELDS, GROUP * FIELDS), ok, tables))
        return carry

    lax.fori_loop(0, bx // GROUP, group, 0)


def unpack_own_edges(load, bx, ok, tables, store):
    half = bx // 2
    for upper in range(2):

        def group(g, carry):
            at = g * GROUP
            values = edge_lanes(load(at, GROUP), upper, ok, tables)
            store(pl.ds(DEPTH + upper * half + at, GROUP), 1, values)
            return carry

        lax.fori_loop(0, half // GROUP, group, 0)


def side_places(bx):
    ix = lax.axis_index("gx")
    return (pl.ds(DEPTH + bx, DEPTH), ix < lax.axis_size("gx") - 1), (pl.ds(0, DEPTH), ix > 0)


def unpack_sides(load, bx, ok, tables, store, vx_ref):
    count = DEPTH * FIELDS
    for n, (planes, inside) in enumerate(side_places(bx)):
        store(planes, 0, own_lanes(load(n * count, count), ok & inside, tables))
    vx = load(2 * count, 1)
    vx_ref[pl.ds(bx + 2 * DEPTH, 1), :, 0 : vx.shape[-1]] = vx


def unpack_side_edges(load, bx, ok, tables, store, vx_ref):
    half = bx // 2
    edge = load(half, DEPTH)
    for upper, (planes, inside) in enumerate(side_places(bx)):
        store(planes, 1, edge_lanes(edge, upper, ok & inside, tables))
    by = edge.shape[-1]
    vx_ref[pl.ds(bx + 2 * DEPTH, 1), :, by : 2 * by] = beside(edge[0:1], FIELDS, 0)


def own_kernel(stack_ref, z_0_ref, z_1_ref, edge_ref, tables_ref, v_ref, *rest):
    bx = v_ref.shape[1] - 2 * DEPTH - 1
    count = bx * FIELDS
    edge_ref[...] = stack_ref[count : count + bx // 2]
    tables_ref[...] = stack_ref[count + bx // 2 :]
    size = GROUP * FIELDS

    def group(g, carry):
        at = pl.ds(g * size, size)
        tiles = stack_ref[at]
        for swap, ref in enumerate((z_0_ref, z_1_ref)):
            ref[at] = half_rows(tiles, swap)
        return carry

    lax.fori_loop(0, bx // GROUP, group, 0)
    for g in range(bx // GROUP):
        vz = stack_ref[pl.ds(g * size, size)].reshape(GROUP, FIELDS, *stack_ref.shape[1:])[:, 1]
        store_next_rows((z_0_ref, z_1_ref), count + g * GROUP // (stack_ref.shape[1] // 2), vz)
    store = store_to([v_ref.at[d] for d in range(3)] + list(rest))
    unpack_own(lambda at, n: stack_ref[pl.ds(at, n)], bx, True, tables_ref, store)


def own_sides_kernel(sides_ref, edge_ref, tables_ref, *refs):
    v_ref, *rest = refs[len(refs) // 2 :]
    bx = v_ref.shape[1] - 2 * DEPTH - 1
    store = store_to([v_ref.at[d] for d in range(3)] + list(rest))
    unpack_sides(lambda at, n: sides_ref[pl.ds(at, n)], bx, True, tables_ref, store, v_ref.at[0])
    load = lambda at, n: edge_ref[pl.ds(at, n)]
    unpack_own_edges(load, bx, True, tables_ref, store)
    unpack_side_edges(load, bx, True, tables_ref, store, v_ref.at[0])


def rows_in_grid(bz):
    iz = lax.axis_index("gz")
    row = iota((1, bz, 1), 1)
    return ((row < bz // 2) & (iz < lax.axis_size("gz") - 1)) | ((row >= bz // 2) & (iz > 0))


def load_both(above, below):
    return lambda at, n: jnp.concatenate([above[pl.ds(at, n)], below[pl.ds(at, n)]], axis=1)


def halo_kernel(face_0_ref, face_1_ref, corner_0_ref, corner_1_ref, tables_ref, halo_ref, next_ref):
    half, by = face_0_ref.shape[1:]
    bz = 2 * half
    bx = halo_ref.shape[1] - 2 * DEPTH - 1
    ok = rows_in_grid(bz)
    store = store_to([halo_ref.at[n] for n in range(7)])

    def faces(above, below):
        unpack_own(load_both(above, below), bx, ok, tables_ref, store)
        for i in range(bx):
            n = i % half
            next_ref[DEPTH + i, half - 1 : half, 0:by] = above[bx * FIELDS + i // half, n : n + 1, :]

    def corners(above, below):
        unpack_sides(load_both(above, below), bx, ok, tables_ref, store, halo_ref.at[0])
        for i in range(2 * DEPTH):
            n = i % half
            to = DEPTH + bx + i if i < DEPTH else i - DEPTH
            next_ref[to, half - 1 : half, 0:by] = above[2 * DEPTH * FIELDS + 1 + i // half, n : n + 1, :]

    by_parity("gz", (face_0_ref, face_1_ref), faces)
    by_parity("gz", (corner_0_ref, corner_1_ref), corners)


def unpack_halo_edges(edge_0_ref, edge_1_ref, tables_ref, halo_ref, next_ref):
    half, by = edge_0_ref.shape[1:]
    bx = halo_ref.shape[1] - 2 * DEPTH - 1
    ok = rows_in_grid(2 * half)
    store = store_to([halo_ref.at[n] for n in range(7)])
    tiles = bx // 2 + DEPTH

    def body(above, below):
        load = load_both(above, below)
        unpack_own_edges(load, bx, ok, tables_ref, store)
        unpack_side_edges(load, bx, ok, tables_ref, store, halo_ref.at[0])
        for n in range(tiles // half):
            rows = above[tiles + n]
            for upper in range(2):
                values = beside(rows, 1, upper)
                for i in range(half):
                    tile = n * half + i
                    if tile < bx // 2:
                        to = DEPTH + upper * (bx // 2) + tile
                    else:
                        to = tile - bx // 2 + (0 if upper else DEPTH + bx)
                    next_ref[to, half - 1 : half, by : 2 * by] = values[i : i + 1]

    by_parity("gz", (edge_0_ref, edge_1_ref), body)


def main_kernel(
    v_ref, p0_ref, pre_ref, power_field_ref, rho_ref, _halo, _next, edge_0_ref, edge_1_ref, tables_ref,
    out_vx_ref, out_vz_ref, out_vy_ref, out_p_ref, out_eta_ref, sum_ref, halo_ref, next_ref,
    va_ref, vb_ref, p_ref, weight_ref,
):
    bx, bz, by = out_p_ref.shape
    rows, lanes = 2 * bz, 2 * by
    nx, nz, ny = lax.axis_size("gx"), lax.axis_size("gz"), lax.axis_size("gy")
    ix, iz, iy = lax.axis_index("gx"), lax.axis_index("gz"), lax.axis_index("gy")
    unpack_halo_edges(edge_0_ref, edge_1_ref, tables_ref, halo_ref, next_ref)

    shape = (rows, lanes)
    r, c = iota(shape, 0), iota(shape, 1)
    zg = iz * bz + jnp.where(r < bz + bz // 2, r, r - rows)
    yg = iy * by + jnp.where(c <= by + DEPTH, c, c - lanes)
    filled = (c <= by + DEPTH) | (c >= lanes - DEPTH)
    inside = filled & (zg >= 0) & (zg < nz * bz) & (yg >= 0) & (yg < ny * by)
    weight_ref[0] = jnp.where(inside, 0.05, 0.0)
    weight_ref[1] = jnp.where(inside & (zg > 0), 0.05, 0.0)
    weight_ref[2] = jnp.where(inside & (yg > 0), 0.05, 0.0)
    weight_ref[3] = jnp.where(inside, 0.0, 1.0)

    def with_halo(own, n, planes):
        return jnp.concatenate([own[planes], halo_ref[n, planes]], axis=1)

    for k in range(1, ITERS + 1):
        old, new = (va_ref, vb_ref) if k % 2 else (vb_ref, va_ref)
        last = k == ITERS

        def load(d, j, count):
            planes = pl.ds(j, count)
            return with_halo(v_ref.at[d], d, planes) if k == 1 else old[d, planes]

        def cells(j, count):
            planes = pl.ds(j, count)
            vx1 = load(0, j, count + 1)
            vx = vx1[:count]
            vz, vy = load(1, j, count), load(2, j, count)
            p = with_halo(p0_ref, 3, planes) if k == 1 else p_ref[planes]
            up = z_up(vz)
            if k == 1:
                after = next_ref[planes]
                after = jnp.concatenate([after, after], axis=1)
                up = jnp.where(iota((1, rows, lanes), 1) == bz + bz // 2 - 1, after, up)
            rx = vx1[1:] - vx
            rz = up - vz
            ry = y_up(vy) - vy
            a = rx - ry
            b = ry - rz
            inv = (a * (a + b) + b * b) * (1.0 / 3.0) + 1.0
            eta = with_halo(pre_ref, 4, planes) * jnp.exp2(with_halo(power_field_ref, 5, planes) * jnp.log(inv))
            quarter = 0.25 * eta
            div = rx + ry + rz
            p = p - quarter * (div + div)
            tx, tz, ty = eta * rx - p, eta * rz - p, eta * ry - p
            sz = quarter + z_down(quarter)
            sy = quarter + y_down(quarter)
            return vx, vz, vy, eta, p, quarter, tx, tz, ty, sz, sy

        def chunk(j, count, carry, start=False):
            planes = pl.ds(j, count)
            vx, vz, vy, eta, p, quarter, tx, tz, ty, sz, sy = cells(j, count)
            vz0, vy0 = load(1, j - 1, 1), load(2, j - 1, 1)
            quarter0, tx0, sz0, sy0, part_z0, part_y0, scale_z0, scale_y0 = carry
            join = lambda first, rest: jnp.concatenate([first, rest[:-1]], axis=0) if count > 1 else first
            bias = weight_ref[3:4]
            sx = quarter + join(quarter0, quarter)
            exz = sz + join(sz0, sz)
            exy = sy + join(sy0, sy)
            ezy = sz + y_down(sz)
            fxz = exz * (vx - z_down(vx))
            fxy = exy * (vx - y_down(vx))
            low_vz, low_vy = join(vz0, vz), join(vy0, vy)
            gzx = exz * (vz - low_vz)
            hyx = exy * (vy - low_vy)
            gzy = ezy * (vz - y_down(vz))
            hyz = ezy * (vy - z_down(vy))
            res_x = (tx - join(tx0, tx)) + ((z_up(fxz) - fxz) + (y_up(fxy) - fxy))
            new_vx = vx + weight_ref[0:1] * reciprocal(sx + bias) * res_x
            part_z = (tz - z_down(tz)) - with_halo(rho_ref, 6, planes) + ((y_up(gzy) - gzy) - gzx)
            part_y = (ty - y_down(ty)) + ((z_up(hyz) - hyz) - hyx)
            scale_z = weight_ref[1:2] * reciprocal(sz + bias)
            scale_y = weight_ref[2:3] * reciprocal(sy + bias)
            new_vz = low_vz + join(scale_z0, scale_z) * (join(part_z0, part_z) + gzx)
            new_vy = low_vy + join(scale_y0, scale_y) * (join(part_y0, part_y) + hyx)
            if last:
                at = pl.ds(j - DEPTH, count)
                out_vx_ref[at] = new_vx[:, 0:bz, 0:by]
                out_p_ref[at] = p[:, 0:bz, 0:by]
                out_eta_ref[at] = eta[:, 0:bz, 0:by]
                sum_ref[...] += jnp.sum(p[:, 0:bz, 0:by], axis=0)
                if not start:
                    at = pl.ds(j - 1 - DEPTH, count)
                    out_vz_ref[at] = new_vz[:, 0:bz, 0:by]
                    out_vy_ref[at] = new_vy[:, 0:bz, 0:by]
            else:
                p_ref[planes] = p
                new[0, planes] = new_vx
                if not start:
                    new[1, pl.ds(j - 1, count)] = new_vz
                    new[2, pl.ds(j - 1, count)] = new_vy
            return tuple(a[-1:] for a in (quarter, tx, sz, sy, part_z, part_y, scale_z, scale_y))

        first, end = k, bx + 2 * DEPTH - k
        if last:
            sum_ref[...] = jnp.zeros((bz, by), jnp.float32)
        _, _, _, _, p, quarter, tx, _, _, sz, sy = cells(first - 1, 1)
        if not last:
            p_ref[pl.ds(first - 1, 1)] = p
        zero = jnp.zeros((1, rows, lanes), jnp.float32)
        carry = chunk(first, 1, (quarter, tx, sz, sy, zero, zero, zero, zero), start=True)
        steps, rest = divmod((end - 1 if last else end) - first, UNROLL)
        carry = lax.fori_loop(
            0, steps, lambda s, carry: chunk(first + 1 + s * UNROLL, UNROLL, carry), carry
        )
        if rest:
            carry = chunk(first + 1 + steps * UNROLL, rest, carry)
        if last:
            quarter0, tx0, sz0, sy0, part_z0, part_y0, scale_z0, scale_y0 = carry
            _, vz, vy, _, _, _, _, _, _, sz, sy = cells(end, 1)
            vz0, vy0 = load(1, end - 1, 1), load(2, end - 1, 1)
            new_vz = vz0 + scale_z0 * (part_z0 + (sz + sz0) * (vz - vz0))
            new_vy = vy0 + scale_y0 * (part_y0 + (sy + sy0) * (vy - vy0))
            out_vz_ref[pl.ds(end - 1 - DEPTH, 1)] = new_vz[:, 0:bz, 0:by]
            out_vy_ref[pl.ds(end - 1 - DEPTH, 1)] = new_vy[:, 0:bz, 0:by]

            @pl.when(ix == 0)
            def _():
                out_vx_ref[0] = jnp.zeros((bz, by), jnp.float32)
        else:
            plane = jnp.zeros((rows, lanes), jnp.float32)

            @pl.when(ix == 0)
            def _():
                for i in range(first, DEPTH):
                    for d in range(3):
                        new[d, i] = plane
                new[0, DEPTH] = plane

            @pl.when(ix == nx - 1)
            def _():
                for i in range(DEPTH + bx, end + 1):
                    for d in range(3):
                        new[d, i] = plane


def final_kernel(p_ref, sum_ref, out_ref, *, cells):
    mean = jnp.sum(sum_ref[...]) * (1.0 / cells)
    out_ref[...] = p_ref[...] - mean


def swap(a, axis, start):
    count = lax.axis_size(axis)
    return lax.ppermute(a, axis, [(i, j) for k in range(start, count - 1, 2) for i, j in ((k, k + 1), (k + 1, k))])


def sum_everywhere(total):
    axes = ("gx", "gy", "gz")
    devices = math.prod(lax.axis_size(a) for a in axes)
    total = total + lax.ppermute(total, axes, [(i, i ^ 1) for i in range(devices)])
    total = jnp.broadcast_to(jnp.sum(total, axis=0, keepdims=True), (devices // 2, total.shape[1]))
    groups = [list(range(n, devices, 2)) for n in range(2)]
    return lax.all_to_all(total, axes, 0, 0, tiled=True, axis_index_groups=groups)


def local(vel_x, vel_y, vel_z, pressure, phase, visc_scale, power_n, density):
    bx, bz, by = pressure.shape
    assert bx % (2 * GROUP) == 0 and bz == 2 * DEPTH and DEPTH == GROUP
    f32 = jnp.float32
    iy, ny = lax.axis_index("gy"), lax.axis_size("gy")
    cells = bx * bz * by * math.prod(lax.axis_size(a) for a in ("gx", "gz", "gy"))
    deep = bx + 2 * DEPTH + 1
    rows, lanes = 2 * bz, 2 * by
    shape = lambda *dims: jax.ShapeDtypeStruct(dims, f32)
    block = shape(bx, bz, by)
    scratch = lambda *dims: pltpu.VMEM(dims, f32)
    limit = lambda mebibytes: pltpu.CompilerParams(vmem_limit_bytes=mebibytes * 1024 * 1024)
    groups = bx // GROUP
    stacked = bx * FIELDS + bx // 2 + 2
    sent = shape(DEPTH * FIELDS + 1, bz, by)
    edge, x_0, x_1, stack = pl.pallas_call(
        pack_kernel,
        out_shape=(shape(bx // 2, bz, by), sent, sent, shape(stacked, bz, by)),
        in_specs=[HBM] * 8,
        out_specs=(HBM,) * 4,
        scratch_shapes=[
            scratch(FIELDS - 1, bx, bz, by),
            pltpu.VMEM((bx, bz, by), jnp.int32),
            scratch(bx // 2, bz, by),
            scratch(stacked, bz, by),
            pltpu.SMEM((PHASES,), f32),
            pltpu.SMEM((PHASES,), f32),
            pltpu.SMEM((PHASES,), f32),
            pltpu.SemaphoreType.DMA((groups, FIELDS)),
            pltpu.SemaphoreType.DMA((groups + groups // 2 + 3,)),
            pltpu.SemaphoreType.DMA((3,)),
        ],
        compiler_params=limit(58),
    )(vel_x, vel_z, vel_y, pressure, phase, visc_scale, power_n, density)

    def edges_beside(edge):
        side = swap(edge, "gy", 0)
        if ny == 2:
            return side
        lane = iota(side.shape, 2) % (by // 2) % LANE_STEP
        return jnp.where((lane <= DEPTH) == (lax.rem(iy, 2) == 0), side, swap(edge, "gy", 1))

    estimate = lambda size: pl.CostEstimate(
        flops=4 * size * bz * by, bytes_accessed=size * bz * by * 4, transcendentals=0
    )

    def unpacking(kernel, tiles, out_shape, *args, aliases={}):
        return pl.pallas_call(
            kernel,
            out_shape=out_shape,
            in_specs=[VMEM] * len(args),
            out_specs=(VMEM,) * len(out_shape),
            input_output_aliases=aliases,
            compiler_params=limit(16),
            cost_estimate=estimate(13 * tiles),
        )(*args)

    field = shape(deep, bz, lanes)
    own_shape = (shape(3, deep, bz, lanes),) + (field,) * 4
    half = lambda tiles, planes: shape(tiles + planes // (bz // 2), bz // 2, by)
    x_0, x_1 = swap(x_0, "gx", 0), swap(x_1, "gx", 1)
    face = half(bx * FIELDS, bx)
    extra = (shape(bx // 2, bz, by), shape(2, bz, by))
    z_0, z_1, edge, tables, *own = unpacking(own_kernel, bx, (face, face) + extra + own_shape, stack)
    face_1, face_0 = swap(z_1, "gz", 1), swap(z_0, "gz", 0)

    tiles = bx // 2 + DEPTH
    edge = pl.pallas_call(
        side_edge_kernel,
        out_shape=shape(tiles, bz, by),
        in_specs=[VMEM] * 3,
        out_specs=VMEM,
        compiler_params=limit(4),
    )(x_0, x_1, edge)
    corner = half(2 * DEPTH * FIELDS + 1, 2 * DEPTH)
    sides, z_0, z_1 = pl.pallas_call(
        sides_kernel,
        out_shape=(shape(2 * DEPTH * FIELDS + 1, bz, by), corner, corner),
        in_specs=[VMEM] * 3,
        out_specs=(VMEM,) * 3,
        compiler_params=limit(4),
    )(x_0, x_1, edge)
    edge = edges_beside(edge)
    corner_1, corner_0 = swap(z_1, "gz", 1), swap(z_0, "gz", 0)
    z_0, z_1 = pl.pallas_call(
        edge_rows_kernel,
        out_shape=(half(tiles, tiles),) * 2,
        in_specs=[VMEM],
        out_specs=(VMEM,) * 2,
        compiler_params=limit(4),
        cost_estimate=estimate(100000),
    )(edge)
    edge_1, edge_0 = swap(z_1, "gz", 1), swap(z_0, "gz", 0)

    own = unpacking(
        own_sides_kernel, 2 * deep, own_shape, sides, edge, tables, *own, aliases={n + 3: n for n in range(5)}
    )
    halo = unpacking(
        halo_kernel, deep, (shape(7, deep, bz, lanes), field), face_0, face_1, corner_0, corner_1, tables
    )
    vx, vz, vy, p, eta, total, _, _ = pl.pallas_call(
        main_kernel,
        out_shape=(block,) * 5 + (shape(bz, by),) + tuple(shape(*a.shape) for a in halo),
        in_specs=[VMEM] * 10,
        out_specs=(VMEM,) * 8,
        input_output_aliases={5: 6, 6: 7},
        scratch_shapes=[
            scratch(3, deep, rows, lanes),
            scratch(3, deep, rows, lanes),
            scratch(deep, rows, lanes),
            scratch(4, rows, lanes),
        ],
        compiler_params=limit(32),
    )(*own, *halo, edge_0, edge_1, tables)

    total = sum_everywhere(total)
    p = pl.pallas_call(
        lambda *refs: final_kernel(*refs, cells=float(cells)),
        out_shape=block,
        in_specs=[VMEM] * 2,
        out_specs=VMEM,
        compiler_params=limit(4),
    )(p, total)
    return (vx, vy, vz, p, eta)


def solution(mesh):
    spec = P("gx", "gz", "gy")
    return jax.shard_map(
        local,
        mesh=mesh,
        in_specs=(spec,) * 5 + (P(),) * 3,
        out_specs=(spec,) * 5,
        check_vma=False,
    )
```

```python
import math

import jax
import jax.numpy as jnp
from jax import lax
from jax.experimental import pallas as pl
from jax.experimental.pallas import tpu as pltpu
from jax.sharding import PartitionSpec as P

ITERS = 4
PHASES = 4
FIELDS = 5
DEPTH = ITERS
LANE_STEP = 2 * DEPTH + 1
UNROLL = 4
GROUP = 4

VMEM = pl.BlockSpec(memory_space=pltpu.VMEM)
HBM = pl.BlockSpec(memory_space=pltpu.HBM)


def z_up(a):
    return pltpu.roll(a, a.shape[-2] - 1, a.ndim - 2)


def z_down(a):
    return pltpu.roll(a, 1, a.ndim - 2)


def y_up(a):
    return pltpu.roll(a, a.shape[-1] - 1, a.ndim - 1)


def y_down(a):
    return pltpu.roll(a, 1, a.ndim - 1)


def reciprocal(a):
    r = pl.reciprocal(a, approx=True)
    return r * (2.0 - a * r)


def iota(shape, axis):
    return lax.broadcasted_iota(jnp.int32, shape, axis)


def odd(axis):
    return lax.rem(lax.axis_index(axis), 2) == 1


def by_parity(axis, pair, body):
    pl.when(jnp.logical_not(odd(axis)))(lambda: body(pair[0], pair[1]))
    pl.when(odd(axis))(lambda: body(pair[1], pair[0]))


def start_copies(sources, targets, sems):
    copies = []
    for g in range(sources[0].shape[0] // GROUP):
        at = pl.ds(g * GROUP, GROUP)
        copies.append(
            [pltpu.make_async_copy(a.at[at], b.at[at], sems.at[g, f]) for f, (a, b) in enumerate(zip(sources, targets))]
        )
        for copy in copies[-1]:
            copy.start()
    return copies


def clean_group(g, field_ref, phase_ref):
    bx, bz, by = phase_ref.shape
    ix, iz, iy = lax.axis_index("gx"), lax.axis_index("gz"), lax.axis_index("gy")
    plane, row, lane = (iota((GROUP, bz, by), d) for d in range(3))
    at = pl.ds(g * GROUP, GROUP)
    vx, vz, vy, p = (field_ref[f, at] for f in range(FIELDS - 1))
    if g == 0:
        vx = jnp.where((plane > 0) | (ix > 0), vx, 0.0)
    vz = jnp.where((row > 0) | (iz > 0), vz, 0.0)
    vy = jnp.where((lane > 0) | (iy > 0), vy, 0.0)
    return vx, vz, vy, p, phase_ref[at].astype(jnp.float32)


def add_edge(edge, a, base):
    by = edge.shape[-1]
    lane = iota((1,) * (edge.ndim - 1) + (by,), edge.ndim - 1)
    first = pltpu.roll(a, base, a.ndim - 1) if base else a
    edge = jnp.where((lane >= base) & (lane <= base + DEPTH), first, edge)
    last = pltpu.roll(a, (base + LANE_STEP) % by, a.ndim - 1)
    return jnp.where((lane > base + DEPTH) & (lane < base + LANE_STEP), last, edge)


def add_edges(edge, fields, upper):
    for f, a in enumerate(fields):
        edge = add_edge(edge, a, edge.shape[-1] // 2 * upper + LANE_STEP * f)
    return edge


def beside(edge, f, upper):
    by = edge.shape[-1]
    iy = lax.axis_index("gy")
    lane = iota((1,) * (edge.ndim - 1) + (by,), edge.ndim - 1)
    right = (lane <= DEPTH) & (iy < lax.axis_size("gy") - 1)
    left = (lane >= by - DEPTH) & (iy > 0)
    shift = by // 2 * upper + LANE_STEP * f
    a = pltpu.roll(edge, by - shift, edge.ndim - 1) if shift else edge
    b = pltpu.roll(edge, (by - LANE_STEP - shift) % by, edge.ndim - 1)
    return jnp.where(right, a, jnp.where(left, b, 0.0))


def pack_kernel(
    vx_hbm, vz_hbm, vy_hbm, p_hbm, phase_hbm, scale_hbm, power_hbm, rho_hbm, edge_hbm, x_0_hbm, x_1_hbm, stack_hbm,
    field_ref, phase_ref, edge_ref, stack_ref, scale_ref, power_ref, rho_ref, sems, out_sems, table_sems,
):
    bx, bz, by = phase_ref.shape
    targets = [field_ref.at[f] for f in range(FIELDS - 1)] + [phase_ref]
    copies = start_copies((vx_hbm, vz_hbm, vy_hbm, p_hbm, phase_hbm), targets, sems)
    table_refs = (scale_ref, power_ref, rho_ref)
    pairs = zip((scale_hbm, power_hbm, rho_hbm), table_refs)
    table_copies = [pltpu.make_async_copy(a, b, table_sems.at[n]) for n, (a, b) in enumerate(pairs)]
    for copy in table_copies:
        copy.start()
    half = bx // GROUP // 2
    outs = []

    def out(source, target):
        outs.append(pltpu.make_async_copy(source, target, out_sems.at[len(outs)]))
        outs[-1].start()

    for g in range(half):
        edge = jnp.zeros((GROUP, bz, by), jnp.float32)
        for upper in range(2):
            at = (g + upper * half) * GROUP
            for copy in copies[g + upper * half]:
                copy.wait()
            fields = clean_group(g + upper * half, field_ref, phase_ref)
            for f, a in enumerate(fields):
                for i in range(GROUP):
                    stack_ref[(at + i) * FIELDS + f] = a[i]
            edge = add_edges(edge, fields, upper)
            at = pl.ds(at * FIELDS, GROUP * FIELDS)
            out(stack_ref.at[at], stack_hbm.at[at])
        at = pl.ds(g * GROUP, GROUP)
        edge_ref[at] = edge
        out(edge_ref.at[at], edge_hbm.at[at])
        stack_ref[pl.ds(bx * FIELDS + g * GROUP, GROUP)] = edge
    count = bx * FIELDS + bx // 2
    row = iota((bz, by), 0)
    for copy in table_copies:
        copy.wait()
    entries = [ref[index] for ref in table_refs for index in range(PHASES)]
    for n in range(2):
        tile = jnp.zeros((bz, by), jnp.float32)
        for r, entry in enumerate(entries[n * bz : (n + 1) * bz]):
            tile = jnp.where(row == r, entry, tile)
        stack_ref[count + n] = tile
    at = pl.ds(bx * FIELDS, count + 2 - bx * FIELDS)
    out(stack_ref.at[at], stack_hbm.at[at])
    count = x_0_hbm.shape[0]
    down, up = stack_ref.at[pl.ds(0, count)], stack_ref.at[pl.ds(bx * FIELDS - count, count)]
    sem = out_sems.at[len(outs)], out_sems.at[len(outs) + 1]

    def send(to_above, to_below):
        pair = pltpu.make_async_copy(up, to_above, sem[0]), pltpu.make_async_copy(down, to_below, sem[1])
        for copy in pair:
            copy.start()
        for copy in pair:
            copy.wait()

    by_parity("gx", (x_0_hbm, x_1_hbm), send)
    for copy in outs:
        copy.wait()


def side_edge_kernel(x_1_ref, x_0_ref, own_edge_ref, edge_ref):
    bz, by = edge_ref.shape[1:]
    own = own_edge_ref.shape[0]
    edge_ref[0:own] = own_edge_ref[...]

    def body(above, below):
        edge = jnp.zeros((DEPTH, bz, by), jnp.float32)
        for upper, (ref, at) in enumerate(((above, 0), (below, 1))):
            block = ref[pl.ds(at, DEPTH * FIELDS)].reshape(DEPTH, FIELDS, bz, by)
            edge = add_edges(edge, [block[:, f] for f in range(FIELDS)], upper)
        edge_ref[own:] = edge
        edge_ref[own] = add_edge(edge[0], above[DEPTH * FIELDS], FIELDS * LANE_STEP)

    by_parity("gx", (x_0_ref, x_1_ref), body)


def half_rows(tiles, swap):
    down = odd("gz") if swap == 0 else jnp.logical_not(odd("gz"))
    half = tiles.shape[-2] // 2
    return jnp.where(down, tiles[..., :half, :], tiles[..., half:, :])


def store_next_rows(refs, at, tiles):
    half = tiles.shape[-2] // 2
    for ref in refs:
        for i in range(tiles.shape[0]):
            ref[at + i // half, i % half : i % half + 1, :] = tiles[i, half : half + 1, :]


def sides_kernel(x_1_ref, x_0_ref, _edge_ref, sides_ref, z_0_ref, z_1_ref):
    count = DEPTH * FIELDS
    bz, by = sides_ref.shape[1:]

    def body(above, below):
        sides_ref[0:count] = above[0:count]
        sides_ref[count : 2 * count] = below[1 : count + 1]
        sides_ref[2 * count] = above[count]

    by_parity("gx", (x_0_ref, x_1_ref), body)
    tiles = sides_ref[...]
    for swap, ref in enumerate((z_0_ref, z_1_ref)):
        ref[0 : 2 * count + 1] = half_rows(tiles, swap)
    vz = tiles[0 : 2 * count].reshape(2 * DEPTH, FIELDS, bz, by)[:, 1]
    store_next_rows((z_0_ref, z_1_ref), 2 * count + 1, vz)


def edge_rows_kernel(edge_ref, z_0_ref, z_1_ref):
    tiles = edge_ref[...]
    for swap, ref in enumerate((z_0_ref, z_1_ref)):
        ref[0 : tiles.shape[0]] = half_rows(tiles, swap)
    store_next_rows((z_0_ref, z_1_ref), tiles.shape[0], tiles)


def lookups(fields, ok, keep, table_ref):
    *rest, phase = fields
    for number in range(3):
        rows = [divmod(number * PHASES + index, table_ref.shape[1]) for index in range(PHASES)]
        table = [table_ref[n, r : r + 1, :] for n, r in rows]
        value = jnp.broadcast_to(table[0], phase.shape)
        for index in range(1, PHASES):
            value = jnp.where(phase == float(index), table[index], value)
        if number == 0:
            value = value * jnp.where(ok, 1.0, 0.0)
            if keep is not None:
                value = jnp.where(keep, value, 0.0)
        elif number == 1:
            value = (0.5 / math.log(2.0)) * (reciprocal(value) - 1.0)
        rest.append(value)
    return rest


def own_lanes(block, ok, tables):
    block = block.reshape(-1, FIELDS, *block.shape[-2:])
    return lookups([block[:, f] for f in range(FIELDS)], ok, None, tables)


def edge_lanes(edge, upper, ok, tables):
    by = edge.shape[-1]
    iy = lax.axis_index("gy")
    lane = iota((1, 1, by), 2)
    keep = ((lane <= DEPTH) & (iy < lax.axis_size("gy") - 1)) | ((lane >= by - DEPTH) & (iy > 0))
    return lookups([beside(edge, f, upper) for f in range(FIELDS)], ok, keep, tables)


def store_to(refs):
    def store(planes, part, values):
        by = values[0].shape[-1]
        for ref, value in zip(refs, values):
            ref[planes, :, part * by : (part + 1) * by] = value

    return store


def unpack_own(load, bx, ok, tables, store):
    def group(g, carry):
        at = g * GROUP
        store(pl.ds(DEPTH + at, GROUP), 0, own_lanes(load(at * FIELDS, GROUP * FIELDS), ok, tables))
        return carry

    lax.fori_loop(0, bx // GROUP, group, 0)


def unpack_own_edges(load, bx, ok, tables, store):
    half = bx // 2
    for upper in range(2):

        def group(g, carry):
            at = g * GROUP
            values = edge_lanes(load(at, GROUP), upper, ok, tables)
            store(pl.ds(DEPTH + upper * half + at, GROUP), 1, values)
            return carry

        lax.fori_loop(0, half // GROUP, group, 0)


def side_places(bx):
    ix = lax.axis_index("gx")
    return (pl.ds(DEPTH + bx, DEPTH), ix < lax.axis_size("gx") - 1), (pl.ds(0, DEPTH), ix > 0)


def unpack_sides(load, bx, ok, tables, store, vx_ref):
    count = DEPTH * FIELDS
    for n, (planes, inside) in enumerate(side_places(bx)):
        store(planes, 0, own_lanes(load(n * count, count), ok & inside, tables))
    vx = load(2 * count, 1)
    vx_ref[pl.ds(bx + 2 * DEPTH, 1), :, 0 : vx.shape[-1]] = vx


def unpack_side_edges(load, bx, ok, tables, store, vx_ref):
    half = bx // 2
    edge = load(half, DEPTH)
    for upper, (planes, inside) in enumerate(side_places(bx)):
        store(planes, 1, edge_lanes(edge, upper, ok & inside, tables))
    by = edge.shape[-1]
    vx_ref[pl.ds(bx + 2 * DEPTH, 1), :, by : 2 * by] = beside(edge[0:1], FIELDS, 0)


def own_kernel(stack_ref, z_0_ref, z_1_ref, edge_ref, tables_ref, v_ref, *rest):
    bx = v_ref.shape[1] - 2 * DEPTH - 1
    count = bx * FIELDS
    edge_ref[...] = stack_ref[count : count + bx // 2]
    tables_ref[...] = stack_ref[count + bx // 2 :]
    size = GROUP * FIELDS

    def group(g, carry):
        at = pl.ds(g * size, size)
        tiles = stack_ref[at]
        for swap, ref in enumerate((z_0_ref, z_1_ref)):
            ref[at] = half_rows(tiles, swap)
        return carry

    lax.fori_loop(0, bx // GROUP, group, 0)
    for g in range(bx // GROUP):
        vz = stack_ref[pl.ds(g * size, size)].reshape(GROUP, FIELDS, *stack_ref.shape[1:])[:, 1]
        store_next_rows((z_0_ref, z_1_ref), count + g * GROUP // (stack_ref.shape[1] // 2), vz)
    store = store_to([v_ref.at[d] for d in range(3)] + list(rest))
    unpack_own(lambda at, n: stack_ref[pl.ds(at, n)], bx, True, tables_ref, store)


def own_sides_kernel(sides_ref, edge_ref, tables_ref, *refs):
    v_ref, *rest = refs[len(refs) // 2 :]
    bx = v_ref.shape[1] - 2 * DEPTH - 1
    store = store_to([v_ref.at[d] for d in range(3)] + list(rest))
    unpack_sides(lambda at, n: sides_ref[pl.ds(at, n)], bx, True, tables_ref, store, v_ref.at[0])
    load = lambda at, n: edge_ref[pl.ds(at, n)]
    unpack_own_edges(load, bx, True, tables_ref, store)
    unpack_side_edges(load, bx, True, tables_ref, store, v_ref.at[0])


def rows_in_grid(bz):
    iz = lax.axis_index("gz")
    row = iota((1, bz, 1), 1)
    return ((row < bz // 2) & (iz < lax.axis_size("gz") - 1)) | ((row >= bz // 2) & (iz > 0))


def load_both(above, below):
    return lambda at, n: jnp.concatenate([above[pl.ds(at, n)], below[pl.ds(at, n)]], axis=1)


def halo_kernel(face_0_ref, face_1_ref, corner_0_ref, corner_1_ref, tables_ref, halo_ref, next_ref):
    half, by = face_0_ref.shape[1:]
    bz = 2 * half
    bx = halo_ref.shape[1] - 2 * DEPTH - 1
    ok = rows_in_grid(bz)
    store = store_to([halo_ref.at[n] for n in range(7)])

    def faces(above, below):
        unpack_own(load_both(above, below), bx, ok, tables_ref, store)
        for i in range(bx):
            n = i % half
            next_ref[DEPTH + i, half - 1 : half, 0:by] = above[bx * FIELDS + i // half, n : n + 1, :]

    def corners(above, below):
        unpack_sides(load_both(above, below), bx, ok, tables_ref, store, halo_ref.at[0])
        for i in range(2 * DEPTH):
            n = i % half
            to = DEPTH + bx + i if i < DEPTH else i - DEPTH
            next_ref[to, half - 1 : half, 0:by] = above[2 * DEPTH * FIELDS + 1 + i // half, n : n + 1, :]

    by_parity("gz", (face_0_ref, face_1_ref), faces)
    by_parity("gz", (corner_0_ref, corner_1_ref), corners)


def unpack_halo_edges(edge_0_ref, edge_1_ref, tables_ref, halo_ref, next_ref):
    half, by = edge_0_ref.shape[1:]
    bx = halo_ref.shape[1] - 2 * DEPTH - 1
    ok = rows_in_grid(2 * half)
    store = store_to([halo_ref.at[n] for n in range(7)])
    tiles = bx // 2 + DEPTH

    def body(above, below):
        load = load_both(above, below)
        unpack_own_edges(load, bx, ok, tables_ref, store)
        unpack_side_edges(load, bx, ok, tables_ref, store, halo_ref.at[0])
        for n in range(tiles // half):
            rows = above[tiles + n]
            for upper in range(2):
                values = beside(rows, 1, upper)
                for i in range(half):
                    tile = n * half + i
                    if tile < bx // 2:
                        to = DEPTH + upper * (bx // 2) + tile
                    else:
                        to = tile - bx // 2 + (0 if upper else DEPTH + bx)
                    next_ref[to, half - 1 : half, by : 2 * by] = values[i : i + 1]

    by_parity("gz", (edge_0_ref, edge_1_ref), body)


def main_kernel(
    v_ref, p0_ref, pre_ref, power_field_ref, rho_ref, _halo, _next, edge_0_ref, edge_1_ref, tables_ref,
    out_vx_ref, out_vz_ref, out_vy_ref, out_p_ref, out_eta_ref, sum_ref, halo_ref, next_ref,
    va_ref, vb_ref, p_ref, weight_ref,
):
    bx, bz, by = out_p_ref.shape
    rows, lanes = 2 * bz, 2 * by
    nx, nz, ny = lax.axis_size("gx"), lax.axis_size("gz"), lax.axis_size("gy")
    ix, iz, iy = lax.axis_index("gx"), lax.axis_index("gz"), lax.axis_index("gy")
    unpack_halo_edges(edge_0_ref, edge_1_ref, tables_ref, halo_ref, next_ref)

    shape = (rows, lanes)
    r, c = iota(shape, 0), iota(shape, 1)
    zg = iz * bz + jnp.where(r < bz + bz // 2, r, r - rows)
    yg = iy * by + jnp.where(c <= by + DEPTH, c, c - lanes)
    filled = (c <= by + DEPTH) | (c >= lanes - DEPTH)
    inside = filled & (zg >= 0) & (zg < nz * bz) & (yg >= 0) & (yg < ny * by)
    weight_ref[0] = jnp.where(inside, 0.05, 0.0)
    weight_ref[1] = jnp.where(inside & (zg > 0), 0.05, 0.0)
    weight_ref[2] = jnp.where(inside & (yg > 0), 0.05, 0.0)
    weight_ref[3] = jnp.where(inside, 0.0, 1.0)

    def with_halo(own, n, planes):
        return jnp.concatenate([own[planes], halo_ref[n, planes]], axis=1)

    for k in range(1, ITERS + 1):
        old, new = (va_ref, vb_ref) if k % 2 else (vb_ref, va_ref)
        last = k == ITERS

        def load(d, j, count):
            planes = pl.ds(j, count)
            return with_halo(v_ref.at[d], d, planes) if k == 1 else old[d, planes]

        def cells(j, count):
            planes = pl.ds(j, count)
            vx1 = load(0, j, count + 1)
            vx = vx1[:count]
            vz, vy = load(1, j, count), load(2, j, count)
            p = with_halo(p0_ref, 3, planes) if k == 1 else p_ref[planes]
            up = z_up(vz)
            if k == 1:
                after = next_ref[planes]
                after = jnp.concatenate([after, after], axis=1)
                up = jnp.where(iota((1, rows, lanes), 1) == bz + bz // 2 - 1, after, up)
            rx = vx1[1:] - vx
            rz = up - vz
            ry = y_up(vy) - vy
            a = rx - ry
            b = ry - rz
            inv = (a * (a + b) + b * b) * (1.0 / 3.0) + 1.0
            eta = with_halo(pre_ref, 4, planes) * jnp.exp2(with_halo(power_field_ref, 5, planes) * jnp.log(inv))
            quarter = 0.25 * eta
            div = rx + ry + rz
            p = p - quarter * (div + div)
            tx, tz, ty = eta * rx - p, eta * rz - p, eta * ry - p
            sz = quarter + z_down(quarter)
            sy = quarter + y_down(quarter)
            return vx, vz, vy, eta, p, quarter, tx, tz, ty, sz, sy

        def chunk(j, count, carry=None, final=False):
            if carry is None:
                below = cells(j - 1, count + 1)
                if not last:
                    p_ref[pl.ds(j - 1, 1)] = below[4][:1]
                vx, vz, vy, eta, p, quarter, tx, tz, ty, sz, sy = (a[1:] for a in below)
                join = lambda n, a: below[n][:-1]
            else:
                vx, vz, vy, eta, p, quarter, tx, tz, ty, sz, sy = cells(j, count)
                first = {1: load(1, j - 1, 1), 2: load(2, j - 1, 1), 5: carry[0], 6: carry[1], 9: carry[2], 10: carry[3]}
                join = lambda n, a: jnp.concatenate([first[n], a[:-1]], axis=0)
            planes = pl.ds(j, count)
            bias = weight_ref[3:4]
            sx = quarter + join(5, quarter)
            exz = sz + join(9, sz)
            exy = sy + join(10, sy)
            ezy = sz + y_down(sz)
            fxz = exz * (vx - z_down(vx))
            fxy = exy * (vx - y_down(vx))
            low_vz, low_vy = join(1, vz), join(2, vy)
            gzx = exz * (vz - low_vz)
            hyx = exy * (vy - low_vy)
            gzy = ezy * (vz - y_down(vz))
            hyz = ezy * (vy - z_down(vy))
            res_x = (tx - join(6, tx)) + ((z_up(fxz) - fxz) + (y_up(fxy) - fxy))
            new_vx = vx + weight_ref[0:1] * reciprocal(sx + bias) * res_x
            part_z = (tz - z_down(tz)) - with_halo(rho_ref, 6, planes) + ((y_up(gzy) - gzy) - gzx)
            part_y = (ty - y_down(ty)) + ((z_up(hyz) - hyz) - hyx)
            scale_z = weight_ref[1:2] * reciprocal(sz + bias)
            scale_y = weight_ref[2:3] * reciprocal(sy + bias)

            def lower(n, a):
                return a[:-1] if carry is None else jnp.concatenate([carry[n], a[:-1]], axis=0)

            skip = 1 if carry is None else 0
            new_vz = low_vz[skip:] + lower(6, scale_z) * (lower(4, part_z) + gzx[skip:])
            new_vy = low_vy[skip:] + lower(7, scale_y) * (lower(5, part_y) + hyx[skip:])
            at = pl.ds(j - 1 + skip - (DEPTH if last else 0), count - skip)
            if last:
                own = count - 1 if final else count
                here = pl.ds(j - DEPTH, own)
                out_vx_ref[here] = new_vx[:own, 0:bz, 0:by]
                out_p_ref[here] = p[:own, 0:bz, 0:by]
                out_eta_ref[here] = eta[:own, 0:bz, 0:by]
                sum_ref[...] += jnp.sum(p[:own, 0:bz, 0:by], axis=0)
                out_vz_ref[at] = new_vz[:, 0:bz, 0:by]
                out_vy_ref[at] = new_vy[:, 0:bz, 0:by]
            else:
                p_ref[planes] = p
                new[0, planes] = new_vx
                new[1, at] = new_vz
                new[2, at] = new_vy
            return tuple(a[-1:] for a in (quarter, tx, sz, sy, part_z, part_y, scale_z, scale_y))

        first, end = k, bx + 2 * DEPTH - k
        if last:
            sum_ref[...] = jnp.zeros((bz, by), jnp.float32)
        count = end - first + 1
        steps = (count - 2) // UNROLL
        start = count - steps * UNROLL
        carry = chunk(first, start)
        loops = steps - 1 if last else steps
        carry = lax.fori_loop(
            0, loops, lambda s, carry: chunk(first + start + s * UNROLL, UNROLL, carry), carry
        )
        if last:
            chunk(end + 1 - UNROLL, UNROLL, carry, final=True)

            @pl.when(ix == 0)
            def _():
                out_vx_ref[0] = jnp.zeros((bz, by), jnp.float32)
        else:
            plane = jnp.zeros((rows, lanes), jnp.float32)

            @pl.when(ix == 0)
            def _():
                for i in range(first, DEPTH):
                    for d in range(3):
                        new[d, i] = plane
                new[0, DEPTH] = plane

            @pl.when(ix == nx - 1)
            def _():
                for i in range(DEPTH + bx, end + 1):
                    for d in range(3):
                        new[d, i] = plane


def final_kernel(p_ref, sum_ref, out_ref, *, cells):
    mean = jnp.sum(sum_ref[...]) * (1.0 / cells)
    out_ref[...] = p_ref[...] - mean


def swap(a, axis, start):
    count = lax.axis_size(axis)
    return lax.ppermute(a, axis, [(i, j) for k in range(start, count - 1, 2) for i, j in ((k, k + 1), (k + 1, k))])


def sum_everywhere(total):
    axes = ("gx", "gy", "gz")
    devices = math.prod(lax.axis_size(a) for a in axes)
    total = total + lax.ppermute(total, axes, [(i, i ^ 1) for i in range(devices)])
    total = jnp.broadcast_to(jnp.sum(total, axis=0, keepdims=True), (devices // 2, total.shape[1]))
    groups = [list(range(n, devices, 2)) for n in range(2)]
    return lax.all_to_all(total, axes, 0, 0, tiled=True, axis_index_groups=groups)


def local(vel_x, vel_y, vel_z, pressure, phase, visc_scale, power_n, density):
    bx, bz, by = pressure.shape
    assert bx % (2 * GROUP) == 0 and bz == 2 * DEPTH and DEPTH == GROUP
    f32 = jnp.float32
    iy, ny = lax.axis_index("gy"), lax.axis_size("gy")
    cells = bx * bz * by * math.prod(lax.axis_size(a) for a in ("gx", "gz", "gy"))
    deep = bx + 2 * DEPTH + 1
    rows, lanes = 2 * bz, 2 * by
    shape = lambda *dims: jax.ShapeDtypeStruct(dims, f32)
    block = shape(bx, bz, by)
    scratch = lambda *dims: pltpu.VMEM(dims, f32)
    limit = lambda mebibytes: pltpu.CompilerParams(vmem_limit_bytes=mebibytes * 1024 * 1024)
    groups = bx // GROUP
    stacked = bx * FIELDS + bx // 2 + 2
    sent = shape(DEPTH * FIELDS + 1, bz, by)
    edge, x_0, x_1, stack = pl.pallas_call(
        pack_kernel,
        out_shape=(shape(bx // 2, bz, by), sent, sent, shape(stacked, bz, by)),
        in_specs=[HBM] * 8,
        out_specs=(HBM,) * 4,
        scratch_shapes=[
            scratch(FIELDS - 1, bx, bz, by),
            pltpu.VMEM((bx, bz, by), jnp.int32),
            scratch(bx // 2, bz, by),
            scratch(stacked, bz, by),
            pltpu.SMEM((PHASES,), f32),
            pltpu.SMEM((PHASES,), f32),
            pltpu.SMEM((PHASES,), f32),
            pltpu.SemaphoreType.DMA((groups, FIELDS)),
            pltpu.SemaphoreType.DMA((groups + groups // 2 + 3,)),
            pltpu.SemaphoreType.DMA((3,)),
        ],
        compiler_params=limit(58),
    )(vel_x, vel_z, vel_y, pressure, phase, visc_scale, power_n, density)

    def edges_beside(edge):
        side = swap(edge, "gy", 0)
        if ny == 2:
            return side
        lane = iota(side.shape, 2) % (by // 2) % LANE_STEP
        return jnp.where((lane <= DEPTH) == (lax.rem(iy, 2) == 0), side, swap(edge, "gy", 1))

    estimate = lambda size: pl.CostEstimate(
        flops=4 * size * bz * by, bytes_accessed=size * bz * by * 4, transcendentals=0
    )

    def unpacking(kernel, tiles, out_shape, *args, aliases={}):
        return pl.pallas_call(
            kernel,
            out_shape=out_shape,
            in_specs=[VMEM] * len(args),
            out_specs=(VMEM,) * len(out_shape),
            input_output_aliases=aliases,
            compiler_params=limit(16),
            cost_estimate=estimate(13 * tiles),
        )(*args)

    field = shape(deep, bz, lanes)
    own_shape = (shape(3, deep, bz, lanes),) + (field,) * 4
    half = lambda tiles, planes: shape(tiles + planes // (bz // 2), bz // 2, by)
    x_1, x_0 = swap(x_1, "gx", 1), swap(x_0, "gx", 0)
    face = half(bx * FIELDS, bx)
    extra = (shape(bx // 2, bz, by), shape(2, bz, by))
    z_0, z_1, edge, tables, *own = unpacking(own_kernel, bx, (face, face) + extra + own_shape, stack)
    face_1, face_0 = swap(z_1, "gz", 1), swap(z_0, "gz", 0)

    tiles = bx // 2 + DEPTH
    edge = pl.pallas_call(
        side_edge_kernel,
        out_shape=shape(tiles, bz, by),
        in_specs=[VMEM] * 3,
        out_specs=VMEM,
        compiler_params=limit(4),
    )(x_1, x_0, edge)
    corner = half(2 * DEPTH * FIELDS + 1, 2 * DEPTH)
    sides, z_0, z_1 = pl.pallas_call(
        sides_kernel,
        out_shape=(shape(2 * DEPTH * FIELDS + 1, bz, by), corner, corner),
        in_specs=[VMEM] * 3,
        out_specs=(VMEM,) * 3,
        compiler_params=limit(4),
    )(x_1, x_0, edge)
    edge = edges_beside(edge)
    corner_1, corner_0 = swap(z_1, "gz", 1), swap(z_0, "gz", 0)
    z_0, z_1 = pl.pallas_call(
        edge_rows_kernel,
        out_shape=(half(tiles, tiles),) * 2,
        in_specs=[VMEM],
        out_specs=(VMEM,) * 2,
        compiler_params=limit(4),
        cost_estimate=estimate(100000),
    )(edge)
    edge_1, edge_0 = swap(z_1, "gz", 1), swap(z_0, "gz", 0)

    own = unpacking(
        own_sides_kernel, 2 * deep, own_shape, sides, edge, tables, *own, aliases={n + 3: n for n in range(5)}
    )
    halo = unpacking(
        halo_kernel, deep, (shape(7, deep, bz, lanes), field), face_0, face_1, corner_0, corner_1, tables
    )
    vx, vz, vy, p, eta, total, _, _ = pl.pallas_call(
        main_kernel,
        out_shape=(block,) * 5 + (shape(bz, by),) + tuple(shape(*a.shape) for a in halo),
        in_specs=[VMEM] * 10,
        out_specs=(VMEM,) * 8,
        input_output_aliases={5: 6, 6: 7},
        scratch_shapes=[
            scratch(3, deep, rows, lanes),
            scratch(3, deep, rows, lanes),
            scratch(deep, rows, lanes),
            scratch(4, rows, lanes),
        ],
        compiler_params=limit(32),
    )(*own, *halo, edge_0, edge_1, tables)

    total = sum_everywhere(total)
    p = pl.pallas_call(
        lambda *refs: final_kernel(*refs, cells=float(cells)),
        out_shape=block,
        in_specs=[VMEM] * 2,
        out_specs=VMEM,
        compiler_params=limit(4),
    )(p, total)
    return (vx, vy, vz, p, eta)


def solution(mesh):
    spec = P("gx", "gz", "gy")
    return jax.shard_map(
        local,
        mesh=mesh,
        in_specs=(spec,) * 5 + (P(),) * 3,
        out_specs=(spec,) * 5,
        check_vma=False,
    )
```

```python
import math

import jax
import jax.numpy as jnp
from jax import lax
from jax.experimental import pallas as pl
from jax.experimental.pallas import tpu as pltpu
from jax.sharding import PartitionSpec as P

ITERS = 4
PHASES = 4
FIELDS = 5
DEPTH = ITERS
LANE_STEP = 2 * DEPTH + 1
UNROLL = 6
GROUP = 4

VMEM = pl.BlockSpec(memory_space=pltpu.VMEM)
HBM = pl.BlockSpec(memory_space=pltpu.HBM)


def z_up(a):
    return pltpu.roll(a, a.shape[-2] - 1, a.ndim - 2)


def z_down(a):
    return pltpu.roll(a, 1, a.ndim - 2)


def y_up(a):
    return pltpu.roll(a, a.shape[-1] - 1, a.ndim - 1)


def y_down(a):
    return pltpu.roll(a, 1, a.ndim - 1)


def reciprocal(a):
    r = pl.reciprocal(a, approx=True)
    return r * (2.0 - a * r)


def iota(shape, axis):
    return lax.broadcasted_iota(jnp.int32, shape, axis)


def odd(axis):
    return lax.rem(lax.axis_index(axis), 2) == 1


def by_parity(axis, pair, body):
    pl.when(jnp.logical_not(odd(axis)))(lambda: body(pair[0], pair[1]))
    pl.when(odd(axis))(lambda: body(pair[1], pair[0]))


def start_copies(sources, targets, sems):
    copies = []
    for g in range(sources[0].shape[0] // GROUP):
        at = pl.ds(g * GROUP, GROUP)
        copies.append(
            [pltpu.make_async_copy(a.at[at], b.at[at], sems.at[g, f]) for f, (a, b) in enumerate(zip(sources, targets))]
        )
        for copy in copies[-1]:
            copy.start()
    return copies


def clean_group(g, field_ref, phase_ref):
    bx, bz, by = phase_ref.shape
    ix, iz, iy = lax.axis_index("gx"), lax.axis_index("gz"), lax.axis_index("gy")
    plane, row, lane = (iota((GROUP, bz, by), d) for d in range(3))
    at = pl.ds(g * GROUP, GROUP)
    vx, vz, vy, p = (field_ref[f, at] for f in range(FIELDS - 1))
    if g == 0:
        vx = jnp.where((plane > 0) | (ix > 0), vx, 0.0)
    vz = jnp.where((row > 0) | (iz > 0), vz, 0.0)
    vy = jnp.where((lane > 0) | (iy > 0), vy, 0.0)
    return vx, vz, vy, p, phase_ref[at].astype(jnp.float32)


def add_edge(edge, a, base):
    by = edge.shape[-1]
    lane = iota((1,) * (edge.ndim - 1) + (by,), edge.ndim - 1)
    first = pltpu.roll(a, base, a.ndim - 1) if base else a
    edge = jnp.where((lane >= base) & (lane <= base + DEPTH), first, edge)
    last = pltpu.roll(a, (base + LANE_STEP) % by, a.ndim - 1)
    return jnp.where((lane > base + DEPTH) & (lane < base + LANE_STEP), last, edge)


def add_edges(edge, fields, upper):
    for f, a in enumerate(fields):
        edge = add_edge(edge, a, edge.shape[-1] // 2 * upper + LANE_STEP * f)
    return edge


def beside(edge, f, upper):
    by = edge.shape[-1]
    iy = lax.axis_index("gy")
    lane = iota((1,) * (edge.ndim - 1) + (by,), edge.ndim - 1)
    right = (lane <= DEPTH) & (iy < lax.axis_size("gy") - 1)
    left = (lane >= by - DEPTH) & (iy > 0)
    shift = by // 2 * upper + LANE_STEP * f
    a = pltpu.roll(edge, by - shift, edge.ndim - 1) if shift else edge
    b = pltpu.roll(edge, (by - LANE_STEP - shift) % by, edge.ndim - 1)
    return jnp.where(right, a, jnp.where(left, b, 0.0))


def pack_kernel(
    vx_hbm, vz_hbm, vy_hbm, p_hbm, phase_hbm, scale_hbm, power_hbm, rho_hbm, edge_hbm, x_0_hbm, x_1_hbm, stack_hbm,
    field_ref, phase_ref, edge_ref, stack_ref, scale_ref, power_ref, rho_ref, sems, out_sems, table_sems,
):
    bx, bz, by = phase_ref.shape
    targets = [field_ref.at[f] for f in range(FIELDS - 1)] + [phase_ref]
    copies = start_copies((vx_hbm, vz_hbm, vy_hbm, p_hbm, phase_hbm), targets, sems)
    table_refs = (scale_ref, power_ref, rho_ref)
    pairs = zip((scale_hbm, power_hbm, rho_hbm), table_refs)
    table_copies = [pltpu.make_async_copy(a, b, table_sems.at[n]) for n, (a, b) in enumerate(pairs)]
    for copy in table_copies:
        copy.start()
    half = bx // GROUP // 2
    outs = []

    def out(source, target):
        outs.append(pltpu.make_async_copy(source, target, out_sems.at[len(outs)]))
        outs[-1].start()

    for g in range(half):
        edge = jnp.zeros((GROUP, bz, by), jnp.float32)
        for upper in range(2):
            at = (g + upper * half) * GROUP
            for copy in copies[g + upper * half]:
                copy.wait()
            fields = clean_group(g + upper * half, field_ref, phase_ref)
            for f, a in enumerate(fields):
                for i in range(GROUP):
                    stack_ref[(at + i) * FIELDS + f] = a[i]
            edge = add_edges(edge, fields, upper)
            at = pl.ds(at * FIELDS, GROUP * FIELDS)
            out(stack_ref.at[at], stack_hbm.at[at])
        at = pl.ds(g * GROUP, GROUP)
        edge_ref[at] = edge
        out(edge_ref.at[at], edge_hbm.at[at])
        stack_ref[pl.ds(bx * FIELDS + g * GROUP, GROUP)] = edge
    count = bx * FIELDS + bx // 2
    row = iota((bz, by), 0)
    for copy in table_copies:
        copy.wait()
    entries = [ref[index] for ref in table_refs for index in range(PHASES)]
    for n in range(2):
        tile = jnp.zeros((bz, by), jnp.float32)
        for r, entry in enumerate(entries[n * bz : (n + 1) * bz]):
            tile = jnp.where(row == r, entry, tile)
        stack_ref[count + n] = tile
    at = pl.ds(bx * FIELDS, count + 2 - bx * FIELDS)
    out(stack_ref.at[at], stack_hbm.at[at])
    count = x_0_hbm.shape[0]
    down, up = stack_ref.at[pl.ds(0, count)], stack_ref.at[pl.ds(bx * FIELDS - count, count)]
    sem = out_sems.at[len(outs)], out_sems.at[len(outs) + 1]

    def send(to_above, to_below):
        pair = pltpu.make_async_copy(up, to_above, sem[0]), pltpu.make_async_copy(down, to_below, sem[1])
        for copy in pair:
            copy.start()
        for copy in pair:
            copy.wait()

    by_parity("gx", (x_0_hbm, x_1_hbm), send)
    for copy in outs:
        copy.wait()


def x_neighbours():
    ix = lax.axis_index("gx")
    return ix < lax.axis_size("gx") - 1, ix > 0


def side_edge_kernel(x_1_ref, x_0_ref, own_edge_ref, edge_ref):
    bz, by = edge_ref.shape[1:]
    own = own_edge_ref.shape[0]
    edge_ref[0:own] = own_edge_ref[...]

    def body(above, below):
        edge = jnp.zeros((DEPTH, bz, by), jnp.float32)
        inside = x_neighbours()
        for upper, (ref, at) in enumerate(((above, 0), (below, 1))):
            block = ref[pl.ds(at, DEPTH * FIELDS)].reshape(DEPTH, FIELDS, bz, by)
            block = jnp.where(inside[upper], block, 0.0)
            edge = add_edges(edge, [block[:, f] for f in range(FIELDS)], upper)
        edge_ref[own:] = edge
        vx = jnp.where(inside[0], above[DEPTH * FIELDS], 0.0)
        edge_ref[own] = add_edge(edge[0], vx, FIELDS * LANE_STEP)

    by_parity("gx", (x_0_ref, x_1_ref), body)


def half_rows(tiles, swap):
    down = odd("gz") if swap == 0 else jnp.logical_not(odd("gz"))
    half = tiles.shape[-2] // 2
    return jnp.where(down, tiles[..., :half, :], tiles[..., half:, :])


def store_next_rows(refs, at, tiles):
    half = tiles.shape[-2] // 2
    for ref in refs:
        for i in range(tiles.shape[0]):
            ref[at + i // half, i % half : i % half + 1, :] = tiles[i, half : half + 1, :]


def sides_kernel(x_1_ref, x_0_ref, _edge_ref, sides_ref, z_0_ref, z_1_ref):
    count = DEPTH * FIELDS
    bz, by = sides_ref.shape[1:]

    def body(above, below):
        inside = x_neighbours()
        sides_ref[0:count] = jnp.where(inside[0], above[0:count], 0.0)
        sides_ref[count : 2 * count] = jnp.where(inside[1], below[1 : count + 1], 0.0)
        sides_ref[2 * count] = jnp.where(inside[0], above[count], 0.0)

    by_parity("gx", (x_0_ref, x_1_ref), body)
    tiles = sides_ref[...]
    for swap, ref in enumerate((z_0_ref, z_1_ref)):
        ref[0 : 2 * count + 1] = half_rows(tiles, swap)
    vz = tiles[0 : 2 * count].reshape(2 * DEPTH, FIELDS, bz, by)[:, 1]
    store_next_rows((z_0_ref, z_1_ref), 2 * count + 1, vz)


def edge_rows_kernel(edge_ref, z_0_ref, z_1_ref):
    tiles = edge_ref[...]
    for swap, ref in enumerate((z_0_ref, z_1_ref)):
        ref[0 : tiles.shape[0]] = half_rows(tiles, swap)
    store_next_rows((z_0_ref, z_1_ref), tiles.shape[0], tiles)


def lookups(fields, ok, keep, table_ref):
    *rest, phase = fields
    if ok is not True:
        rest = [jnp.where(ok, a, 0.0) for a in rest]
    for number in range(3):
        rows = [divmod(number * PHASES + index, table_ref.shape[1]) for index in range(PHASES)]
        table = [table_ref[n, r : r + 1, :] for n, r in rows]
        value = jnp.broadcast_to(table[0], phase.shape)
        for index in range(1, PHASES):
            value = jnp.where(phase == float(index), table[index], value)
        if number == 0:
            value = value * jnp.where(ok, 1.0, 0.0)
            if keep is not None:
                value = jnp.where(keep, value, 0.0)
        elif number == 1:
            value = (0.5 / math.log(2.0)) * (reciprocal(value) - 1.0)
        rest.append(value)
    return rest


def own_lanes(block, ok, tables):
    block = block.reshape(-1, FIELDS, *block.shape[-2:])
    return lookups([block[:, f] for f in range(FIELDS)], ok, None, tables)


def edge_lanes(edge, upper, ok, tables):
    by = edge.shape[-1]
    iy = lax.axis_index("gy")
    lane = iota((1, 1, by), 2)
    keep = ((lane <= DEPTH) & (iy < lax.axis_size("gy") - 1)) | ((lane >= by - DEPTH) & (iy > 0))
    return lookups([beside(edge, f, upper) for f in range(FIELDS)], ok, keep, tables)


def store_to(refs):
    def store(planes, part, values):
        by = values[0].shape[-1]
        for ref, value in zip(refs, values):
            ref[planes, :, part * by : (part + 1) * by] = value

    return store


def unpack_own(load, bx, ok, tables, store):
    def group(g, carry):
        at = g * GROUP
        store(pl.ds(DEPTH + at, GROUP), 0, own_lanes(load(at * FIELDS, GROUP * FIELDS), ok, tables))
        return carry

    lax.fori_loop(0, bx // GROUP, group, 0)


def unpack_own_edges(load, bx, ok, tables, store):
    half = bx // 2
    for upper in range(2):

        def group(g, carry):
            at = g * GROUP
            values = edge_lanes(load(at, GROUP), upper, ok, tables)
            store(pl.ds(DEPTH + upper * half + at, GROUP), 1, values)
            return carry

        lax.fori_loop(0, half // GROUP, group, 0)


def side_places(bx):
    return zip((pl.ds(DEPTH + bx, DEPTH), pl.ds(0, DEPTH)), x_neighbours())


def unpack_sides(load, bx, ok, tables, store, vx_ref):
    count = DEPTH * FIELDS
    for n, (planes, inside) in enumerate(side_places(bx)):
        store(planes, 0, own_lanes(load(n * count, count), ok & inside, tables))
    vx = jnp.where(ok, load(2 * count, 1), 0.0)
    vx_ref[pl.ds(bx + 2 * DEPTH, 1), :, 0 : vx.shape[-1]] = vx


def unpack_side_edges(load, bx, ok, tables, store, vx_ref):
    half = bx // 2
    edge = load(half, DEPTH)
    for upper, (planes, inside) in enumerate(side_places(bx)):
        store(planes, 1, edge_lanes(edge, upper, ok & inside, tables))
    by = edge.shape[-1]
    vx_ref[pl.ds(bx + 2 * DEPTH, 1), :, by : 2 * by] = jnp.where(ok, beside(edge[0:1], FIELDS, 0), 0.0)


def own_kernel(stack_ref, z_0_ref, z_1_ref, edge_ref, tables_ref, v_ref, *rest):
    bx = v_ref.shape[1] - 2 * DEPTH - 1
    count = bx * FIELDS
    edge_ref[...] = stack_ref[count : count + bx // 2]
    tables_ref[...] = stack_ref[count + bx // 2 :]
    size = GROUP * FIELDS

    def group(g, carry):
        at = pl.ds(g * size, size)
        tiles = stack_ref[at]
        for swap, ref in enumerate((z_0_ref, z_1_ref)):
            ref[at] = half_rows(tiles, swap)
        return carry

    lax.fori_loop(0, bx // GROUP, group, 0)
    for g in range(bx // GROUP):
        vz = stack_ref[pl.ds(g * size, size)].reshape(GROUP, FIELDS, *stack_ref.shape[1:])[:, 1]
        store_next_rows((z_0_ref, z_1_ref), count + g * GROUP // (stack_ref.shape[1] // 2), vz)
    store = store_to([v_ref.at[d] for d in range(3)] + list(rest))
    unpack_own(lambda at, n: stack_ref[pl.ds(at, n)], bx, True, tables_ref, store)


def own_sides_kernel(sides_ref, edge_ref, tables_ref, *refs):
    v_ref, *rest = refs[len(refs) // 2 :]
    bx = v_ref.shape[1] - 2 * DEPTH - 1
    store = store_to([v_ref.at[d] for d in range(3)] + list(rest))
    unpack_sides(lambda at, n: sides_ref[pl.ds(at, n)], bx, True, tables_ref, store, v_ref.at[0])
    load = lambda at, n: edge_ref[pl.ds(at, n)]
    unpack_own_edges(load, bx, True, tables_ref, store)
    unpack_side_edges(load, bx, True, tables_ref, store, v_ref.at[0])


def rows_in_grid(bz):
    iz = lax.axis_index("gz")
    row = iota((1, bz, 1), 1)
    return ((row < bz // 2) & (iz < lax.axis_size("gz") - 1)) | ((row >= bz // 2) & (iz > 0))


def load_both(above, below):
    return lambda at, n: jnp.concatenate([above[pl.ds(at, n)], below[pl.ds(at, n)]], axis=1)


def halo_kernel(face_0_ref, face_1_ref, corner_0_ref, corner_1_ref, tables_ref, halo_ref, next_ref):
    half, by = face_0_ref.shape[1:]
    bz = 2 * half
    bx = halo_ref.shape[1] - 2 * DEPTH - 1
    ok = rows_in_grid(bz)
    store = store_to([halo_ref.at[n] for n in range(7)])

    def faces(above, below):
        unpack_own(load_both(above, below), bx, ok, tables_ref, store)
        for i in range(bx):
            n = i % half
            row = above[bx * FIELDS + i // half, n : n + 1, :]
            next_ref[DEPTH + i, half - 1 : half, 0:by] = jnp.where(ok[0, 0:1], row, 0.0)

    def corners(above, below):
        unpack_sides(load_both(above, below), bx, ok, tables_ref, store, halo_ref.at[0])
        for i in range(2 * DEPTH):
            n = i % half
            to = DEPTH + bx + i if i < DEPTH else i - DEPTH
            row = above[2 * DEPTH * FIELDS + 1 + i // half, n : n + 1, :]
            next_ref[to, half - 1 : half, 0:by] = jnp.where(ok[0, 0:1], row, 0.0)

    by_parity("gz", (face_0_ref, face_1_ref), faces)
    by_parity("gz", (corner_0_ref, corner_1_ref), corners)


def unpack_halo_edges(edge_0_ref, edge_1_ref, tables_ref, halo_ref, next_ref):
    half, by = edge_0_ref.shape[1:]
    bx = halo_ref.shape[1] - 2 * DEPTH - 1
    ok = rows_in_grid(2 * half)
    store = store_to([halo_ref.at[n] for n in range(7)])
    tiles = bx // 2 + DEPTH

    def body(above, below):
        load = load_both(above, below)
        unpack_own_edges(load, bx, ok, tables_ref, store)
        unpack_side_edges(load, bx, ok, tables_ref, store, halo_ref.at[0])
        for n in range(tiles // half):
            rows = above[tiles + n]
            for upper in range(2):
                values = jnp.where(ok[0, 0:1], beside(rows, 1, upper), 0.0)
                for i in range(half):
                    tile = n * half + i
                    if tile < bx // 2:
                        to = DEPTH + upper * (bx // 2) + tile
                    else:
                        to = tile - bx // 2 + (0 if upper else DEPTH + bx)
                    next_ref[to, half - 1 : half, by : 2 * by] = values[i : i + 1]

    by_parity("gz", (edge_0_ref, edge_1_ref), body)


def main_kernel(
    v_ref, p0_ref, pre_ref, power_field_ref, rho_ref, _halo, _next, edge_0_ref, edge_1_ref, tables_ref,
    out_vx_ref, out_vz_ref, out_vy_ref, out_p_ref, out_eta_ref, sum_ref, halo_ref, next_ref,
    va_ref, vb_ref, p_ref, weight_ref,
):
    bx, bz, by = out_p_ref.shape
    rows, lanes = 2 * bz, 2 * by
    nx, nz, ny = lax.axis_size("gx"), lax.axis_size("gz"), lax.axis_size("gy")
    ix, iz, iy = lax.axis_index("gx"), lax.axis_index("gz"), lax.axis_index("gy")
    unpack_halo_edges(edge_0_ref, edge_1_ref, tables_ref, halo_ref, next_ref)

    shape = (rows, lanes)
    r, c = iota(shape, 0), iota(shape, 1)
    zg = iz * bz + jnp.where(r < bz + bz // 2, r, r - rows)
    yg = iy * by + jnp.where(c <= by + DEPTH, c, c - lanes)
    filled = (c <= by + DEPTH) | (c >= lanes - DEPTH)
    inside = filled & (zg >= 0) & (zg < nz * bz) & (yg >= 0) & (yg < ny * by)
    weight_ref[0] = jnp.where(inside, 0.05, 0.0)
    weight_ref[1] = jnp.where(inside & (zg > 0), 0.05, 0.0)
    weight_ref[2] = jnp.where(inside & (yg > 0), 0.05, 0.0)
    weight_ref[3] = jnp.where(inside, 0.0, 1.0)

    def with_halo(own, n, planes):
        return jnp.concatenate([own[planes], halo_ref[n, planes]], axis=1)

    for k in range(1, ITERS + 1):
        old, new = (va_ref, vb_ref) if k % 2 else (vb_ref, va_ref)
        last = k == ITERS

        def load(d, j, count):
            planes = pl.ds(j, count)
            return with_halo(v_ref.at[d], d, planes) if k == 1 else old[d, planes]

        def cells(j, count):
            planes = pl.ds(j, count)
            vx1 = load(0, j, count + 1)
            vx = vx1[:count]
            vz, vy = load(1, j, count), load(2, j, count)
            p = with_halo(p0_ref, 3, planes) if k == 1 else p_ref[planes]
            up = z_up(vz)
            if k == 1:
                after = next_ref[planes]
                after = jnp.concatenate([after, after], axis=1)
                up = jnp.where(iota((1, rows, lanes), 1) == bz + bz // 2 - 1, after, up)
            rx = vx1[1:] - vx
            rz = up - vz
            ry = y_up(vy) - vy
            a = rx - ry
            b = ry - rz
            inv = (a * (a + b) + b * b) * (1.0 / 3.0) + 1.0
            eta = with_halo(pre_ref, 4, planes) * jnp.exp2(with_halo(power_field_ref, 5, planes) * jnp.log(inv))
            quarter = 0.25 * eta
            div = rx + ry + rz
            p = p - quarter * (div + div)
            tx, tz, ty = eta * rx - p, eta * rz - p, eta * ry - p
            sz = quarter + z_down(quarter)
            sy = quarter + y_down(quarter)
            return vx, vz, vy, eta, p, quarter, tx, tz, ty, sz, sy

        def chunk(j, count, carry=None, final=False):
            if carry is None:
                below = cells(j - 1, count + 1)
                if not last:
                    p_ref[pl.ds(j - 1, 1)] = below[4][:1]
                vx, vz, vy, eta, p, quarter, tx, tz, ty, sz, sy = (a[1:] for a in below)
                join = lambda n, a: below[n][:-1]
            else:
                vx, vz, vy, eta, p, quarter, tx, tz, ty, sz, sy = cells(j, count)
                first = {1: load(1, j - 1, 1), 2: load(2, j - 1, 1), 5: carry[0], 6: carry[1], 9: carry[2], 10: carry[3]}
                join = lambda n, a: jnp.concatenate([first[n], a[:-1]], axis=0)
            planes = pl.ds(j, count)
            bias = weight_ref[3:4]
            sx = quarter + join(5, quarter)
            exz = sz + join(9, sz)
            exy = sy + join(10, sy)
            ezy = sz + y_down(sz)
            fxz = exz * (vx - z_down(vx))
            fxy = exy * (vx - y_down(vx))
            low_vz, low_vy = join(1, vz), join(2, vy)
            gzx = exz * (vz - low_vz)
            hyx = exy * (vy - low_vy)
            gzy = ezy * (vz - y_down(vz))
            hyz = ezy * (vy - z_down(vy))
            res_x = (tx - join(6, tx)) + ((z_up(fxz) - fxz) + (y_up(fxy) - fxy))
            new_vx = vx + weight_ref[0:1] * reciprocal(sx + bias) * res_x
            part_z = (tz - z_down(tz)) - with_halo(rho_ref, 6, planes) + ((y_up(gzy) - gzy) - gzx)
            part_y = (ty - y_down(ty)) + ((z_up(hyz) - hyz) - hyx)
            scale_z = weight_ref[1:2] * reciprocal(sz + bias)
            scale_y = weight_ref[2:3] * reciprocal(sy + bias)

            def lower(n, a):
                return a[:-1] if carry is None else jnp.concatenate([carry[n], a[:-1]], axis=0)

            skip = 1 if carry is None else 0
            new_vz = low_vz[skip:] + lower(6, scale_z) * (lower(4, part_z) + gzx[skip:])
            new_vy = low_vy[skip:] + lower(7, scale_y) * (lower(5, part_y) + hyx[skip:])
            at = pl.ds(j - 1 + skip - (DEPTH if last else 0), count - skip)
            if last:
                own = count - 1 if final else count
                here = pl.ds(j - DEPTH, own)
                out_vx_ref[here] = new_vx[:own, 0:bz, 0:by]
                out_p_ref[here] = p[:own, 0:bz, 0:by]
                out_eta_ref[here] = eta[:own, 0:bz, 0:by]
                sum_ref[...] += jnp.sum(p[:own, 0:bz, 0:by], axis=0)
                out_vz_ref[at] = new_vz[:, 0:bz, 0:by]
                out_vy_ref[at] = new_vy[:, 0:bz, 0:by]
            else:
                p_ref[planes] = p
                new[0, planes] = new_vx
                new[1, at] = new_vz
                new[2, at] = new_vy
            return tuple(a[-1:] for a in (quarter, tx, sz, sy, part_z, part_y, scale_z, scale_y))

        first, end = k, bx + 2 * DEPTH - k
        if last:
            sum_ref[...] = jnp.zeros((bz, by), jnp.float32)
        count = end - first + 1
        steps = (count - 2) // UNROLL
        start = count - steps * UNROLL
        carry = chunk(first, start)
        loops = steps - 1 if last else steps
        carry = lax.fori_loop(
            0, loops, lambda s, carry: chunk(first + start + s * UNROLL, UNROLL, carry), carry
        )
        if last:
            chunk(end + 1 - UNROLL, UNROLL, carry, final=True)

            @pl.when(ix == 0)
            def _():
                out_vx_ref[0] = jnp.zeros((bz, by), jnp.float32)
        else:
            plane = jnp.zeros((rows, lanes), jnp.float32)

            @pl.when(ix == 0)
            def _():
                for i in range(first, DEPTH):
                    for d in range(3):
                        new[d, i] = plane
                new[0, DEPTH] = plane

            @pl.when(ix == nx - 1)
            def _():
                for i in range(DEPTH + bx, end + 1):
                    for d in range(3):
                        new[d, i] = plane


def final_kernel(p_ref, sum_ref, out_ref, *, cells):
    mean = jnp.sum(sum_ref[...]) * (1.0 / cells)
    out_ref[...] = p_ref[...] - mean


def swap(a, axis, start):
    count = lax.axis_size(axis)
    partner = {i: i for i in range(count)}
    for i in range(start, count - 1, 2):
        partner[i], partner[i + 1] = i + 1, i
    return lax.ppermute(a, axis, list(partner.items()))


def sum_everywhere(total):
    axes = ("gx", "gy", "gz")
    devices = math.prod(lax.axis_size(a) for a in axes)
    total = total + lax.ppermute(total, axes, [(i, i ^ 1) for i in range(devices)])
    total = jnp.broadcast_to(jnp.sum(total, axis=0, keepdims=True), (devices // 2, total.shape[1]))
    groups = [list(range(n, devices, 2)) for n in range(2)]
    return lax.all_to_all(total, axes, 0, 0, tiled=True, axis_index_groups=groups)


def local(vel_x, vel_y, vel_z, pressure, phase, visc_scale, power_n, density):
    bx, bz, by = pressure.shape
    assert bx % (2 * GROUP) == 0 and bz == 2 * DEPTH and DEPTH == GROUP
    f32 = jnp.float32
    iy, ny = lax.axis_index("gy"), lax.axis_size("gy")
    cells = bx * bz * by * math.prod(lax.axis_size(a) for a in ("gx", "gz", "gy"))
    deep = bx + 2 * DEPTH + 1
    rows, lanes = 2 * bz, 2 * by
    shape = lambda *dims: jax.ShapeDtypeStruct(dims, f32)
    block = shape(bx, bz, by)
    scratch = lambda *dims: pltpu.VMEM(dims, f32)
    limit = lambda mebibytes: pltpu.CompilerParams(vmem_limit_bytes=mebibytes * 1024 * 1024)
    groups = bx // GROUP
    stacked = bx * FIELDS + bx // 2 + 2
    sent = shape(DEPTH * FIELDS + 1, bz, by)
    edge, x_0, x_1, stack = pl.pallas_call(
        pack_kernel,
        out_shape=(shape(bx // 2, bz, by), sent, sent, shape(stacked, bz, by)),
        in_specs=[HBM] * 8,
        out_specs=(HBM,) * 4,
        scratch_shapes=[
            scratch(FIELDS - 1, bx, bz, by),
            pltpu.VMEM((bx, bz, by), jnp.int32),
            scratch(bx // 2, bz, by),
            scratch(stacked, bz, by),
            pltpu.SMEM((PHASES,), f32),
            pltpu.SMEM((PHASES,), f32),
            pltpu.SMEM((PHASES,), f32),
            pltpu.SemaphoreType.DMA((groups, FIELDS)),
            pltpu.SemaphoreType.DMA((groups + groups // 2 + 3,)),
            pltpu.SemaphoreType.DMA((3,)),
        ],
        compiler_params=limit(58),
    )(vel_x, vel_z, vel_y, pressure, phase, visc_scale, power_n, density)

    def edges_beside(edge):
        side = swap(edge, "gy", 0)
        if ny == 2:
            return side
        lane = iota(side.shape, 2) % (by // 2) % LANE_STEP
        return jnp.where((lane <= DEPTH) == (lax.rem(iy, 2) == 0), side, swap(edge, "gy", 1))

    estimate = lambda size: pl.CostEstimate(
        flops=4 * size * bz * by, bytes_accessed=size * bz * by * 4, transcendentals=0
    )

    def unpacking(kernel, tiles, out_shape, *args, aliases={}):
        return pl.pallas_call(
            kernel,
            out_shape=out_shape,
            in_specs=[VMEM] * len(args),
            out_specs=(VMEM,) * len(out_shape),
            input_output_aliases=aliases,
            compiler_params=limit(16),
            cost_estimate=estimate(13 * tiles),
        )(*args)

    field = shape(deep, bz, lanes)
    own_shape = (shape(3, deep, bz, lanes),) + (field,) * 4
    half = lambda tiles, planes: shape(tiles + planes // (bz // 2), bz // 2, by)
    x_1, x_0 = swap(x_1, "gx", 1), swap(x_0, "gx", 0)
    face = half(bx * FIELDS, bx)
    extra = (shape(bx // 2, bz, by), shape(2, bz, by))
    z_0, z_1, edge, tables, *own = unpacking(own_kernel, bx, (face, face) + extra + own_shape, stack)
    face_1, face_0 = swap(z_1, "gz", 1), swap(z_0, "gz", 0)

    tiles = bx // 2 + DEPTH
    edge = pl.pallas_call(
        side_edge_kernel,
        out_shape=shape(tiles, bz, by),
        in_specs=[VMEM] * 3,
        out_specs=VMEM,
        compiler_params=limit(4),
    )(x_1, x_0, edge)
    corner = half(2 * DEPTH * FIELDS + 1, 2 * DEPTH)
    sides, z_0, z_1 = pl.pallas_call(
        sides_kernel,
        out_shape=(shape(2 * DEPTH * FIELDS + 1, bz, by), corner, corner),
        in_specs=[VMEM] * 3,
        out_specs=(VMEM,) * 3,
        compiler_params=limit(4),
    )(x_1, x_0, edge)
    edge = edges_beside(edge)
    corner_1, corner_0 = swap(z_1, "gz", 1), swap(z_0, "gz", 0)
    z_0, z_1 = pl.pallas_call(
        edge_rows_kernel,
        out_shape=(half(tiles, tiles),) * 2,
        in_specs=[VMEM],
        out_specs=(VMEM,) * 2,
        compiler_params=limit(4),
        cost_estimate=estimate(100000),
    )(edge)
    edge_1, edge_0 = swap(z_1, "gz", 1), swap(z_0, "gz", 0)

    own = unpacking(
        own_sides_kernel, 2 * deep, own_shape, sides, edge, tables, *own, aliases={n + 3: n for n in range(5)}
    )
    halo = unpacking(
        halo_kernel, deep, (shape(7, deep, bz, lanes), field), face_0, face_1, corner_0, corner_1, tables
    )
    vx, vz, vy, p, eta, total, _, _ = pl.pallas_call(
        main_kernel,
        out_shape=(block,) * 5 + (shape(bz, by),) + tuple(shape(*a.shape) for a in halo),
        in_specs=[VMEM] * 10,
        out_specs=(VMEM,) * 8,
        input_output_aliases={5: 6, 6: 7},
        scratch_shapes=[
            scratch(3, deep, rows, lanes),
            scratch(3, deep, rows, lanes),
            scratch(deep, rows, lanes),
            scratch(4, rows, lanes),
        ],
        compiler_params=limit(32),
    )(*own, *halo, edge_0, edge_1, tables)

    total = sum_everywhere(total)
    p = pl.pallas_call(
        lambda *refs: final_kernel(*refs, cells=float(cells)),
        out_shape=block,
        in_specs=[VMEM] * 2,
        out_specs=VMEM,
        compiler_params=limit(4),
    )(p, total)
    return (vx, vy, vz, p, eta)


def solution(mesh):
    spec = P("gx", "gz", "gy")
    return jax.shard_map(
        local,
        mesh=mesh,
        in_specs=(spec,) * 5 + (P(),) * 3,
        out_specs=(spec,) * 5,
        check_vma=False,
    )
```

```python
import math

import jax
import jax.numpy as jnp
from jax import lax
from jax.experimental import pallas as pl
from jax.experimental.pallas import tpu as pltpu
from jax.sharding import PartitionSpec as P

ITERS = 4
PHASES = 4
FIELDS = 5
DEPTH = ITERS
LANE_STEP = 2 * DEPTH + 1
UNROLL = 8
GROUP = 4

VMEM = pl.BlockSpec(memory_space=pltpu.VMEM)
HBM = pl.BlockSpec(memory_space=pltpu.HBM)


def z_up(a):
    return pltpu.roll(a, a.shape[-2] - 1, a.ndim - 2)


def z_down(a):
    return pltpu.roll(a, 1, a.ndim - 2)


def y_up(a):
    return pltpu.roll(a, a.shape[-1] - 1, a.ndim - 1)


def y_down(a):
    return pltpu.roll(a, 1, a.ndim - 1)


def reciprocal(a):
    return pl.reciprocal(a, approx=True)


def iota(shape, axis):
    return lax.broadcasted_iota(jnp.int32, shape, axis)


def odd(axis):
    return lax.rem(lax.axis_index(axis), 2) == 1


def by_parity(axis, pair, body):
    pl.when(jnp.logical_not(odd(axis)))(lambda: body(pair[0], pair[1]))
    pl.when(odd(axis))(lambda: body(pair[1], pair[0]))


def start_copies(sources, targets, sems):
    copies = []
    for g in range(sources[0].shape[0] // GROUP):
        at = pl.ds(g * GROUP, GROUP)
        copies.append(
            [pltpu.make_async_copy(a.at[at], b.at[at], sems.at[g, f]) for f, (a, b) in enumerate(zip(sources, targets))]
        )
        for copy in copies[-1]:
            copy.start()
    return copies


def clean_group(g, field_ref, phase_ref):
    bx, bz, by = phase_ref.shape
    ix, iz, iy = lax.axis_index("gx"), lax.axis_index("gz"), lax.axis_index("gy")
    plane, row, lane = (iota((GROUP, bz, by), d) for d in range(3))
    at = pl.ds(g * GROUP, GROUP)
    vx, vz, vy, p = (field_ref[f, at] for f in range(FIELDS - 1))
    if g == 0:
        vx = jnp.where((plane > 0) | (ix > 0), vx, 0.0)
    vz = jnp.where((row > 0) | (iz > 0), vz, 0.0)
    vy = jnp.where((lane > 0) | (iy > 0), vy, 0.0)
    return vx, vz, vy, p, phase_ref[at].astype(jnp.float32)


def add_edge(edge, a, base):
    by = edge.shape[-1]
    lane = iota((1,) * (edge.ndim - 1) + (by,), edge.ndim - 1)
    first = pltpu.roll(a, base, a.ndim - 1) if base else a
    edge = jnp.where((lane >= base) & (lane <= base + DEPTH), first, edge)
    last = pltpu.roll(a, (base + LANE_STEP) % by, a.ndim - 1)
    return jnp.where((lane > base + DEPTH) & (lane < base + LANE_STEP), last, edge)


def add_edges(edge, fields, upper):
    for f, a in enumerate(fields):
        edge = add_edge(edge, a, edge.shape[-1] // 2 * upper + LANE_STEP * f)
    return edge


def beside(edge, f, upper):
    by = edge.shape[-1]
    iy = lax.axis_index("gy")
    lane = iota((1,) * (edge.ndim - 1) + (by,), edge.ndim - 1)
    right = (lane <= DEPTH) & (iy < lax.axis_size("gy") - 1)
    left = (lane >= by - DEPTH) & (iy > 0)
    shift = by // 2 * upper + LANE_STEP * f
    a = pltpu.roll(edge, by - shift, edge.ndim - 1) if shift else edge
    b = pltpu.roll(edge, (by - LANE_STEP - shift) % by, edge.ndim - 1)
    return jnp.where(right, a, jnp.where(left, b, 0.0))


def pack_kernel(
    vx_hbm, vz_hbm, vy_hbm, p_hbm, phase_hbm, scale_hbm, power_hbm, rho_hbm, edge_hbm, x_0_hbm, x_1_hbm, stack_hbm,
    field_ref, phase_ref, edge_ref, stack_ref, scale_ref, power_ref, rho_ref, sems, out_sems, table_sems,
):
    bx, bz, by = phase_ref.shape
    targets = [field_ref.at[f] for f in range(FIELDS - 1)] + [phase_ref]
    copies = start_copies((vx_hbm, vz_hbm, vy_hbm, p_hbm, phase_hbm), targets, sems)
    table_refs = (scale_ref, power_ref, rho_ref)
    pairs = zip((scale_hbm, power_hbm, rho_hbm), table_refs)
    table_copies = [pltpu.make_async_copy(a, b, table_sems.at[n]) for n, (a, b) in enumerate(pairs)]
    for copy in table_copies:
        copy.start()
    half = bx // GROUP // 2
    outs = []

    def out(source, target):
        outs.append(pltpu.make_async_copy(source, target, out_sems.at[len(outs)]))
        outs[-1].start()

    for g in range(half):
        edge = jnp.zeros((GROUP, bz, by), jnp.float32)
        for upper in range(2):
            at = (g + upper * half) * GROUP
            for copy in copies[g + upper * half]:
                copy.wait()
            fields = clean_group(g + upper * half, field_ref, phase_ref)
            for f, a in enumerate(fields):
                for i in range(GROUP):
                    stack_ref[(at + i) * FIELDS + f] = a[i]
            edge = add_edges(edge, fields, upper)
            at = pl.ds(at * FIELDS, GROUP * FIELDS)
            out(stack_ref.at[at], stack_hbm.at[at])
        at = pl.ds(g * GROUP, GROUP)
        edge_ref[at] = edge
        out(edge_ref.at[at], edge_hbm.at[at])
        stack_ref[pl.ds(bx * FIELDS + g * GROUP, GROUP)] = edge
    count = bx * FIELDS + bx // 2
    row = iota((bz, by), 0)
    for copy in table_copies:
        copy.wait()
    entries = [ref[index] for ref in table_refs for index in range(PHASES)]
    for n in range(2):
        tile = jnp.zeros((bz, by), jnp.float32)
        for r, entry in enumerate(entries[n * bz : (n + 1) * bz]):
            tile = jnp.where(row == r, entry, tile)
        stack_ref[count + n] = tile
    at = pl.ds(bx * FIELDS, count + 2 - bx * FIELDS)
    out(stack_ref.at[at], stack_hbm.at[at])
    count = x_0_hbm.shape[0]
    down, up = stack_ref.at[pl.ds(0, count)], stack_ref.at[pl.ds(bx * FIELDS - count, count)]
    sem = out_sems.at[len(outs)], out_sems.at[len(outs) + 1]

    def send(to_above, to_below):
        pair = pltpu.make_async_copy(up, to_above, sem[0]), pltpu.make_async_copy(down, to_below, sem[1])
        for copy in pair:
            copy.start()
        for copy in pair:
            copy.wait()

    by_parity("gx", (x_0_hbm, x_1_hbm), send)
    for copy in outs:
        copy.wait()


def side_edge_kernel(x_1_ref, x_0_ref, own_edge_ref, edge_ref):
    bz, by = edge_ref.shape[1:]
    own = own_edge_ref.shape[0]
    edge_ref[0:own] = own_edge_ref[...]

    def body(above, below):
        edge = jnp.zeros((DEPTH, bz, by), jnp.float32)
        for upper, (ref, at) in enumerate(((above, 0), (below, 1))):
            block = ref[pl.ds(at, DEPTH * FIELDS)].reshape(DEPTH, FIELDS, bz, by)
            edge = add_edges(edge, [block[:, f] for f in range(FIELDS)], upper)
        edge_ref[own:] = edge
        edge_ref[own] = add_edge(edge[0], above[DEPTH * FIELDS], FIELDS * LANE_STEP)

    by_parity("gx", (x_0_ref, x_1_ref), body)


def half_rows(tiles, swap):
    down = odd("gz") if swap == 0 else jnp.logical_not(odd("gz"))
    half = tiles.shape[-2] // 2
    return jnp.where(down, tiles[..., :half, :], tiles[..., half:, :])


def store_next_rows(refs, at, tiles):
    half = tiles.shape[-2] // 2
    for ref in refs:
        for i in range(tiles.shape[0]):
            ref[at + i // half, i % half : i % half + 1, :] = tiles[i, half : half + 1, :]


def sides_kernel(x_1_ref, x_0_ref, _edge_ref, sides_ref, z_0_ref, z_1_ref):
    count = DEPTH * FIELDS
    bz, by = sides_ref.shape[1:]

    def body(above, below):
        sides_ref[0:count] = above[0:count]
        sides_ref[count : 2 * count] = below[1 : count + 1]
        sides_ref[2 * count] = above[count]

    by_parity("gx", (x_0_ref, x_1_ref), body)
    tiles = sides_ref[...]
    for swap, ref in enumerate((z_0_ref, z_1_ref)):
        ref[0 : 2 * count + 1] = half_rows(tiles, swap)
    vz = tiles[0 : 2 * count].reshape(2 * DEPTH, FIELDS, bz, by)[:, 1]
    store_next_rows((z_0_ref, z_1_ref), 2 * count + 1, vz)


def edge_rows_kernel(edge_ref, z_0_ref, z_1_ref):
    tiles = edge_ref[...]
    for swap, ref in enumerate((z_0_ref, z_1_ref)):
        ref[0 : tiles.shape[0]] = half_rows(tiles, swap)
    store_next_rows((z_0_ref, z_1_ref), tiles.shape[0], tiles)


def lookups(fields, ok, keep, table_ref):
    *rest, phase = fields
    for number in range(3):
        rows = [divmod(number * PHASES + index, table_ref.shape[1]) for index in range(PHASES)]
        table = [table_ref[n, r : r + 1, :] for n, r in rows]
        value = jnp.broadcast_to(table[0], phase.shape)
        for index in range(1, PHASES):
            value = jnp.where(phase == float(index), table[index], value)
        if number == 0:
            value = value * jnp.where(ok, 1.0, 0.0)
            if keep is not None:
                value = jnp.where(keep, value, 0.0)
        elif number == 1:
            value = (0.5 / math.log(2.0)) * (reciprocal(value) - 1.0)
        rest.append(value)
    return rest


def own_lanes(block, ok, tables):
    block = block.reshape(-1, FIELDS, *block.shape[-2:])
    return lookups([block[:, f] for f in range(FIELDS)], ok, None, tables)


def edge_lanes(edge, upper, ok, tables):
    by = edge.shape[-1]
    iy = lax.axis_index("gy")
    lane = iota((1, 1, by), 2)
    keep = ((lane <= DEPTH) & (iy < lax.axis_size("gy") - 1)) | ((lane >= by - DEPTH) & (iy > 0))
    return lookups([beside(edge, f, upper) for f in range(FIELDS)], ok, keep, tables)


def store_to(refs):
    def store(planes, part, values):
        by = values[0].shape[-1]
        for ref, value in zip(refs, values):
            ref[planes, :, part * by : (part + 1) * by] = value

    return store


def unpack_own(load, bx, ok, tables, store):
    def group(g, carry):
        at = g * GROUP
        store(pl.ds(DEPTH + at, GROUP), 0, own_lanes(load(at * FIELDS, GROUP * FIELDS), ok, tables))
        return carry

    lax.fori_loop(0, bx // GROUP, group, 0)


def unpack_own_edges(load, bx, ok, tables, store):
    half = bx // 2
    for upper in range(2):

        def group(g, carry):
            at = g * GROUP
            values = edge_lanes(load(at, GROUP), upper, ok, tables)
            store(pl.ds(DEPTH + upper * half + at, GROUP), 1, values)
            return carry

        lax.fori_loop(0, half // GROUP, group, 0)


def side_places(bx):
    ix = lax.axis_index("gx")
    return (pl.ds(DEPTH + bx, DEPTH), ix < lax.axis_size("gx") - 1), (pl.ds(0, DEPTH), ix > 0)


def unpack_sides(load, bx, ok, tables, store, vx_ref):
    count = DEPTH * FIELDS
    for n, (planes, inside) in enumerate(side_places(bx)):
        store(planes, 0, own_lanes(load(n * count, count), ok & inside, tables))
    vx = load(2 * count, 1)
    vx_ref[pl.ds(bx + 2 * DEPTH, 1), :, 0 : vx.shape[-1]] = vx


def unpack_side_edges(load, bx, ok, tables, store, vx_ref):
    half = bx // 2
    edge = load(half, DEPTH)
    for upper, (planes, inside) in enumerate(side_places(bx)):
        store(planes, 1, edge_lanes(edge, upper, ok & inside, tables))
    by = edge.shape[-1]
    vx_ref[pl.ds(bx + 2 * DEPTH, 1), :, by : 2 * by] = beside(edge[0:1], FIELDS, 0)


def own_kernel(stack_ref, z_0_ref, z_1_ref, edge_ref, tables_ref, v_ref, *rest):
    bx = v_ref.shape[1] - 2 * DEPTH - 1
    count = bx * FIELDS
    edge_ref[...] = stack_ref[count : count + bx // 2]
    tables_ref[...] = stack_ref[count + bx // 2 :]
    size = GROUP * FIELDS

    def group(g, carry):
        at = pl.ds(g * size, size)
        tiles = stack_ref[at]
        for swap, ref in enumerate((z_0_ref, z_1_ref)):
            ref[at] = half_rows(tiles, swap)
        return carry

    lax.fori_loop(0, bx // GROUP, group, 0)
    for g in range(bx // GROUP):
        vz = stack_ref[pl.ds(g * size, size)].reshape(GROUP, FIELDS, *stack_ref.shape[1:])[:, 1]
        store_next_rows((z_0_ref, z_1_ref), count + g * GROUP // (stack_ref.shape[1] // 2), vz)
    store = store_to([v_ref.at[d] for d in range(3)] + list(rest))
    unpack_own(lambda at, n: stack_ref[pl.ds(at, n)], bx, True, tables_ref, store)


def own_sides_kernel(sides_ref, edge_ref, tables_ref, *refs):
    v_ref, *rest = refs[len(refs) // 2 :]
    bx = v_ref.shape[1] - 2 * DEPTH - 1
    store = store_to([v_ref.at[d] for d in range(3)] + list(rest))
    unpack_sides(lambda at, n: sides_ref[pl.ds(at, n)], bx, True, tables_ref, store, v_ref.at[0])
    load = lambda at, n: edge_ref[pl.ds(at, n)]
    unpack_own_edges(load, bx, True, tables_ref, store)
    unpack_side_edges(load, bx, True, tables_ref, store, v_ref.at[0])


def rows_in_grid(bz):
    iz = lax.axis_index("gz")
    row = iota((1, bz, 1), 1)
    return ((row < bz // 2) & (iz < lax.axis_size("gz") - 1)) | ((row >= bz // 2) & (iz > 0))


def load_both(above, below):
    return lambda at, n: jnp.concatenate([above[pl.ds(at, n)], below[pl.ds(at, n)]], axis=1)


def halo_kernel(face_0_ref, face_1_ref, corner_0_ref, corner_1_ref, tables_ref, halo_ref, next_ref):
    half, by = face_0_ref.shape[1:]
    bz = 2 * half
    bx = halo_ref.shape[1] - 2 * DEPTH - 1
    ok = rows_in_grid(bz)
    store = store_to([halo_ref.at[n] for n in range(7)])

    def faces(above, below):
        unpack_own(load_both(above, below), bx, ok, tables_ref, store)
        for i in range(bx):
            n = i % half
            next_ref[DEPTH + i, half - 1 : half, 0:by] = above[bx * FIELDS + i // half, n : n + 1, :]

    def corners(above, below):
        unpack_sides(load_both(above, below), bx, ok, tables_ref, store, halo_ref.at[0])
        for i in range(2 * DEPTH):
            n = i % half
            to = DEPTH + bx + i if i < DEPTH else i - DEPTH
            next_ref[to, half - 1 : half, 0:by] = above[2 * DEPTH * FIELDS + 1 + i // half, n : n + 1, :]

    by_parity("gz", (face_0_ref, face_1_ref), faces)
    by_parity("gz", (corner_0_ref, corner_1_ref), corners)


def unpack_halo_edges(edge_0_ref, edge_1_ref, tables_ref, halo_ref, next_ref):
    half, by = edge_0_ref.shape[1:]
    bx = halo_ref.shape[1] - 2 * DEPTH - 1
    ok = rows_in_grid(2 * half)
    store = store_to([halo_ref.at[n] for n in range(7)])
    tiles = bx // 2 + DEPTH

    def body(above, below):
        load = load_both(above, below)
        unpack_own_edges(load, bx, ok, tables_ref, store)
        unpack_side_edges(load, bx, ok, tables_ref, store, halo_ref.at[0])
        for n in range(tiles // half):
            rows = above[tiles + n]
            for upper in range(2):
                values = beside(rows, 1, upper)
                for i in range(half):
                    tile = n * half + i
                    if tile < bx // 2:
                        to = DEPTH + upper * (bx // 2) + tile
                    else:
                        to = tile - bx // 2 + (0 if upper else DEPTH + bx)
                    next_ref[to, half - 1 : half, by : 2 * by] = values[i : i + 1]

    by_parity("gz", (edge_0_ref, edge_1_ref), body)


def main_kernel(
    v_ref, p0_ref, pre_ref, power_field_ref, rho_ref, _halo, _next, edge_0_ref, edge_1_ref, tables_ref,
    out_vx_ref, out_vz_ref, out_vy_ref, out_p_ref, out_eta_ref, sum_ref, halo_ref, next_ref,
    va_ref, vb_ref, p_ref, weight_ref,
):
    bx, bz, by = out_p_ref.shape
    rows, lanes = 2 * bz, 2 * by
    nx, nz, ny = lax.axis_size("gx"), lax.axis_size("gz"), lax.axis_size("gy")
    ix, iz, iy = lax.axis_index("gx"), lax.axis_index("gz"), lax.axis_index("gy")
    unpack_halo_edges(edge_0_ref, edge_1_ref, tables_ref, halo_ref, next_ref)

    shape = (rows, lanes)
    r, c = iota(shape, 0), iota(shape, 1)
    zg = iz * bz + jnp.where(r < bz + bz // 2, r, r - rows)
    yg = iy * by + jnp.where(c <= by + DEPTH, c, c - lanes)
    filled = (c <= by + DEPTH) | (c >= lanes - DEPTH)
    inside = filled & (zg >= 0) & (zg < nz * bz) & (yg >= 0) & (yg < ny * by)
    weight_ref[0] = jnp.where(inside, 0.05, 0.0)
    weight_ref[1] = jnp.where(inside & (zg > 0), 0.05, 0.0)
    weight_ref[2] = jnp.where(inside & (yg > 0), 0.05, 0.0)
    weight_ref[3] = jnp.where(inside, 0.0, 1.0)

    def with_halo(own, n, planes):
        return jnp.concatenate([own[planes], halo_ref[n, planes]], axis=1)

    for k in range(1, ITERS + 1):
        old, new = (va_ref, vb_ref) if k % 2 else (vb_ref, va_ref)
        last = k == ITERS

        def load(d, j, count):
            planes = pl.ds(j, count)
            return with_halo(v_ref.at[d], d, planes) if k == 1 else old[d, planes]

        def cells(j, count):
            planes = pl.ds(j, count)
            vx1 = load(0, j, count + 1)
            vx = vx1[:count]
            vz, vy = load(1, j, count), load(2, j, count)
            p = with_halo(p0_ref, 3, planes) if k == 1 else p_ref[planes]
            up = z_up(vz)
            if k == 1:
                after = next_ref[planes]
                after = jnp.concatenate([after, after], axis=1)
                up = jnp.where(iota((1, rows, lanes), 1) == bz + bz // 2 - 1, after, up)
            rx = vx1[1:] - vx
            rz = up - vz
            ry = y_up(vy) - vy
            a = rx - ry
            b = ry - rz
            inv = (a * (a + b) + b * b) * (1.0 / 3.0) + 1.0
            eta = with_halo(pre_ref, 4, planes) * jnp.exp2(with_halo(power_field_ref, 5, planes) * jnp.log(inv))
            quarter = 0.25 * eta
            div = rx + ry + rz
            p = p - quarter * (div + div)
            tx, tz, ty = eta * rx - p, eta * rz - p, eta * ry - p
            sz = quarter + z_down(quarter)
            sy = quarter + y_down(quarter)
            return vx, vz, vy, eta, p, quarter, tx, tz, ty, sz, sy

        def chunk(j, count, carry=None, final=False):
            if carry is None:
                below = cells(j - 1, count + 1)
                if not last:
                    p_ref[pl.ds(j - 1, 1)] = below[4][:1]
                vx, vz, vy, eta, p, quarter, tx, tz, ty, sz, sy = (a[1:] for a in below)
                join = lambda n, a: below[n][:-1]
            else:
                vx, vz, vy, eta, p, quarter, tx, tz, ty, sz, sy = cells(j, count)
                first = {1: load(1, j - 1, 1), 2: load(2, j - 1, 1), 5: carry[0], 6: carry[1], 9: carry[2], 10: carry[3]}
                join = lambda n, a: jnp.concatenate([first[n], a[:-1]], axis=0)
            planes = pl.ds(j, count)
            bias = weight_ref[3:4]
            sx = quarter + join(5, quarter)
            exz = sz + join(9, sz)
            exy = sy + join(10, sy)
            ezy = sz + y_down(sz)
            fxz = exz * (vx - z_down(vx))
            fxy = exy * (vx - y_down(vx))
            low_vz, low_vy = join(1, vz), join(2, vy)
            gzx = exz * (vz - low_vz)
            hyx = exy * (vy - low_vy)
            gzy = ezy * (vz - y_down(vz))
            hyz = ezy * (vy - z_down(vy))
            res_x = (tx - join(6, tx)) + ((z_up(fxz) - fxz) + (y_up(fxy) - fxy))
            new_vx = vx + weight_ref[0:1] * reciprocal(sx + bias) * res_x
            part_z = (tz - z_down(tz)) - with_halo(rho_ref, 6, planes) + ((y_up(gzy) - gzy) - gzx)
            part_y = (ty - y_down(ty)) + ((z_up(hyz) - hyz) - hyx)
            scale_z = weight_ref[1:2] * reciprocal(sz + bias)
            scale_y = weight_ref[2:3] * reciprocal(sy + bias)

            def lower(n, a):
                return a[:-1] if carry is None else jnp.concatenate([carry[n], a[:-1]], axis=0)

            skip = 1 if carry is None else 0
            new_vz = low_vz[skip:] + lower(6, scale_z) * (lower(4, part_z) + gzx[skip:])
            new_vy = low_vy[skip:] + lower(7, scale_y) * (lower(5, part_y) + hyx[skip:])
            at = pl.ds(j - 1 + skip - (DEPTH if last else 0), count - skip)
            if last:
                own = count - 1 if final else count
                here = pl.ds(j - DEPTH, own)
                out_vx_ref[here] = new_vx[:own, 0:bz, 0:by]
                out_p_ref[here] = p[:own, 0:bz, 0:by]
                out_eta_ref[here] = eta[:own, 0:bz, 0:by]
                sum_ref[...] += jnp.sum(p[:own, 0:bz, 0:by], axis=0)
                out_vz_ref[at] = new_vz[:, 0:bz, 0:by]
                out_vy_ref[at] = new_vy[:, 0:bz, 0:by]
            else:
                p_ref[planes] = p
                new[0, planes] = new_vx
                new[1, at] = new_vz
                new[2, at] = new_vy
            return tuple(a[-1:] for a in (quarter, tx, sz, sy, part_z, part_y, scale_z, scale_y))

        first, end = k, bx + 2 * DEPTH - k
        if last:
            sum_ref[...] = jnp.zeros((bz, by), jnp.float32)
        count = end - first + 1
        steps = (count - 2) // UNROLL
        start = count - steps * UNROLL
        carry = chunk(first, start)
        loops = steps - 1 if last else steps
        carry = lax.fori_loop(
            0, loops, lambda s, carry: chunk(first + start + s * UNROLL, UNROLL, carry), carry
        )
        if last:
            chunk(end + 1 - UNROLL, UNROLL, carry, final=True)

            @pl.when(ix == 0)
            def _():
                out_vx_ref[0] = jnp.zeros((bz, by), jnp.float32)
        else:
            plane = jnp.zeros((rows, lanes), jnp.float32)

            @pl.when(ix == 0)
            def _():
                for i in range(first, DEPTH):
                    for d in range(3):
                        new[d, i] = plane
                new[0, DEPTH] = plane

            @pl.when(ix == nx - 1)
            def _():
                for i in range(DEPTH + bx, end + 1):
                    for d in range(3):
                        new[d, i] = plane


def final_kernel(p_ref, sum_ref, out_ref, *, cells):
    mean = jnp.sum(sum_ref[...]) * (1.0 / cells)
    out_ref[...] = p_ref[...] - mean


def swap(a, axis, start):
    count = lax.axis_size(axis)
    return lax.ppermute(a, axis, [(i, j) for k in range(start, count - 1, 2) for i, j in ((k, k + 1), (k + 1, k))])


def sum_everywhere(total):
    axes = ("gx", "gy", "gz")
    devices = math.prod(lax.axis_size(a) for a in axes)
    total = total + lax.ppermute(total, axes, [(i, i ^ 1) for i in range(devices)])
    total = jnp.broadcast_to(jnp.sum(total, axis=0, keepdims=True), (devices // 2, total.shape[1]))
    groups = [list(range(n, devices, 2)) for n in range(2)]
    return lax.all_to_all(total, axes, 0, 0, tiled=True, axis_index_groups=groups)


def local(vel_x, vel_y, vel_z, pressure, phase, visc_scale, power_n, density):
    bx, bz, by = pressure.shape
    assert bx % (2 * GROUP) == 0 and bz == 2 * DEPTH and DEPTH == GROUP
    f32 = jnp.float32
    iy, ny = lax.axis_index("gy"), lax.axis_size("gy")
    cells = bx * bz * by * math.prod(lax.axis_size(a) for a in ("gx", "gz", "gy"))
    deep = bx + 2 * DEPTH + 1
    rows, lanes = 2 * bz, 2 * by
    shape = lambda *dims: jax.ShapeDtypeStruct(dims, f32)
    block = shape(bx, bz, by)
    scratch = lambda *dims: pltpu.VMEM(dims, f32)
    limit = lambda mebibytes: pltpu.CompilerParams(vmem_limit_bytes=mebibytes * 1024 * 1024)
    groups = bx // GROUP
    stacked = bx * FIELDS + bx // 2 + 2
    sent = shape(DEPTH * FIELDS + 1, bz, by)
    edge, x_0, x_1, stack = pl.pallas_call(
        pack_kernel,
        out_shape=(shape(bx // 2, bz, by), sent, sent, shape(stacked, bz, by)),
        in_specs=[HBM] * 8,
        out_specs=(HBM,) * 4,
        scratch_shapes=[
            scratch(FIELDS - 1, bx, bz, by),
            pltpu.VMEM((bx, bz, by), jnp.int32),
            scratch(bx // 2, bz, by),
            scratch(stacked, bz, by),
            pltpu.SMEM((PHASES,), f32),
            pltpu.SMEM((PHASES,), f32),
            pltpu.SMEM((PHASES,), f32),
            pltpu.SemaphoreType.DMA((groups, FIELDS)),
            pltpu.SemaphoreType.DMA((groups + groups // 2 + 3,)),
            pltpu.SemaphoreType.DMA((3,)),
        ],
        compiler_params=limit(58),
    )(vel_x, vel_z, vel_y, pressure, phase, visc_scale, power_n, density)

    def edges_beside(edge):
        side = swap(edge, "gy", 0)
        if ny == 2:
            return side
        lane = iota(side.shape, 2) % (by // 2) % LANE_STEP
        return jnp.where((lane <= DEPTH) == (lax.rem(iy, 2) == 0), side, swap(edge, "gy", 1))

    estimate = lambda size: pl.CostEstimate(
        flops=4 * size * bz * by, bytes_accessed=size * bz * by * 4, transcendentals=0
    )

    def unpacking(kernel, tiles, out_shape, *args, aliases={}):
        return pl.pallas_call(
            kernel,
            out_shape=out_shape,
            in_specs=[VMEM] * len(args),
            out_specs=(VMEM,) * len(out_shape),
            input_output_aliases=aliases,
            compiler_params=limit(16),
            cost_estimate=estimate(13 * tiles),
        )(*args)

    field = shape(deep, bz, lanes)
    own_shape = (shape(3, deep, bz, lanes),) + (field,) * 4
    half = lambda tiles, planes: shape(tiles + planes // (bz // 2), bz // 2, by)
    x_1, x_0 = swap(x_1, "gx", 1), swap(x_0, "gx", 0)
    face = half(bx * FIELDS, bx)
    extra = (shape(bx // 2, bz, by), shape(2, bz, by))
    z_0, z_1, edge, tables, *own = unpacking(own_kernel, bx, (face, face) + extra + own_shape, stack)
    face_1, face_0 = swap(z_1, "gz", 1), swap(z_0, "gz", 0)

    tiles = bx // 2 + DEPTH
    edge = pl.pallas_call(
        side_edge_kernel,
        out_shape=shape(tiles, bz, by),
        in_specs=[VMEM] * 3,
        out_specs=VMEM,
        compiler_params=limit(4),
    )(x_1, x_0, edge)
    corner = half(2 * DEPTH * FIELDS + 1, 2 * DEPTH)
    sides, z_0, z_1 = pl.pallas_call(
        sides_kernel,
        out_shape=(shape(2 * DEPTH * FIELDS + 1, bz, by), corner, corner),
        in_specs=[VMEM] * 3,
        out_specs=(VMEM,) * 3,
        compiler_params=limit(4),
    )(x_1, x_0, edge)
    edge = edges_beside(edge)
    corner_1, corner_0 = swap(z_1, "gz", 1), swap(z_0, "gz", 0)
    z_0, z_1 = pl.pallas_call(
        edge_rows_kernel,
        out_shape=(half(tiles, tiles),) * 2,
        in_specs=[VMEM],
        out_specs=(VMEM,) * 2,
        compiler_params=limit(4),
        cost_estimate=estimate(100000),
    )(edge)
    edge_1, edge_0 = swap(z_1, "gz", 1), swap(z_0, "gz", 0)

    own = unpacking(
        own_sides_kernel, 2 * deep, own_shape, sides, edge, tables, *own, aliases={n + 3: n for n in range(5)}
    )
    halo = unpacking(
        halo_kernel, deep, (shape(7, deep, bz, lanes), field), face_0, face_1, corner_0, corner_1, tables
    )
    vx, vz, vy, p, eta, total, _, _ = pl.pallas_call(
        main_kernel,
        out_shape=(block,) * 5 + (shape(bz, by),) + tuple(shape(*a.shape) for a in halo),
        in_specs=[VMEM] * 10,
        out_specs=(VMEM,) * 8,
        input_output_aliases={5: 6, 6: 7},
        scratch_shapes=[
            scratch(3, deep, rows, lanes),
            scratch(3, deep, rows, lanes),
            scratch(deep, rows, lanes),
            scratch(4, rows, lanes),
        ],
        compiler_params=limit(32),
    )(*own, *halo, edge_0, edge_1, tables)

    total = sum_everywhere(total)
    p = pl.pallas_call(
        lambda *refs: final_kernel(*refs, cells=float(cells)),
        out_shape=block,
        in_specs=[VMEM] * 2,
        out_specs=VMEM,
        compiler_params=limit(4),
    )(p, total)
    return (vx, vy, vz, p, eta)


def solution(mesh):
    spec = P("gx", "gz", "gy")
    return jax.shard_map(
        local,
        mesh=mesh,
        in_specs=(spec,) * 5 + (P(),) * 3,
        out_specs=(spec,) * 5,
        check_vma=False,
    )
```

```python
import math

import jax
import jax.numpy as jnp
from jax import lax
from jax.experimental import pallas as pl
from jax.experimental.pallas import tpu as pltpu
from jax.sharding import PartitionSpec as P

ITERS = 4
PHASES = 4
FIELDS = 5
DEPTH = ITERS
LANE_STEP = 2 * DEPTH + 1
UNROLL = 12
GROUP = 4

VMEM = pl.BlockSpec(memory_space=pltpu.VMEM)
HBM = pl.BlockSpec(memory_space=pltpu.HBM)


def z_up(a):
    return pltpu.roll(a, a.shape[-2] - 1, a.ndim - 2)


def z_down(a):
    return pltpu.roll(a, 1, a.ndim - 2)


def y_up(a):
    return pltpu.roll(a, a.shape[-1] - 1, a.ndim - 1)


def y_down(a):
    return pltpu.roll(a, 1, a.ndim - 1)


def reciprocal(a):
    return pl.reciprocal(a, approx=True)


def iota(shape, axis):
    return lax.broadcasted_iota(jnp.int32, shape, axis)


def odd(axis):
    return lax.rem(lax.axis_index(axis), 2) == 1


def by_parity(axis, pair, body):
    pl.when(jnp.logical_not(odd(axis)))(lambda: body(pair[0], pair[1]))
    pl.when(odd(axis))(lambda: body(pair[1], pair[0]))


def start_copies(sources, targets, sems):
    copies = []
    for g in range(sources[0].shape[0] // GROUP):
        at = pl.ds(g * GROUP, GROUP)
        copies.append(
            [pltpu.make_async_copy(a.at[at], b.at[at], sems.at[g, f]) for f, (a, b) in enumerate(zip(sources, targets))]
        )
        for copy in copies[-1]:
            copy.start()
    return copies


def clean_group(g, field_ref, phase_ref):
    bx, bz, by = phase_ref.shape
    ix, iz, iy = lax.axis_index("gx"), lax.axis_index("gz"), lax.axis_index("gy")
    plane, row, lane = (iota((GROUP, bz, by), d) for d in range(3))
    at = pl.ds(g * GROUP, GROUP)
    vx, vz, vy, p = (field_ref[f, at] for f in range(FIELDS - 1))
    if g == 0:
        vx = jnp.where((plane > 0) | (ix > 0), vx, 0.0)
    vz = jnp.where((row > 0) | (iz > 0), vz, 0.0)
    vy = jnp.where((lane > 0) | (iy > 0), vy, 0.0)
    return vx, vz, vy, p, phase_ref[at].astype(jnp.float32)


def add_edge(edge, a, base):
    by = edge.shape[-1]
    lane = iota((1,) * (edge.ndim - 1) + (by,), edge.ndim - 1)
    first = pltpu.roll(a, base, a.ndim - 1) if base else a
    edge = jnp.where((lane >= base) & (lane <= base + DEPTH), first, edge)
    last = pltpu.roll(a, (base + LANE_STEP) % by, a.ndim - 1)
    return jnp.where((lane > base + DEPTH) & (lane < base + LANE_STEP), last, edge)


def add_edges(edge, fields, upper):
    for f, a in enumerate(fields):
        edge = add_edge(edge, a, edge.shape[-1] // 2 * upper + LANE_STEP * f)
    return edge


def beside(edge, f, upper):
    by = edge.shape[-1]
    iy = lax.axis_index("gy")
    lane = iota((1,) * (edge.ndim - 1) + (by,), edge.ndim - 1)
    right = (lane <= DEPTH) & (iy < lax.axis_size("gy") - 1)
    left = (lane >= by - DEPTH) & (iy > 0)
    shift = by // 2 * upper + LANE_STEP * f
    a = pltpu.roll(edge, by - shift, edge.ndim - 1) if shift else edge
    b = pltpu.roll(edge, (by - LANE_STEP - shift) % by, edge.ndim - 1)
    return jnp.where(right, a, jnp.where(left, b, 0.0))


def pack_kernel(
    vx_hbm, vz_hbm, vy_hbm, p_hbm, phase_hbm, scale_hbm, power_hbm, rho_hbm, edge_hbm, x_0_hbm, x_1_hbm, stack_hbm,
    field_ref, phase_ref, edge_ref, stack_ref, scale_ref, power_ref, rho_ref, sems, out_sems, table_sems,
):
    bx, bz, by = phase_ref.shape
    targets = [field_ref.at[f] for f in range(FIELDS - 1)] + [phase_ref]
    copies = start_copies((vx_hbm, vz_hbm, vy_hbm, p_hbm, phase_hbm), targets, sems)
    table_refs = (scale_ref, power_ref, rho_ref)
    pairs = zip((scale_hbm, power_hbm, rho_hbm), table_refs)
    table_copies = [pltpu.make_async_copy(a, b, table_sems.at[n]) for n, (a, b) in enumerate(pairs)]
    for copy in table_copies:
        copy.start()
    groups = bx // GROUP
    half = groups // 2
    outs = []

    def out(source, target):
        outs.append(pltpu.make_async_copy(source, target, out_sems.at[len(outs)]))
        outs[-1].start()

    count = DEPTH * FIELDS
    sems_x = [out_sems.at[out_sems.shape[0] - 1 - n] for n in range(3)]

    def x_copies(to_above, to_below):
        return (
            pltpu.make_async_copy(stack_ref.at[pl.ds(0, count + 1)], to_below, sems_x[0]),
            pltpu.make_async_copy(stack_ref.at[pl.ds(0, 1)], to_above.at[pl.ds(0, 1)], sems_x[1]),
            pltpu.make_async_copy(
                stack_ref.at[pl.ds(bx * FIELDS - count, count)], to_above.at[pl.ds(1, count)], sems_x[2]
            ),
        )

    def start_x(above, below):
        for copy in x_copies(above, below):
            copy.start()

    def wait_x(above, below):
        for copy in x_copies(above, below):
            copy.wait()

    edges = {}
    order = [0, groups - 1] + list(range(1, groups - 1))
    for g in order:
        for copy in copies[g]:
            copy.wait()
        fields = clean_group(g, field_ref, phase_ref)
        for f, a in enumerate(fields):
            for i in range(GROUP):
                stack_ref[(g * GROUP + i) * FIELDS + f] = a[i]
        at = pl.ds(g * GROUP * FIELDS, GROUP * FIELDS)
        out(stack_ref.at[at], stack_hbm.at[at])
        if g == 1:
            by_parity("gx", (x_0_hbm, x_1_hbm), start_x)
        upper, n = divmod(g, half)
        edge = edges.get(n, jnp.zeros((GROUP, bz, by), jnp.float32))
        edges[n] = add_edges(edge, fields, upper)
        if n + half * (1 - upper) in order[: order.index(g)]:
            at = pl.ds(n * GROUP, GROUP)
            edge_ref[at] = edges[n]
            out(edge_ref.at[at], edge_hbm.at[at])
            stack_ref[pl.ds(bx * FIELDS + n * GROUP, GROUP)] = edges[n]
    end = bx * FIELDS + bx // 2
    row = iota((bz, by), 0)
    for copy in table_copies:
        copy.wait()
    entries = [ref[index] for ref in table_refs for index in range(PHASES)]
    for n in range(2):
        tile = jnp.zeros((bz, by), jnp.float32)
        for r, entry in enumerate(entries[n * bz : (n + 1) * bz]):
            tile = jnp.where(row == r, entry, tile)
        stack_ref[end + n] = tile
    at = pl.ds(bx * FIELDS, end + 2 - bx * FIELDS)
    out(stack_ref.at[at], stack_hbm.at[at])
    by_parity("gx", (x_0_hbm, x_1_hbm), wait_x)
    for copy in outs:
        copy.wait()


def side_edge_kernel(x_1_ref, x_0_ref, own_edge_ref, edge_ref):
    bz, by = edge_ref.shape[1:]
    own = own_edge_ref.shape[0]
    edge_ref[0:own] = own_edge_ref[...]

    def body(above, below):
        edge = jnp.zeros((DEPTH, bz, by), jnp.float32)
        for upper, (ref, at) in enumerate(((above, 0), (below, 1))):
            block = ref[pl.ds(at, DEPTH * FIELDS)].reshape(DEPTH, FIELDS, bz, by)
            edge = add_edges(edge, [block[:, f] for f in range(FIELDS)], upper)
        edge_ref[own:] = edge
        edge_ref[own] = add_edge(edge[0], above[DEPTH * FIELDS], FIELDS * LANE_STEP)

    by_parity("gx", (x_0_ref, x_1_ref), body)


def half_rows(tiles, swap):
    down = odd("gz") if swap == 0 else jnp.logical_not(odd("gz"))
    half = tiles.shape[-2] // 2
    return jnp.where(down, tiles[..., :half, :], tiles[..., half:, :])


def store_next_rows(refs, at, tiles):
    half = tiles.shape[-2] // 2
    for ref in refs:
        for i in range(tiles.shape[0]):
            ref[at + i // half, i % half : i % half + 1, :] = tiles[i, half : half + 1, :]


def sides_kernel(x_1_ref, x_0_ref, _edge_ref, sides_ref, z_0_ref, z_1_ref):
    count = DEPTH * FIELDS
    bz, by = sides_ref.shape[1:]

    def body(above, below):
        sides_ref[0:count] = above[0:count]
        sides_ref[count : 2 * count] = below[1 : count + 1]
        sides_ref[2 * count] = above[count]

    by_parity("gx", (x_0_ref, x_1_ref), body)
    tiles = sides_ref[...]
    for swap, ref in enumerate((z_0_ref, z_1_ref)):
        ref[0 : 2 * count + 1] = half_rows(tiles, swap)
    vz = tiles[0 : 2 * count].reshape(2 * DEPTH, FIELDS, bz, by)[:, 1]
    store_next_rows((z_0_ref, z_1_ref), 2 * count + 1, vz)


def edge_rows_kernel(edge_ref, z_0_ref, z_1_ref):
    tiles = edge_ref[...]
    for swap, ref in enumerate((z_0_ref, z_1_ref)):
        ref[0 : tiles.shape[0]] = half_rows(tiles, swap)
    store_next_rows((z_0_ref, z_1_ref), tiles.shape[0], tiles)


def lookups(fields, ok, keep, table_ref):
    *rest, phase = fields
    for number in range(3):
        rows = [divmod(number * PHASES + index, table_ref.shape[1]) for index in range(PHASES)]
        table = [table_ref[n, r : r + 1, :] for n, r in rows]
        value = jnp.broadcast_to(table[0], phase.shape)
        for index in range(1, PHASES):
            value = jnp.where(phase == float(index), table[index], value)
        if number == 0:
            value = value * jnp.where(ok, 1.0, 0.0)
            if keep is not None:
                value = jnp.where(keep, value, 0.0)
        elif number == 1:
            value = (0.5 / math.log(2.0)) * (reciprocal(value) - 1.0)
        rest.append(value)
    return rest


def own_lanes(block, ok, tables):
    block = block.reshape(-1, FIELDS, *block.shape[-2:])
    return lookups([block[:, f] for f in range(FIELDS)], ok, None, tables)


def edge_lanes(edge, upper, ok, tables):
    by = edge.shape[-1]
    iy = lax.axis_index("gy")
    lane = iota((1, 1, by), 2)
    keep = ((lane <= DEPTH) & (iy < lax.axis_size("gy") - 1)) | ((lane >= by - DEPTH) & (iy > 0))
    return lookups([beside(edge, f, upper) for f in range(FIELDS)], ok, keep, tables)


def store_to(refs):
    def store(planes, part, values):
        by = values[0].shape[-1]
        for ref, value in zip(refs, values):
            ref[planes, :, part * by : (part + 1) * by] = value

    return store


def unpack_own(load, bx, ok, tables, store):
    def group(g, carry):
        at = g * GROUP
        store(pl.ds(DEPTH + at, GROUP), 0, own_lanes(load(at * FIELDS, GROUP * FIELDS), ok, tables))
        return carry

    lax.fori_loop(0, bx // GROUP, group, 0)


def unpack_own_edges(load, bx, ok, tables, store):
    half = bx // 2
    for upper in range(2):

        def group(g, carry):
            at = g * GROUP
            values = edge_lanes(load(at, GROUP), upper, ok, tables)
            store(pl.ds(DEPTH + upper * half + at, GROUP), 1, values)
            return carry

        lax.fori_loop(0, half // GROUP, group, 0)


def side_places(bx):
    ix = lax.axis_index("gx")
    return (pl.ds(DEPTH + bx, DEPTH), ix < lax.axis_size("gx") - 1), (pl.ds(0, DEPTH), ix > 0)


def unpack_sides(load, bx, ok, tables, store, vx_ref):
    count = DEPTH * FIELDS
    for n, (planes, inside) in enumerate(side_places(bx)):
        store(planes, 0, own_lanes(load(n * count, count), ok & inside, tables))
    vx = load(2 * count, 1)
    vx_ref[pl.ds(bx + 2 * DEPTH, 1), :, 0 : vx.shape[-1]] = vx


def unpack_side_edges(load, bx, ok, tables, store, vx_ref):
    half = bx // 2
    edge = load(half, DEPTH)
    for upper, (planes, inside) in enumerate(side_places(bx)):
        store(planes, 1, edge_lanes(edge, upper, ok & inside, tables))
    by = edge.shape[-1]
    vx_ref[pl.ds(bx + 2 * DEPTH, 1), :, by : 2 * by] = beside(edge[0:1], FIELDS, 0)


def make_weights(weight_ref):
    shape = weight_ref.shape[1:]
    rows, lanes = shape
    bz, by = rows // 2, lanes // 2
    nz, ny = lax.axis_size("gz"), lax.axis_size("gy")
    iz, iy = lax.axis_index("gz"), lax.axis_index("gy")
    r, c = iota(shape, 0), iota(shape, 1)
    zg = iz * bz + jnp.where(r < bz + bz // 2, r, r - rows)
    yg = iy * by + jnp.where(c <= by + DEPTH, c, c - lanes)
    filled = (c <= by + DEPTH) | (c >= lanes - DEPTH)
    inside = filled & (zg >= 0) & (zg < nz * bz) & (yg >= 0) & (yg < ny * by)
    weight_ref[0] = jnp.where(inside, 0.05, 0.0)
    weight_ref[1] = jnp.where(inside & (zg > 0), 0.05, 0.0)
    weight_ref[2] = jnp.where(inside & (yg > 0), 0.05, 0.0)
    weight_ref[3] = jnp.where(inside, 0.0, 1.0)


def own_kernel(stack_ref, z_0_ref, z_1_ref, edge_ref, tables_ref, weight_ref, v_ref, *rest):
    bx = v_ref.shape[1] - 2 * DEPTH - 1
    make_weights(weight_ref)
    count = bx * FIELDS
    edge_ref[...] = stack_ref[count : count + bx // 2]
    tables_ref[...] = stack_ref[count + bx // 2 :]
    size = GROUP * FIELDS

    def group(g, carry):
        at = pl.ds(g * size, size)
        tiles = stack_ref[at]
        for swap, ref in enumerate((z_0_ref, z_1_ref)):
            ref[at] = half_rows(tiles, swap)
        return carry

    lax.fori_loop(0, bx // GROUP, group, 0)
    for g in range(bx // GROUP):
        vz = stack_ref[pl.ds(g * size, size)].reshape(GROUP, FIELDS, *stack_ref.shape[1:])[:, 1]
        store_next_rows((z_0_ref, z_1_ref), count + g * GROUP // (stack_ref.shape[1] // 2), vz)
    store = store_to([v_ref.at[d] for d in range(3)] + list(rest))
    unpack_own(lambda at, n: stack_ref[pl.ds(at, n)], bx, True, tables_ref, store)


def own_sides_kernel(sides_ref, edge_ref, tables_ref, *refs):
    v_ref, *rest = refs[len(refs) // 2 :]
    bx = v_ref.shape[1] - 2 * DEPTH - 1
    store = store_to([v_ref.at[d] for d in range(3)] + list(rest))
    unpack_sides(lambda at, n: sides_ref[pl.ds(at, n)], bx, True, tables_ref, store, v_ref.at[0])
    load = lambda at, n: edge_ref[pl.ds(at, n)]
    unpack_own_edges(load, bx, True, tables_ref, store)
    unpack_side_edges(load, bx, True, tables_ref, store, v_ref.at[0])


def rows_in_grid(bz):
    iz = lax.axis_index("gz")
    row = iota((1, bz, 1), 1)
    return ((row < bz // 2) & (iz < lax.axis_size("gz") - 1)) | ((row >= bz // 2) & (iz > 0))


def load_both(above, below):
    return lambda at, n: jnp.concatenate([above[pl.ds(at, n)], below[pl.ds(at, n)]], axis=1)


def halo_kernel(face_0_ref, face_1_ref, corner_0_ref, corner_1_ref, tables_ref, halo_ref, next_ref):
    half, by = face_0_ref.shape[1:]
    bz = 2 * half
    bx = halo_ref.shape[1] - 2 * DEPTH - 1
    ok = rows_in_grid(bz)
    store = store_to([halo_ref.at[n] for n in range(7)])

    def faces(above, below):
        unpack_own(load_both(above, below), bx, ok, tables_ref, store)
        for i in range(bx):
            n = i % half
            next_ref[DEPTH + i, half - 1 : half, 0:by] = above[bx * FIELDS + i // half, n : n + 1, :]

    def corners(above, below):
        unpack_sides(load_both(above, below), bx, ok, tables_ref, store, halo_ref.at[0])
        for i in range(2 * DEPTH):
            n = i % half
            to = DEPTH + bx + i if i < DEPTH else i - DEPTH
            next_ref[to, half - 1 : half, 0:by] = above[2 * DEPTH * FIELDS + 1 + i // half, n : n + 1, :]

    by_parity("gz", (face_0_ref, face_1_ref), faces)
    by_parity("gz", (corner_0_ref, corner_1_ref), corners)


def unpack_halo_edges(edge_0_ref, edge_1_ref, tables_ref, halo_ref, next_ref):
    half, by = edge_0_ref.shape[1:]
    bx = halo_ref.shape[1] - 2 * DEPTH - 1
    ok = rows_in_grid(2 * half)
    store = store_to([halo_ref.at[n] for n in range(7)])
    tiles = bx // 2 + DEPTH

    def body(above, below):
        load = load_both(above, below)
        unpack_own_edges(load, bx, ok, tables_ref, store)
        unpack_side_edges(load, bx, ok, tables_ref, store, halo_ref.at[0])
        for n in range(tiles // half):
            rows = above[tiles + n]
            for upper in range(2):
                values = beside(rows, 1, upper)
                for i in range(half):
                    tile = n * half + i
                    if tile < bx // 2:
                        to = DEPTH + upper * (bx // 2) + tile
                    else:
                        to = tile - bx // 2 + (0 if upper else DEPTH + bx)
                    next_ref[to, half - 1 : half, by : 2 * by] = values[i : i + 1]

    by_parity("gz", (edge_0_ref, edge_1_ref), body)


def main_kernel(
    v_ref, p0_ref, pre_ref, power_field_ref, rho_ref, _halo, _next, edge_0_ref, edge_1_ref, tables_ref, weight_ref,
    out_vx_ref, out_vz_ref, out_vy_ref, out_p_ref, out_eta_ref, sum_ref, halo_ref, next_ref,
    va_ref, vb_ref, p_ref,
):
    bx, bz, by = out_p_ref.shape
    rows, lanes = 2 * bz, 2 * by
    nx, ix = lax.axis_size("gx"), lax.axis_index("gx")
    unpack_halo_edges(edge_0_ref, edge_1_ref, tables_ref, halo_ref, next_ref)

    def with_halo(own, n, planes):
        return jnp.concatenate([own[planes], halo_ref[n, planes]], axis=1)

    for k in range(1, ITERS + 1):
        old, new = (va_ref, vb_ref) if k % 2 else (vb_ref, va_ref)
        last = k == ITERS

        def load(d, j, count):
            planes = pl.ds(j, count)
            return with_halo(v_ref.at[d], d, planes) if k == 1 else old[d, planes]

        def cells(j, count):
            planes = pl.ds(j, count)
            vx1 = load(0, j, count + 1)
            vx = vx1[:count]
            vz, vy = load(1, j, count), load(2, j, count)
            p = with_halo(p0_ref, 3, planes) if k == 1 else p_ref[planes]
            up = z_up(vz)
            if k == 1:
                after = next_ref[planes]
                after = jnp.concatenate([after, after], axis=1)
                up = jnp.where(iota((1, rows, lanes), 1) == bz + bz // 2 - 1, after, up)
            rx = vx1[1:] - vx
            rz = up - vz
            ry = y_up(vy) - vy
            a = rx - ry
            b = ry - rz
            inv = (a * (a + b) + b * b) * (1.0 / 3.0) + 1.0
            eta = with_halo(pre_ref, 4, planes) * jnp.exp2(with_halo(power_field_ref, 5, planes) * jnp.log(inv))
            quarter = 0.25 * eta
            div = rx + ry + rz
            p = p - quarter * (div + div)
            tx, tz, ty = eta * rx - p, eta * rz - p, eta * ry - p
            sz = quarter + z_down(quarter)
            sy = quarter + y_down(quarter)
            return vx, vz, vy, eta, p, quarter, tx, tz, ty, sz, sy

        def chunk(j, count, carry=None, final=False):
            if carry is None:
                below = cells(j - 1, count + 1)
                if not last:
                    p_ref[pl.ds(j - 1, 1)] = below[4][:1]
                vx, vz, vy, eta, p, quarter, tx, tz, ty, sz, sy = (a[1:] for a in below)
                join = lambda n, a: below[n][:-1]
            else:
                vx, vz, vy, eta, p, quarter, tx, tz, ty, sz, sy = cells(j, count)
                first = {1: load(1, j - 1, 1), 2: load(2, j - 1, 1), 5: carry[0], 6: carry[1], 9: carry[2], 10: carry[3]}
                join = lambda n, a: jnp.concatenate([first[n], a[:-1]], axis=0)
            planes = pl.ds(j, count)
            bias = weight_ref[3:4]
            sx = quarter + join(5, quarter)
            exz = sz + join(9, sz)
            exy = sy + join(10, sy)
            ezy = sz + y_down(sz)
            fxz = exz * (vx - z_down(vx))
            fxy = exy * (vx - y_down(vx))
            low_vz, low_vy = join(1, vz), join(2, vy)
            gzx = exz * (vz - low_vz)
            hyx = exy * (vy - low_vy)
            gzy = ezy * (vz - y_down(vz))
            hyz = ezy * (vy - z_down(vy))
            res_x = (tx - join(6, tx)) + ((z_up(fxz) - fxz) + (y_up(fxy) - fxy))
            new_vx = vx + weight_ref[0:1] * reciprocal(sx + bias) * res_x
            part_z = (tz - z_down(tz)) - with_halo(rho_ref, 6, planes) + ((y_up(gzy) - gzy) - gzx)
            part_y = (ty - y_down(ty)) + ((z_up(hyz) - hyz) - hyx)
            scale_z = weight_ref[1:2] * reciprocal(sz + bias)
            scale_y = weight_ref[2:3] * reciprocal(sy + bias)

            def lower(n, a):
                return a[:-1] if carry is None else jnp.concatenate([carry[n], a[:-1]], axis=0)

            skip = 1 if carry is None else 0
            new_vz = low_vz[skip:] + lower(6, scale_z) * (lower(4, part_z) + gzx[skip:])
            new_vy = low_vy[skip:] + lower(7, scale_y) * (lower(5, part_y) + hyx[skip:])
            at = pl.ds(j - 1 + skip - (DEPTH if last else 0), count - skip)
            if last:
                own = count - 1 if final else count
                here = pl.ds(j - DEPTH, own)
                out_vx_ref[here] = new_vx[:own, 0:bz, 0:by]
                out_p_ref[here] = p[:own, 0:bz, 0:by]
                out_eta_ref[here] = eta[:own, 0:bz, 0:by]
                sum_ref[...] += jnp.sum(p[:own, 0:bz, 0:by], axis=0)
                out_vz_ref[at] = new_vz[:, 0:bz, 0:by]
                out_vy_ref[at] = new_vy[:, 0:bz, 0:by]
            else:
                p_ref[planes] = p
                new[0, planes] = new_vx
                new[1, at] = new_vz
                new[2, at] = new_vy
            return tuple(a[-1:] for a in (quarter, tx, sz, sy, part_z, part_y, scale_z, scale_y))

        first, end = k, bx + 2 * DEPTH - k
        if last:
            sum_ref[...] = jnp.zeros((bz, by), jnp.float32)
        count = end - first + 1
        steps = (count - 2) // UNROLL
        start = count - steps * UNROLL
        carry = chunk(first, start)
        loops = steps - 1 if last else steps
        carry = lax.fori_loop(
            0, loops, lambda s, carry: chunk(first + start + s * UNROLL, UNROLL, carry), carry
        )
        if last:
            chunk(end + 1 - UNROLL, UNROLL, carry, final=True)

            @pl.when(ix == 0)
            def _():
                out_vx_ref[0] = jnp.zeros((bz, by), jnp.float32)
        else:
            plane = jnp.zeros((rows, lanes), jnp.float32)

            @pl.when(ix == 0)
            def _():
                for i in range(first, DEPTH):
                    for d in range(3):
                        new[d, i] = plane
                new[0, DEPTH] = plane

            @pl.when(ix == nx - 1)
            def _():
                for i in range(DEPTH + bx, end + 1):
                    for d in range(3):
                        new[d, i] = plane


def final_kernel(p_ref, sum_ref, out_ref, *, cells):
    mean = jnp.sum(sum_ref[...]) * (1.0 / cells)
    out_ref[...] = p_ref[...] - mean


def swap(a, axis, start):
    count = lax.axis_size(axis)
    return lax.ppermute(a, axis, [(i, j) for k in range(start, count - 1, 2) for i, j in ((k, k + 1), (k + 1, k))])


def sum_everywhere(total):
    axes = ("gx", "gy", "gz")
    devices = math.prod(lax.axis_size(a) for a in axes)
    total = total + lax.ppermute(total, axes, [(i, i ^ 1) for i in range(devices)])
    total = jnp.broadcast_to(jnp.sum(total, axis=0, keepdims=True), (devices // 2, total.shape[1]))
    groups = [list(range(n, devices, 2)) for n in range(2)]
    return lax.all_to_all(total, axes, 0, 0, tiled=True, axis_index_groups=groups)


def local(vel_x, vel_y, vel_z, pressure, phase, visc_scale, power_n, density):
    bx, bz, by = pressure.shape
    assert bx % (2 * GROUP) == 0 and bz == 2 * DEPTH and DEPTH == GROUP
    f32 = jnp.float32
    iy, ny = lax.axis_index("gy"), lax.axis_size("gy")
    cells = bx * bz * by * math.prod(lax.axis_size(a) for a in ("gx", "gz", "gy"))
    deep = bx + 2 * DEPTH + 1
    rows, lanes = 2 * bz, 2 * by
    shape = lambda *dims: jax.ShapeDtypeStruct(dims, f32)
    block = shape(bx, bz, by)
    scratch = lambda *dims: pltpu.VMEM(dims, f32)
    limit = lambda mebibytes: pltpu.CompilerParams(vmem_limit_bytes=mebibytes * 1024 * 1024)
    groups = bx // GROUP
    stacked = bx * FIELDS + bx // 2 + 2
    sent = shape(DEPTH * FIELDS + 1, bz, by)
    edge, x_0, x_1, stack = pl.pallas_call(
        pack_kernel,
        out_shape=(shape(bx // 2, bz, by), sent, sent, shape(stacked, bz, by)),
        in_specs=[HBM] * 8,
        out_specs=(HBM,) * 4,
        scratch_shapes=[
            scratch(FIELDS - 1, bx, bz, by),
            pltpu.VMEM((bx, bz, by), jnp.int32),
            scratch(bx // 2, bz, by),
            scratch(stacked, bz, by),
            pltpu.SMEM((PHASES,), f32),
            pltpu.SMEM((PHASES,), f32),
            pltpu.SMEM((PHASES,), f32),
            pltpu.SemaphoreType.DMA((groups, FIELDS)),
            pltpu.SemaphoreType.DMA((groups + groups // 2 + 4,)),
            pltpu.SemaphoreType.DMA((3,)),
        ],
        compiler_params=limit(58),
    )(vel_x, vel_z, vel_y, pressure, phase, visc_scale, power_n, density)

    def edges_beside(edge):
        side = swap(edge, "gy", 0)
        if ny == 2:
            return side
        lane = iota(side.shape, 2) % (by // 2) % LANE_STEP
        return jnp.where((lane <= DEPTH) == (lax.rem(iy, 2) == 0), side, swap(edge, "gy", 1))

    estimate = lambda size: pl.CostEstimate(
        flops=4 * size * bz * by, bytes_accessed=size * bz * by * 4, transcendentals=0
    )

    def unpacking(kernel, tiles, out_shape, *args, aliases={}):
        return pl.pallas_call(
            kernel,
            out_shape=out_shape,
            in_specs=[VMEM] * len(args),
            out_specs=(VMEM,) * len(out_shape),
            input_output_aliases=aliases,
            compiler_params=limit(16),
            cost_estimate=estimate(13 * tiles),
        )(*args)

    field = shape(deep, bz, lanes)
    own_shape = (shape(3, deep, bz, lanes),) + (field,) * 4
    half = lambda tiles, planes: shape(tiles + planes // (bz // 2), bz // 2, by)
    x_1, x_0 = swap(x_1, "gx", 1), swap(x_0, "gx", 0)
    face = half(bx * FIELDS, bx)
    extra = (shape(bx // 2, bz, by), shape(2, bz, by), shape(4, rows, lanes))
    z_0, z_1, edge, tables, weights, *own = unpacking(own_kernel, bx, (face, face) + extra + own_shape, stack)
    face_1, face_0 = swap(z_1, "gz", 1), swap(z_0, "gz", 0)

    tiles = bx // 2 + DEPTH
    edge = pl.pallas_call(
        side_edge_kernel,
        out_shape=shape(tiles, bz, by),
        in_specs=[VMEM] * 3,
        out_specs=VMEM,
        compiler_params=limit(4),
    )(x_1, x_0, edge)
    corner = half(2 * DEPTH * FIELDS + 1, 2 * DEPTH)
    sides, z_0, z_1 = pl.pallas_call(
        sides_kernel,
        out_shape=(shape(2 * DEPTH * FIELDS + 1, bz, by), corner, corner),
        in_specs=[VMEM] * 3,
        out_specs=(VMEM,) * 3,
        compiler_params=limit(4),
    )(x_1, x_0, edge)
    edge = edges_beside(edge)
    corner_1, corner_0 = swap(z_1, "gz", 1), swap(z_0, "gz", 0)
    z_0, z_1 = pl.pallas_call(
        edge_rows_kernel,
        out_shape=(half(tiles, tiles),) * 2,
        in_specs=[VMEM],
        out_specs=(VMEM,) * 2,
        compiler_params=limit(4),
        cost_estimate=estimate(100000),
    )(edge)
    edge_1, edge_0 = swap(z_1, "gz", 1), swap(z_0, "gz", 0)

    own = unpacking(
        own_sides_kernel, 2 * deep, own_shape, sides, edge, tables, *own, aliases={n + 3: n for n in range(5)}
    )
    halo = unpacking(
        halo_kernel, deep, (shape(7, deep, bz, lanes), field), face_0, face_1, corner_0, corner_1, tables
    )
    vx, vz, vy, p, eta, total, _, _ = pl.pallas_call(
        main_kernel,
        out_shape=(block,) * 5 + (shape(bz, by),) + tuple(shape(*a.shape) for a in halo),
        in_specs=[VMEM] * 11,
        out_specs=(VMEM,) * 8,
        input_output_aliases={5: 6, 6: 7},
        scratch_shapes=[
            scratch(3, deep, rows, lanes),
            scratch(3, deep, rows, lanes),
            scratch(deep, rows, lanes),
        ],
        compiler_params=limit(32),
    )(*own, *halo, edge_0, edge_1, tables, weights)

    total = sum_everywhere(total)
    p = pl.pallas_call(
        lambda *refs: final_kernel(*refs, cells=float(cells)),
        out_shape=block,
        in_specs=[VMEM] * 2,
        out_specs=VMEM,
        compiler_params=limit(4),
    )(p, total)
    return (vx, vy, vz, p, eta)


def solution(mesh):
    spec = P("gx", "gz", "gy")
    return jax.shard_map(
        local,
        mesh=mesh,
        in_specs=(spec,) * 5 + (P(),) * 3,
        out_specs=(spec,) * 5,
        check_vma=False,
    )
```

```python
import math

import jax
import jax.numpy as jnp
from jax import lax
from jax.experimental import pallas as pl
from jax.experimental.pallas import tpu as pltpu
from jax.sharding import PartitionSpec as P

ITERS = 4
PHASES = 4
FIELDS = 5
DEPTH = ITERS
LANE_STEP = 2 * DEPTH + 1
GROUP = 4

VMEM = pl.BlockSpec(memory_space=pltpu.VMEM)
HBM = pl.BlockSpec(memory_space=pltpu.HBM)


def z_up(a):
    return pltpu.roll(a, a.shape[-2] - 1, a.ndim - 2)


def z_down(a):
    return pltpu.roll(a, 1, a.ndim - 2)


def y_up(a):
    return pltpu.roll(a, a.shape[-1] - 1, a.ndim - 1)


def y_down(a):
    return pltpu.roll(a, 1, a.ndim - 1)


def reciprocal(a):
    return pl.reciprocal(a, approx=True)


def iota(shape, axis):
    return lax.broadcasted_iota(jnp.int32, shape, axis)


def odd(axis):
    return lax.rem(lax.axis_index(axis), 2) == 1


def by_parity(axis, pair, body):
    pl.when(jnp.logical_not(odd(axis)))(lambda: body(pair[0], pair[1]))
    pl.when(odd(axis))(lambda: body(pair[1], pair[0]))


def start_copies(sources, targets, sems, order):
    copies = {}
    for g in order:
        at = pl.ds(g * GROUP, GROUP)
        copies[g] = [
            pltpu.make_async_copy(a.at[at], b.at[at], sems.at[g, f]) for f, (a, b) in enumerate(zip(sources, targets))
        ]
        for copy in copies[g]:
            copy.start()
    return copies


def clean_group(g, field_ref, phase_ref):
    bx, bz, by = phase_ref.shape
    ix, iz, iy = lax.axis_index("gx"), lax.axis_index("gz"), lax.axis_index("gy")
    plane, row, lane = (iota((GROUP, bz, by), d) for d in range(3))
    at = pl.ds(g * GROUP, GROUP)
    vx, vz, vy, p = (field_ref[f, at] for f in range(FIELDS - 1))
    if g == 0:
        vx = jnp.where((plane > 0) | (ix > 0), vx, 0.0)
    vz = jnp.where((row > 0) | (iz > 0), vz, 0.0)
    vy = jnp.where((lane > 0) | (iy > 0), vy, 0.0)
    return vx, vz, vy, p, phase_ref[at].astype(jnp.float32)


def add_edge(edge, a, base):
    by = edge.shape[-1]
    lane = iota((1,) * (edge.ndim - 1) + (by,), edge.ndim - 1)
    first = pltpu.roll(a, base, a.ndim - 1) if base else a
    edge = jnp.where((lane >= base) & (lane <= base + DEPTH), first, edge)
    last = pltpu.roll(a, (base + LANE_STEP) % by, a.ndim - 1)
    return jnp.where((lane > base + DEPTH) & (lane < base + LANE_STEP), last, edge)


def add_edges(edge, fields, upper):
    for f, a in enumerate(fields):
        edge = add_edge(edge, a, edge.shape[-1] // 2 * upper + LANE_STEP * f)
    return edge


def beside(edge, f, upper):
    by = edge.shape[-1]
    iy = lax.axis_index("gy")
    lane = iota((1,) * (edge.ndim - 1) + (by,), edge.ndim - 1)
    right = (lane <= DEPTH) & (iy < lax.axis_size("gy") - 1)
    left = (lane >= by - DEPTH) & (iy > 0)
    shift = by // 2 * upper + LANE_STEP * f
    a = pltpu.roll(edge, by - shift, edge.ndim - 1) if shift else edge
    b = pltpu.roll(edge, (by - LANE_STEP - shift) % by, edge.ndim - 1)
    return jnp.where(right, a, jnp.where(left, b, 0.0))


def pack_kernel(
    vx_hbm, vz_hbm, vy_hbm, p_hbm, phase_hbm, scale_hbm, power_hbm, rho_hbm, edge_hbm, x_0_hbm, x_1_hbm, stack_hbm,
    field_ref, phase_ref, edge_ref, stack_ref, scale_ref, power_ref, rho_ref, sems, out_sems, table_sems,
):
    bx, bz, by = phase_ref.shape
    targets = [field_ref.at[f] for f in range(FIELDS - 1)] + [phase_ref]
    groups = bx // GROUP
    order = [0, groups - 1] + list(range(1, groups - 1))
    copies = start_copies((vx_hbm, vz_hbm, vy_hbm, p_hbm, phase_hbm), targets, sems, order)
    table_refs = (scale_ref, power_ref, rho_ref)
    pairs = zip((scale_hbm, power_hbm, rho_hbm), table_refs)
    table_copies = [pltpu.make_async_copy(a, b, table_sems.at[n]) for n, (a, b) in enumerate(pairs)]
    for copy in table_copies:
        copy.start()
    half = groups // 2
    outs = []

    def out(source, target):
        outs.append(pltpu.make_async_copy(source, target, out_sems.at[len(outs)]))
        outs[-1].start()

    count = DEPTH * FIELDS
    sems_x = [out_sems.at[out_sems.shape[0] - 1 - n] for n in range(3)]

    def x_copies(to_above, to_below):
        return (
            pltpu.make_async_copy(stack_ref.at[pl.ds(0, count + 1)], to_below, sems_x[0]),
            pltpu.make_async_copy(stack_ref.at[pl.ds(0, 1)], to_above.at[pl.ds(0, 1)], sems_x[1]),
            pltpu.make_async_copy(
                stack_ref.at[pl.ds(bx * FIELDS - count, count)], to_above.at[pl.ds(1, count)], sems_x[2]
            ),
        )

    def start_x(above, below):
        for copy in x_copies(above, below):
            copy.start()

    def wait_x(above, below):
        for copy in x_copies(above, below):
            copy.wait()

    edges = {}
    for g in order:
        for copy in copies[g]:
            copy.wait()
        fields = clean_group(g, field_ref, phase_ref)
        for f, a in enumerate(fields):
            for i in range(GROUP):
                stack_ref[(g * GROUP + i) * FIELDS + f] = a[i]
        at = pl.ds(g * GROUP * FIELDS, GROUP * FIELDS)
        out(stack_ref.at[at], stack_hbm.at[at])
        if g == 1:
            by_parity("gx", (x_0_hbm, x_1_hbm), start_x)
        upper, n = divmod(g, half)
        edge = edges.get(n, jnp.zeros((GROUP, bz, by), jnp.float32))
        edges[n] = add_edges(edge, fields, upper)
        if n + half * (1 - upper) in order[: order.index(g)]:
            at = pl.ds(n * GROUP, GROUP)
            edge_ref[at] = edges[n]
            out(edge_ref.at[at], edge_hbm.at[at])
            stack_ref[pl.ds(bx * FIELDS + n * GROUP, GROUP)] = edges[n]
    end = bx * FIELDS + bx // 2
    row = iota((bz, by), 0)
    for copy in table_copies:
        copy.wait()
    entries = [ref[index] for ref in table_refs for index in range(PHASES)]
    for n in range(2):
        tile = jnp.zeros((bz, by), jnp.float32)
        for r, entry in enumerate(entries[n * bz : (n + 1) * bz]):
            tile = jnp.where(row == r, entry, tile)
        stack_ref[end + n] = tile
    at = pl.ds(bx * FIELDS, end + 2 - bx * FIELDS)
    out(stack_ref.at[at], stack_hbm.at[at])
    by_parity("gx", (x_0_hbm, x_1_hbm), wait_x)
    for copy in outs:
        copy.wait()


def side_edge_kernel(x_1_ref, x_0_ref, own_edge_ref, edge_ref):
    bz, by = edge_ref.shape[1:]
    own = own_edge_ref.shape[0]
    edge_ref[0:own] = own_edge_ref[...]

    def body(above, below):
        edge = jnp.zeros((DEPTH, bz, by), jnp.float32)
        for upper, (ref, at) in enumerate(((above, 0), (below, 1))):
            block = ref[pl.ds(at, DEPTH * FIELDS)].reshape(DEPTH, FIELDS, bz, by)
            edge = add_edges(edge, [block[:, f] for f in range(FIELDS)], upper)
        edge_ref[own:] = edge
        edge_ref[own] = add_edge(edge[0], above[DEPTH * FIELDS], FIELDS * LANE_STEP)

    by_parity("gx", (x_0_ref, x_1_ref), body)


def half_rows(tiles, swap):
    down = odd("gz") if swap == 0 else jnp.logical_not(odd("gz"))
    half = tiles.shape[-2] // 2
    return jnp.where(down, tiles[..., :half, :], tiles[..., half:, :])


def store_next_rows(refs, at, tiles):
    half = tiles.shape[-2] // 2
    for ref in refs:
        for i in range(tiles.shape[0]):
            ref[at + i // half, i % half : i % half + 1, :] = tiles[i, half : half + 1, :]


def sides_kernel(x_1_ref, x_0_ref, _edge_ref, sides_ref, z_0_ref, z_1_ref):
    count = DEPTH * FIELDS
    bz, by = sides_ref.shape[1:]

    def body(above, below):
        sides_ref[0:count] = above[0:count]
        sides_ref[count : 2 * count] = below[1 : count + 1]
        sides_ref[2 * count] = above[count]

    by_parity("gx", (x_0_ref, x_1_ref), body)
    tiles = sides_ref[...]
    for swap, ref in enumerate((z_0_ref, z_1_ref)):
        ref[0 : 2 * count + 1] = half_rows(tiles, swap)
    vz = tiles[0 : 2 * count].reshape(2 * DEPTH, FIELDS, bz, by)[:, 1]
    store_next_rows((z_0_ref, z_1_ref), 2 * count + 1, vz)


def edge_rows_kernel(edge_ref, z_0_ref, z_1_ref):
    tiles = edge_ref[...]
    for swap, ref in enumerate((z_0_ref, z_1_ref)):
        ref[0 : tiles.shape[0]] = half_rows(tiles, swap)
    store_next_rows((z_0_ref, z_1_ref), tiles.shape[0], tiles)


def lookups(fields, ok, keep, table_ref):
    *rest, phase = fields
    for number in range(3):
        rows = [divmod(number * PHASES + index, table_ref.shape[1]) for index in range(PHASES)]
        table = [table_ref[n, r : r + 1, :] for n, r in rows]
        value = jnp.broadcast_to(table[0], phase.shape)
        for index in range(1, PHASES):
            value = jnp.where(phase == float(index), table[index], value)
        if number == 0:
            value = value * jnp.where(ok, 1.0, 0.0)
            if keep is not None:
                value = jnp.where(keep, value, 0.0)
        elif number == 1:
            value = (0.5 / math.log(2.0)) * (reciprocal(value) - 1.0)
        rest.append(value)
    return rest


def own_lanes(block, ok, tables):
    block = block.reshape(-1, FIELDS, *block.shape[-2:])
    return lookups([block[:, f] for f in range(FIELDS)], ok, None, tables)


def edge_lanes(edge, upper, ok, tables):
    by = edge.shape[-1]
    iy = lax.axis_index("gy")
    lane = iota((1, 1, by), 2)
    keep = ((lane <= DEPTH) & (iy < lax.axis_size("gy") - 1)) | ((lane >= by - DEPTH) & (iy > 0))
    return lookups([beside(edge, f, upper) for f in range(FIELDS)], ok, keep, tables)


def store_to(refs):
    def store(planes, part, values):
        by = values[0].shape[-1]
        for ref, value in zip(refs, values):
            ref[planes, :, part * by : (part + 1) * by] = value

    return store


def unpack_own(load, bx, ok, tables, store):
    def group(g, carry):
        at = g * GROUP
        store(pl.ds(DEPTH + at, GROUP), 0, own_lanes(load(at * FIELDS, GROUP * FIELDS), ok, tables))
        return carry

    lax.fori_loop(0, bx // GROUP, group, 0)


def unpack_own_edges(load, bx, ok, tables, store):
    half = bx // 2
    for upper in range(2):

        def group(g, carry):
            at = g * GROUP
            values = edge_lanes(load(at, GROUP), upper, ok, tables)
            store(pl.ds(DEPTH + upper * half + at, GROUP), 1, values)
            return carry

        lax.fori_loop(0, half // GROUP, group, 0)


def side_places(bx):
    ix = lax.axis_index("gx")
    return (pl.ds(DEPTH + bx, DEPTH), ix < lax.axis_size("gx") - 1), (pl.ds(0, DEPTH), ix > 0)


def unpack_sides(load, bx, ok, tables, store, vx_ref):
    count = DEPTH * FIELDS
    for n, (planes, inside) in enumerate(side_places(bx)):
        store(planes, 0, own_lanes(load(n * count, count), ok & inside, tables))
    vx = load(2 * count, 1)
    vx_ref[pl.ds(bx + 2 * DEPTH, 1), :, 0 : vx.shape[-1]] = vx


def unpack_side_edges(load, bx, ok, tables, store, vx_ref):
    half = bx // 2
    edge = load(half, DEPTH)
    for upper, (planes, inside) in enumerate(side_places(bx)):
        store(planes, 1, edge_lanes(edge, upper, ok & inside, tables))
    by = edge.shape[-1]
    vx_ref[pl.ds(bx + 2 * DEPTH, 1), :, by : 2 * by] = beside(edge[0:1], FIELDS, 0)


def make_weights(weight_ref):
    shape = weight_ref.shape[1:]
    rows, lanes = shape
    bz, by = rows // 2, lanes // 2
    nz, ny = lax.axis_size("gz"), lax.axis_size("gy")
    iz, iy = lax.axis_index("gz"), lax.axis_index("gy")
    r, c = iota(shape, 0), iota(shape, 1)
    zg = iz * bz + jnp.where(r < bz + bz // 2, r, r - rows)
    yg = iy * by + jnp.where(c <= by + DEPTH, c, c - lanes)
    filled = (c <= by + DEPTH) | (c >= lanes - DEPTH)
    inside = filled & (zg >= 0) & (zg < nz * bz) & (yg >= 0) & (yg < ny * by)
    weight_ref[0] = jnp.where(inside, 0.05, 0.0)
    weight_ref[1] = jnp.where(inside & (zg > 0), 0.05, 0.0)
    weight_ref[2] = jnp.where(inside & (yg > 0), 0.05, 0.0)
    weight_ref[3] = jnp.where(inside, 0.0, 1.0)


def own_kernel(stack_ref, z_0_ref, z_1_ref, edge_ref, tables_ref, weight_ref, v_ref, *rest):
    bx = v_ref.shape[1] - 2 * DEPTH - 1
    make_weights(weight_ref)
    count = bx * FIELDS
    edge_ref[...] = stack_ref[count : count + bx // 2]
    tables_ref[...] = stack_ref[count + bx // 2 :]
    size = GROUP * FIELDS

    def group(g, carry):
        at = pl.ds(g * size, size)
        tiles = stack_ref[at]
        for swap, ref in enumerate((z_0_ref, z_1_ref)):
            ref[at] = half_rows(tiles, swap)
        return carry

    lax.fori_loop(0, bx // GROUP, group, 0)
    for g in range(bx // GROUP):
        vz = stack_ref[pl.ds(g * size, size)].reshape(GROUP, FIELDS, *stack_ref.shape[1:])[:, 1]
        store_next_rows((z_0_ref, z_1_ref), count + g * GROUP // (stack_ref.shape[1] // 2), vz)
    store = store_to([v_ref.at[d] for d in range(3)] + list(rest))
    unpack_own(lambda at, n: stack_ref[pl.ds(at, n)], bx, True, tables_ref, store)


def own_sides_kernel(sides_ref, edge_ref, tables_ref, *refs):
    v_ref, *rest = refs[len(refs) // 2 :]
    bx = v_ref.shape[1] - 2 * DEPTH - 1
    store = store_to([v_ref.at[d] for d in range(3)] + list(rest))
    unpack_sides(lambda at, n: sides_ref[pl.ds(at, n)], bx, True, tables_ref, store, v_ref.at[0])
    load = lambda at, n: edge_ref[pl.ds(at, n)]
    unpack_own_edges(load, bx, True, tables_ref, store)
    unpack_side_edges(load, bx, True, tables_ref, store, v_ref.at[0])


def rows_in_grid(bz):
    iz = lax.axis_index("gz")
    row = iota((1, bz, 1), 1)
    return ((row < bz // 2) & (iz < lax.axis_size("gz") - 1)) | ((row >= bz // 2) & (iz > 0))


def load_both(above, below):
    return lambda at, n: jnp.concatenate([above[pl.ds(at, n)], below[pl.ds(at, n)]], axis=1)


def halo_kernel(face_0_ref, face_1_ref, corner_0_ref, corner_1_ref, tables_ref, halo_ref, next_ref):
    half, by = face_0_ref.shape[1:]
    bz = 2 * half
    bx = halo_ref.shape[1] - 2 * DEPTH - 1
    ok = rows_in_grid(bz)
    store = store_to([halo_ref.at[n] for n in range(7)])

    def faces(above, below):
        unpack_own(load_both(above, below), bx, ok, tables_ref, store)
        for i in range(bx):
            n = i % half
            next_ref[DEPTH + i, half - 1 : half, 0:by] = above[bx * FIELDS + i // half, n : n + 1, :]

    def corners(above, below):
        unpack_sides(load_both(above, below), bx, ok, tables_ref, store, halo_ref.at[0])
        for i in range(2 * DEPTH):
            n = i % half
            to = DEPTH + bx + i if i < DEPTH else i - DEPTH
            next_ref[to, half - 1 : half, 0:by] = above[2 * DEPTH * FIELDS + 1 + i // half, n : n + 1, :]

    by_parity("gz", (face_0_ref, face_1_ref), faces)
    by_parity("gz", (corner_0_ref, corner_1_ref), corners)


def unpack_halo_edges(edge_0_ref, edge_1_ref, tables_ref, halo_ref, next_ref):
    half, by = edge_0_ref.shape[1:]
    bx = halo_ref.shape[1] - 2 * DEPTH - 1
    ok = rows_in_grid(2 * half)
    store = store_to([halo_ref.at[n] for n in range(7)])
    tiles = bx // 2 + DEPTH

    def body(above, below):
        load = load_both(above, below)
        unpack_own_edges(load, bx, ok, tables_ref, store)
        unpack_side_edges(load, bx, ok, tables_ref, store, halo_ref.at[0])
        for n in range(tiles // half):
            rows = above[tiles + n]
            for upper in range(2):
                values = beside(rows, 1, upper)
                for i in range(half):
                    tile = n * half + i
                    if tile < bx // 2:
                        to = DEPTH + upper * (bx // 2) + tile
                    else:
                        to = tile - bx // 2 + (0 if upper else DEPTH + bx)
                    next_ref[to, half - 1 : half, by : 2 * by] = values[i : i + 1]

    by_parity("gz", (edge_0_ref, edge_1_ref), body)


def main_kernel(
    v_ref, p0_ref, pre_ref, power_field_ref, rho_ref, _halo, _next, edge_0_ref, edge_1_ref, tables_ref, weight_ref,
    out_vx_ref, out_vz_ref, out_vy_ref, out_p_ref, out_eta_ref, sum_ref, halo_ref, next_ref,
    va_ref, vb_ref, p_ref,
):
    bx, bz, by = out_p_ref.shape
    rows, lanes = 2 * bz, 2 * by
    nx, ix = lax.axis_size("gx"), lax.axis_index("gx")
    unpack_halo_edges(edge_0_ref, edge_1_ref, tables_ref, halo_ref, next_ref)

    def with_halo(own, n, planes):
        return jnp.concatenate([own[planes], halo_ref[n, planes]], axis=1)

    for k in range(1, ITERS + 1):
        old, new = (va_ref, vb_ref) if k % 2 else (vb_ref, va_ref)
        last = k == ITERS

        def load(d, j, count):
            planes = pl.ds(j, count)
            return with_halo(v_ref.at[d], d, planes) if k == 1 else old[d, planes]

        def cells(j, count):
            planes = pl.ds(j, count)
            vx1 = load(0, j, count + 1)
            vx = vx1[:count]
            vz, vy = load(1, j, count), load(2, j, count)
            p = with_halo(p0_ref, 3, planes) if k == 1 else p_ref[planes]
            up = z_up(vz)
            if k == 1:
                after = next_ref[planes]
                after = jnp.concatenate([after, after], axis=1)
                up = jnp.where(iota((1, rows, lanes), 1) == bz + bz // 2 - 1, after, up)
            rx = vx1[1:] - vx
            rz = up - vz
            ry = y_up(vy) - vy
            a = rx - ry
            b = ry - rz
            inv = (a * (a + b) + b * b) * (1.0 / 3.0) + 1.0
            eta = with_halo(pre_ref, 4, planes) * jnp.exp2(with_halo(power_field_ref, 5, planes) * jnp.log(inv))
            quarter = 0.25 * eta
            div = rx + ry + rz
            p = p - quarter * (div + div)
            tx, tz, ty = eta * rx - p, eta * rz - p, eta * ry - p
            sz = quarter + z_down(quarter)
            sy = quarter + y_down(quarter)
            return vx, vz, vy, eta, p, quarter, tx, tz, ty, sz, sy

        first, end = k, bx + 2 * DEPTH - k
        count = end - first + 1
        below = cells(first - 1, count + 1)
        vx, vz, vy, eta, p, quarter, tx, tz, ty, sz, sy = (a[1:] for a in below)
        vx0, vz0, vy0, _, _, quarter0, tx0, _, _, sz0, sy0 = (a[:-1] for a in below)
        bias = weight_ref[3:4]
        sx = quarter + quarter0
        exz = sz + sz0
        exy = sy + sy0
        ezy = sz + y_down(sz)
        fxz = exz * (vx - z_down(vx))
        fxy = exy * (vx - y_down(vx))
        gzx = exz * (vz - vz0)
        hyx = exy * (vy - vy0)
        gzy = ezy * (vz - y_down(vz))
        hyz = ezy * (vy - z_down(vy))
        res_x = (tx - tx0) + ((z_up(fxz) - fxz) + (y_up(fxy) - fxy))
        new_vx = vx + weight_ref[0:1] * reciprocal(sx + bias) * res_x
        part_z = (tz - z_down(tz)) - with_halo(rho_ref, 6, pl.ds(first, count)) + ((y_up(gzy) - gzy) - gzx)
        part_y = (ty - y_down(ty)) + ((z_up(hyz) - hyz) - hyx)
        scale_z = weight_ref[1:2] * reciprocal(sz + bias)
        scale_y = weight_ref[2:3] * reciprocal(sy + bias)
        new_vz = vz[:-1] + scale_z[:-1] * (part_z[:-1] + gzx[1:])
        new_vy = vy[:-1] + scale_y[:-1] * (part_y[:-1] + hyx[1:])
        if last:
            out_vx_ref[...] = new_vx[:-1, 0:bz, 0:by]
            out_vz_ref[...] = new_vz[:, 0:bz, 0:by]
            out_vy_ref[...] = new_vy[:, 0:bz, 0:by]
            out_p_ref[...] = p[:-1, 0:bz, 0:by]
            out_eta_ref[...] = eta[:-1, 0:bz, 0:by]
            sum_ref[...] = jnp.sum(p[:-1, 0:bz, 0:by], axis=0)

            @pl.when(ix == 0)
            def _():
                out_vx_ref[0] = jnp.zeros((bz, by), jnp.float32)
        else:
            p_ref[pl.ds(first - 1, count + 1)] = below[4]
            new[0, pl.ds(first, count)] = new_vx
            new[1, pl.ds(first, count - 1)] = new_vz
            new[2, pl.ds(first, count - 1)] = new_vy
            plane = jnp.zeros((rows, lanes), jnp.float32)

            @pl.when(ix == 0)
            def _():
                for i in range(first, DEPTH):
                    for d in range(3):
                        new[d, i] = plane
                new[0, DEPTH] = plane

            @pl.when(ix == nx - 1)
            def _():
                for i in range(DEPTH + bx, end + 1):
                    for d in range(3):
                        new[d, i] = plane


def final_kernel(p_ref, sum_ref, out_ref, *, cells):
    mean = jnp.sum(sum_ref[...]) * (1.0 / cells)
    out_ref[...] = p_ref[...] - mean


def swap(a, axis, start):
    count = lax.axis_size(axis)
    return lax.ppermute(a, axis, [(i, j) for k in range(start, count - 1, 2) for i, j in ((k, k + 1), (k + 1, k))])


def sum_everywhere(total):
    axes = ("gx", "gy", "gz")
    devices = math.prod(lax.axis_size(a) for a in axes)
    total = total + lax.ppermute(total, axes, [(i, i ^ 1) for i in range(devices)])
    total = jnp.broadcast_to(jnp.sum(total, axis=0, keepdims=True), (devices // 2, total.shape[1]))
    groups = [list(range(n, devices, 2)) for n in range(2)]
    return lax.all_to_all(total, axes, 0, 0, tiled=True, axis_index_groups=groups)


def local(vel_x, vel_y, vel_z, pressure, phase, visc_scale, power_n, density):
    bx, bz, by = pressure.shape
    assert bx % (2 * GROUP) == 0 and bz == 2 * DEPTH and DEPTH == GROUP
    f32 = jnp.float32
    iy, ny = lax.axis_index("gy"), lax.axis_size("gy")
    cells = bx * bz * by * math.prod(lax.axis_size(a) for a in ("gx", "gz", "gy"))
    deep = bx + 2 * DEPTH + 1
    rows, lanes = 2 * bz, 2 * by
    shape = lambda *dims: jax.ShapeDtypeStruct(dims, f32)
    block = shape(bx, bz, by)
    scratch = lambda *dims: pltpu.VMEM(dims, f32)
    limit = lambda mebibytes: pltpu.CompilerParams(vmem_limit_bytes=mebibytes * 1024 * 1024)
    groups = bx // GROUP
    stacked = bx * FIELDS + bx // 2 + 2
    sent = shape(DEPTH * FIELDS + 1, bz, by)
    edge, x_0, x_1, stack = pl.pallas_call(
        pack_kernel,
        out_shape=(shape(bx // 2, bz, by), sent, sent, shape(stacked, bz, by)),
        in_specs=[HBM] * 8,
        out_specs=(HBM,) * 4,
        scratch_shapes=[
            scratch(FIELDS - 1, bx, bz, by),
            pltpu.VMEM((bx, bz, by), jnp.int32),
            scratch(bx // 2, bz, by),
            scratch(stacked, bz, by),
            pltpu.SMEM((PHASES,), f32),
            pltpu.SMEM((PHASES,), f32),
            pltpu.SMEM((PHASES,), f32),
            pltpu.SemaphoreType.DMA((groups, FIELDS)),
            pltpu.SemaphoreType.DMA((groups + groups // 2 + 4,)),
            pltpu.SemaphoreType.DMA((3,)),
        ],
        compiler_params=limit(58),
    )(vel_x, vel_z, vel_y, pressure, phase, visc_scale, power_n, density)

    def edges_beside(edge):
        side = swap(edge, "gy", 0)
        if ny == 2:
            return side
        lane = iota(side.shape, 2) % (by // 2) % LANE_STEP
        return jnp.where((lane <= DEPTH) == (lax.rem(iy, 2) == 0), side, swap(edge, "gy", 1))

    estimate = lambda size: pl.CostEstimate(
        flops=4 * size * bz * by, bytes_accessed=size * bz * by * 4, transcendentals=0
    )

    def unpacking(kernel, tiles, out_shape, *args, aliases={}):
        return pl.pallas_call(
            kernel,
            out_shape=out_shape,
            in_specs=[VMEM] * len(args),
            out_specs=(VMEM,) * len(out_shape),
            input_output_aliases=aliases,
            compiler_params=limit(16),
            cost_estimate=estimate(13 * tiles),
        )(*args)

    field = shape(deep, bz, lanes)
    own_shape = (shape(3, deep, bz, lanes),) + (field,) * 4
    half = lambda tiles, planes: shape(tiles + planes // (bz // 2), bz // 2, by)
    x_1, x_0 = swap(x_1, "gx", 1), swap(x_0, "gx", 0)
    face = half(bx * FIELDS, bx)
    extra = (shape(bx // 2, bz, by), shape(2, bz, by), shape(4, rows, lanes))
    z_0, z_1, edge, tables, weights, *own = unpacking(own_kernel, bx, (face, face) + extra + own_shape, stack)
    face_1, face_0 = swap(z_1, "gz", 1), swap(z_0, "gz", 0)

    tiles = bx // 2 + DEPTH
    edge = pl.pallas_call(
        side_edge_kernel,
        out_shape=shape(tiles, bz, by),
        in_specs=[VMEM] * 3,
        out_specs=VMEM,
        compiler_params=limit(4),
    )(x_1, x_0, edge)
    corner = half(2 * DEPTH * FIELDS + 1, 2 * DEPTH)
    sides, z_0, z_1 = pl.pallas_call(
        sides_kernel,
        out_shape=(shape(2 * DEPTH * FIELDS + 1, bz, by), corner, corner),
        in_specs=[VMEM] * 3,
        out_specs=(VMEM,) * 3,
        compiler_params=limit(4),
    )(x_1, x_0, edge)
    edge = edges_beside(edge)
    corner_1, corner_0 = swap(z_1, "gz", 1), swap(z_0, "gz", 0)
    z_0, z_1 = pl.pallas_call(
        edge_rows_kernel,
        out_shape=(half(tiles, tiles),) * 2,
        in_specs=[VMEM],
        out_specs=(VMEM,) * 2,
        compiler_params=limit(4),
        cost_estimate=estimate(100000),
    )(edge)
    edge_1, edge_0 = swap(z_1, "gz", 1), swap(z_0, "gz", 0)

    own = unpacking(
        own_sides_kernel, 2 * deep, own_shape, sides, edge, tables, *own, aliases={n + 3: n for n in range(5)}
    )
    halo = unpacking(
        halo_kernel, deep, (shape(7, deep, bz, lanes), field), face_0, face_1, corner_0, corner_1, tables
    )
    vx, vz, vy, p, eta, total, _, _ = pl.pallas_call(
        main_kernel,
        out_shape=(block,) * 5 + (shape(bz, by),) + tuple(shape(*a.shape) for a in halo),
        in_specs=[VMEM] * 11,
        out_specs=(VMEM,) * 8,
        input_output_aliases={5: 6, 6: 7},
        scratch_shapes=[
            scratch(3, deep, rows, lanes),
            scratch(3, deep, rows, lanes),
            scratch(deep, rows, lanes),
        ],
        compiler_params=limit(32),
    )(*own, *halo, edge_0, edge_1, tables, weights)

    total = sum_everywhere(total)
    p = pl.pallas_call(
        lambda *refs: final_kernel(*refs, cells=float(cells)),
        out_shape=block,
        in_specs=[VMEM] * 2,
        out_specs=VMEM,
        compiler_params=limit(4),
    )(p, total)
    return (vx, vy, vz, p, eta)


def solution(mesh):
    spec = P("gx", "gz", "gy")
    return jax.shard_map(
        local,
        mesh=mesh,
        in_specs=(spec,) * 5 + (P(),) * 3,
        out_specs=(spec,) * 5,
        check_vma=False,
    )
```

```python
import math

import jax
import jax.numpy as jnp
from jax import lax
from jax.experimental import pallas as pl
from jax.experimental.pallas import tpu as pltpu
from jax.sharding import PartitionSpec as P

ITERS = 4
PHASES = 4
FIELDS = 5
DEPTH = ITERS
LANE_STEP = 2 * DEPTH + 1
GROUP = 4

VMEM = pl.BlockSpec(memory_space=pltpu.VMEM)
HBM = pl.BlockSpec(memory_space=pltpu.HBM)


def z_up(a):
    return pltpu.roll(a, a.shape[-2] - 1, a.ndim - 2)


def z_down(a):
    return pltpu.roll(a, 1, a.ndim - 2)


def y_up(a):
    return pltpu.roll(a, a.shape[-1] - 1, a.ndim - 1)


def y_down(a):
    return pltpu.roll(a, 1, a.ndim - 1)


def reciprocal(a):
    return pl.reciprocal(a, approx=True)


def iota(shape, axis):
    return lax.broadcasted_iota(jnp.int32, shape, axis)


def odd(axis):
    return lax.rem(lax.axis_index(axis), 2) == 1


def by_parity(axis, pair, body):
    pl.when(jnp.logical_not(odd(axis)))(lambda: body(pair[0], pair[1]))
    pl.when(odd(axis))(lambda: body(pair[1], pair[0]))


def start_copies(sources, targets, sems, order):
    copies = {}
    for g in order:
        at = pl.ds(g * GROUP, GROUP)
        copies[g] = [
            pltpu.make_async_copy(a.at[at], b.at[at], sems.at[g, f]) for f, (a, b) in enumerate(zip(sources, targets))
        ]
        for copy in copies[g]:
            copy.start()
    return copies


def clean_group(g, field_ref, phase_ref):
    bx, bz, by = phase_ref.shape
    ix, iz, iy = lax.axis_index("gx"), lax.axis_index("gz"), lax.axis_index("gy")
    plane, row, lane = (iota((GROUP, bz, by), d) for d in range(3))
    at = pl.ds(g * GROUP, GROUP)
    vx, vz, vy, p = (field_ref[f, at] for f in range(FIELDS - 1))
    if g == 0:
        vx = jnp.where((plane > 0) | (ix > 0), vx, 0.0)
    vz = jnp.where((row > 0) | (iz > 0), vz, 0.0)
    vy = jnp.where((lane > 0) | (iy > 0), vy, 0.0)
    return vx, vz, vy, p, phase_ref[at].astype(jnp.float32)


def add_edge(edge, a, base):
    by = edge.shape[-1]
    lane = iota((1,) * (edge.ndim - 1) + (by,), edge.ndim - 1)
    first = pltpu.roll(a, base, a.ndim - 1) if base else a
    edge = jnp.where((lane >= base) & (lane <= base + DEPTH), first, edge)
    last = pltpu.roll(a, (base + LANE_STEP) % by, a.ndim - 1)
    return jnp.where((lane > base + DEPTH) & (lane < base + LANE_STEP), last, edge)


def add_edges(edge, fields, upper):
    for f, a in enumerate(fields):
        edge = add_edge(edge, a, edge.shape[-1] // 2 * upper + LANE_STEP * f)
    return edge


def beside(edge, f, upper):
    by = edge.shape[-1]
    iy = lax.axis_index("gy")
    lane = iota((1,) * (edge.ndim - 1) + (by,), edge.ndim - 1)
    right = (lane <= DEPTH) & (iy < lax.axis_size("gy") - 1)
    left = (lane >= by - DEPTH) & (iy > 0)
    shift = by // 2 * upper + LANE_STEP * f
    a = pltpu.roll(edge, by - shift, edge.ndim - 1) if shift else edge
    b = pltpu.roll(edge, (by - LANE_STEP - shift) % by, edge.ndim - 1)
    return jnp.where(right, a, jnp.where(left, b, 0.0))


def pack_kernel(
    vx_hbm, vz_hbm, vy_hbm, p_hbm, phase_hbm, scale_hbm, power_hbm, rho_hbm, edge_hbm, x_0_hbm, x_1_hbm, stack_hbm,
    field_ref, phase_ref, edge_ref, stack_ref, scale_ref, power_ref, rho_ref, sems, out_sems, table_sems,
):
    bx, bz, by = phase_ref.shape
    targets = [field_ref.at[f] for f in range(FIELDS - 1)] + [phase_ref]
    groups = bx // GROUP
    order = [0, groups - 1] + list(range(1, groups - 1))
    copies = start_copies((vx_hbm, vz_hbm, vy_hbm, p_hbm, phase_hbm), targets, sems, order)
    table_refs = (scale_ref, power_ref, rho_ref)
    pairs = zip((scale_hbm, power_hbm, rho_hbm), table_refs)
    table_copies = [pltpu.make_async_copy(a, b, table_sems.at[n]) for n, (a, b) in enumerate(pairs)]
    for copy in table_copies:
        copy.start()
    half = groups // 2
    outs = []

    def out(source, target):
        outs.append(pltpu.make_async_copy(source, target, out_sems.at[len(outs)]))
        outs[-1].start()

    count = DEPTH * FIELDS
    sems_x = [out_sems.at[out_sems.shape[0] - 1 - n] for n in range(3)]

    def x_copies(to_above, to_below):
        return (
            pltpu.make_async_copy(stack_ref.at[pl.ds(0, count + 1)], to_below, sems_x[0]),
            pltpu.make_async_copy(stack_ref.at[pl.ds(0, 1)], to_above.at[pl.ds(0, 1)], sems_x[1]),
            pltpu.make_async_copy(
                stack_ref.at[pl.ds(bx * FIELDS - count, count)], to_above.at[pl.ds(1, count)], sems_x[2]
            ),
        )

    def start_x(above, below):
        for copy in x_copies(above, below):
            copy.start()

    def wait_x(above, below):
        for copy in x_copies(above, below):
            copy.wait()

    edges = {}
    for g in order:
        for copy in copies[g]:
            copy.wait()
        fields = clean_group(g, field_ref, phase_ref)
        for f, a in enumerate(fields):
            for i in range(GROUP):
                stack_ref[(g * GROUP + i) * FIELDS + f] = a[i]
        at = pl.ds(g * GROUP * FIELDS, GROUP * FIELDS)
        out(stack_ref.at[at], stack_hbm.at[at])
        if g == 1:
            by_parity("gx", (x_0_hbm, x_1_hbm), start_x)
        upper, n = divmod(g, half)
        edge = edges.get(n, jnp.zeros((GROUP, bz, by), jnp.float32))
        edges[n] = add_edges(edge, fields, upper)
        if n + half * (1 - upper) in order[: order.index(g)]:
            at = pl.ds(n * GROUP, GROUP)
            edge_ref[at] = edges[n]
            out(edge_ref.at[at], edge_hbm.at[at])
            stack_ref[pl.ds(bx * FIELDS + n * GROUP, GROUP)] = edges[n]
    end = bx * FIELDS + bx // 2
    row = iota((bz, by), 0)
    for copy in table_copies:
        copy.wait()
    entries = [ref[index] for ref in table_refs for index in range(PHASES)]
    for n in range(2):
        tile = jnp.zeros((bz, by), jnp.float32)
        for r, entry in enumerate(entries[n * bz : (n + 1) * bz]):
            tile = jnp.where(row == r, entry, tile)
        stack_ref[end + n] = tile
    at = pl.ds(bx * FIELDS, end + 2 - bx * FIELDS)
    out(stack_ref.at[at], stack_hbm.at[at])
    by_parity("gx", (x_0_hbm, x_1_hbm), wait_x)
    for copy in outs:
        copy.wait()


def side_edge_kernel(x_1_ref, x_0_ref, own_edge_ref, edge_ref):
    bz, by = edge_ref.shape[1:]
    own = own_edge_ref.shape[0]
    edge_ref[0:own] = own_edge_ref[...]

    def body(above, below):
        edge = jnp.zeros((DEPTH, bz, by), jnp.float32)
        for upper, (ref, at) in enumerate(((above, 0), (below, 1))):
            block = ref[pl.ds(at, DEPTH * FIELDS)].reshape(DEPTH, FIELDS, bz, by)
            edge = add_edges(edge, [block[:, f] for f in range(FIELDS)], upper)
        edge_ref[own:] = edge
        edge_ref[own] = add_edge(edge[0], above[DEPTH * FIELDS], FIELDS * LANE_STEP)

    by_parity("gx", (x_0_ref, x_1_ref), body)


def half_rows(tiles, swap):
    down = odd("gz") if swap == 0 else jnp.logical_not(odd("gz"))
    half = tiles.shape[-2] // 2
    return jnp.where(down, tiles[..., :half, :], tiles[..., half:, :])


def store_next_rows(refs, at, tiles):
    half = tiles.shape[-2] // 2
    for ref in refs:
        for i in range(tiles.shape[0]):
            ref[at + i // half, i % half : i % half + 1, :] = tiles[i, half : half + 1, :]


def sides_kernel(x_1_ref, x_0_ref, _edge_ref, sides_ref, z_0_ref, z_1_ref):
    count = DEPTH * FIELDS
    bz, by = sides_ref.shape[1:]

    def body(above, below):
        sides_ref[0:count] = above[0:count]
        sides_ref[count : 2 * count] = below[1 : count + 1]
        sides_ref[2 * count] = above[count]

    by_parity("gx", (x_0_ref, x_1_ref), body)
    tiles = sides_ref[...]
    for swap, ref in enumerate((z_0_ref, z_1_ref)):
        ref[0 : 2 * count + 1] = half_rows(tiles, swap)
    vz = tiles[0 : 2 * count].reshape(2 * DEPTH, FIELDS, bz, by)[:, 1]
    store_next_rows((z_0_ref, z_1_ref), 2 * count + 1, vz)


def edge_rows_kernel(edge_ref, z_0_ref, z_1_ref):
    tiles = edge_ref[...]
    for swap, ref in enumerate((z_0_ref, z_1_ref)):
        ref[0 : tiles.shape[0]] = half_rows(tiles, swap)
    store_next_rows((z_0_ref, z_1_ref), tiles.shape[0], tiles)


def lookups(fields, ok, keep, table_ref):
    *rest, phase = fields
    for number in range(3):
        rows = [divmod(number * PHASES + index, table_ref.shape[1]) for index in range(PHASES)]
        table = [table_ref[n, r : r + 1, :] for n, r in rows]
        value = jnp.broadcast_to(table[0], phase.shape)
        for index in range(1, PHASES):
            value = jnp.where(phase == float(index), table[index], value)
        if number == 0:
            value = value * jnp.where(ok, 1.0, 0.0)
            if keep is not None:
                value = jnp.where(keep, value, 0.0)
        elif number == 1:
            value = (0.5 / math.log(2.0)) * (reciprocal(value) - 1.0)
        rest.append(value)
    return rest


def own_lanes(block, ok, tables):
    block = block.reshape(-1, FIELDS, *block.shape[-2:])
    return lookups([block[:, f] for f in range(FIELDS)], ok, None, tables)


def edge_lanes(edge, upper, ok, tables):
    by = edge.shape[-1]
    iy = lax.axis_index("gy")
    lane = iota((1, 1, by), 2)
    keep = ((lane <= DEPTH) & (iy < lax.axis_size("gy") - 1)) | ((lane >= by - DEPTH) & (iy > 0))
    return lookups([beside(edge, f, upper) for f in range(FIELDS)], ok, keep, tables)


def store_to(refs):
    def store(planes, part, values):
        by = values[0].shape[-1]
        for ref, value in zip(refs, values):
            ref[planes, :, part * by : (part + 1) * by] = value

    return store


def unpack_own(load, bx, ok, tables, store):
    def group(g, carry):
        at = g * GROUP
        store(pl.ds(DEPTH + at, GROUP), 0, own_lanes(load(at * FIELDS, GROUP * FIELDS), ok, tables))
        return carry

    lax.fori_loop(0, bx // GROUP, group, 0)


def unpack_own_edges(load, bx, ok, tables, store):
    half = bx // 2
    for upper in range(2):

        def group(g, carry):
            at = g * GROUP
            values = edge_lanes(load(at, GROUP), upper, ok, tables)
            store(pl.ds(DEPTH + upper * half + at, GROUP), 1, values)
            return carry

        lax.fori_loop(0, half // GROUP, group, 0)


def side_places(bx):
    ix = lax.axis_index("gx")
    return (pl.ds(DEPTH + bx, DEPTH), ix < lax.axis_size("gx") - 1), (pl.ds(0, DEPTH), ix > 0)


def unpack_sides(load, bx, ok, tables, store, vx_ref):
    count = DEPTH * FIELDS
    for n, (planes, inside) in enumerate(side_places(bx)):
        store(planes, 0, own_lanes(load(n * count, count), ok & inside, tables))
    vx = load(2 * count, 1)
    vx_ref[pl.ds(bx + 2 * DEPTH, 1), :, 0 : vx.shape[-1]] = vx


def unpack_side_edges(load, bx, ok, tables, store, vx_ref):
    half = bx // 2
    edge = load(half, DEPTH)
    for upper, (planes, inside) in enumerate(side_places(bx)):
        store(planes, 1, edge_lanes(edge, upper, ok & inside, tables))
    by = edge.shape[-1]
    vx_ref[pl.ds(bx + 2 * DEPTH, 1), :, by : 2 * by] = beside(edge[0:1], FIELDS, 0)


def make_weights(weight_ref):
    shape = weight_ref.shape[1:]
    rows, lanes = shape
    bz, by = rows // 2, lanes // 2
    nz, ny = lax.axis_size("gz"), lax.axis_size("gy")
    iz, iy = lax.axis_index("gz"), lax.axis_index("gy")
    r, c = iota(shape, 0), iota(shape, 1)
    zg = iz * bz + jnp.where(r < bz + bz // 2, r, r - rows)
    yg = iy * by + jnp.where(c <= by + DEPTH, c, c - lanes)
    filled = (c <= by + DEPTH) | (c >= lanes - DEPTH)
    inside = filled & (zg >= 0) & (zg < nz * bz) & (yg >= 0) & (yg < ny * by)
    weight_ref[0] = jnp.where(inside, 0.05, 0.0)
    weight_ref[1] = jnp.where(inside & (zg > 0), 0.05, 0.0)
    weight_ref[2] = jnp.where(inside & (yg > 0), 0.05, 0.0)
    weight_ref[3] = jnp.where(inside, 0.0, 1.0)


def own_kernel(stack_ref, z_0_ref, z_1_ref, edge_ref, tables_ref, weight_ref, v_ref, *rest):
    bx = v_ref.shape[1] - 2 * DEPTH - 1
    make_weights(weight_ref)
    count = bx * FIELDS
    edge_ref[...] = stack_ref[count : count + bx // 2]
    tables_ref[...] = stack_ref[count + bx // 2 :]
    size = GROUP * FIELDS

    def group(g, carry):
        at = pl.ds(g * size, size)
        tiles = stack_ref[at]
        for swap, ref in enumerate((z_0_ref, z_1_ref)):
            ref[at] = half_rows(tiles, swap)
        return carry

    lax.fori_loop(0, bx // GROUP, group, 0)
    for g in range(bx // GROUP):
        vz = stack_ref[pl.ds(g * size, size)].reshape(GROUP, FIELDS, *stack_ref.shape[1:])[:, 1]
        store_next_rows((z_0_ref, z_1_ref), count + g * GROUP // (stack_ref.shape[1] // 2), vz)
    store = store_to([v_ref.at[d] for d in range(3)] + list(rest))
    unpack_own(lambda at, n: stack_ref[pl.ds(at, n)], bx, True, tables_ref, store)


def own_sides_kernel(sides_ref, edge_ref, tables_ref, *refs):
    v_ref, *rest = refs[len(refs) // 2 :]
    bx = v_ref.shape[1] - 2 * DEPTH - 1
    store = store_to([v_ref.at[d] for d in range(3)] + list(rest))
    unpack_sides(lambda at, n: sides_ref[pl.ds(at, n)], bx, True, tables_ref, store, v_ref.at[0])
    load = lambda at, n: edge_ref[pl.ds(at, n)]
    unpack_own_edges(load, bx, True, tables_ref, store)
    unpack_side_edges(load, bx, True, tables_ref, store, v_ref.at[0])


def rows_in_grid(bz):
    iz = lax.axis_index("gz")
    row = iota((1, bz, 1), 1)
    return ((row < bz // 2) & (iz < lax.axis_size("gz") - 1)) | ((row >= bz // 2) & (iz > 0))


def load_both(above, below):
    return lambda at, n: jnp.concatenate([above[pl.ds(at, n)], below[pl.ds(at, n)]], axis=1)


def halo_kernel(face_0_ref, face_1_ref, corner_0_ref, corner_1_ref, tables_ref, halo_ref, next_ref):
    half, by = face_0_ref.shape[1:]
    bz = 2 * half
    bx = halo_ref.shape[1] - 2 * DEPTH - 1
    ok = rows_in_grid(bz)
    store = store_to([halo_ref.at[n] for n in range(7)])

    def faces(above, below):
        unpack_own(load_both(above, below), bx, ok, tables_ref, store)
        for i in range(bx):
            n = i % half
            next_ref[DEPTH + i, half - 1 : half, 0:by] = above[bx * FIELDS + i // half, n : n + 1, :]

    def corners(above, below):
        unpack_sides(load_both(above, below), bx, ok, tables_ref, store, halo_ref.at[0])
        for i in range(2 * DEPTH):
            n = i % half
            to = DEPTH + bx + i if i < DEPTH else i - DEPTH
            next_ref[to, half - 1 : half, 0:by] = above[2 * DEPTH * FIELDS + 1 + i // half, n : n + 1, :]

    by_parity("gz", (face_0_ref, face_1_ref), faces)
    by_parity("gz", (corner_0_ref, corner_1_ref), corners)


def unpack_halo_edges(edge_0_ref, edge_1_ref, tables_ref, halo_ref, next_ref):
    half, by = edge_0_ref.shape[1:]
    bx = halo_ref.shape[1] - 2 * DEPTH - 1
    ok = rows_in_grid(2 * half)
    store = store_to([halo_ref.at[n] for n in range(7)])
    tiles = bx // 2 + DEPTH

    def body(above, below):
        load = load_both(above, below)
        unpack_own_edges(load, bx, ok, tables_ref, store)
        unpack_side_edges(load, bx, ok, tables_ref, store, halo_ref.at[0])
        for n in range(tiles // half):
            rows = above[tiles + n]
            for upper in range(2):
                values = beside(rows, 1, upper)
                for i in range(half):
                    tile = n * half + i
                    if tile < bx // 2:
                        to = DEPTH + upper * (bx // 2) + tile
                    else:
                        to = tile - bx // 2 + (0 if upper else DEPTH + bx)
                    next_ref[to, half - 1 : half, by : 2 * by] = values[i : i + 1]

    by_parity("gz", (edge_0_ref, edge_1_ref), body)


class Cells:
    def __init__(self, own, side):
        self.own, self.side = own, side

    def map(self, f, *others):
        parts = [(o.own, o.side) if isinstance(o, Cells) else (o, o) for o in others]
        return Cells(f(self.own, *(p[0] for p in parts)), f(self.side, *(p[1] for p in parts)))

    def __getitem__(self, at):
        return Cells(self.own[at], self.side[at])

    def __add__(self, other):
        return self.map(jnp.add, other)

    def __sub__(self, other):
        return self.map(jnp.subtract, other)

    def __mul__(self, other):
        return self.map(jnp.multiply, other)

    def along_z(self, up):
        bz, by = self.side.shape[-2:]
        move = z_up if up else z_down
        side = move(self.side)
        across = iota((1, bz, by), 1) == (bz - 1 if up else 0)
        return Cells(move(self.own), jnp.where(across, pltpu.roll(side, by // 2, 2), side))

    def along_y(self, up):
        bz, by = self.side.shape[-2:]
        one, half = (by - 1, by // 2 - 1) if up else (1, by // 2 + 1)
        lane = iota((1, bz, by), 2)
        own_end, side_end, halo_end = (by - 1, by - 1, by // 2 - 1) if up else (0, 0, by // 2)
        first, second = self.own[:, 0:bz], self.own[:, bz:]
        side = pltpu.roll(self.side, one, 2)
        first_moved = pltpu.roll(first, one, 2)
        own = jnp.concatenate(
            [
                jnp.where(lane == own_end, side, first_moved),
                jnp.where(lane == own_end, pltpu.roll(self.side, half, 2), pltpu.roll(second, one, 2)),
            ],
            axis=1,
        )
        side = jnp.where(lane == halo_end, pltpu.roll(second, half, 2), side)
        return Cells(own, jnp.where(lane == side_end, first_moved, side))


def join_sides(own, halo):
    by = own.shape[-1]
    lane = iota((1,) * (own.ndim - 1) + (by,), own.ndim - 1)
    middle = (lane >= by // 4) & (lane < by - by // 4)
    return jnp.where(middle, pltpu.roll(halo, by // 2, own.ndim - 1), own)


def main_kernel(
    v_ref, p0_ref, pre_ref, power_field_ref, rho_ref, _halo, _next, edge_0_ref, edge_1_ref, tables_ref, weight_ref,
    out_vx_ref, out_vz_ref, out_vy_ref, out_p_ref, out_eta_ref, sum_ref, halo_ref, next_ref,
    own_a_ref, own_b_ref, side_a_ref, side_b_ref, side_constant_ref,
):
    bx, bz, by = out_p_ref.shape
    rows, lanes = 2 * bz, 2 * by
    deep = halo_ref.shape[1]
    nx, ix = lax.axis_size("gx"), lax.axis_index("gx")
    unpack_halo_edges(edge_0_ref, edge_1_ref, tables_ref, halo_ref, next_ref)

    fields = [v_ref.at[d] for d in range(3)] + [p0_ref, pre_ref, power_field_ref, rho_ref]
    for n, ref in enumerate(fields):
        target = side_b_ref.at[n] if n < 4 else side_constant_ref.at[n - 4]
        target[...] = join_sides(ref[:, :, by:lanes], halo_ref[n, :, :, by:lanes])
    weights = [
        Cells(weight_ref[n : n + 1, :, 0:by], join_sides(weight_ref[n : n + 1, 0:bz, by:lanes], weight_ref[n : n + 1, bz:rows, by:lanes]))
        for n in range(4)
    ]

    def own_rows(n, planes):
        return jnp.concatenate([fields[n][planes, :, 0:by], halo_ref[n, planes, :, 0:by]], axis=1)

    def constant(n, planes):
        return Cells(own_rows(4 + n, planes), side_constant_ref[n, planes])

    for k in range(1, ITERS + 1):
        old = (own_a_ref, side_a_ref) if k % 2 == 0 else (own_b_ref, side_b_ref)
        new = (own_b_ref, side_b_ref) if k % 2 == 0 else (own_a_ref, side_a_ref)
        last = k == ITERS

        def load(n, j, count):
            planes = pl.ds(j, count)
            return Cells(own_rows(n, planes) if k == 1 else old[0][n, planes], old[1][n, planes])

        first, end = k, bx + 2 * DEPTH - k
        count = end - first + 1
        planes = pl.ds(first - 1, count + 1)
        vx1 = load(0, first - 1, count + 2)
        vx, vz, vy, p = (load(n, first - 1, count + 1) for n in range(4))
        up = vz.along_z(True)
        if k == 1:
            after = next_ref[planes]
            both = jnp.concatenate([after[..., 0:by]] * 2, axis=1)
            own = jnp.where(iota((1, rows, by), 1) == bz + bz // 2 - 1, both, up.own)
            lane = iota((1, bz, by), 2)
            here = (iota((1, bz, by), 1) == bz // 2 - 1) & (lane >= by // 4) & (lane < by - by // 4)
            up = Cells(own, jnp.where(here, pltpu.roll(after[..., by:lanes], by // 2, 2), up.side))
        rx = vx1[1:] - vx
        rz = up - vz
        ry = vy.along_y(True) - vy
        a = rx - ry
        b = ry - rz
        inv = (a * (a + b) + b * b) * (1.0 / 3.0) + 1.0
        exponent = constant(1, planes) * inv.map(jnp.log)
        eta = constant(0, planes) * exponent.map(jnp.exp2)
        quarter = eta * 0.25
        div = rx + ry + rz
        p = p - quarter * (div + div)
        tx, tz, ty = eta * rx - p, eta * rz - p, eta * ry - p
        sz = quarter + quarter.along_z(False)
        sy = quarter + quarter.along_y(False)
        if not last:
            new[0][3, planes], new[1][3, planes] = p.own, p.side
        vx0, vz0, vy0, quarter0, tx0, sz0, sy0 = (c[:-1] for c in (vx, vz, vy, quarter, tx, sz, sy))
        vx, vz, vy, eta, p, quarter, tx, tz, ty, sz, sy = (c[1:] for c in (vx, vz, vy, eta, p, quarter, tx, tz, ty, sz, sy))
        sx = quarter + quarter0
        exz = sz + sz0
        exy = sy + sy0
        ezy = sz + sz.along_y(False)
        fxz = exz * (vx - vx.along_z(False))
        fxy = exy * (vx - vx.along_y(False))
        gzx = exz * (vz - vz0)
        hyx = exy * (vy - vy0)
        gzy = ezy * (vz - vz.along_y(False))
        hyz = ezy * (vy - vy.along_z(False))
        res_x = (tx - tx0) + ((fxz.along_z(True) - fxz) + (fxy.along_y(True) - fxy))
        rho = constant(2, pl.ds(first, count))
        part_z = (tz - tz.along_z(False)) - rho + ((gzy.along_y(True) - gzy) - gzx)
        part_y = (ty - ty.along_y(False)) + ((hyz.along_z(True) - hyz) - hyx)
        scale_x, scale_z, scale_y = (
            (total + weights[3]).map(reciprocal) * weight for total, weight in zip((sx, sz, sy), weights)
        )
        new_vx = vx + scale_x * res_x
        new_vz = vz[:-1] + scale_z[:-1] * (part_z[:-1] + gzx[1:])
        new_vy = vy[:-1] + scale_y[:-1] * (part_y[:-1] + hyx[1:])
        if last:
            out_vx_ref[...] = new_vx.own[:-1, 0:bz]
            out_vz_ref[...] = new_vz.own[:, 0:bz]
            out_vy_ref[...] = new_vy.own[:, 0:bz]
            out_p_ref[...] = p.own[:-1, 0:bz]
            out_eta_ref[...] = eta.own[:-1, 0:bz]
            sum_ref[...] = jnp.sum(p.own[:-1, 0:bz], axis=0)

            @pl.when(ix == 0)
            def _():
                out_vx_ref[0] = jnp.zeros((bz, by), jnp.float32)
        else:
            for d, value in enumerate((new_vx, new_vz, new_vy)):
                at = pl.ds(first, count if d == 0 else count - 1)
                new[0][d, at], new[1][d, at] = value.own, value.side

            def clear(d, i):
                for ref in new:
                    ref[d, i] = jnp.zeros(ref.shape[2:], jnp.float32)

            @pl.when(ix == 0)
            def _():
                for i in range(first, DEPTH):
                    for d in range(3):
                        clear(d, i)
                clear(0, DEPTH)

            @pl.when(ix == nx - 1)
            def _():
                for i in range(DEPTH + bx, end + 1):
                    for d in range(3):
                        clear(d, i)


def final_kernel(p_ref, sum_ref, out_ref, *, cells):
    mean = jnp.sum(sum_ref[...]) * (1.0 / cells)
    out_ref[...] = p_ref[...] - mean


def swap(a, axis, start):
    count = lax.axis_size(axis)
    return lax.ppermute(a, axis, [(i, j) for k in range(start, count - 1, 2) for i, j in ((k, k + 1), (k + 1, k))])


def sum_everywhere(total):
    axes = ("gx", "gy", "gz")
    devices = math.prod(lax.axis_size(a) for a in axes)
    total = total + lax.ppermute(total, axes, [(i, i ^ 1) for i in range(devices)])
    total = jnp.broadcast_to(jnp.sum(total, axis=0, keepdims=True), (devices // 2, total.shape[1]))
    groups = [list(range(n, devices, 2)) for n in range(2)]
    return lax.all_to_all(total, axes, 0, 0, tiled=True, axis_index_groups=groups)


def local(vel_x, vel_y, vel_z, pressure, phase, visc_scale, power_n, density):
    bx, bz, by = pressure.shape
    assert bx % (2 * GROUP) == 0 and bz == 2 * DEPTH and DEPTH == GROUP
    f32 = jnp.float32
    iy, ny = lax.axis_index("gy"), lax.axis_size("gy")
    cells = bx * bz * by * math.prod(lax.axis_size(a) for a in ("gx", "gz", "gy"))
    deep = bx + 2 * DEPTH + 1
    rows, lanes = 2 * bz, 2 * by
    shape = lambda *dims: jax.ShapeDtypeStruct(dims, f32)
    block = shape(bx, bz, by)
    scratch = lambda *dims: pltpu.VMEM(dims, f32)
    limit = lambda mebibytes: pltpu.CompilerParams(vmem_limit_bytes=mebibytes * 1024 * 1024)
    groups = bx // GROUP
    stacked = bx * FIELDS + bx // 2 + 2
    sent = shape(DEPTH * FIELDS + 1, bz, by)
    edge, x_0, x_1, stack = pl.pallas_call(
        pack_kernel,
        out_shape=(shape(bx // 2, bz, by), sent, sent, shape(stacked, bz, by)),
        in_specs=[HBM] * 8,
        out_specs=(HBM,) * 4,
        scratch_shapes=[
            scratch(FIELDS - 1, bx, bz, by),
            pltpu.VMEM((bx, bz, by), jnp.int32),
            scratch(bx // 2, bz, by),
            scratch(stacked, bz, by),
            pltpu.SMEM((PHASES,), f32),
            pltpu.SMEM((PHASES,), f32),
            pltpu.SMEM((PHASES,), f32),
            pltpu.SemaphoreType.DMA((groups, FIELDS)),
            pltpu.SemaphoreType.DMA((groups + groups // 2 + 4,)),
            pltpu.SemaphoreType.DMA((3,)),
        ],
        compiler_params=limit(58),
    )(vel_x, vel_z, vel_y, pressure, phase, visc_scale, power_n, density)

    def edges_beside(edge):
        side = swap(edge, "gy", 0)
        if ny == 2:
            return side
        lane = iota(side.shape, 2) % (by // 2) % LANE_STEP
        return jnp.where((lane <= DEPTH) == (lax.rem(iy, 2) == 0), side, swap(edge, "gy", 1))

    estimate = lambda size: pl.CostEstimate(
        flops=4 * size * bz * by, bytes_accessed=size * bz * by * 4, transcendentals=0
    )

    def unpacking(kernel, tiles, out_shape, *args, aliases={}):
        return pl.pallas_call(
            kernel,
            out_shape=out_shape,
            in_specs=[VMEM] * len(args),
            out_specs=(VMEM,) * len(out_shape),
            input_output_aliases=aliases,
            compiler_params=limit(16),
            cost_estimate=estimate(13 * tiles),
        )(*args)

    field = shape(deep, bz, lanes)
    own_shape = (shape(3, deep, bz, lanes),) + (field,) * 4
    half = lambda tiles, planes: shape(tiles + planes // (bz // 2), bz // 2, by)
    x_1, x_0 = swap(x_1, "gx", 1), swap(x_0, "gx", 0)
    face = half(bx * FIELDS, bx)
    extra = (shape(bx // 2, bz, by), shape(2, bz, by), shape(4, rows, lanes))
    z_0, z_1, edge, tables, weights, *own = unpacking(own_kernel, bx, (face, face) + extra + own_shape, stack)
    face_1, face_0 = swap(z_1, "gz", 1), swap(z_0, "gz", 0)

    tiles = bx // 2 + DEPTH
    edge = pl.pallas_call(
        side_edge_kernel,
        out_shape=shape(tiles, bz, by),
        in_specs=[VMEM] * 3,
        out_specs=VMEM,
        compiler_params=limit(4),
    )(x_1, x_0, edge)
    corner = half(2 * DEPTH * FIELDS + 1, 2 * DEPTH)
    sides, z_0, z_1 = pl.pallas_call(
        sides_kernel,
        out_shape=(shape(2 * DEPTH * FIELDS + 1, bz, by), corner, corner),
        in_specs=[VMEM] * 3,
        out_specs=(VMEM,) * 3,
        compiler_params=limit(4),
    )(x_1, x_0, edge)
    edge = edges_beside(edge)
    corner_1, corner_0 = swap(z_1, "gz", 1), swap(z_0, "gz", 0)
    z_0, z_1 = pl.pallas_call(
        edge_rows_kernel,
        out_shape=(half(tiles, tiles),) * 2,
        in_specs=[VMEM],
        out_specs=(VMEM,) * 2,
        compiler_params=limit(4),
        cost_estimate=estimate(100000),
    )(edge)
    edge_1, edge_0 = swap(z_1, "gz", 1), swap(z_0, "gz", 0)

    own = unpacking(
        own_sides_kernel, 2 * deep, own_shape, sides, edge, tables, *own, aliases={n + 3: n for n in range(5)}
    )
    halo = unpacking(
        halo_kernel, deep, (shape(7, deep, bz, lanes), field), face_0, face_1, corner_0, corner_1, tables
    )
    vx, vz, vy, p, eta, total, _, _ = pl.pallas_call(
        main_kernel,
        out_shape=(block,) * 5 + (shape(bz, by),) + tuple(shape(*a.shape) for a in halo),
        in_specs=[VMEM] * 11,
        out_specs=(VMEM,) * 8,
        input_output_aliases={5: 6, 6: 7},
        scratch_shapes=[
            scratch(4, deep, rows, by),
            scratch(4, deep, rows, by),
            scratch(4, deep, bz, by),
            scratch(4, deep, bz, by),
            scratch(3, deep, bz, by),
        ],
        compiler_params=limit(32),
    )(*own, *halo, edge_0, edge_1, tables, weights)

    total = sum_everywhere(total)
    p = pl.pallas_call(
        lambda *refs: final_kernel(*refs, cells=float(cells)),
        out_shape=block,
        in_specs=[VMEM] * 2,
        out_specs=VMEM,
        compiler_params=limit(4),
    )(p, total)
    return (vx, vy, vz, p, eta)


def solution(mesh):
    spec = P("gx", "gz", "gy")
    return jax.shard_map(
        local,
        mesh=mesh,
        in_specs=(spec,) * 5 + (P(),) * 3,
        out_specs=(spec,) * 5,
        check_vma=False,
    )
```

```python
import math

import jax
import jax.numpy as jnp
from jax import lax
from jax.experimental import pallas as pl
from jax.experimental.pallas import tpu as pltpu
from jax.sharding import PartitionSpec as P

ITERS = 4
PHASES = 4
FIELDS = 5
DEPTH = ITERS
LANE_STEP = 2 * DEPTH + 1
GROUP = 4

VMEM = pl.BlockSpec(memory_space=pltpu.VMEM)
HBM = pl.BlockSpec(memory_space=pltpu.HBM)


def z_up(a):
    return pltpu.roll(a, a.shape[-2] - 1, a.ndim - 2)


def z_down(a):
    return pltpu.roll(a, 1, a.ndim - 2)


def y_up(a):
    return pltpu.roll(a, a.shape[-1] - 1, a.ndim - 1)


def y_down(a):
    return pltpu.roll(a, 1, a.ndim - 1)


def reciprocal(a):
    return pl.reciprocal(a, approx=True)


def iota(shape, axis):
    return lax.broadcasted_iota(jnp.int32, shape, axis)


def odd(axis):
    return lax.rem(lax.axis_index(axis), 2) == 1


def by_parity(axis, pair, body):
    pl.when(jnp.logical_not(odd(axis)))(lambda: body(pair[0], pair[1]))
    pl.when(odd(axis))(lambda: body(pair[1], pair[0]))


def start_copies(sources, targets, sems, order):
    copies = {}
    for g in order:
        at = pl.ds(g * GROUP, GROUP)
        copies[g] = [
            pltpu.make_async_copy(a.at[at], b.at[at], sems.at[g, f]) for f, (a, b) in enumerate(zip(sources, targets))
        ]
        for copy in copies[g]:
            copy.start()
    return copies


def clean_group(g, field_ref, phase_ref):
    bx, bz, by = phase_ref.shape
    ix, iz, iy = lax.axis_index("gx"), lax.axis_index("gz"), lax.axis_index("gy")
    plane, row, lane = (iota((GROUP, bz, by), d) for d in range(3))
    at = pl.ds(g * GROUP, GROUP)
    vx, vz, vy, p = (field_ref[f, at] for f in range(FIELDS - 1))
    if g == 0:
        vx = jnp.where((plane > 0) | (ix > 0), vx, 0.0)
    vz = jnp.where((row > 0) | (iz > 0), vz, 0.0)
    vy = jnp.where((lane > 0) | (iy > 0), vy, 0.0)
    return vx, vz, vy, p, phase_ref[at].astype(jnp.float32)


def add_edge(edge, a, base):
    by = edge.shape[-1]
    lane = iota((1,) * (edge.ndim - 1) + (by,), edge.ndim - 1)
    first = pltpu.roll(a, base, a.ndim - 1) if base else a
    edge = jnp.where((lane >= base) & (lane <= base + DEPTH), first, edge)
    last = pltpu.roll(a, (base + LANE_STEP) % by, a.ndim - 1)
    return jnp.where((lane > base + DEPTH) & (lane < base + LANE_STEP), last, edge)


def add_edges(edge, fields, upper):
    for f, a in enumerate(fields):
        edge = add_edge(edge, a, edge.shape[-1] // 2 * upper + LANE_STEP * f)
    return edge


def beside(edge, f, upper):
    by = edge.shape[-1]
    iy = lax.axis_index("gy")
    lane = iota((1,) * (edge.ndim - 1) + (by,), edge.ndim - 1)
    right = (lane <= DEPTH) & (iy < lax.axis_size("gy") - 1)
    left = (lane >= by - DEPTH) & (iy > 0)
    shift = by // 2 * upper + LANE_STEP * f
    a = pltpu.roll(edge, by - shift, edge.ndim - 1) if shift else edge
    b = pltpu.roll(edge, (by - LANE_STEP - shift) % by, edge.ndim - 1)
    return jnp.where(right, a, jnp.where(left, b, 0.0))


def pack_kernel(
    vx_hbm, vz_hbm, vy_hbm, p_hbm, phase_hbm, scale_hbm, power_hbm, rho_hbm, edge_hbm, x_0_hbm, x_1_hbm, stack_hbm,
    field_ref, phase_ref, edge_ref, stack_ref, scale_ref, power_ref, rho_ref, sems, out_sems, table_sems,
):
    bx, bz, by = phase_ref.shape
    targets = [field_ref.at[f] for f in range(FIELDS - 1)] + [phase_ref]
    groups = bx // GROUP
    order = [0, groups - 1] + list(range(1, groups - 1))
    copies = start_copies((vx_hbm, vz_hbm, vy_hbm, p_hbm, phase_hbm), targets, sems, order)
    table_refs = (scale_ref, power_ref, rho_ref)
    pairs = zip((scale_hbm, power_hbm, rho_hbm), table_refs)
    table_copies = [pltpu.make_async_copy(a, b, table_sems.at[n]) for n, (a, b) in enumerate(pairs)]
    for copy in table_copies:
        copy.start()
    half = groups // 2
    outs = []

    def out(source, target):
        outs.append(pltpu.make_async_copy(source, target, out_sems.at[len(outs)]))
        outs[-1].start()

    count = DEPTH * FIELDS
    sems_x = [out_sems.at[out_sems.shape[0] - 1 - n] for n in range(3)]

    def x_copies(to_above, to_below):
        return (
            pltpu.make_async_copy(stack_ref.at[pl.ds(0, count + 1)], to_below, sems_x[0]),
            pltpu.make_async_copy(stack_ref.at[pl.ds(0, 1)], to_above.at[pl.ds(0, 1)], sems_x[1]),
            pltpu.make_async_copy(
                stack_ref.at[pl.ds(bx * FIELDS - count, count)], to_above.at[pl.ds(1, count)], sems_x[2]
            ),
        )

    def start_x(above, below):
        for copy in x_copies(above, below):
            copy.start()

    def wait_x(above, below):
        for copy in x_copies(above, below):
            copy.wait()

    edges = {}
    for g in order:
        for copy in copies[g]:
            copy.wait()
        fields = clean_group(g, field_ref, phase_ref)
        for f, a in enumerate(fields):
            for i in range(GROUP):
                stack_ref[(g * GROUP + i) * FIELDS + f] = a[i]
        at = pl.ds(g * GROUP * FIELDS, GROUP * FIELDS)
        out(stack_ref.at[at], stack_hbm.at[at])
        if g == 1:
            by_parity("gx", (x_0_hbm, x_1_hbm), start_x)
        upper, n = divmod(g, half)
        edge = edges.get(n, jnp.zeros((GROUP, bz, by), jnp.float32))
        edges[n] = add_edges(edge, fields, upper)
        if n + half * (1 - upper) in order[: order.index(g)]:
            at = pl.ds(n * GROUP, GROUP)
            edge_ref[at] = edges[n]
            out(edge_ref.at[at], edge_hbm.at[at])
            stack_ref[pl.ds(bx * FIELDS + n * GROUP, GROUP)] = edges[n]
    end = bx * FIELDS + bx // 2
    row = iota((bz, by), 0)
    for copy in table_copies:
        copy.wait()
    entries = [ref[index] for ref in table_refs for index in range(PHASES)]
    for n in range(2):
        tile = jnp.zeros((bz, by), jnp.float32)
        for r, entry in enumerate(entries[n * bz : (n + 1) * bz]):
            tile = jnp.where(row == r, entry, tile)
        stack_ref[end + n] = tile
    at = pl.ds(bx * FIELDS, end + 2 - bx * FIELDS)
    out(stack_ref.at[at], stack_hbm.at[at])
    by_parity("gx", (x_0_hbm, x_1_hbm), wait_x)
    for copy in outs:
        copy.wait()


def side_edge_kernel(x_1_ref, x_0_ref, own_edge_ref, edge_ref):
    bz, by = edge_ref.shape[1:]
    own = own_edge_ref.shape[0]
    edge_ref[0:own] = own_edge_ref[...]

    def body(above, below):
        edge = jnp.zeros((DEPTH, bz, by), jnp.float32)
        for upper, (ref, at) in enumerate(((above, 0), (below, 1))):
            block = ref[pl.ds(at, DEPTH * FIELDS)].reshape(DEPTH, FIELDS, bz, by)
            edge = add_edges(edge, [block[:, f] for f in range(FIELDS)], upper)
        edge_ref[own:] = edge
        edge_ref[own] = add_edge(edge[0], above[DEPTH * FIELDS], FIELDS * LANE_STEP)

    by_parity("gx", (x_0_ref, x_1_ref), body)


def half_rows(tiles, swap):
    down = odd("gz") if swap == 0 else jnp.logical_not(odd("gz"))
    half = tiles.shape[-2] // 2
    return jnp.where(down, tiles[..., :half, :], tiles[..., half:, :])


def store_next_rows(refs, at, tiles):
    half = tiles.shape[-2] // 2
    for ref in refs:
        for i in range(tiles.shape[0]):
            ref[at + i // half, i % half : i % half + 1, :] = tiles[i, half : half + 1, :]


def sides_kernel(x_1_ref, x_0_ref, _edge_ref, sides_ref, z_0_ref, z_1_ref):
    count = DEPTH * FIELDS
    bz, by = sides_ref.shape[1:]

    def body(above, below):
        sides_ref[0:count] = above[0:count]
        sides_ref[count : 2 * count] = below[1 : count + 1]
        sides_ref[2 * count] = above[count]

    by_parity("gx", (x_0_ref, x_1_ref), body)
    tiles = sides_ref[...]
    for swap, ref in enumerate((z_0_ref, z_1_ref)):
        ref[0 : 2 * count + 1] = half_rows(tiles, swap)
    vz = tiles[0 : 2 * count].reshape(2 * DEPTH, FIELDS, bz, by)[:, 1]
    store_next_rows((z_0_ref, z_1_ref), 2 * count + 1, vz)


def edge_rows_kernel(edge_ref, z_0_ref, z_1_ref):
    tiles = edge_ref[...]
    for swap, ref in enumerate((z_0_ref, z_1_ref)):
        ref[0 : tiles.shape[0]] = half_rows(tiles, swap)
    store_next_rows((z_0_ref, z_1_ref), tiles.shape[0], tiles)


def lookups(fields, ok, keep, table_ref):
    *rest, phase = fields
    for number in range(3):
        rows = [divmod(number * PHASES + index, table_ref.shape[1]) for index in range(PHASES)]
        table = [table_ref[n, r : r + 1, :] for n, r in rows]
        value = jnp.broadcast_to(table[0], phase.shape)
        for index in range(1, PHASES):
            value = jnp.where(phase == float(index), table[index], value)
        if number == 0:
            value = value * jnp.where(ok, 1.0, 0.0)
            if keep is not None:
                value = jnp.where(keep, value, 0.0)
        elif number == 1:
            value = (0.5 / math.log(2.0)) * (reciprocal(value) - 1.0)
        rest.append(value)
    return rest


def own_lanes(block, ok, tables):
    block = block.reshape(-1, FIELDS, *block.shape[-2:])
    return lookups([block[:, f] for f in range(FIELDS)], ok, None, tables)


def edge_lanes(edge, upper, ok, tables):
    by = edge.shape[-1]
    iy = lax.axis_index("gy")
    lane = iota((1, 1, by), 2)
    keep = ((lane <= DEPTH) & (iy < lax.axis_size("gy") - 1)) | ((lane >= by - DEPTH) & (iy > 0))
    return lookups([beside(edge, f, upper) for f in range(FIELDS)], ok, keep, tables)


def store_to(refs):
    def store(planes, part, values):
        by = values[0].shape[-1]
        for ref, value in zip(refs, values):
            ref[planes, :, part * by : (part + 1) * by] = value

    return store


def unpack_own(load, bx, ok, tables, store):
    def group(g, carry):
        at = g * GROUP
        store(pl.ds(DEPTH + at, GROUP), 0, own_lanes(load(at * FIELDS, GROUP * FIELDS), ok, tables))
        return carry

    lax.fori_loop(0, bx // GROUP, group, 0)


def unpack_own_edges(load, bx, ok, tables, store):
    half = bx // 2
    for upper in range(2):

        def group(g, carry):
            at = g * GROUP
            values = edge_lanes(load(at, GROUP), upper, ok, tables)
            store(pl.ds(DEPTH + upper * half + at, GROUP), 1, values)
            return carry

        lax.fori_loop(0, half // GROUP, group, 0)


def side_places(bx):
    ix = lax.axis_index("gx")
    return (pl.ds(DEPTH + bx, DEPTH), ix < lax.axis_size("gx") - 1), (pl.ds(0, DEPTH), ix > 0)


def unpack_sides(load, bx, ok, tables, store, vx_ref):
    count = DEPTH * FIELDS
    for n, (planes, inside) in enumerate(side_places(bx)):
        store(planes, 0, own_lanes(load(n * count, count), ok & inside, tables))
    vx = load(2 * count, 1)
    vx_ref[pl.ds(bx + 2 * DEPTH, 1), :, 0 : vx.shape[-1]] = vx


def unpack_side_edges(load, bx, ok, tables, store, vx_ref):
    half = bx // 2
    edge = load(half, DEPTH)
    for upper, (planes, inside) in enumerate(side_places(bx)):
        store(planes, 1, edge_lanes(edge, upper, ok & inside, tables))
    by = edge.shape[-1]
    vx_ref[pl.ds(bx + 2 * DEPTH, 1), :, by : 2 * by] = beside(edge[0:1], FIELDS, 0)


def make_weights(weight_ref):
    shape = weight_ref.shape[1:]
    rows, lanes = shape
    bz, by = rows // 2, lanes // 2
    nz, ny = lax.axis_size("gz"), lax.axis_size("gy")
    iz, iy = lax.axis_index("gz"), lax.axis_index("gy")
    r, c = iota(shape, 0), iota(shape, 1)
    zg = iz * bz + jnp.where(r < bz + bz // 2, r, r - rows)
    yg = iy * by + jnp.where(c <= by + DEPTH, c, c - lanes)
    filled = (c <= by + DEPTH) | (c >= lanes - DEPTH)
    inside = filled & (zg >= 0) & (zg < nz * bz) & (yg >= 0) & (yg < ny * by)
    weight_ref[0] = jnp.where(inside, 0.05, 0.0)
    weight_ref[1] = jnp.where(inside & (zg > 0), 0.05, 0.0)
    weight_ref[2] = jnp.where(inside & (yg > 0), 0.05, 0.0)
    weight_ref[3] = jnp.where(inside, 0.0, 1.0)


def own_kernel(stack_ref, z_0_ref, z_1_ref, edge_ref, tables_ref, weight_ref, v_ref, *rest):
    bx = v_ref.shape[1] - 2 * DEPTH - 1
    make_weights(weight_ref)
    count = bx * FIELDS
    edge_ref[...] = stack_ref[count : count + bx // 2]
    tables_ref[...] = stack_ref[count + bx // 2 :]
    size = GROUP * FIELDS

    def group(g, carry):
        at = pl.ds(g * size, size)
        tiles = stack_ref[at]
        for swap, ref in enumerate((z_0_ref, z_1_ref)):
            ref[at] = half_rows(tiles, swap)
        return carry

    lax.fori_loop(0, bx // GROUP, group, 0)
    for g in range(bx // GROUP):
        vz = stack_ref[pl.ds(g * size, size)].reshape(GROUP, FIELDS, *stack_ref.shape[1:])[:, 1]
        store_next_rows((z_0_ref, z_1_ref), count + g * GROUP // (stack_ref.shape[1] // 2), vz)
    store = store_to([v_ref.at[d] for d in range(3)] + list(rest))
    unpack_own(lambda at, n: stack_ref[pl.ds(at, n)], bx, True, tables_ref, store)


def own_sides_kernel(sides_ref, edge_ref, tables_ref, *refs):
    v_ref, *rest = refs[len(refs) // 2 :]
    bx = v_ref.shape[1] - 2 * DEPTH - 1
    store = store_to([v_ref.at[d] for d in range(3)] + list(rest))
    unpack_sides(lambda at, n: sides_ref[pl.ds(at, n)], bx, True, tables_ref, store, v_ref.at[0])
    load = lambda at, n: edge_ref[pl.ds(at, n)]
    unpack_own_edges(load, bx, True, tables_ref, store)
    unpack_side_edges(load, bx, True, tables_ref, store, v_ref.at[0])


def rows_in_grid(bz):
    iz = lax.axis_index("gz")
    row = iota((1, bz, 1), 1)
    return ((row < bz // 2) & (iz < lax.axis_size("gz") - 1)) | ((row >= bz // 2) & (iz > 0))


def load_both(above, below):
    return lambda at, n: jnp.concatenate([above[pl.ds(at, n)], below[pl.ds(at, n)]], axis=1)


def halo_kernel(face_0_ref, face_1_ref, corner_0_ref, corner_1_ref, tables_ref, halo_ref, next_ref):
    half, by = face_0_ref.shape[1:]
    bz = 2 * half
    bx = halo_ref.shape[1] - 2 * DEPTH - 1
    ok = rows_in_grid(bz)
    store = store_to([halo_ref.at[n] for n in range(7)])

    def faces(above, below):
        unpack_own(load_both(above, below), bx, ok, tables_ref, store)
        for i in range(bx):
            n = i % half
            next_ref[DEPTH + i, half - 1 : half, 0:by] = above[bx * FIELDS + i // half, n : n + 1, :]

    def corners(above, below):
        unpack_sides(load_both(above, below), bx, ok, tables_ref, store, halo_ref.at[0])
        for i in range(2 * DEPTH):
            n = i % half
            to = DEPTH + bx + i if i < DEPTH else i - DEPTH
            next_ref[to, half - 1 : half, 0:by] = above[2 * DEPTH * FIELDS + 1 + i // half, n : n + 1, :]

    by_parity("gz", (face_0_ref, face_1_ref), faces)
    by_parity("gz", (corner_0_ref, corner_1_ref), corners)


def unpack_halo_edges(edge_0_ref, edge_1_ref, tables_ref, halo_ref, next_ref):
    half, by = edge_0_ref.shape[1:]
    bx = halo_ref.shape[1] - 2 * DEPTH - 1
    ok = rows_in_grid(2 * half)
    store = store_to([halo_ref.at[n] for n in range(7)])
    tiles = bx // 2 + DEPTH

    def body(above, below):
        load = load_both(above, below)
        unpack_own_edges(load, bx, ok, tables_ref, store)
        unpack_side_edges(load, bx, ok, tables_ref, store, halo_ref.at[0])
        for n in range(tiles // half):
            rows = above[tiles + n]
            for upper in range(2):
                values = beside(rows, 1, upper)
                for i in range(half):
                    tile = n * half + i
                    if tile < bx // 2:
                        to = DEPTH + upper * (bx // 2) + tile
                    else:
                        to = tile - bx // 2 + (0 if upper else DEPTH + bx)
                    next_ref[to, half - 1 : half, by : 2 * by] = values[i : i + 1]

    by_parity("gz", (edge_0_ref, edge_1_ref), body)


def main_kernel(
    v_ref, p0_ref, pre_ref, power_field_ref, rho_ref, _halo, _next, edge_0_ref, edge_1_ref, tables_ref, weight_ref,
    out_vx_ref, out_vz_ref, out_vy_ref, out_p_ref, out_eta_ref, sum_ref, halo_ref, next_ref,
    va_ref, vb_ref, p_ref,
):
    bx, bz, by = out_p_ref.shape
    rows, lanes = 2 * bz, 2 * by
    nx, ix = lax.axis_size("gx"), lax.axis_index("gx")
    unpack_halo_edges(edge_0_ref, edge_1_ref, tables_ref, halo_ref, next_ref)

    def with_halo(own, n, planes):
        return jnp.concatenate([own[planes], halo_ref[n, planes]], axis=1)

    for k in range(1, ITERS + 1):
        old, new = (va_ref, vb_ref) if k % 2 else (vb_ref, va_ref)
        last = k == ITERS

        def load(d, j, count):
            planes = pl.ds(j, count)
            return with_halo(v_ref.at[d], d, planes) if k == 1 else old[d, planes]

        def cells(j, count):
            planes = pl.ds(j, count)
            vx1 = load(0, j, count + 1)
            vx = vx1[:count]
            vz, vy = load(1, j, count), load(2, j, count)
            p = with_halo(p0_ref, 3, planes) if k == 1 else p_ref[planes]
            up = z_up(vz)
            if k == 1:
                after = next_ref[planes]
                after = jnp.concatenate([after, after], axis=1)
                up = jnp.where(iota((1, rows, lanes), 1) == bz + bz // 2 - 1, after, up)
            rx = vx1[1:] - vx
            rz = up - vz
            ry = y_up(vy) - vy
            a = rx - ry
            b = ry - rz
            inv = (a * (a + b) + b * b) * (1.0 / 3.0) + 1.0
            eta = with_halo(pre_ref, 4, planes) * jnp.exp2(with_halo(power_field_ref, 5, planes) * jnp.log(inv))
            quarter = 0.25 * eta
            div = rx + ry + rz
            p = p - quarter * (div + div)
            tx, tz, ty = eta * rx - p, eta * rz - p, eta * ry - p
            sz = quarter + z_down(quarter)
            sy = quarter + y_down(quarter)
            return vx, vz, vy, eta, p, quarter, tx, tz, ty, sz, sy

        first, end = k, bx + 2 * DEPTH - k
        count = end - first + 1
        below = cells(first - 1, count + 1)
        vx, vz, vy, eta, p, quarter, tx, tz, ty, sz, sy = (a[1:] for a in below)
        vx0, vz0, vy0, _, _, quarter0, tx0, _, _, sz0, sy0 = (a[:-1] for a in below)
        bias = weight_ref[3:4]
        sx = quarter + quarter0
        exz = sz + sz0
        exy = sy + sy0
        ezy = sy + z_down(sy)
        fxz = exz * (vx - z_down(vx))
        fxy = exy * (vx - y_down(vx))
        gzx = exz * (vz - vz0)
        hyx = exy * (vy - vy0)
        gzy = ezy * (vz - y_down(vz))
        hyz = ezy * (vy - z_down(vy))
        res_x = (tx - tx0) + ((z_up(fxz) - fxz) + (y_up(fxy) - fxy))
        new_vx = vx + weight_ref[0:1] * reciprocal(sx + bias) * res_x
        part_z = (tz - z_down(tz)) - with_halo(rho_ref, 6, pl.ds(first, count)) + ((y_up(gzy) - gzy) - gzx)
        part_y = (ty - y_down(ty)) + ((z_up(hyz) - hyz) - hyx)
        scale_z = weight_ref[1:2] * reciprocal(sz + bias)
        scale_y = weight_ref[2:3] * reciprocal(sy + bias)
        new_vz = vz[:-1] + scale_z[:-1] * (part_z[:-1] + gzx[1:])
        new_vy = vy[:-1] + scale_y[:-1] * (part_y[:-1] + hyx[1:])
        if last:
            out_vx_ref[...] = new_vx[:-1, 0:bz, 0:by]
            out_vz_ref[...] = new_vz[:, 0:bz, 0:by]
            out_vy_ref[...] = new_vy[:, 0:bz, 0:by]
            out_p_ref[...] = p[:-1, 0:bz, 0:by]
            out_eta_ref[...] = eta[:-1, 0:bz, 0:by]
            sum_ref[...] = jnp.sum(p[:-1, 0:bz, 0:by], axis=0)

            @pl.when(ix == 0)
            def _():
                out_vx_ref[0] = jnp.zeros((bz, by), jnp.float32)
        else:
            p_ref[pl.ds(first - 1, count + 1)] = below[4]
            new[0, pl.ds(first, count)] = new_vx
            new[1, pl.ds(first, count - 1)] = new_vz
            new[2, pl.ds(first, count - 1)] = new_vy
            plane = jnp.zeros((rows, lanes), jnp.float32)

            @pl.when(ix == 0)
            def _():
                for i in range(first, DEPTH):
                    for d in range(3):
                        new[d, i] = plane
                new[0, DEPTH] = plane

            @pl.when(ix == nx - 1)
            def _():
                for i in range(DEPTH + bx, end + 1):
                    for d in range(3):
                        new[d, i] = plane


def final_kernel(p_ref, sum_ref, out_ref, *, cells):
    mean = jnp.sum(sum_ref[...]) * (1.0 / cells)
    out_ref[...] = p_ref[...] - mean


def swap(a, axis, start):
    count = lax.axis_size(axis)
    return lax.ppermute(a, axis, [(i, j) for k in range(start, count - 1, 2) for i, j in ((k, k + 1), (k + 1, k))])


def sum_everywhere(total):
    axes = ("gx", "gy", "gz")
    devices = math.prod(lax.axis_size(a) for a in axes)
    total = total + lax.ppermute(total, axes, [(i, i ^ 1) for i in range(devices)])
    total = jnp.broadcast_to(jnp.sum(total, axis=0, keepdims=True), (devices // 2, total.shape[1]))
    groups = [list(range(n, devices, 2)) for n in range(2)]
    return lax.all_to_all(total, axes, 0, 0, tiled=True, axis_index_groups=groups)


def local(vel_x, vel_y, vel_z, pressure, phase, visc_scale, power_n, density):
    bx, bz, by = pressure.shape
    assert bx % (2 * GROUP) == 0 and bz == 2 * DEPTH and DEPTH == GROUP
    f32 = jnp.float32
    iy, ny = lax.axis_index("gy"), lax.axis_size("gy")
    cells = bx * bz * by * math.prod(lax.axis_size(a) for a in ("gx", "gz", "gy"))
    deep = bx + 2 * DEPTH + 1
    rows, lanes = 2 * bz, 2 * by
    shape = lambda *dims: jax.ShapeDtypeStruct(dims, f32)
    block = shape(bx, bz, by)
    scratch = lambda *dims: pltpu.VMEM(dims, f32)
    limit = lambda mebibytes: pltpu.CompilerParams(vmem_limit_bytes=mebibytes * 1024 * 1024)
    groups = bx // GROUP
    stacked = bx * FIELDS + bx // 2 + 2
    sent = shape(DEPTH * FIELDS + 1, bz, by)
    edge, x_0, x_1, stack = pl.pallas_call(
        pack_kernel,
        out_shape=(shape(bx // 2, bz, by), sent, sent, shape(stacked, bz, by)),
        in_specs=[HBM] * 8,
        out_specs=(HBM,) * 4,
        scratch_shapes=[
            scratch(FIELDS - 1, bx, bz, by),
            pltpu.VMEM((bx, bz, by), jnp.int32),
            scratch(bx // 2, bz, by),
            scratch(stacked, bz, by),
            pltpu.SMEM((PHASES,), f32),
            pltpu.SMEM((PHASES,), f32),
            pltpu.SMEM((PHASES,), f32),
            pltpu.SemaphoreType.DMA((groups, FIELDS)),
            pltpu.SemaphoreType.DMA((groups + groups // 2 + 4,)),
            pltpu.SemaphoreType.DMA((3,)),
        ],
        compiler_params=limit(58),
    )(vel_x, vel_z, vel_y, pressure, phase, visc_scale, power_n, density)

    def edges_beside(edge):
        side = swap(edge, "gy", 0)
        if ny == 2:
            return side
        lane = iota(side.shape, 2) % (by // 2) % LANE_STEP
        return jnp.where((lane <= DEPTH) == (lax.rem(iy, 2) == 0), side, swap(edge, "gy", 1))

    estimate = lambda size: pl.CostEstimate(
        flops=4 * size * bz * by, bytes_accessed=size * bz * by * 4, transcendentals=0
    )

    def unpacking(kernel, tiles, out_shape, *args, aliases={}):
        return pl.pallas_call(
            kernel,
            out_shape=out_shape,
            in_specs=[VMEM] * len(args),
            out_specs=(VMEM,) * len(out_shape),
            input_output_aliases=aliases,
            compiler_params=limit(16),
            cost_estimate=estimate(13 * tiles),
        )(*args)

    field = shape(deep, bz, lanes)
    own_shape = (shape(3, deep, bz, lanes),) + (field,) * 4
    half = lambda tiles, planes: shape(tiles + planes // (bz // 2), bz // 2, by)
    x_1, x_0 = swap(x_1, "gx", 1), swap(x_0, "gx", 0)
    face = half(bx * FIELDS, bx)
    extra = (shape(bx // 2, bz, by), shape(2, bz, by), shape(4, rows, lanes))
    z_0, z_1, edge, tables, weights, *own = unpacking(own_kernel, bx, (face, face) + extra + own_shape, stack)
    face_1, face_0 = swap(z_1, "gz", 1), swap(z_0, "gz", 0)

    tiles = bx // 2 + DEPTH
    edge = pl.pallas_call(
        side_edge_kernel,
        out_shape=shape(tiles, bz, by),
        in_specs=[VMEM] * 3,
        out_specs=VMEM,
        compiler_params=limit(4),
    )(x_1, x_0, edge)
    corner = half(2 * DEPTH * FIELDS + 1, 2 * DEPTH)
    sides, z_0, z_1 = pl.pallas_call(
        sides_kernel,
        out_shape=(shape(2 * DEPTH * FIELDS + 1, bz, by), corner, corner),
        in_specs=[VMEM] * 3,
        out_specs=(VMEM,) * 3,
        compiler_params=limit(4),
    )(x_1, x_0, edge)
    edge = edges_beside(edge)
    corner_1, corner_0 = swap(z_1, "gz", 1), swap(z_0, "gz", 0)
    z_0, z_1 = pl.pallas_call(
        edge_rows_kernel,
        out_shape=(half(tiles, tiles),) * 2,
        in_specs=[VMEM],
        out_specs=(VMEM,) * 2,
        compiler_params=limit(4),
        cost_estimate=estimate(100000),
    )(edge)
    edge_1, edge_0 = swap(z_1, "gz", 1), swap(z_0, "gz", 0)

    own = unpacking(
        own_sides_kernel, 2 * deep, own_shape, sides, edge, tables, *own, aliases={n + 3: n for n in range(5)}
    )
    halo = unpacking(
        halo_kernel, deep, (shape(7, deep, bz, lanes), field), face_0, face_1, corner_0, corner_1, tables
    )
    vx, vz, vy, p, eta, total, _, _ = pl.pallas_call(
        main_kernel,
        out_shape=(block,) * 5 + (shape(bz, by),) + tuple(shape(*a.shape) for a in halo),
        in_specs=[VMEM] * 11,
        out_specs=(VMEM,) * 8,
        input_output_aliases={5: 6, 6: 7},
        scratch_shapes=[
            scratch(3, deep, rows, lanes),
            scratch(3, deep, rows, lanes),
            scratch(deep, rows, lanes),
        ],
        compiler_params=limit(32),
    )(*own, *halo, edge_0, edge_1, tables, weights)

    total = sum_everywhere(total)
    p = pl.pallas_call(
        lambda *refs: final_kernel(*refs, cells=float(cells)),
        out_shape=block,
        in_specs=[VMEM] * 2,
        out_specs=VMEM,
        compiler_params=limit(4),
    )(p, total)
    return (vx, vy, vz, p, eta)


def solution(mesh):
    spec = P("gx", "gz", "gy")
    return jax.shard_map(
        local,
        mesh=mesh,
        in_specs=(spec,) * 5 + (P(),) * 3,
        out_specs=(spec,) * 5,
        check_vma=False,
    )
```

```python
import math

import jax
import jax.numpy as jnp
from jax import lax
from jax.experimental import pallas as pl
from jax.experimental.pallas import tpu as pltpu
from jax.sharding import PartitionSpec as P

ITERS = 4
PHASES = 4
FIELDS = 5
DEPTH = ITERS
LANE_STEP = 2 * DEPTH + 1
GROUP = 4

VMEM = pl.BlockSpec(memory_space=pltpu.VMEM)
HBM = pl.BlockSpec(memory_space=pltpu.HBM)


def z_up(a):
    return pltpu.roll(a, a.shape[-2] - 1, a.ndim - 2)


def z_down(a):
    return pltpu.roll(a, 1, a.ndim - 2)


def y_up(a):
    return pltpu.roll(a, a.shape[-1] - 1, a.ndim - 1)


def y_down(a):
    return pltpu.roll(a, 1, a.ndim - 1)


def reciprocal(a):
    return pl.reciprocal(a, approx=True)


def iota(shape, axis):
    return lax.broadcasted_iota(jnp.int32, shape, axis)


def odd(axis):
    return lax.rem(lax.axis_index(axis), 2) == 1


def by_parity(axis, pair, body):
    pl.when(jnp.logical_not(odd(axis)))(lambda: body(pair[0], pair[1]))
    pl.when(odd(axis))(lambda: body(pair[1], pair[0]))


def start_copies(sources, targets, sems, order):
    copies = {}
    for g in order:
        at = pl.ds(g * GROUP, GROUP)
        copies[g] = [
            pltpu.make_async_copy(a.at[at], b.at[at], sems.at[g, f]) for f, (a, b) in enumerate(zip(sources, targets))
        ]
        for copy in copies[g]:
            copy.start()
    return copies


def clean_group(g, field_ref, phase_ref):
    bx, bz, by = phase_ref.shape
    ix, iz, iy = lax.axis_index("gx"), lax.axis_index("gz"), lax.axis_index("gy")
    plane, row, lane = (iota((GROUP, bz, by), d) for d in range(3))
    at = pl.ds(g * GROUP, GROUP)
    vx, vz, vy, p = (field_ref[f, at] for f in range(FIELDS - 1))
    if g == 0:
        vx = jnp.where((plane > 0) | (ix > 0), vx, 0.0)
    vz = jnp.where((row > 0) | (iz > 0), vz, 0.0)
    vy = jnp.where((lane > 0) | (iy > 0), vy, 0.0)
    return vx, vz, vy, p, phase_ref[at].astype(jnp.float32)


def add_edge(edge, a, base):
    by = edge.shape[-1]
    lane = iota((1,) * (edge.ndim - 1) + (by,), edge.ndim - 1)
    first = pltpu.roll(a, base, a.ndim - 1) if base else a
    edge = jnp.where((lane >= base) & (lane <= base + DEPTH), first, edge)
    last = pltpu.roll(a, (base + LANE_STEP) % by, a.ndim - 1)
    return jnp.where((lane > base + DEPTH) & (lane < base + LANE_STEP), last, edge)


def add_edges(edge, fields, upper):
    for f, a in enumerate(fields):
        edge = add_edge(edge, a, edge.shape[-1] // 2 * upper + LANE_STEP * f)
    return edge


def beside(edge, f, upper):
    by = edge.shape[-1]
    iy = lax.axis_index("gy")
    lane = iota((1,) * (edge.ndim - 1) + (by,), edge.ndim - 1)
    right = (lane <= DEPTH) & (iy < lax.axis_size("gy") - 1)
    left = (lane >= by - DEPTH) & (iy > 0)
    shift = by // 2 * upper + LANE_STEP * f
    a = pltpu.roll(edge, by - shift, edge.ndim - 1) if shift else edge
    b = pltpu.roll(edge, (by - LANE_STEP - shift) % by, edge.ndim - 1)
    return jnp.where(right, a, jnp.where(left, b, 0.0))


def pack_kernel(
    vx_hbm, vz_hbm, vy_hbm, p_hbm, phase_hbm, scale_hbm, power_hbm, rho_hbm, edge_hbm, x_0_hbm, x_1_hbm, stack_hbm,
    field_ref, phase_ref, edge_ref, stack_ref, scale_ref, power_ref, rho_ref, sems, out_sems, table_sems,
):
    bx, bz, by = phase_ref.shape
    targets = [field_ref.at[f] for f in range(FIELDS - 1)] + [phase_ref]
    groups = bx // GROUP
    order = [0, groups - 1] + list(range(1, groups - 1))
    copies = start_copies((vx_hbm, vz_hbm, vy_hbm, p_hbm, phase_hbm), targets, sems, order)
    table_refs = (scale_ref, power_ref, rho_ref)
    pairs = zip((scale_hbm, power_hbm, rho_hbm), table_refs)
    table_copies = [pltpu.make_async_copy(a, b, table_sems.at[n]) for n, (a, b) in enumerate(pairs)]
    for copy in table_copies:
        copy.start()
    half = groups // 2
    outs = []

    def out(source, target):
        outs.append(pltpu.make_async_copy(source, target, out_sems.at[len(outs)]))
        outs[-1].start()

    count = DEPTH * FIELDS
    sems_x = [out_sems.at[out_sems.shape[0] - 1 - n] for n in range(3)]

    def x_copies(to_above, to_below):
        return (
            pltpu.make_async_copy(stack_ref.at[pl.ds(0, count + 1)], to_below, sems_x[0]),
            pltpu.make_async_copy(stack_ref.at[pl.ds(0, 1)], to_above.at[pl.ds(0, 1)], sems_x[1]),
            pltpu.make_async_copy(
                stack_ref.at[pl.ds(bx * FIELDS - count, count)], to_above.at[pl.ds(1, count)], sems_x[2]
            ),
        )

    def start_x(above, below):
        for copy in x_copies(above, below):
            copy.start()

    def wait_x(above, below):
        for copy in x_copies(above, below):
            copy.wait()

    edges = {}
    for g in order:
        for copy in copies[g]:
            copy.wait()
        fields = clean_group(g, field_ref, phase_ref)
        for f, a in enumerate(fields):
            for i in range(GROUP):
                stack_ref[(g * GROUP + i) * FIELDS + f] = a[i]
        at = pl.ds(g * GROUP * FIELDS, GROUP * FIELDS)
        out(stack_ref.at[at], stack_hbm.at[at])
        if g == 1:
            by_parity("gx", (x_0_hbm, x_1_hbm), start_x)
        upper, n = divmod(g, half)
        edge = edges.get(n, jnp.zeros((GROUP, bz, by), jnp.float32))
        edges[n] = add_edges(edge, fields, upper)
        if n + half * (1 - upper) in order[: order.index(g)]:
            at = pl.ds(n * GROUP, GROUP)
            edge_ref[at] = edges[n]
            out(edge_ref.at[at], edge_hbm.at[at])
            stack_ref[pl.ds(bx * FIELDS + n * GROUP, GROUP)] = edges[n]
    end = bx * FIELDS + bx // 2
    row = iota((bz, by), 0)
    for copy in table_copies:
        copy.wait()
    entries = [ref[index] for ref in table_refs for index in range(PHASES)]
    for n in range(2):
        tile = jnp.zeros((bz, by), jnp.float32)
        for r, entry in enumerate(entries[n * bz : (n + 1) * bz]):
            tile = jnp.where(row == r, entry, tile)
        stack_ref[end + n] = tile
    at = pl.ds(bx * FIELDS, end + 2 - bx * FIELDS)
    out(stack_ref.at[at], stack_hbm.at[at])
    by_parity("gx", (x_0_hbm, x_1_hbm), wait_x)
    for copy in outs:
        copy.wait()


def side_edge_kernel(x_1_ref, x_0_ref, own_edge_ref, edge_ref):
    bz, by = edge_ref.shape[1:]
    own = own_edge_ref.shape[0]
    edge_ref[0:own] = own_edge_ref[...]

    def body(above, below):
        edge = jnp.zeros((DEPTH, bz, by), jnp.float32)
        for upper, (ref, at) in enumerate(((above, 0), (below, 1))):
            block = ref[pl.ds(at, DEPTH * FIELDS)].reshape(DEPTH, FIELDS, bz, by)
            edge = add_edges(edge, [block[:, f] for f in range(FIELDS)], upper)
        edge_ref[own:] = edge
        edge_ref[own] = add_edge(edge[0], above[DEPTH * FIELDS], FIELDS * LANE_STEP)

    by_parity("gx", (x_0_ref, x_1_ref), body)


def half_rows(tiles, swap):
    down = odd("gz") if swap == 0 else jnp.logical_not(odd("gz"))
    half = tiles.shape[-2] // 2
    return jnp.where(down, tiles[..., :half, :], tiles[..., half:, :])


def store_next_rows(refs, at, tiles):
    half = tiles.shape[-2] // 2
    for ref in refs:
        for i in range(tiles.shape[0]):
            ref[at + i // half, i % half : i % half + 1, :] = tiles[i, half : half + 1, :]


def sides_kernel(x_1_ref, x_0_ref, _edge_ref, sides_ref, z_0_ref, z_1_ref):
    count = DEPTH * FIELDS
    bz, by = sides_ref.shape[1:]

    def body(above, below):
        sides_ref[0:count] = above[0:count]
        sides_ref[count : 2 * count] = below[1 : count + 1]
        sides_ref[2 * count] = above[count]

    by_parity("gx", (x_0_ref, x_1_ref), body)
    tiles = sides_ref[...]
    for swap, ref in enumerate((z_0_ref, z_1_ref)):
        ref[0 : 2 * count + 1] = half_rows(tiles, swap)
    vz = tiles[0 : 2 * count].reshape(2 * DEPTH, FIELDS, bz, by)[:, 1]
    store_next_rows((z_0_ref, z_1_ref), 2 * count + 1, vz)


def edge_rows_kernel(edge_ref, z_0_ref, z_1_ref):
    tiles = edge_ref[...]
    for swap, ref in enumerate((z_0_ref, z_1_ref)):
        ref[0 : tiles.shape[0]] = half_rows(tiles, swap)
    store_next_rows((z_0_ref, z_1_ref), tiles.shape[0], tiles)


def lookups(fields, ok, keep, table_ref):
    *rest, phase = fields
    for number in range(3):
        rows = [divmod(number * PHASES + index, table_ref.shape[1]) for index in range(PHASES)]
        table = [table_ref[n, r : r + 1, :] for n, r in rows]
        value = jnp.broadcast_to(table[0], phase.shape)
        for index in range(1, PHASES):
            value = jnp.where(phase == float(index), table[index], value)
        if number == 0:
            value = value * jnp.where(ok, 1.0, 0.0)
            if keep is not None:
                value = jnp.where(keep, value, 0.0)
        elif number == 1:
            value = (0.5 / math.log(2.0)) * (reciprocal(value) - 1.0)
        rest.append(value)
    return rest


def own_lanes(block, ok, tables):
    block = block.reshape(-1, FIELDS, *block.shape[-2:])
    return lookups([block[:, f] for f in range(FIELDS)], ok, None, tables)


def edge_lanes(edge, upper, ok, tables):
    by = edge.shape[-1]
    iy = lax.axis_index("gy")
    lane = iota((1, 1, by), 2)
    keep = ((lane <= DEPTH) & (iy < lax.axis_size("gy") - 1)) | ((lane >= by - DEPTH) & (iy > 0))
    return lookups([beside(edge, f, upper) for f in range(FIELDS)], ok, keep, tables)


def store_to(refs):
    def store(planes, part, values):
        by = values[0].shape[-1]
        for ref, value in zip(refs, values):
            ref[planes, :, part * by : (part + 1) * by] = value

    return store


def unpack_own(load, bx, ok, tables, store):
    for at in range(0, bx, GROUP):
        store(pl.ds(DEPTH + at, GROUP), 0, own_lanes(load(at * FIELDS, GROUP * FIELDS), ok, tables))


def unpack_own_edges(load, bx, ok, tables, store):
    half = bx // 2
    for at in range(0, half, GROUP):
        edge = load(at, GROUP)
        for upper in range(2):
            store(pl.ds(DEPTH + upper * half + at, GROUP), 1, edge_lanes(edge, upper, ok, tables))


def side_places(bx):
    ix = lax.axis_index("gx")
    return (pl.ds(DEPTH + bx, DEPTH), ix < lax.axis_size("gx") - 1), (pl.ds(0, DEPTH), ix > 0)


def unpack_sides(load, bx, ok, tables, store, vx_ref):
    count = DEPTH * FIELDS
    for n, (planes, inside) in enumerate(side_places(bx)):
        store(planes, 0, own_lanes(load(n * count, count), ok & inside, tables))
    vx = load(2 * count, 1)
    vx_ref[pl.ds(bx + 2 * DEPTH, 1), :, 0 : vx.shape[-1]] = vx


def unpack_side_edges(load, bx, ok, tables, store, vx_ref):
    half = bx // 2
    edge = load(half, DEPTH)
    for upper, (planes, inside) in enumerate(side_places(bx)):
        store(planes, 1, edge_lanes(edge, upper, ok & inside, tables))
    by = edge.shape[-1]
    vx_ref[pl.ds(bx + 2 * DEPTH, 1), :, by : 2 * by] = beside(edge[0:1], FIELDS, 0)


def make_weights(weight_ref):
    shape = weight_ref.shape[1:]
    rows, lanes = shape
    bz, by = rows // 2, lanes // 2
    nz, ny = lax.axis_size("gz"), lax.axis_size("gy")
    iz, iy = lax.axis_index("gz"), lax.axis_index("gy")
    r, c = iota(shape, 0), iota(shape, 1)
    zg = iz * bz + jnp.where(r < bz + bz // 2, r, r - rows)
    yg = iy * by + jnp.where(c <= by + DEPTH, c, c - lanes)
    filled = (c <= by + DEPTH) | (c >= lanes - DEPTH)
    inside = filled & (zg >= 0) & (zg < nz * bz) & (yg >= 0) & (yg < ny * by)
    weight_ref[0] = jnp.where(inside, 0.05, 0.0)
    weight_ref[1] = jnp.where(inside & (zg > 0), 0.05, 0.0)
    weight_ref[2] = jnp.where(inside & (yg > 0), 0.05, 0.0)
    weight_ref[3] = jnp.where(inside, 0.0, 1.0)


def own_kernel(stack_ref, z_0_ref, z_1_ref, edge_ref, tables_ref, weight_ref, v_ref, *rest):
    bx = v_ref.shape[1] - 2 * DEPTH - 1
    make_weights(weight_ref)
    count = bx * FIELDS
    edge_ref[...] = stack_ref[count : count + bx // 2]
    tables_ref[...] = stack_ref[count + bx // 2 :]
    size = GROUP * FIELDS

    for g in range(bx // GROUP):
        at = pl.ds(g * size, size)
        tiles = stack_ref[at]
        for swap, ref in enumerate((z_0_ref, z_1_ref)):
            ref[at] = half_rows(tiles, swap)
        vz = stack_ref[pl.ds(g * size, size)].reshape(GROUP, FIELDS, *stack_ref.shape[1:])[:, 1]
        store_next_rows((z_0_ref, z_1_ref), count + g * GROUP // (stack_ref.shape[1] // 2), vz)
    store = store_to([v_ref.at[d] for d in range(3)] + list(rest))
    unpack_own(lambda at, n: stack_ref[pl.ds(at, n)], bx, True, tables_ref, store)


def own_sides_kernel(sides_ref, edge_ref, tables_ref, *refs):
    v_ref, *rest = refs[len(refs) // 2 :]
    bx = v_ref.shape[1] - 2 * DEPTH - 1
    store = store_to([v_ref.at[d] for d in range(3)] + list(rest))
    unpack_sides(lambda at, n: sides_ref[pl.ds(at, n)], bx, True, tables_ref, store, v_ref.at[0])
    load = lambda at, n: edge_ref[pl.ds(at, n)]
    unpack_own_edges(load, bx, True, tables_ref, store)
    unpack_side_edges(load, bx, True, tables_ref, store, v_ref.at[0])


def rows_in_grid(bz):
    iz = lax.axis_index("gz")
    row = iota((1, bz, 1), 1)
    return ((row < bz // 2) & (iz < lax.axis_size("gz") - 1)) | ((row >= bz // 2) & (iz > 0))


def load_both(above, below):
    return lambda at, n: jnp.concatenate([above[pl.ds(at, n)], below[pl.ds(at, n)]], axis=1)


def halo_kernel(face_0_ref, face_1_ref, corner_0_ref, corner_1_ref, tables_ref, halo_ref, next_ref):
    half, by = face_0_ref.shape[1:]
    bz = 2 * half
    bx = halo_ref.shape[1] - 2 * DEPTH - 1
    ok = rows_in_grid(bz)
    store = store_to([halo_ref.at[n] for n in range(7)])

    def faces(above, below):
        unpack_own(load_both(above, below), bx, ok, tables_ref, store)
        for i in range(bx):
            n = i % half
            next_ref[DEPTH + i, half - 1 : half, 0:by] = above[bx * FIELDS + i // half, n : n + 1, :]

    def corners(above, below):
        unpack_sides(load_both(above, below), bx, ok, tables_ref, store, halo_ref.at[0])
        for i in range(2 * DEPTH):
            n = i % half
            to = DEPTH + bx + i if i < DEPTH else i - DEPTH
            next_ref[to, half - 1 : half, 0:by] = above[2 * DEPTH * FIELDS + 1 + i // half, n : n + 1, :]

    by_parity("gz", (face_0_ref, face_1_ref), faces)
    by_parity("gz", (corner_0_ref, corner_1_ref), corners)


def unpack_halo_edges(edge_0_ref, edge_1_ref, tables_ref, halo_ref, next_ref):
    half, by = edge_0_ref.shape[1:]
    bx = halo_ref.shape[1] - 2 * DEPTH - 1
    ok = rows_in_grid(2 * half)
    store = store_to([halo_ref.at[n] for n in range(7)])
    tiles = bx // 2 + DEPTH

    def body(above, below):
        load = load_both(above, below)
        unpack_own_edges(load, bx, ok, tables_ref, store)
        unpack_side_edges(load, bx, ok, tables_ref, store, halo_ref.at[0])
        for n in range(tiles // half):
            rows = above[tiles + n]
            for upper in range(2):
                values = beside(rows, 1, upper)
                for i in range(half):
                    tile = n * half + i
                    if tile < bx // 2:
                        to = DEPTH + upper * (bx // 2) + tile
                    else:
                        to = tile - bx // 2 + (0 if upper else DEPTH + bx)
                    next_ref[to, half - 1 : half, by : 2 * by] = values[i : i + 1]

    by_parity("gz", (edge_0_ref, edge_1_ref), body)


def main_kernel(
    v_ref, p0_ref, pre_ref, power_field_ref, rho_ref, _halo, _next, edge_0_ref, edge_1_ref, tables_ref, weight_ref,
    out_vx_ref, out_vz_ref, out_vy_ref, out_p_ref, out_eta_ref, sum_ref, halo_ref, next_ref,
    va_ref, vb_ref, p_ref,
):
    bx, bz, by = out_p_ref.shape
    rows, lanes = 2 * bz, 2 * by
    nx, ix = lax.axis_size("gx"), lax.axis_index("gx")
    unpack_halo_edges(edge_0_ref, edge_1_ref, tables_ref, halo_ref, next_ref)

    def with_halo(own, n, planes):
        return jnp.concatenate([own[planes], halo_ref[n, planes]], axis=1)

    for k in range(1, ITERS + 1):
        old, new = (va_ref, vb_ref) if k % 2 else (vb_ref, va_ref)
        last = k == ITERS

        def load(d, j, count):
            planes = pl.ds(j, count)
            return with_halo(v_ref.at[d], d, planes) if k == 1 else old[d, planes]

        def cells(j, count):
            planes = pl.ds(j, count)
            vx1 = load(0, j, count + 1)
            vx = vx1[:count]
            vz, vy = load(1, j, count), load(2, j, count)
            p = with_halo(p0_ref, 3, planes) if k == 1 else p_ref[planes]
            up = z_up(vz)
            if k == 1:
                after = next_ref[planes]
                after = jnp.concatenate([after, after], axis=1)
                up = jnp.where(iota((1, rows, lanes), 1) == bz + bz // 2 - 1, after, up)
            rx = vx1[1:] - vx
            rz = up - vz
            ry = y_up(vy) - vy
            a = rx - ry
            b = ry - rz
            inv = (a * (a + b) + b * b) * (1.0 / 3.0) + 1.0
            eta = with_halo(pre_ref, 4, planes) * jnp.exp2(with_halo(power_field_ref, 5, planes) * jnp.log(inv))
            quarter = 0.25 * eta
            div = rx + ry + rz
            p = p - quarter * (div + div)
            tx, tz, ty = eta * rx - p, eta * rz - p, eta * ry - p
            sz = quarter + z_down(quarter)
            sy = quarter + y_down(quarter)
            return vx, vz, vy, eta, p, quarter, tx, tz, ty, sz, sy

        first, end = k, bx + 2 * DEPTH - k
        count = end - first + 1
        below = cells(first - 1, count + 1)
        vx, vz, vy, eta, p, quarter, tx, tz, ty, sz, sy = (a[1:] for a in below)
        vx0, vz0, vy0, _, _, quarter0, tx0, _, _, sz0, sy0 = (a[:-1] for a in below)
        bias = weight_ref[3:4]
        sx = quarter + quarter0
        exz = sz + sz0
        exy = sy + sy0
        ezy = sy + z_down(sy)
        fxz = exz * (vx - z_down(vx))
        fxy = exy * (vx - y_down(vx))
        gzx = exz * (vz - vz0)
        hyx = exy * (vy - vy0)
        gzy = ezy * (vz - y_down(vz))
        hyz = ezy * (vy - z_down(vy))
        res_x = (tx - tx0) + ((z_up(fxz) - fxz) + (y_up(fxy) - fxy))
        new_vx = vx + weight_ref[0:1] * reciprocal(sx + bias) * res_x
        part_z = (tz - z_down(tz)) - with_halo(rho_ref, 6, pl.ds(first, count)) + ((y_up(gzy) - gzy) - gzx)
        part_y = (ty - y_down(ty)) + ((z_up(hyz) - hyz) - hyx)
        scale_z = weight_ref[1:2] * reciprocal(sz + bias)
        scale_y = weight_ref[2:3] * reciprocal(sy + bias)
        new_vz = vz[:-1] + scale_z[:-1] * (part_z[:-1] + gzx[1:])
        new_vy = vy[:-1] + scale_y[:-1] * (part_y[:-1] + hyx[1:])
        if last:
            out_vx_ref[...] = new_vx[:-1, 0:bz, 0:by]
            out_vz_ref[...] = new_vz[:, 0:bz, 0:by]
            out_vy_ref[...] = new_vy[:, 0:bz, 0:by]
            out_p_ref[...] = p[:-1, 0:bz, 0:by]
            out_eta_ref[...] = eta[:-1, 0:bz, 0:by]
            sum_ref[...] = jnp.sum(p[:-1, 0:bz, 0:by], axis=0)

            @pl.when(ix == 0)
            def _():
                out_vx_ref[0] = jnp.zeros((bz, by), jnp.float32)
        else:
            p_ref[pl.ds(first - 1, count + 1)] = below[4]
            new[0, pl.ds(first, count)] = new_vx
            new[1, pl.ds(first, count - 1)] = new_vz
            new[2, pl.ds(first, count - 1)] = new_vy
            plane = jnp.zeros((rows, lanes), jnp.float32)

            @pl.when(ix == 0)
            def _():
                for i in range(first, DEPTH):
                    for d in range(3):
                        new[d, i] = plane
                new[0, DEPTH] = plane

            @pl.when(ix == nx - 1)
            def _():
                for i in range(DEPTH + bx, end + 1):
                    for d in range(3):
                        new[d, i] = plane


def final_kernel(p_ref, sum_ref, out_ref, *, cells):
    mean = jnp.sum(sum_ref[...]) * (1.0 / cells)
    out_ref[...] = p_ref[...] - mean


def swap(a, axis, start):
    count = lax.axis_size(axis)
    return lax.ppermute(a, axis, [(i, j) for k in range(start, count - 1, 2) for i, j in ((k, k + 1), (k + 1, k))])


def sum_everywhere(total):
    axes = ("gx", "gy", "gz")
    devices = math.prod(lax.axis_size(a) for a in axes)
    total = total + lax.ppermute(total, axes, [(i, i ^ 1) for i in range(devices)])
    total = jnp.broadcast_to(jnp.sum(total, axis=0, keepdims=True), (devices // 2, total.shape[1]))
    groups = [list(range(n, devices, 2)) for n in range(2)]
    return lax.all_to_all(total, axes, 0, 0, tiled=True, axis_index_groups=groups)


def local(vel_x, vel_y, vel_z, pressure, phase, visc_scale, power_n, density):
    bx, bz, by = pressure.shape
    assert bx % (2 * GROUP) == 0 and bz == 2 * DEPTH and DEPTH == GROUP
    f32 = jnp.float32
    iy, ny = lax.axis_index("gy"), lax.axis_size("gy")
    cells = bx * bz * by * math.prod(lax.axis_size(a) for a in ("gx", "gz", "gy"))
    deep = bx + 2 * DEPTH + 1
    rows, lanes = 2 * bz, 2 * by
    shape = lambda *dims: jax.ShapeDtypeStruct(dims, f32)
    block = shape(bx, bz, by)
    scratch = lambda *dims: pltpu.VMEM(dims, f32)
    limit = lambda mebibytes: pltpu.CompilerParams(vmem_limit_bytes=mebibytes * 1024 * 1024)
    groups = bx // GROUP
    stacked = bx * FIELDS + bx // 2 + 2
    sent = shape(DEPTH * FIELDS + 1, bz, by)
    edge, x_0, x_1, stack = pl.pallas_call(
        pack_kernel,
        out_shape=(shape(bx // 2, bz, by), sent, sent, shape(stacked, bz, by)),
        in_specs=[HBM] * 8,
        out_specs=(HBM,) * 4,
        scratch_shapes=[
            scratch(FIELDS - 1, bx, bz, by),
            pltpu.VMEM((bx, bz, by), jnp.int32),
            scratch(bx // 2, bz, by),
            scratch(stacked, bz, by),
            pltpu.SMEM((PHASES,), f32),
            pltpu.SMEM((PHASES,), f32),
            pltpu.SMEM((PHASES,), f32),
            pltpu.SemaphoreType.DMA((groups, FIELDS)),
            pltpu.SemaphoreType.DMA((groups + groups // 2 + 4,)),
            pltpu.SemaphoreType.DMA((3,)),
        ],
        compiler_params=limit(58),
    )(vel_x, vel_z, vel_y, pressure, phase, visc_scale, power_n, density)

    def edges_beside(edge):
        side = swap(edge, "gy", 0)
        if ny == 2:
            return side
        lane = iota(side.shape, 2) % (by // 2) % LANE_STEP
        return jnp.where((lane <= DEPTH) == (lax.rem(iy, 2) == 0), side, swap(edge, "gy", 1))

    estimate = lambda size: pl.CostEstimate(
        flops=4 * size * bz * by, bytes_accessed=size * bz * by * 4, transcendentals=0
    )

    def unpacking(kernel, tiles, out_shape, *args, aliases={}):
        return pl.pallas_call(
            kernel,
            out_shape=out_shape,
            in_specs=[VMEM] * len(args),
            out_specs=(VMEM,) * len(out_shape),
            input_output_aliases=aliases,
            compiler_params=limit(16),
            cost_estimate=estimate(13 * tiles),
        )(*args)

    field = shape(deep, bz, lanes)
    own_shape = (shape(3, deep, bz, lanes),) + (field,) * 4
    half = lambda tiles, planes: shape(tiles + planes // (bz // 2), bz // 2, by)
    x_1, x_0 = swap(x_1, "gx", 1), swap(x_0, "gx", 0)
    face = half(bx * FIELDS, bx)
    extra = (shape(bx // 2, bz, by), shape(2, bz, by), shape(4, rows, lanes))
    z_0, z_1, edge, tables, weights, *own = unpacking(own_kernel, bx, (face, face) + extra + own_shape, stack)
    face_1, face_0 = swap(z_1, "gz", 1), swap(z_0, "gz", 0)

    tiles = bx // 2 + DEPTH
    edge = pl.pallas_call(
        side_edge_kernel,
        out_shape=shape(tiles, bz, by),
        in_specs=[VMEM] * 3,
        out_specs=VMEM,
        compiler_params=limit(4),
    )(x_1, x_0, edge)
    corner = half(2 * DEPTH * FIELDS + 1, 2 * DEPTH)
    sides, z_0, z_1 = pl.pallas_call(
        sides_kernel,
        out_shape=(shape(2 * DEPTH * FIELDS + 1, bz, by), corner, corner),
        in_specs=[VMEM] * 3,
        out_specs=(VMEM,) * 3,
        compiler_params=limit(4),
    )(x_1, x_0, edge)
    edge = edges_beside(edge)
    corner_1, corner_0 = swap(z_1, "gz", 1), swap(z_0, "gz", 0)
    z_0, z_1 = pl.pallas_call(
        edge_rows_kernel,
        out_shape=(half(tiles, tiles),) * 2,
        in_specs=[VMEM],
        out_specs=(VMEM,) * 2,
        compiler_params=limit(4),
        cost_estimate=estimate(100000),
    )(edge)
    edge_1, edge_0 = swap(z_1, "gz", 1), swap(z_0, "gz", 0)

    own = unpacking(
        own_sides_kernel, 2 * deep, own_shape, sides, edge, tables, *own, aliases={n + 3: n for n in range(5)}
    )
    halo = unpacking(
        halo_kernel, deep, (shape(7, deep, bz, lanes), field), face_0, face_1, corner_0, corner_1, tables
    )
    vx, vz, vy, p, eta, total, _, _ = pl.pallas_call(
        main_kernel,
        out_shape=(block,) * 5 + (shape(bz, by),) + tuple(shape(*a.shape) for a in halo),
        in_specs=[VMEM] * 11,
        out_specs=(VMEM,) * 8,
        input_output_aliases={5: 6, 6: 7},
        scratch_shapes=[
            scratch(3, deep, rows, lanes),
            scratch(3, deep, rows, lanes),
            scratch(deep, rows, lanes),
        ],
        compiler_params=limit(32),
    )(*own, *halo, edge_0, edge_1, tables, weights)

    total = sum_everywhere(total)
    p = pl.pallas_call(
        lambda *refs: final_kernel(*refs, cells=float(cells)),
        out_shape=block,
        in_specs=[VMEM] * 2,
        out_specs=VMEM,
        compiler_params=limit(4),
    )(p, total)
    return (vx, vy, vz, p, eta)


def solution(mesh):
    spec = P("gx", "gz", "gy")
    return jax.shard_map(
        local,
        mesh=mesh,
        in_specs=(spec,) * 5 + (P(),) * 3,
        out_specs=(spec,) * 5,
        check_vma=False,
    )
```

```python
import math

import jax
import jax.numpy as jnp
from jax import lax
from jax.experimental import pallas as pl
from jax.experimental.pallas import tpu as pltpu
from jax.sharding import PartitionSpec as P

ITERS = 4
PHASES = 4
FIELDS = 5
DEPTH = ITERS
LANE_STEP = 2 * DEPTH + 1
GROUP = 4

VMEM = pl.BlockSpec(memory_space=pltpu.VMEM)
HBM = pl.BlockSpec(memory_space=pltpu.HBM)


def z_up(a):
    return pltpu.roll(a, a.shape[-2] - 1, a.ndim - 2)


def z_down(a):
    return pltpu.roll(a, 1, a.ndim - 2)


def y_up(a):
    return pltpu.roll(a, a.shape[-1] - 1, a.ndim - 1)


def y_down(a):
    return pltpu.roll(a, 1, a.ndim - 1)


def reciprocal(a):
    return pl.reciprocal(a, approx=True)


def iota(shape, axis):
    return lax.broadcasted_iota(jnp.int32, shape, axis)


def odd(axis):
    return lax.rem(lax.axis_index(axis), 2) == 1


def by_parity(axis, pair, body):
    pl.when(jnp.logical_not(odd(axis)))(lambda: body(pair[0], pair[1]))
    pl.when(odd(axis))(lambda: body(pair[1], pair[0]))


def start_copies(sources, targets, sems):
    half = sources[0].shape[0] // 2
    copies = {}
    for n in range(2):
        at = pl.ds(n * half, half)
        copies[n * (half // GROUP)] = [
            pltpu.make_async_copy(a.at[at], b.at[at], sems.at[n, f]) for f, (a, b) in enumerate(zip(sources, targets))
        ]
    for half_copies in copies.values():
        for copy in half_copies:
            copy.start()
    return copies


def clean_group(g, field_ref, phase_ref):
    bx, bz, by = phase_ref.shape
    ix, iz, iy = lax.axis_index("gx"), lax.axis_index("gz"), lax.axis_index("gy")
    plane, row, lane = (iota((GROUP, bz, by), d) for d in range(3))
    at = pl.ds(g * GROUP, GROUP)
    vx, vz, vy, p = (field_ref[f, at] for f in range(FIELDS - 1))
    if g == 0:
        vx = jnp.where((plane > 0) | (ix > 0), vx, 0.0)
    vz = jnp.where((row > 0) | (iz > 0), vz, 0.0)
    vy = jnp.where((lane > 0) | (iy > 0), vy, 0.0)
    return vx, vz, vy, p, phase_ref[at].astype(jnp.float32)


def add_edge(edge, a, base):
    by = edge.shape[-1]
    lane = iota((1,) * (edge.ndim - 1) + (by,), edge.ndim - 1)
    first = pltpu.roll(a, base, a.ndim - 1) if base else a
    edge = jnp.where((lane >= base) & (lane <= base + DEPTH), first, edge)
    last = pltpu.roll(a, (base + LANE_STEP) % by, a.ndim - 1)
    return jnp.where((lane > base + DEPTH) & (lane < base + LANE_STEP), last, edge)


def add_edges(edge, fields, upper):
    for f, a in enumerate(fields):
        edge = add_edge(edge, a, edge.shape[-1] // 2 * upper + LANE_STEP * f)
    return edge


def beside(edge, f, upper):
    by = edge.shape[-1]
    iy = lax.axis_index("gy")
    lane = iota((1,) * (edge.ndim - 1) + (by,), edge.ndim - 1)
    right = (lane <= DEPTH) & (iy < lax.axis_size("gy") - 1)
    left = (lane >= by - DEPTH) & (iy > 0)
    shift = by // 2 * upper + LANE_STEP * f
    a = pltpu.roll(edge, by - shift, edge.ndim - 1) if shift else edge
    b = pltpu.roll(edge, (by - LANE_STEP - shift) % by, edge.ndim - 1)
    return jnp.where(right, a, jnp.where(left, b, 0.0))


def pack_kernel(
    vx_hbm, vz_hbm, vy_hbm, p_hbm, phase_hbm, scale_hbm, power_hbm, rho_hbm, edge_hbm, x_0_hbm, x_1_hbm, stack_hbm,
    field_ref, phase_ref, edge_ref, stack_ref, scale_ref, power_ref, rho_ref, sems, out_sems, table_sems,
):
    bx, bz, by = phase_ref.shape
    targets = [field_ref.at[f] for f in range(FIELDS - 1)] + [phase_ref]
    copies = start_copies((vx_hbm, vz_hbm, vy_hbm, p_hbm, phase_hbm), targets, sems)
    table_refs = (scale_ref, power_ref, rho_ref)
    pairs = zip((scale_hbm, power_hbm, rho_hbm), table_refs)
    table_copies = [pltpu.make_async_copy(a, b, table_sems.at[n]) for n, (a, b) in enumerate(pairs)]
    for copy in table_copies:
        copy.start()
    groups = bx // GROUP
    half = groups // 2
    order = list(range(half)) + list(range(groups - 1, half, -1)) + [half]
    outs = []

    def out(source, target):
        outs.append(pltpu.make_async_copy(source, target, out_sems.at[len(outs)]))
        outs[-1].start()

    count = DEPTH * FIELDS
    sems_x = [out_sems.at[out_sems.shape[0] - 1 - n] for n in range(3)]

    def x_copies(to_above, to_below):
        return (
            pltpu.make_async_copy(stack_ref.at[pl.ds(0, count + 1)], to_below, sems_x[0]),
            pltpu.make_async_copy(stack_ref.at[pl.ds(0, 1)], to_above.at[pl.ds(0, 1)], sems_x[1]),
            pltpu.make_async_copy(
                stack_ref.at[pl.ds(bx * FIELDS - count, count)], to_above.at[pl.ds(1, count)], sems_x[2]
            ),
        )

    def start_x(above, below):
        for copy in x_copies(above, below):
            copy.start()

    def wait_x(above, below):
        for copy in x_copies(above, below):
            copy.wait()

    edges = {}
    for g in order:
        if g in (0, groups - 1):
            for copy in copies[0 if g == 0 else half]:
                copy.wait()
        fields = clean_group(g, field_ref, phase_ref)
        for f, a in enumerate(fields):
            for i in range(GROUP):
                stack_ref[(g * GROUP + i) * FIELDS + f] = a[i]
        at = pl.ds(g * GROUP * FIELDS, GROUP * FIELDS)
        out(stack_ref.at[at], stack_hbm.at[at])
        if g == groups - 1:
            by_parity("gx", (x_0_hbm, x_1_hbm), start_x)
        upper, n = divmod(g, half)
        edge = edges.get(n, jnp.zeros((GROUP, bz, by), jnp.float32))
        edges[n] = add_edges(edge, fields, upper)
        if n + half * (1 - upper) in order[: order.index(g)]:
            at = pl.ds(n * GROUP, GROUP)
            edge_ref[at] = edges[n]
            out(edge_ref.at[at], edge_hbm.at[at])
            stack_ref[pl.ds(bx * FIELDS + n * GROUP, GROUP)] = edges[n]
    end = bx * FIELDS + bx // 2
    row = iota((bz, by), 0)
    for copy in table_copies:
        copy.wait()
    entries = [ref[index] for ref in table_refs for index in range(PHASES)]
    for n in range(2):
        tile = jnp.zeros((bz, by), jnp.float32)
        for r, entry in enumerate(entries[n * bz : (n + 1) * bz]):
            tile = jnp.where(row == r, entry, tile)
        stack_ref[end + n] = tile
    at = pl.ds(bx * FIELDS, end + 2 - bx * FIELDS)
    out(stack_ref.at[at], stack_hbm.at[at])
    by_parity("gx", (x_0_hbm, x_1_hbm), wait_x)
    for copy in outs:
        copy.wait()


def side_edge_kernel(x_1_ref, x_0_ref, own_edge_ref, edge_ref):
    bz, by = edge_ref.shape[1:]
    own = own_edge_ref.shape[0]
    edge_ref[0:own] = own_edge_ref[...]

    def body(above, below):
        edge = jnp.zeros((DEPTH, bz, by), jnp.float32)
        for upper, (ref, at) in enumerate(((above, 0), (below, 1))):
            block = ref[pl.ds(at, DEPTH * FIELDS)].reshape(DEPTH, FIELDS, bz, by)
            edge = add_edges(edge, [block[:, f] for f in range(FIELDS)], upper)
        edge_ref[own:] = edge
        edge_ref[own] = add_edge(edge[0], above[DEPTH * FIELDS], FIELDS * LANE_STEP)

    by_parity("gx", (x_0_ref, x_1_ref), body)


def half_rows(tiles, swap):
    down = odd("gz") if swap == 0 else jnp.logical_not(odd("gz"))
    half = tiles.shape[-2] // 2
    return jnp.where(down, tiles[..., :half, :], tiles[..., half:, :])


def store_next_rows(refs, at, tiles):
    half = tiles.shape[-2] // 2
    for ref in refs:
        for i in range(tiles.shape[0]):
            ref[at + i // half, i % half : i % half + 1, :] = tiles[i, half : half + 1, :]


def sides_kernel(x_1_ref, x_0_ref, _edge_ref, sides_ref, z_0_ref, z_1_ref):
    count = DEPTH * FIELDS
    bz, by = sides_ref.shape[1:]

    def body(above, below):
        sides_ref[0:count] = above[0:count]
        sides_ref[count : 2 * count] = below[1 : count + 1]
        sides_ref[2 * count] = above[count]

    by_parity("gx", (x_0_ref, x_1_ref), body)
    tiles = sides_ref[...]
    for swap, ref in enumerate((z_0_ref, z_1_ref)):
        ref[0 : 2 * count + 1] = half_rows(tiles, swap)
    vz = tiles[0 : 2 * count].reshape(2 * DEPTH, FIELDS, bz, by)[:, 1]
    store_next_rows((z_0_ref, z_1_ref), 2 * count + 1, vz)


def edge_rows_kernel(edge_ref, z_0_ref, z_1_ref):
    tiles = edge_ref[...]
    for swap, ref in enumerate((z_0_ref, z_1_ref)):
        ref[0 : tiles.shape[0]] = half_rows(tiles, swap)
    store_next_rows((z_0_ref, z_1_ref), tiles.shape[0], tiles)


def lookups(fields, ok, keep, table_ref):
    *rest, phase = fields
    for number in range(3):
        rows = [divmod(number * PHASES + index, table_ref.shape[1]) for index in range(PHASES)]
        table = [table_ref[n, r : r + 1, :] for n, r in rows]
        value = jnp.broadcast_to(table[0], phase.shape)
        for index in range(1, PHASES):
            value = jnp.where(phase == float(index), table[index], value)
        if number == 0:
            value = value * jnp.where(ok, 1.0, 0.0)
            if keep is not None:
                value = jnp.where(keep, value, 0.0)
        elif number == 1:
            value = (0.5 / math.log(2.0)) * (reciprocal(value) - 1.0)
        rest.append(value)
    return rest


def own_lanes(block, ok, tables):
    block = block.reshape(-1, FIELDS, *block.shape[-2:])
    return lookups([block[:, f] for f in range(FIELDS)], ok, None, tables)


def edge_lanes(edge, upper, ok, tables):
    by = edge.shape[-1]
    iy = lax.axis_index("gy")
    lane = iota((1, 1, by), 2)
    keep = ((lane <= DEPTH) & (iy < lax.axis_size("gy") - 1)) | ((lane >= by - DEPTH) & (iy > 0))
    return lookups([beside(edge, f, upper) for f in range(FIELDS)], ok, keep, tables)


def store_to(refs):
    def store(planes, part, values):
        by = values[0].shape[-1]
        for ref, value in zip(refs, values):
            ref[planes, :, part * by : (part + 1) * by] = value

    return store


def unpack_own(load, bx, ok, tables, store):
    for at in range(0, bx, GROUP):
        store(pl.ds(DEPTH + at, GROUP), 0, own_lanes(load(at * FIELDS, GROUP * FIELDS), ok, tables))


def unpack_own_edges(load, bx, ok, tables, store):
    half = bx // 2
    for at in range(0, half, GROUP):
        edge = load(at, GROUP)
        for upper in range(2):
            store(pl.ds(DEPTH + upper * half + at, GROUP), 1, edge_lanes(edge, upper, ok, tables))


def side_places(bx):
    ix = lax.axis_index("gx")
    return (pl.ds(DEPTH + bx, DEPTH), ix < lax.axis_size("gx") - 1), (pl.ds(0, DEPTH), ix > 0)


def unpack_sides(load, bx, ok, tables, store, vx_ref):
    count = DEPTH * FIELDS
    for n, (planes, inside) in enumerate(side_places(bx)):
        store(planes, 0, own_lanes(load(n * count, count), ok & inside, tables))
    vx = load(2 * count, 1)
    vx_ref[pl.ds(bx + 2 * DEPTH, 1), :, 0 : vx.shape[-1]] = vx


def unpack_side_edges(load, bx, ok, tables, store, vx_ref):
    half = bx // 2
    edge = load(half, DEPTH)
    for upper, (planes, inside) in enumerate(side_places(bx)):
        store(planes, 1, edge_lanes(edge, upper, ok & inside, tables))
    by = edge.shape[-1]
    vx_ref[pl.ds(bx + 2 * DEPTH, 1), :, by : 2 * by] = beside(edge[0:1], FIELDS, 0)


def make_weights(weight_ref):
    shape = weight_ref.shape[1:]
    rows, lanes = shape
    bz, by = rows // 2, lanes // 2
    nz, ny = lax.axis_size("gz"), lax.axis_size("gy")
    iz, iy = lax.axis_index("gz"), lax.axis_index("gy")
    r, c = iota(shape, 0), iota(shape, 1)
    zg = iz * bz + jnp.where(r < bz + bz // 2, r, r - rows)
    yg = iy * by + jnp.where(c <= by + DEPTH, c, c - lanes)
    filled = (c <= by + DEPTH) | (c >= lanes - DEPTH)
    inside = filled & (zg >= 0) & (zg < nz * bz) & (yg >= 0) & (yg < ny * by)
    weight_ref[0] = jnp.where(inside, 0.05, 0.0)
    weight_ref[1] = jnp.where(inside & (zg > 0), 0.05, 0.0)
    weight_ref[2] = jnp.where(inside & (yg > 0), 0.05, 0.0)
    weight_ref[3] = jnp.where(inside, 0.0, 1.0)


def own_kernel(stack_ref, z_0_ref, z_1_ref, edge_ref, tables_ref, weight_ref, v_ref, *rest):
    bx = v_ref.shape[1] - 2 * DEPTH - 1
    make_weights(weight_ref)
    count = bx * FIELDS
    edge_ref[...] = stack_ref[count : count + bx // 2]
    tables_ref[...] = stack_ref[count + bx // 2 :]
    size = GROUP * FIELDS

    for g in range(bx // GROUP):
        at = pl.ds(g * size, size)
        tiles = stack_ref[at]
        for swap, ref in enumerate((z_0_ref, z_1_ref)):
            ref[at] = half_rows(tiles, swap)
        vz = stack_ref[pl.ds(g * size, size)].reshape(GROUP, FIELDS, *stack_ref.shape[1:])[:, 1]
        store_next_rows((z_0_ref, z_1_ref), count + g * GROUP // (stack_ref.shape[1] // 2), vz)
    store = store_to([v_ref.at[d] for d in range(3)] + list(rest))
    unpack_own(lambda at, n: stack_ref[pl.ds(at, n)], bx, True, tables_ref, store)


def own_sides_kernel(sides_ref, edge_ref, tables_ref, *refs):
    v_ref, *rest = refs[len(refs) // 2 :]
    bx = v_ref.shape[1] - 2 * DEPTH - 1
    store = store_to([v_ref.at[d] for d in range(3)] + list(rest))
    unpack_sides(lambda at, n: sides_ref[pl.ds(at, n)], bx, True, tables_ref, store, v_ref.at[0])
    load = lambda at, n: edge_ref[pl.ds(at, n)]
    unpack_own_edges(load, bx, True, tables_ref, store)
    unpack_side_edges(load, bx, True, tables_ref, store, v_ref.at[0])


def rows_in_grid(bz):
    iz = lax.axis_index("gz")
    row = iota((1, bz, 1), 1)
    return ((row < bz // 2) & (iz < lax.axis_size("gz") - 1)) | ((row >= bz // 2) & (iz > 0))


def load_both(above, below):
    return lambda at, n: jnp.concatenate([above[pl.ds(at, n)], below[pl.ds(at, n)]], axis=1)


def halo_kernel(face_0_ref, face_1_ref, corner_0_ref, corner_1_ref, tables_ref, halo_ref, next_ref):
    half, by = face_0_ref.shape[1:]
    bz = 2 * half
    bx = halo_ref.shape[1] - 2 * DEPTH - 1
    ok = rows_in_grid(bz)
    store = store_to([halo_ref.at[n] for n in range(7)])

    def faces(above, below):
        unpack_own(load_both(above, below), bx, ok, tables_ref, store)
        for i in range(bx):
            n = i % half
            next_ref[DEPTH + i, half - 1 : half, 0:by] = above[bx * FIELDS + i // half, n : n + 1, :]

    def corners(above, below):
        unpack_sides(load_both(above, below), bx, ok, tables_ref, store, halo_ref.at[0])
        for i in range(2 * DEPTH):
            n = i % half
            to = DEPTH + bx + i if i < DEPTH else i - DEPTH
            next_ref[to, half - 1 : half, 0:by] = above[2 * DEPTH * FIELDS + 1 + i // half, n : n + 1, :]

    by_parity("gz", (face_0_ref, face_1_ref), faces)
    by_parity("gz", (corner_0_ref, corner_1_ref), corners)


def unpack_halo_edges(edge_0_ref, edge_1_ref, tables_ref, halo_ref, next_ref):
    half, by = edge_0_ref.shape[1:]
    bx = halo_ref.shape[1] - 2 * DEPTH - 1
    ok = rows_in_grid(2 * half)
    store = store_to([halo_ref.at[n] for n in range(7)])
    tiles = bx // 2 + DEPTH

    def body(above, below):
        load = load_both(above, below)
        unpack_own_edges(load, bx, ok, tables_ref, store)
        unpack_side_edges(load, bx, ok, tables_ref, store, halo_ref.at[0])
        for n in range(tiles // half):
            rows = above[tiles + n]
            for upper in range(2):
                values = beside(rows, 1, upper)
                for i in range(half):
                    tile = n * half + i
                    if tile < bx // 2:
                        to = DEPTH + upper * (bx // 2) + tile
                    else:
                        to = tile - bx // 2 + (0 if upper else DEPTH + bx)
                    next_ref[to, half - 1 : half, by : 2 * by] = values[i : i + 1]

    by_parity("gz", (edge_0_ref, edge_1_ref), body)


def main_kernel(
    v_ref, p0_ref, pre_ref, power_field_ref, rho_ref, _halo, _next, edge_0_ref, edge_1_ref, tables_ref, weight_ref,
    out_vx_ref, out_vz_ref, out_vy_ref, out_p_ref, out_eta_ref, sum_ref, halo_ref, next_ref,
    va_ref, vb_ref, p_ref,
):
    bx, bz, by = out_p_ref.shape
    rows, lanes = 2 * bz, 2 * by
    nx, ix = lax.axis_size("gx"), lax.axis_index("gx")
    unpack_halo_edges(edge_0_ref, edge_1_ref, tables_ref, halo_ref, next_ref)

    def with_halo(own, n, planes):
        return jnp.concatenate([own[planes], halo_ref[n, planes]], axis=1)

    for k in range(1, ITERS + 1):
        old, new = (va_ref, vb_ref) if k % 2 else (vb_ref, va_ref)
        last = k == ITERS

        def load(d, j, count):
            planes = pl.ds(j, count)
            return with_halo(v_ref.at[d], d, planes) if k == 1 else old[d, planes]

        def cells(j, count):
            planes = pl.ds(j, count)
            vx1 = load(0, j, count + 1)
            vx = vx1[:count]
            vz, vy = load(1, j, count), load(2, j, count)
            p = with_halo(p0_ref, 3, planes) if k == 1 else p_ref[planes]
            up = z_up(vz)
            if k == 1:
                after = next_ref[planes]
                after = jnp.concatenate([after, after], axis=1)
                up = jnp.where(iota((1, rows, lanes), 1) == bz + bz // 2 - 1, after, up)
            rx = vx1[1:] - vx
            rz = up - vz
            ry = y_up(vy) - vy
            a = rx - ry
            b = ry - rz
            inv = (a * (a + b) + b * b) * (1.0 / 3.0) + 1.0
            eta = with_halo(pre_ref, 4, planes) * jnp.exp2(with_halo(power_field_ref, 5, planes) * jnp.log(inv))
            quarter = 0.25 * eta
            div = rx + ry + rz
            p = p - quarter * (div + div)
            tx, tz, ty = eta * rx - p, eta * rz - p, eta * ry - p
            sz = quarter + z_down(quarter)
            sy = quarter + y_down(quarter)
            return vx, vz, vy, eta, p, quarter, tx, tz, ty, sz, sy

        first, end = k, bx + 2 * DEPTH - k
        count = end - first + 1
        below = cells(first - 1, count + 1)
        vx, vz, vy, eta, p, quarter, tx, tz, ty, sz, sy = (a[1:] for a in below)
        vx0, vz0, vy0, _, _, quarter0, tx0, _, _, sz0, sy0 = (a[:-1] for a in below)
        bias = weight_ref[3:4]
        sx = quarter + quarter0
        exz = sz + sz0
        exy = sy + sy0
        ezy = sy + z_down(sy)
        fxz = exz * (vx - z_down(vx))
        fxy = exy * (vx - y_down(vx))
        gzx = exz * (vz - vz0)
        hyx = exy * (vy - vy0)
        gzy = ezy * (vz - y_down(vz))
        hyz = ezy * (vy - z_down(vy))
        res_x = (tx - tx0) + ((z_up(fxz) - fxz) + (y_up(fxy) - fxy))
        new_vx = vx + weight_ref[0:1] * reciprocal(sx + bias) * res_x
        part_z = (tz - z_down(tz)) - with_halo(rho_ref, 6, pl.ds(first, count)) + ((y_up(gzy) - gzy) - gzx)
        part_y = (ty - y_down(ty)) + ((z_up(hyz) - hyz) - hyx)
        scale_z = weight_ref[1:2] * reciprocal(sz + bias)
        scale_y = weight_ref[2:3] * reciprocal(sy + bias)
        new_vz = vz[:-1] + scale_z[:-1] * (part_z[:-1] + gzx[1:])
        new_vy = vy[:-1] + scale_y[:-1] * (part_y[:-1] + hyx[1:])
        if last:
            out_vx_ref[...] = new_vx[:-1, 0:bz, 0:by]
            out_vz_ref[...] = new_vz[:, 0:bz, 0:by]
            out_vy_ref[...] = new_vy[:, 0:bz, 0:by]
            out_p_ref[...] = p[:-1, 0:bz, 0:by]
            out_eta_ref[...] = eta[:-1, 0:bz, 0:by]
            sum_ref[...] = jnp.sum(p[:-1, 0:bz, 0:by], axis=0)

            @pl.when(ix == 0)
            def _():
                out_vx_ref[0] = jnp.zeros((bz, by), jnp.float32)
        else:
            p_ref[pl.ds(first - 1, count + 1)] = below[4]
            new[0, pl.ds(first, count)] = new_vx
            new[1, pl.ds(first, count - 1)] = new_vz
            new[2, pl.ds(first, count - 1)] = new_vy
            plane = jnp.zeros((rows, lanes), jnp.float32)

            @pl.when(ix == 0)
            def _():
                for i in range(first, DEPTH):
                    for d in range(3):
                        new[d, i] = plane
                new[0, DEPTH] = plane

            @pl.when(ix == nx - 1)
            def _():
                for i in range(DEPTH + bx, end + 1):
                    for d in range(3):
                        new[d, i] = plane


def final_kernel(p_ref, sum_ref, out_ref, *, cells):
    mean = jnp.sum(sum_ref[...]) * (1.0 / cells)
    out_ref[...] = p_ref[...] - mean


def swap(a, axis, start):
    count = lax.axis_size(axis)
    return lax.ppermute(a, axis, [(i, j) for k in range(start, count - 1, 2) for i, j in ((k, k + 1), (k + 1, k))])


def sum_everywhere(total):
    axes = ("gx", "gy", "gz")
    devices = math.prod(lax.axis_size(a) for a in axes)
    total = total + lax.ppermute(total, axes, [(i, i ^ 1) for i in range(devices)])
    total = jnp.broadcast_to(jnp.sum(total, axis=0, keepdims=True), (devices // 2, total.shape[1]))
    groups = [list(range(n, devices, 2)) for n in range(2)]
    return lax.all_to_all(total, axes, 0, 0, tiled=True, axis_index_groups=groups)


def local(vel_x, vel_y, vel_z, pressure, phase, visc_scale, power_n, density):
    bx, bz, by = pressure.shape
    assert bx % (2 * GROUP) == 0 and bz == 2 * DEPTH and DEPTH == GROUP
    f32 = jnp.float32
    iy, ny = lax.axis_index("gy"), lax.axis_size("gy")
    cells = bx * bz * by * math.prod(lax.axis_size(a) for a in ("gx", "gz", "gy"))
    deep = bx + 2 * DEPTH + 1
    rows, lanes = 2 * bz, 2 * by
    shape = lambda *dims: jax.ShapeDtypeStruct(dims, f32)
    block = shape(bx, bz, by)
    scratch = lambda *dims: pltpu.VMEM(dims, f32)
    limit = lambda mebibytes: pltpu.CompilerParams(vmem_limit_bytes=mebibytes * 1024 * 1024)
    groups = bx // GROUP
    stacked = bx * FIELDS + bx // 2 + 2
    sent = shape(DEPTH * FIELDS + 1, bz, by)
    edge, x_0, x_1, stack = pl.pallas_call(
        pack_kernel,
        out_shape=(shape(bx // 2, bz, by), sent, sent, shape(stacked, bz, by)),
        in_specs=[HBM] * 8,
        out_specs=(HBM,) * 4,
        scratch_shapes=[
            scratch(FIELDS - 1, bx, bz, by),
            pltpu.VMEM((bx, bz, by), jnp.int32),
            scratch(bx // 2, bz, by),
            scratch(stacked, bz, by),
            pltpu.SMEM((PHASES,), f32),
            pltpu.SMEM((PHASES,), f32),
            pltpu.SMEM((PHASES,), f32),
            pltpu.SemaphoreType.DMA((groups, FIELDS)),
            pltpu.SemaphoreType.DMA((groups + groups // 2 + 4,)),
            pltpu.SemaphoreType.DMA((3,)),
        ],
        compiler_params=limit(58),
    )(vel_x, vel_z, vel_y, pressure, phase, visc_scale, power_n, density)

    def edges_beside(edge):
        side = swap(edge, "gy", 0)
        if ny == 2:
            return side
        lane = iota(side.shape, 2) % (by // 2) % LANE_STEP
        return jnp.where((lane <= DEPTH) == (lax.rem(iy, 2) == 0), side, swap(edge, "gy", 1))

    estimate = lambda size: pl.CostEstimate(
        flops=4 * size * bz * by, bytes_accessed=size * bz * by * 4, transcendentals=0
    )

    def unpacking(kernel, tiles, out_shape, *args, aliases={}):
        return pl.pallas_call(
            kernel,
            out_shape=out_shape,
            in_specs=[VMEM] * len(args),
            out_specs=(VMEM,) * len(out_shape),
            input_output_aliases=aliases,
            compiler_params=limit(16),
            cost_estimate=estimate(13 * tiles),
        )(*args)

    field = shape(deep, bz, lanes)
    own_shape = (shape(3, deep, bz, lanes),) + (field,) * 4
    half = lambda tiles, planes: shape(tiles + planes // (bz // 2), bz // 2, by)
    x_1, x_0 = swap(x_1, "gx", 1), swap(x_0, "gx", 0)
    face = half(bx * FIELDS, bx)
    extra = (shape(bx // 2, bz, by), shape(2, bz, by), shape(4, rows, lanes))
    z_0, z_1, edge, tables, weights, *own = unpacking(own_kernel, bx, (face, face) + extra + own_shape, stack)
    face_1, face_0 = swap(z_1, "gz", 1), swap(z_0, "gz", 0)

    tiles = bx // 2 + DEPTH
    edge = pl.pallas_call(
        side_edge_kernel,
        out_shape=shape(tiles, bz, by),
        in_specs=[VMEM] * 3,
        out_specs=VMEM,
        compiler_params=limit(4),
    )(x_1, x_0, edge)
    corner = half(2 * DEPTH * FIELDS + 1, 2 * DEPTH)
    sides, z_0, z_1 = pl.pallas_call(
        sides_kernel,
        out_shape=(shape(2 * DEPTH * FIELDS + 1, bz, by), corner, corner),
        in_specs=[VMEM] * 3,
        out_specs=(VMEM,) * 3,
        compiler_params=limit(4),
    )(x_1, x_0, edge)
    edge = edges_beside(edge)
    corner_1, corner_0 = swap(z_1, "gz", 1), swap(z_0, "gz", 0)
    z_0, z_1 = pl.pallas_call(
        edge_rows_kernel,
        out_shape=(half(tiles, tiles),) * 2,
        in_specs=[VMEM],
        out_specs=(VMEM,) * 2,
        compiler_params=limit(4),
        cost_estimate=estimate(100000),
    )(edge)
    edge_1, edge_0 = swap(z_1, "gz", 1), swap(z_0, "gz", 0)

    own = unpacking(
        own_sides_kernel, 2 * deep, own_shape, sides, edge, tables, *own, aliases={n + 3: n for n in range(5)}
    )
    halo = unpacking(
        halo_kernel, deep, (shape(7, deep, bz, lanes), field), face_0, face_1, corner_0, corner_1, tables
    )
    vx, vz, vy, p, eta, total, _, _ = pl.pallas_call(
        main_kernel,
        out_shape=(block,) * 5 + (shape(bz, by),) + tuple(shape(*a.shape) for a in halo),
        in_specs=[VMEM] * 11,
        out_specs=(VMEM,) * 8,
        input_output_aliases={5: 6, 6: 7},
        scratch_shapes=[
            scratch(3, deep, rows, lanes),
            scratch(3, deep, rows, lanes),
            scratch(deep, rows, lanes),
        ],
        compiler_params=limit(32),
    )(*own, *halo, edge_0, edge_1, tables, weights)

    total = sum_everywhere(total)
    p = pl.pallas_call(
        lambda *refs: final_kernel(*refs, cells=float(cells)),
        out_shape=block,
        in_specs=[VMEM] * 2,
        out_specs=VMEM,
        compiler_params=limit(4),
    )(p, total)
    return (vx, vy, vz, p, eta)


def solution(mesh):
    spec = P("gx", "gz", "gy")
    return jax.shard_map(
        local,
        mesh=mesh,
        in_specs=(spec,) * 5 + (P(),) * 3,
        out_specs=(spec,) * 5,
        check_vma=False,
    )
```

```python
import math

import jax
import jax.numpy as jnp
from jax import lax
from jax.experimental import pallas as pl
from jax.experimental.pallas import tpu as pltpu
from jax.sharding import PartitionSpec as P

ITERS = 4
PHASES = 4
FIELDS = 5
DEPTH = ITERS
LANE_STEP = 2 * DEPTH + 1
GROUP = 4

VMEM = pl.BlockSpec(memory_space=pltpu.VMEM)
HBM = pl.BlockSpec(memory_space=pltpu.HBM)


def z_up(a):
    return pltpu.roll(a, a.shape[-2] - 1, a.ndim - 2)


def z_down(a):
    return pltpu.roll(a, 1, a.ndim - 2)


def y_up(a):
    return pltpu.roll(a, a.shape[-1] - 1, a.ndim - 1)


def y_down(a):
    return pltpu.roll(a, 1, a.ndim - 1)


def reciprocal(a):
    return pl.reciprocal(a, approx=True)


def iota(shape, axis):
    return lax.broadcasted_iota(jnp.int32, shape, axis)


def odd(axis):
    return lax.rem(lax.axis_index(axis), 2) == 1


def by_parity(axis, pair, body):
    pl.when(jnp.logical_not(odd(axis)))(lambda: body(pair[0], pair[1]))
    pl.when(odd(axis))(lambda: body(pair[1], pair[0]))


def start_copies(sources, targets, sems):
    half = sources[0].shape[0] // 2
    copies = {}
    for n in range(2):
        at = pl.ds(n * half, half)
        copies[n * (half // GROUP)] = [
            pltpu.make_async_copy(a.at[at], b.at[at], sems.at[n, f]) for f, (a, b) in enumerate(zip(sources, targets))
        ]
    for half_copies in copies.values():
        for copy in half_copies:
            copy.start()
    return copies


def clean_group(g, field_ref, phase_ref):
    bx, bz, by = phase_ref.shape
    ix, iz, iy = lax.axis_index("gx"), lax.axis_index("gz"), lax.axis_index("gy")
    plane, row, lane = (iota((GROUP, bz, by), d) for d in range(3))
    at = pl.ds(g * GROUP, GROUP)
    vx, vz, vy, p = (field_ref[f, at] for f in range(FIELDS - 1))
    if g == 0:
        vx = jnp.where((plane > 0) | (ix > 0), vx, 0.0)
    vz = jnp.where((row > 0) | (iz > 0), vz, 0.0)
    vy = jnp.where((lane > 0) | (iy > 0), vy, 0.0)
    return vx, vz, vy, p, phase_ref[at].astype(jnp.float32)


def add_edge(edge, a, base):
    lane = iota((1,) * (edge.ndim - 1) + edge.shape[-1:], edge.ndim - 1)
    return jnp.where((lane >= base) & (lane < base + LANE_STEP), pltpu.roll(a, base + DEPTH, a.ndim - 1), edge)


def add_edges(edge, fields, upper):
    for f, a in enumerate(fields):
        edge = add_edge(edge, a, edge.shape[-1] // 2 * upper + LANE_STEP * f)
    return edge


def beside(edge, f, upper):
    by = edge.shape[-1]
    iy = lax.axis_index("gy")
    lane = iota((1,) * (edge.ndim - 1) + (by,), edge.ndim - 1)
    right = (lane <= DEPTH) & (iy < lax.axis_size("gy") - 1)
    left = (lane >= by - DEPTH) & (iy > 0)
    shift = by // 2 * upper + LANE_STEP * f
    return jnp.where(right | left, pltpu.roll(edge, by - DEPTH - shift, edge.ndim - 1), 0.0)


def pack_kernel(
    vx_hbm, vz_hbm, vy_hbm, p_hbm, phase_hbm, scale_hbm, power_hbm, rho_hbm, edge_hbm, x_0_hbm, x_1_hbm, stack_hbm,
    field_ref, phase_ref, edge_ref, stack_ref, scale_ref, power_ref, rho_ref, sems, out_sems, table_sems,
):
    bx, bz, by = phase_ref.shape
    targets = [field_ref.at[f] for f in range(FIELDS - 1)] + [phase_ref]
    copies = start_copies((vx_hbm, vz_hbm, vy_hbm, p_hbm, phase_hbm), targets, sems)
    table_refs = (scale_ref, power_ref, rho_ref)
    pairs = zip((scale_hbm, power_hbm, rho_hbm), table_refs)
    table_copies = [pltpu.make_async_copy(a, b, table_sems.at[n]) for n, (a, b) in enumerate(pairs)]
    for copy in table_copies:
        copy.start()
    groups = bx // GROUP
    half = groups // 2
    order = list(range(half)) + list(range(groups - 1, half, -1)) + [half]
    outs = []

    def out(source, target):
        outs.append(pltpu.make_async_copy(source, target, out_sems.at[len(outs)]))
        outs[-1].start()

    count = DEPTH * FIELDS
    sems_x = [out_sems.at[out_sems.shape[0] - 1 - n] for n in range(3)]

    def x_copies(to_above, to_below):
        return (
            pltpu.make_async_copy(stack_ref.at[pl.ds(0, count + 1)], to_below, sems_x[0]),
            pltpu.make_async_copy(stack_ref.at[pl.ds(0, 1)], to_above.at[pl.ds(0, 1)], sems_x[1]),
            pltpu.make_async_copy(
                stack_ref.at[pl.ds(bx * FIELDS - count, count)], to_above.at[pl.ds(1, count)], sems_x[2]
            ),
        )

    def start_x(above, below):
        for copy in x_copies(above, below):
            copy.start()

    def wait_x(above, below):
        for copy in x_copies(above, below):
            copy.wait()

    edges = {}
    for g in order:
        if g in (0, groups - 1):
            for copy in copies[0 if g == 0 else half]:
                copy.wait()
        fields = clean_group(g, field_ref, phase_ref)
        for f, a in enumerate(fields):
            for i in range(GROUP):
                stack_ref[(g * GROUP + i) * FIELDS + f] = a[i]
        at = pl.ds(g * GROUP * FIELDS, GROUP * FIELDS)
        out(stack_ref.at[at], stack_hbm.at[at])
        if g == groups - 1:
            by_parity("gx", (x_0_hbm, x_1_hbm), start_x)
        upper, n = divmod(g, half)
        edge = edges.get(n, jnp.zeros((GROUP, bz, by), jnp.float32))
        edges[n] = add_edges(edge, fields, upper)
        if n + half * (1 - upper) in order[: order.index(g)]:
            at = pl.ds(n * GROUP, GROUP)
            edge_ref[at] = edges[n]
            out(edge_ref.at[at], edge_hbm.at[at])
            stack_ref[pl.ds(bx * FIELDS + n * GROUP, GROUP)] = edges[n]
    end = bx * FIELDS + bx // 2
    row = iota((bz, by), 0)
    for copy in table_copies:
        copy.wait()
    entries = [ref[index] for ref in table_refs for index in range(PHASES)]
    for n in range(2):
        tile = jnp.zeros((bz, by), jnp.float32)
        for r, entry in enumerate(entries[n * bz : (n + 1) * bz]):
            tile = jnp.where(row == r, entry, tile)
        stack_ref[end + n] = tile
    at = pl.ds(bx * FIELDS, end + 2 - bx * FIELDS)
    out(stack_ref.at[at], stack_hbm.at[at])
    by_parity("gx", (x_0_hbm, x_1_hbm), wait_x)
    for copy in outs:
        copy.wait()


def side_edge_kernel(x_1_ref, x_0_ref, own_edge_ref, edge_ref):
    bz, by = edge_ref.shape[1:]
    own = own_edge_ref.shape[0]
    edge_ref[0:own] = own_edge_ref[...]

    def body(above, below):
        edge = jnp.zeros((DEPTH, bz, by), jnp.float32)
        for upper, (ref, at) in enumerate(((above, 0), (below, 1))):
            block = ref[pl.ds(at, DEPTH * FIELDS)].reshape(DEPTH, FIELDS, bz, by)
            edge = add_edges(edge, [block[:, f] for f in range(FIELDS)], upper)
        edge_ref[own:] = edge
        edge_ref[own] = add_edge(edge[0], above[DEPTH * FIELDS], FIELDS * LANE_STEP)

    by_parity("gx", (x_0_ref, x_1_ref), body)


def half_rows(tiles, swap):
    down = odd("gz") if swap == 0 else jnp.logical_not(odd("gz"))
    half = tiles.shape[-2] // 2
    return jnp.where(down, tiles[..., :half, :], tiles[..., half:, :])


def store_next_rows(refs, at, tiles):
    half = tiles.shape[-2] // 2
    for ref in refs:
        for i in range(tiles.shape[0]):
            ref[at + i // half, i % half : i % half + 1, :] = tiles[i, half : half + 1, :]


def sides_kernel(x_1_ref, x_0_ref, _edge_ref, sides_ref, z_0_ref, z_1_ref):
    count = DEPTH * FIELDS
    bz, by = sides_ref.shape[1:]

    def body(above, below):
        sides_ref[0:count] = above[0:count]
        sides_ref[count : 2 * count] = below[1 : count + 1]
        sides_ref[2 * count] = above[count]

    by_parity("gx", (x_0_ref, x_1_ref), body)
    tiles = sides_ref[...]
    for swap, ref in enumerate((z_0_ref, z_1_ref)):
        ref[0 : 2 * count + 1] = half_rows(tiles, swap)
    vz = tiles[0 : 2 * count].reshape(2 * DEPTH, FIELDS, bz, by)[:, 1]
    store_next_rows((z_0_ref, z_1_ref), 2 * count + 1, vz)


def edge_rows_kernel(edge_ref, z_0_ref, z_1_ref):
    tiles = edge_ref[...]
    for swap, ref in enumerate((z_0_ref, z_1_ref)):
        ref[0 : tiles.shape[0]] = half_rows(tiles, swap)
    store_next_rows((z_0_ref, z_1_ref), tiles.shape[0], tiles)


def lookups(fields, ok, keep, table_ref):
    *rest, phase = fields
    for number in range(3):
        rows = [divmod(number * PHASES + index, table_ref.shape[1]) for index in range(PHASES)]
        table = [table_ref[n, r : r + 1, :] for n, r in rows]
        value = jnp.broadcast_to(table[0], phase.shape)
        for index in range(1, PHASES):
            value = jnp.where(phase == float(index), table[index], value)
        if number == 0:
            value = value * jnp.where(ok, 1.0, 0.0)
            if keep is not None:
                value = jnp.where(keep, value, 0.0)
        elif number == 1:
            value = (0.5 / math.log(2.0)) * (reciprocal(value) - 1.0)
        rest.append(value)
    return rest


def own_lanes(block, ok, tables):
    block = block.reshape(-1, FIELDS, *block.shape[-2:])
    return lookups([block[:, f] for f in range(FIELDS)], ok, None, tables)


def edge_lanes(edge, upper, ok, tables):
    by = edge.shape[-1]
    iy = lax.axis_index("gy")
    lane = iota((1, 1, by), 2)
    keep = ((lane <= DEPTH) & (iy < lax.axis_size("gy") - 1)) | ((lane >= by - DEPTH) & (iy > 0))
    return lookups([beside(edge, f, upper) for f in range(FIELDS)], ok, keep, tables)


def store_to(refs):
    def store(planes, part, values):
        by = values[0].shape[-1]
        for ref, value in zip(refs, values):
            ref[planes, :, part * by : (part + 1) * by] = value

    return store


def unpack_own(load, bx, ok, tables, store):
    for at in range(0, bx, GROUP):
        store(pl.ds(DEPTH + at, GROUP), 0, own_lanes(load(at * FIELDS, GROUP * FIELDS), ok, tables))


def unpack_own_edges(load, bx, ok, tables, store):
    half = bx // 2
    for at in range(0, half, GROUP):
        edge = load(at, GROUP)
        for upper in range(2):
            store(pl.ds(DEPTH + upper * half + at, GROUP), 1, edge_lanes(edge, upper, ok, tables))


def side_places(bx):
    ix = lax.axis_index("gx")
    return (pl.ds(DEPTH + bx, DEPTH), ix < lax.axis_size("gx") - 1), (pl.ds(0, DEPTH), ix > 0)


def unpack_sides(load, bx, ok, tables, store, vx_ref):
    count = DEPTH * FIELDS
    for n, (planes, inside) in enumerate(side_places(bx)):
        store(planes, 0, own_lanes(load(n * count, count), ok & inside, tables))
    vx = load(2 * count, 1)
    vx_ref[pl.ds(bx + 2 * DEPTH, 1), :, 0 : vx.shape[-1]] = vx


def unpack_side_edges(load, bx, ok, tables, store, vx_ref):
    half = bx // 2
    edge = load(half, DEPTH)
    for upper, (planes, inside) in enumerate(side_places(bx)):
        store(planes, 1, edge_lanes(edge, upper, ok & inside, tables))
    by = edge.shape[-1]
    vx_ref[pl.ds(bx + 2 * DEPTH, 1), :, by : 2 * by] = beside(edge[0:1], FIELDS, 0)


def make_weights(weight_ref):
    shape = weight_ref.shape[1:]
    rows, lanes = shape
    bz, by = rows // 2, lanes // 2
    nz, ny = lax.axis_size("gz"), lax.axis_size("gy")
    iz, iy = lax.axis_index("gz"), lax.axis_index("gy")
    r, c = iota(shape, 0), iota(shape, 1)
    zg = iz * bz + jnp.where(r < bz + bz // 2, r, r - rows)
    yg = iy * by + jnp.where(c <= by + DEPTH, c, c - lanes)
    filled = (c <= by + DEPTH) | (c >= lanes - DEPTH)
    inside = filled & (zg >= 0) & (zg < nz * bz) & (yg >= 0) & (yg < ny * by)
    weight_ref[0] = jnp.where(inside, 0.05, 0.0)
    weight_ref[1] = jnp.where(inside & (zg > 0), 0.05, 0.0)
    weight_ref[2] = jnp.where(inside & (yg > 0), 0.05, 0.0)
    weight_ref[3] = jnp.where(inside, 0.0, 1.0)


def own_kernel(stack_ref, z_0_ref, z_1_ref, edge_ref, tables_ref, weight_ref, v_ref, *rest):
    bx = v_ref.shape[1] - 2 * DEPTH - 1
    make_weights(weight_ref)
    count = bx * FIELDS
    edge_ref[...] = stack_ref[count : count + bx // 2]
    tables_ref[...] = stack_ref[count + bx // 2 :]
    size = GROUP * FIELDS

    for g in range(bx // GROUP):
        at = pl.ds(g * size, size)
        tiles = stack_ref[at]
        for swap, ref in enumerate((z_0_ref, z_1_ref)):
            ref[at] = half_rows(tiles, swap)
        vz = stack_ref[pl.ds(g * size, size)].reshape(GROUP, FIELDS, *stack_ref.shape[1:])[:, 1]
        store_next_rows((z_0_ref, z_1_ref), count + g * GROUP // (stack_ref.shape[1] // 2), vz)
    store = store_to([v_ref.at[d] for d in range(3)] + list(rest))
    unpack_own(lambda at, n: stack_ref[pl.ds(at, n)], bx, True, tables_ref, store)


def own_sides_kernel(sides_ref, edge_ref, tables_ref, *refs):
    v_ref, *rest = refs[len(refs) // 2 :]
    bx = v_ref.shape[1] - 2 * DEPTH - 1
    store = store_to([v_ref.at[d] for d in range(3)] + list(rest))
    unpack_sides(lambda at, n: sides_ref[pl.ds(at, n)], bx, True, tables_ref, store, v_ref.at[0])
    load = lambda at, n: edge_ref[pl.ds(at, n)]
    unpack_own_edges(load, bx, True, tables_ref, store)
    unpack_side_edges(load, bx, True, tables_ref, store, v_ref.at[0])


def rows_in_grid(bz):
    iz = lax.axis_index("gz")
    row = iota((1, bz, 1), 1)
    return ((row < bz // 2) & (iz < lax.axis_size("gz") - 1)) | ((row >= bz // 2) & (iz > 0))


def load_both(above, below):
    return lambda at, n: jnp.concatenate([above[pl.ds(at, n)], below[pl.ds(at, n)]], axis=1)


def halo_kernel(face_0_ref, face_1_ref, corner_0_ref, corner_1_ref, tables_ref, halo_ref, next_ref):
    half, by = face_0_ref.shape[1:]
    bz = 2 * half
    bx = halo_ref.shape[1] - 2 * DEPTH - 1
    ok = rows_in_grid(bz)
    store = store_to([halo_ref.at[n] for n in range(7)])

    def faces(above, below):
        unpack_own(load_both(above, below), bx, ok, tables_ref, store)
        for i in range(bx):
            n = i % half
            next_ref[DEPTH + i, half - 1 : half, 0:by] = above[bx * FIELDS + i // half, n : n + 1, :]

    def corners(above, below):
        unpack_sides(load_both(above, below), bx, ok, tables_ref, store, halo_ref.at[0])
        for i in range(2 * DEPTH):
            n = i % half
            to = DEPTH + bx + i if i < DEPTH else i - DEPTH
            next_ref[to, half - 1 : half, 0:by] = above[2 * DEPTH * FIELDS + 1 + i // half, n : n + 1, :]

    by_parity("gz", (face_0_ref, face_1_ref), faces)
    by_parity("gz", (corner_0_ref, corner_1_ref), corners)


def unpack_halo_edges(edge_0_ref, edge_1_ref, tables_ref, halo_ref, next_ref):
    half, by = edge_0_ref.shape[1:]
    bx = halo_ref.shape[1] - 2 * DEPTH - 1
    ok = rows_in_grid(2 * half)
    store = store_to([halo_ref.at[n] for n in range(7)])
    tiles = bx // 2 + DEPTH

    def body(above, below):
        load = load_both(above, below)
        unpack_own_edges(load, bx, ok, tables_ref, store)
        unpack_side_edges(load, bx, ok, tables_ref, store, halo_ref.at[0])
        for n in range(tiles // half):
            rows = above[tiles + n]
            for upper in range(2):
                values = beside(rows, 1, upper)
                for i in range(half):
                    tile = n * half + i
                    if tile < bx // 2:
                        to = DEPTH + upper * (bx // 2) + tile
                    else:
                        to = tile - bx // 2 + (0 if upper else DEPTH + bx)
                    next_ref[to, half - 1 : half, by : 2 * by] = values[i : i + 1]

    by_parity("gz", (edge_0_ref, edge_1_ref), body)


def main_kernel(
    v_ref, p0_ref, pre_ref, power_field_ref, rho_ref, _halo, _next, edge_0_ref, edge_1_ref, tables_ref, weight_ref,
    out_vx_ref, out_vz_ref, out_vy_ref, out_p_ref, out_eta_ref, sum_ref, halo_ref, next_ref,
    va_ref, vb_ref, p_ref,
):
    bx, bz, by = out_p_ref.shape
    rows, lanes = 2 * bz, 2 * by
    nx, ix = lax.axis_size("gx"), lax.axis_index("gx")
    unpack_halo_edges(edge_0_ref, edge_1_ref, tables_ref, halo_ref, next_ref)

    def with_halo(own, n, planes):
        return jnp.concatenate([own[planes], halo_ref[n, planes]], axis=1)

    for k in range(1, ITERS + 1):
        old, new = (va_ref, vb_ref) if k % 2 else (vb_ref, va_ref)
        last = k == ITERS

        def load(d, j, count):
            planes = pl.ds(j, count)
            return with_halo(v_ref.at[d], d, planes) if k == 1 else old[d, planes]

        def cells(j, count):
            planes = pl.ds(j, count)
            vx1 = load(0, j, count + 1)
            vx = vx1[:count]
            vz, vy = load(1, j, count), load(2, j, count)
            p = with_halo(p0_ref, 3, planes) if k == 1 else p_ref[planes]
            up = z_up(vz)
            if k == 1:
                after = next_ref[planes]
                after = jnp.concatenate([after, after], axis=1)
                up = jnp.where(iota((1, rows, lanes), 1) == bz + bz // 2 - 1, after, up)
            rx = vx1[1:] - vx
            rz = up - vz
            ry = y_up(vy) - vy
            a = rx - ry
            b = ry - rz
            inv = (a * (a + b) + b * b) * (1.0 / 3.0) + 1.0
            eta = with_halo(pre_ref, 4, planes) * jnp.exp2(with_halo(power_field_ref, 5, planes) * jnp.log(inv))
            quarter = 0.25 * eta
            div = rx + ry + rz
            p = p - quarter * (div + div)
            tx, tz, ty = eta * rx - p, eta * rz - p, eta * ry - p
            sz = quarter + z_down(quarter)
            sy = quarter + y_down(quarter)
            return vx, vz, vy, eta, p, quarter, tx, tz, ty, sz, sy

        first, end = k, bx + 2 * DEPTH - k
        count = end - first + 1
        below = cells(first - 1, count + 1)
        vx, vz, vy, eta, p, quarter, tx, tz, ty, sz, sy = (a[1:] for a in below)
        vx0, vz0, vy0, _, _, quarter0, tx0, _, _, sz0, sy0 = (a[:-1] for a in below)
        bias = weight_ref[3:4]
        sx = quarter + quarter0
        exz = sz + sz0
        exy = sy + sy0
        ezy = sy + z_down(sy)
        fxz = exz * (vx - z_down(vx))
        fxy = exy * (vx - y_down(vx))
        gzx = exz * (vz - vz0)
        hyx = exy * (vy - vy0)
        gzy = ezy * (vz - y_down(vz))
        hyz = ezy * (vy - z_down(vy))
        res_x = (tx - tx0) + ((z_up(fxz) - fxz) + (y_up(fxy) - fxy))
        new_vx = vx + weight_ref[0:1] * reciprocal(sx + bias) * res_x
        part_z = (tz - z_down(tz)) - with_halo(rho_ref, 6, pl.ds(first, count)) + ((y_up(gzy) - gzy) - gzx)
        part_y = (ty - y_down(ty)) + ((z_up(hyz) - hyz) - hyx)
        scale_z = weight_ref[1:2] * reciprocal(sz + bias)
        scale_y = weight_ref[2:3] * reciprocal(sy + bias)
        new_vz = vz[:-1] + scale_z[:-1] * (part_z[:-1] + gzx[1:])
        new_vy = vy[:-1] + scale_y[:-1] * (part_y[:-1] + hyx[1:])
        if last:
            out_vx_ref[...] = new_vx[:-1, 0:bz, 0:by]
            out_vz_ref[...] = new_vz[:, 0:bz, 0:by]
            out_vy_ref[...] = new_vy[:, 0:bz, 0:by]
            out_p_ref[...] = p[:-1, 0:bz, 0:by]
            out_eta_ref[...] = eta[:-1, 0:bz, 0:by]
            sum_ref[...] = jnp.sum(p[:-1, 0:bz, 0:by], axis=0)

            @pl.when(ix == 0)
            def _():
                out_vx_ref[0] = jnp.zeros((bz, by), jnp.float32)
        else:
            p_ref[pl.ds(first - 1, count + 1)] = below[4]
            new[0, pl.ds(first, count)] = new_vx
            new[1, pl.ds(first, count - 1)] = new_vz
            new[2, pl.ds(first, count - 1)] = new_vy
            plane = jnp.zeros((rows, lanes), jnp.float32)

            @pl.when(ix == 0)
            def _():
                for i in range(first, DEPTH):
                    for d in range(3):
                        new[d, i] = plane
                new[0, DEPTH] = plane

            @pl.when(ix == nx - 1)
            def _():
                for i in range(DEPTH + bx, end + 1):
                    for d in range(3):
                        new[d, i] = plane


def final_kernel(p_ref, sum_ref, out_ref, *, cells):
    mean = jnp.sum(sum_ref[...]) * (1.0 / cells)
    out_ref[...] = p_ref[...] - mean


def swap(a, axis, start):
    count = lax.axis_size(axis)
    return lax.ppermute(a, axis, [(i, j) for k in range(start, count - 1, 2) for i, j in ((k, k + 1), (k + 1, k))])


def sum_everywhere(total):
    axes = ("gx", "gy", "gz")
    devices = math.prod(lax.axis_size(a) for a in axes)
    total = total + lax.ppermute(total, axes, [(i, i ^ 1) for i in range(devices)])
    total = jnp.broadcast_to(jnp.sum(total, axis=0, keepdims=True), (devices // 2, total.shape[1]))
    groups = [list(range(n, devices, 2)) for n in range(2)]
    return lax.all_to_all(total, axes, 0, 0, tiled=True, axis_index_groups=groups)


def local(vel_x, vel_y, vel_z, pressure, phase, visc_scale, power_n, density):
    bx, bz, by = pressure.shape
    assert bx % (2 * GROUP) == 0 and bz == 2 * DEPTH and DEPTH == GROUP
    f32 = jnp.float32
    iy, ny = lax.axis_index("gy"), lax.axis_size("gy")
    cells = bx * bz * by * math.prod(lax.axis_size(a) for a in ("gx", "gz", "gy"))
    deep = bx + 2 * DEPTH + 1
    rows, lanes = 2 * bz, 2 * by
    shape = lambda *dims: jax.ShapeDtypeStruct(dims, f32)
    block = shape(bx, bz, by)
    scratch = lambda *dims: pltpu.VMEM(dims, f32)
    limit = lambda mebibytes: pltpu.CompilerParams(vmem_limit_bytes=mebibytes * 1024 * 1024)
    groups = bx // GROUP
    stacked = bx * FIELDS + bx // 2 + 2
    sent = shape(DEPTH * FIELDS + 1, bz, by)
    edge, x_0, x_1, stack = pl.pallas_call(
        pack_kernel,
        out_shape=(shape(bx // 2, bz, by), sent, sent, shape(stacked, bz, by)),
        in_specs=[HBM] * 8,
        out_specs=(HBM,) * 4,
        scratch_shapes=[
            scratch(FIELDS - 1, bx, bz, by),
            pltpu.VMEM((bx, bz, by), jnp.int32),
            scratch(bx // 2, bz, by),
            scratch(stacked, bz, by),
            pltpu.SMEM((PHASES,), f32),
            pltpu.SMEM((PHASES,), f32),
            pltpu.SMEM((PHASES,), f32),
            pltpu.SemaphoreType.DMA((groups, FIELDS)),
            pltpu.SemaphoreType.DMA((groups + groups // 2 + 4,)),
            pltpu.SemaphoreType.DMA((3,)),
        ],
        compiler_params=limit(58),
    )(vel_x, vel_z, vel_y, pressure, phase, visc_scale, power_n, density)

    def edges_beside(edge):
        side = swap(edge, "gy", 0)
        if ny == 2:
            return side
        lane = iota(side.shape, 2) % (by // 2) % LANE_STEP
        return jnp.where((lane >= DEPTH) == (lax.rem(iy, 2) == 0), side, swap(edge, "gy", 1))

    estimate = lambda size: pl.CostEstimate(
        flops=4 * size * bz * by, bytes_accessed=size * bz * by * 4, transcendentals=0
    )

    def unpacking(kernel, tiles, out_shape, *args, aliases={}):
        return pl.pallas_call(
            kernel,
            out_shape=out_shape,
            in_specs=[VMEM] * len(args),
            out_specs=(VMEM,) * len(out_shape),
            input_output_aliases=aliases,
            compiler_params=limit(16),
            cost_estimate=estimate(13 * tiles),
        )(*args)

    field = shape(deep, bz, lanes)
    own_shape = (shape(3, deep, bz, lanes),) + (field,) * 4
    half = lambda tiles, planes: shape(tiles + planes // (bz // 2), bz // 2, by)
    x_1, x_0 = swap(x_1, "gx", 1), swap(x_0, "gx", 0)
    face = half(bx * FIELDS, bx)
    extra = (shape(bx // 2, bz, by), shape(2, bz, by), shape(4, rows, lanes))
    z_0, z_1, edge, tables, weights, *own = unpacking(own_kernel, bx, (face, face) + extra + own_shape, stack)
    face_1, face_0 = swap(z_1, "gz", 1), swap(z_0, "gz", 0)

    tiles = bx // 2 + DEPTH
    edge = pl.pallas_call(
        side_edge_kernel,
        out_shape=shape(tiles, bz, by),
        in_specs=[VMEM] * 3,
        out_specs=VMEM,
        compiler_params=limit(4),
    )(x_1, x_0, edge)
    corner = half(2 * DEPTH * FIELDS + 1, 2 * DEPTH)
    sides, z_0, z_1 = pl.pallas_call(
        sides_kernel,
        out_shape=(shape(2 * DEPTH * FIELDS + 1, bz, by), corner, corner),
        in_specs=[VMEM] * 3,
        out_specs=(VMEM,) * 3,
        compiler_params=limit(4),
    )(x_1, x_0, edge)
    edge = edges_beside(edge)
    corner_1, corner_0 = swap(z_1, "gz", 1), swap(z_0, "gz", 0)
    z_0, z_1 = pl.pallas_call(
        edge_rows_kernel,
        out_shape=(half(tiles, tiles),) * 2,
        in_specs=[VMEM],
        out_specs=(VMEM,) * 2,
        compiler_params=limit(4),
        cost_estimate=estimate(100000),
    )(edge)
    edge_1, edge_0 = swap(z_1, "gz", 1), swap(z_0, "gz", 0)

    own = unpacking(
        own_sides_kernel, 2 * deep, own_shape, sides, edge, tables, *own, aliases={n + 3: n for n in range(5)}
    )
    halo = unpacking(
        halo_kernel, deep, (shape(7, deep, bz, lanes), field), face_0, face_1, corner_0, corner_1, tables
    )
    vx, vz, vy, p, eta, total, _, _ = pl.pallas_call(
        main_kernel,
        out_shape=(block,) * 5 + (shape(bz, by),) + tuple(shape(*a.shape) for a in halo),
        in_specs=[VMEM] * 11,
        out_specs=(VMEM,) * 8,
        input_output_aliases={5: 6, 6: 7},
        scratch_shapes=[
            scratch(3, deep, rows, lanes),
            scratch(3, deep, rows, lanes),
            scratch(deep, rows, lanes),
        ],
        compiler_params=limit(32),
    )(*own, *halo, edge_0, edge_1, tables, weights)

    total = sum_everywhere(total)
    p = pl.pallas_call(
        lambda *refs: final_kernel(*refs, cells=float(cells)),
        out_shape=block,
        in_specs=[VMEM] * 2,
        out_specs=VMEM,
        compiler_params=limit(4),
    )(p, total)
    return (vx, vy, vz, p, eta)


def solution(mesh):
    spec = P("gx", "gz", "gy")
    return jax.shard_map(
        local,
        mesh=mesh,
        in_specs=(spec,) * 5 + (P(),) * 3,
        out_specs=(spec,) * 5,
        check_vma=False,
    )
```
